32 devices in a mesh: group: 2 (over x), kvp: 16 (over z, y, core).
Axes of the slice: x: 2, y: 2, z: 4, core: 2. Of those that a mesh axis runs over, the one named last changes fastest.
Arguments:
- queries: bfloat16 [8, 8192], P('group'), parts along dimension 0, may hold values from -240 to 240
- key_cache: bfloat16 [1536, 64, 512], P(('group', 'kvp')), parts along dimension 0, may hold values from -6 to 6
- value_cache: bfloat16 [1536, 64, 512], P(('group', 'kvp')), parts along dimension 0, may hold values from -6 to 6
- key_scale: float32 [1536, 4], P(('group', 'kvp')), parts along dimension 0, may hold values from 0.5 to 2
- value_scale: float32 [1536, 4], P(('group', 'kvp')), parts along dimension 0, may hold values from 0.5 to 2
- page_table: int32 [8, 192], P('group', 'kvp'), parts along dimension 0, may hold values from 0 to 47, as said below
- lengths: int32 [8], P('group'), parts along dimension 0, may hold values from 9217 to 12288, as said below
- out_weight: bfloat16 [8192, 16384], P('kvp'), may hold values from -2 to 2
Outputs:
- projected: bfloat16 [8, 16384], P('group'), parts along dimension 0
The draws below stay inside these ranges and needn't reach their ends.
There are 2 independent parts, one for each index of `group`. The reference program is written for one: setup_inputs(seed, part) draws one part's arguments, and reference() takes and returns one part's arrays. A program takes and returns all parts, laid end to end along the dimension named above; an argument that names none is the same for every part. Nothing has to cross between parts.
Inputs may be any that keep to these rules, and one draw needn't show every extreme that they name: `page_table`: every kvp index's 48 slots are each used by exactly one page of one request. `lengths`: some request uses its whole cache of 12288 positions.
All inputs are finite; a program needn't handle non-finite values.
Results may differ from the reference program's by a relative error of at most 0.0064.
Values may be sent and summed in bfloat16 or wider, within the bound.
No kernel may reach another device: no remote copies, remote signals or barrier semaphores. Data moves between devices by JAX's collectives and lax.ppermute only.
A program may use at most 128 MiB of HBM per device.

```python
import math
import jax
import jax.numpy as jnp
from jax import lax

D = 16384
QH = 64
KVH = 4
HD = 128
PAGE = 64
ROWS = 4
PPD = 12
SLOTS_DEV = 48
SLOTS = 768
PAGES = 192
CTX = 12288
N_KVP = 16


def draw_queries(key, part):
    key = jax.random.fold_in(key, 1)
    first_key = jax.random.fold_in(key, 0)
    base = jnp.clip(jax.random.normal(first_key, (ROWS, QH, HD), jnp.float32), -6.0, 6.0)
    return base.reshape(ROWS, QH * HD).astype(jnp.bfloat16)


def draw_page_table(key, part):
    key = jax.random.fold_in(key, 2)
    device_keys = jax.random.split(key, N_KVP)
    shuffled = jax.vmap(lambda single: jax.random.permutation(single, SLOTS_DEV))(device_keys).astype(jnp.int32)
    shuffled = jnp.transpose(shuffled.reshape(N_KVP, ROWS, PPD), (1, 0, 2))
    return shuffled.reshape(ROWS, N_KVP * PPD).astype(jnp.int32)


def draw_lengths(key, part):
    key = jax.random.fold_in(key, 3)
    first_key, second_key = jax.random.split(key)
    shortfall = jax.random.randint(first_key, (ROWS,), 0, CTX // 4, dtype=jnp.int32)
    full_row = jax.random.randint(second_key, (), 0, ROWS, dtype=jnp.int32)
    shortfall = jnp.where(jnp.arange(ROWS, dtype=jnp.int32) == full_row, 0, shortfall)
    return (CTX - shortfall).astype(jnp.int32)


def level_of(stream_key, extent, shards, smallest, high):
    loudness, own = 1.0, jax.random.fold_in(stream_key, 6)
    for dim, shards_of in shards:
        draws = jnp.exp(jax.random.uniform(jax.random.fold_in(own, dim), (shards_of,), jnp.float32, smallest / len(shards), high / len(shards)))
        loudness = loudness * jnp.repeat(draws, extent[dim] // shards_of).reshape([-1 if axis == dim else 1 for axis in range(len(extent))])
    return loudness


def centred(own_key, dims, width, reach, cuts=(), kind=jnp.bfloat16):
    drawn = jax.random.normal(own_key, dims, jnp.float32) * width
    if len(cuts) > 0:
        drawn = level_of(own_key, dims, cuts, -0.22, 0.18) * drawn
    return jnp.clip(drawn, min=-reach, max=reach).astype(kind)


def setup_inputs(seed: int = 0, part: int = 0) -> dict:
    key_of = jax.random.split(jax.random.key(seed), 9)
    own_keys = jax.random.split(jax.random.fold_in(key_of[8], part), 9)
    queries = draw_queries(jax.random.fold_in(jax.random.fold_in(key_of[8], part), 71), part)
    key_cache = centred(own_keys[1], (SLOTS, PAGE, KVH * HD), 1.0, 6.0, ((0, 16),))
    value_cache = centred(own_keys[2], (SLOTS, PAGE, KVH * HD), 1.0, 6.0, ((0, 16),))
    key_scale = jnp.clip(jnp.exp(math.log(2.0) - 1.3862944 * jax.random.uniform(own_keys[3], (SLOTS, KVH), jnp.float32) ** level_of(own_keys[3], (SLOTS, KVH), ((0, 16),), -0.2, 0.2)), 0.5, 2.0)
    value_scale = jnp.clip(jnp.exp(math.log(2.0) - 1.3862944 * jax.random.uniform(own_keys[4], (SLOTS, KVH), jnp.float32) ** level_of(own_keys[4], (SLOTS, KVH), ((0, 16),), -0.2, 0.2)), 0.5, 2.0)
    page_table = draw_page_table(jax.random.fold_in(jax.random.fold_in(key_of[8], part), 71), part)
    lengths = draw_lengths(jax.random.fold_in(jax.random.fold_in(key_of[8], part), 71), part)
    out_weight = centred(key_of[7], (QH * HD, D), 8 ** -0.5, 2.0, ((0, 16),))
    return {"queries": queries, "key_cache": key_cache, "value_cache": value_cache, "key_scale": key_scale, "value_scale": value_scale, "page_table": page_table, "lengths": lengths, "out_weight": out_weight}


def combine_blocks(partials, maxima, totals, axis):
    highest = lax.optimization_barrier(jnp.max(maxima, axis=axis, keepdims=True))
    rescale = jnp.exp(maxima - highest)
    numerator = lax.optimization_barrier(jnp.sum(partials * rescale[..., None], axis=axis))
    denominator = lax.optimization_barrier(jnp.sum(totals * rescale, axis=axis))
    return numerator / denominator[..., None]

def row_attention(query_row, key_rows, value_rows, key_factor_rows, value_factor_rows, length):
    group_size = QH // KVH
    query = query_row.reshape(KVH, group_size, HD).astype(jnp.float32)
    page_keys = key_rows.reshape(N_KVP, PPD * PAGE, KVH, HD).astype(jnp.float32)
    page_values = value_rows.reshape(N_KVP, PPD * PAGE, KVH, HD).astype(jnp.float32)
    raw_scores = jnp.einsum('kgd,ntkd->nkgt', query, page_keys, precision=lax.Precision.HIGHEST)
    raw_scores = raw_scores.reshape(N_KVP, KVH, group_size, PPD, PAGE)
    key_factor = jnp.transpose(key_factor_rows.reshape(N_KVP, PPD, KVH), (0, 2, 1)) * (1.0 / math.sqrt(HD))
    value_factor = jnp.transpose(value_factor_rows.reshape(N_KVP, PPD, KVH), (0, 2, 1))
    scores = raw_scores * key_factor[:, :, None, :, None]
    positions = jnp.arange(PAGES * PAGE, dtype=jnp.int32).reshape(N_KVP, PPD, PAGE)
    visible = (positions < length)[:, None, None, :, :]
    maxima = lax.optimization_barrier(jnp.max(jnp.where(visible, scores, -1e+30), axis=(3, 4)))
    probs = jnp.where(visible, jnp.exp(scores - maxima[..., None, None]), 0.0)
    totals = lax.optimization_barrier(jnp.sum(probs, axis=(3, 4)))
    weights = (probs * value_factor[:, :, None, :, None]).astype(jnp.bfloat16)
    weights = weights.reshape(N_KVP, KVH, group_size, PPD * PAGE).astype(jnp.float32)
    partials = jnp.einsum('nkgt,ntkd->nkgd', weights, page_values, precision=lax.Precision.HIGHEST)
    rounded = lax.optimization_barrier(partials.astype(jnp.bfloat16)).astype(jnp.float32)
    rounded = rounded.reshape(N_KVP, QH, HD)
    return combine_blocks(rounded, maxima.reshape(N_KVP, QH), totals.reshape(N_KVP, QH), 0)

def reference(queries, key_cache, value_cache, key_scale, value_scale, page_table, lengths, out_weight):
    offsets = jnp.arange(PAGES, dtype=jnp.int32) // PPD * SLOTS_DEV
    global_slots = (page_table + offsets[None, :]).astype(jnp.int32)

    def one_row(packed):
        query_row, slots, length = packed
        return row_attention(query_row, key_cache[slots], value_cache[slots], key_scale[slots], value_scale[slots], length)
    attended = lax.map(one_row, (queries, global_slots, lengths))
    attended_rounded = attended.astype(jnp.bfloat16).reshape(ROWS, QH * HD)
    return jnp.dot(attended_rounded, out_weight, preferred_element_type=jnp.float32).astype(jnp.bfloat16)
```

```python
import functools
import math

import jax
import jax.numpy as jnp
from jax import lax
from jax.experimental import pallas as pl
from jax.experimental.pallas import tpu as pltpu
from jax.sharding import PartitionSpec as P

HD = 128
PAGE = 64
ATTEND_VMEM = 24 * 1024 * 1024
PROJECT_VMEM = 40 * 1024 * 1024


def split_two(value):
    high = value.astype(jnp.bfloat16).astype(jnp.float32)
    low = (value - high).astype(jnp.bfloat16).astype(jnp.float32)
    return high, low


def attend_kernel(
    heads_dev, table, lengths, key_scale, value_scale, queries, keys, values, packed,
    key_buf, value_buf, query_rows, staged, sems,
):
    rows, pages = table.shape
    kv_heads = key_scale.shape[0]
    heads = queries.shape[1] // HD
    group = heads // kv_heads
    devices, stacked, _ = packed.shape
    part_rows = stacked // 2
    context = pages * PAGE

    for r in range(rows):
        for which, source, target in ((0, keys, key_buf), (1, values, value_buf)):
            for p in range(pages):
                pltpu.make_async_copy(
                    source.at[table[r, p]], target.at[r, pl.ds(p * PAGE, PAGE), :], sems.at[which, r]
                ).start()

    for h in range(heads):
        query_rows[h * rows : (h + 1) * rows, :] = queries[:, h * HD : (h + 1) * HD].astype(jnp.float32)
    if part_rows > rows * heads_dev:
        staged[...] = jnp.zeros_like(staged)

    first = lax.axis_index("kvp") * context
    place = first + lax.broadcasted_iota(jnp.int32, (group, context), 1)
    lane = lax.broadcasted_iota(jnp.int32, (group, HD), 1)

    def factors(scales, r, k, times):
        columns = []
        for p in range(0, pages, 2):
            left = scales[k, table[r, p]] * times
            right = scales[k, table[r, p + 1]] * times
            columns.append(jnp.where(lane < PAGE, left, right))
        return jnp.concatenate(columns, axis=1)

    for r in range(rows):
        pltpu.make_async_copy(key_buf.at[r], key_buf.at[r], sems.at[0, r]).wait()
        visible = place < lengths[r]
        query = query_rows[pl.ds(r, heads, stride=rows), :].astype(jnp.bfloat16)
        probs = []
        stats = []
        for k in range(kv_heads):
            scores = lax.dot_general(
                query[k * group : (k + 1) * group],
                key_buf[r, :, k * HD : (k + 1) * HD],
                (((1,), (1,)), ((), ())),
                preferred_element_type=jnp.float32,
            )
            scores = scores * factors(key_scale, r, k, 1.0 / math.sqrt(HD))
            highest = jnp.max(jnp.where(visible, scores, -1e30), axis=1, keepdims=True)
            high, low = split_two(highest)
            prob = jnp.where(visible, jnp.exp(scores - (high + low)), 0.0)
            total_high, total_low = split_two(jnp.sum(prob, axis=1, keepdims=True))
            stats.append(
                jnp.where(lane == 0, high, jnp.where(lane == 1, low, jnp.where(lane == 2, total_high, total_low)))
            )
            probs.append((prob * factors(value_scale, r, k, 1.0)).astype(jnp.bfloat16))
        pltpu.make_async_copy(value_buf.at[r], value_buf.at[r], sems.at[1, r]).wait()
        for k in range(kv_heads):
            partial = jnp.dot(
                probs[k], value_buf[r, :, k * HD : (k + 1) * HD], preferred_element_type=jnp.float32
            )
            for start in range(0, group, heads_dev):
                d = (k * group + start) // heads_dev
                here = slice(r * heads_dev, (r + 1) * heads_dev)
                staged[0, d, here, :] = partial[start : start + heads_dev]
                staged[1, d, here, :] = stats[k][start : start + heads_dev]
    packed[:, :part_rows, :] = staged[0].astype(jnp.bfloat16)
    packed[:, part_rows:, :] = staged[1].astype(jnp.bfloat16)


def project_kernel(heads_dev, packed, weight, terms, weight_buf, attended, sems):
    devices, rows, width = terms.shape
    copies = []
    for d in range(devices):
        copy = pltpu.make_async_copy(weight.at[:, pl.ds(d * width, width)], weight_buf.at[d], sems.at[d])
        copy.start()
        copies.append(copy)
    part_rows = packed.shape[1] // 2
    partial = packed[:, :part_rows, :].astype(jnp.float32)
    stats = packed[:, part_rows:, :].astype(jnp.float32)
    maxima = stats[:, :, 0:1] + stats[:, :, 1:2]
    totals = stats[:, :, 2:3] + stats[:, :, 3:4]
    rescale = jnp.exp(maxima - jnp.max(maxima, axis=0, keepdims=True))
    attended[...] = jnp.sum(partial * rescale, axis=0) / jnp.sum(totals * rescale, axis=0)
    left = jnp.concatenate(
        [attended[pl.ds(j, rows, stride=heads_dev), :].astype(jnp.bfloat16) for j in range(heads_dev)], axis=1
    )
    for d in range(devices):
        copies[d].wait()
        terms[d] = jnp.dot(left, weight_buf[d], preferred_element_type=jnp.float32).astype(terms.dtype)


def body(queries, key_cache, value_cache, key_scale, value_scale, page_table, lengths, out_weight, *, devices):
    rows, pages = page_table.shape
    heads_dev = out_weight.shape[0] // HD
    heads = queries.shape[1] // HD
    features = out_weight.shape[1]
    columns = key_cache.shape[2]
    part_rows = -(-rows * heads_dev // 16) * 16
    smem = pl.BlockSpec(memory_space=pltpu.SMEM)
    vmem = pl.BlockSpec(memory_space=pltpu.VMEM)
    hbm = pl.BlockSpec(memory_space=pltpu.HBM)
    packed = pl.pallas_call(
        functools.partial(attend_kernel, heads_dev),
        out_shape=jax.ShapeDtypeStruct((devices, 2 * part_rows, HD), jnp.bfloat16),
        in_specs=[smem, smem, smem, smem, vmem, hbm, hbm],
        out_specs=vmem,
        scratch_shapes=[
            pltpu.VMEM((rows, pages * PAGE, columns), jnp.bfloat16),
            pltpu.VMEM((rows, pages * PAGE, columns), jnp.bfloat16),
            pltpu.VMEM((heads * rows, HD), jnp.float32),
            pltpu.VMEM((2, devices, part_rows, HD), jnp.float32),
            pltpu.SemaphoreType.DMA((2, rows)),
        ],
        compiler_params=pltpu.CompilerParams(vmem_limit_bytes=ATTEND_VMEM),
        cost_estimate=pl.CostEstimate(
            flops=4 * heads * rows * pages * PAGE * HD,
            bytes_accessed=4 * rows * pages * PAGE * columns,
            transcendentals=heads * rows * pages * PAGE,
        ),
        name="attend",
    )(page_table, lengths, key_scale.T, value_scale.T, queries, key_cache, value_cache)

    received = lax.all_to_all(packed, "kvp", split_axis=0, concat_axis=0, tiled=True)

    width = features // devices
    terms = pl.pallas_call(
        functools.partial(project_kernel, heads_dev),
        out_shape=jax.ShapeDtypeStruct((devices, rows, width), jnp.bfloat16),
        in_specs=[vmem, hbm],
        out_specs=vmem,
        scratch_shapes=[
            pltpu.VMEM((devices, heads_dev * HD, width), jnp.bfloat16),
            pltpu.VMEM((part_rows, HD), jnp.float32),
            pltpu.SemaphoreType.DMA((devices,)),
        ],
        compiler_params=pltpu.CompilerParams(vmem_limit_bytes=PROJECT_VMEM),
        cost_estimate=pl.CostEstimate(
            flops=2 * rows * out_weight.size, bytes_accessed=2 * out_weight.size, transcendentals=0
        ),
        name="project",
    )(received, out_weight)

    spread = lax.all_to_all(terms, "kvp", split_axis=0, concat_axis=0, tiled=True)
    mine = jnp.sum(spread.astype(jnp.float32), axis=0).astype(jnp.bfloat16)
    return lax.all_gather(mine, "kvp", axis=1, tiled=True)


def solution(mesh):
    placed = (
        P("group", None),
        P(("group", "kvp"), None, None),
        P(("group", "kvp"), None, None),
        P(("group", "kvp"), None),
        P(("group", "kvp"), None),
        P("group", "kvp"),
        P("group"),
        P("kvp", None),
    )
    return jax.shard_map(
        functools.partial(body, devices=mesh.shape["kvp"]),
        mesh=mesh,
        in_specs=placed,
        out_specs=P("group", None),
        check_vma=False,
    )
```

```python
import functools
import math

import jax
import jax.numpy as jnp
from jax import lax
from jax.experimental import pallas as pl
from jax.experimental.pallas import tpu as pltpu
from jax.sharding import PartitionSpec as P

HD = 128
PAGE = 64
ATTEND_VMEM = 24 * 1024 * 1024
PROJECT_VMEM = 40 * 1024 * 1024
SMALL_VMEM = 8 * 1024 * 1024
VMEM = pl.BlockSpec(memory_space=pltpu.VMEM)
HBM = pl.BlockSpec(memory_space=pltpu.HBM)


def split_two(value):
    high = value.astype(jnp.bfloat16).astype(jnp.float32)
    low = (value - high).astype(jnp.bfloat16).astype(jnp.float32)
    return high, low


def attend_kernel(heads_dev, devices, *refs):
    table_hbm, lengths_hbm, key_scale_hbm, value_scale_hbm, queries_hbm, keys, values = refs[:7]
    packed = refs[7 : 7 + devices]
    (table, lengths, key_scale, value_scale, queries, key_buf, value_buf, query_rows, staged, small_sems, sems) = refs[
        7 + devices :
    ]
    rows, pages = table.shape
    kv_heads = key_scale.shape[0]
    heads = queries.shape[1] // HD
    group = heads // kv_heads
    part_rows = packed[0].shape[0] // 2
    context = pages * PAGE
    pieces = sems.shape[1]
    piece = keys.shape[0] // pieces

    small = []
    for i, (source, target) in enumerate(
        (
            (table_hbm, table),
            (lengths_hbm, lengths),
            (key_scale_hbm, key_scale),
            (value_scale_hbm, value_scale),
            (queries_hbm, queries),
        )
    ):
        small.append(pltpu.make_async_copy(source, target, small_sems.at[i]))
        small[-1].start()
    large = []
    for which, source, target in ((0, keys, key_buf), (1, values, value_buf)):
        large.append([])
        for i in range(pieces):
            here = pl.ds(i * piece, piece)
            large[-1].append(pltpu.make_async_copy(source.at[here], target.at[here], sems.at[which, i]))
            large[-1][-1].start()

    if part_rows > rows * heads_dev:
        staged[...] = jnp.zeros_like(staged)
    me = lax.axis_index("kvp")
    place = me * context + lax.broadcasted_iota(jnp.int32, (group, context), 1)
    lane = lax.broadcasted_iota(jnp.int32, (group, HD), 1)
    zeros = jnp.zeros((group, HD), jnp.bfloat16)
    for copy in small:
        copy.wait()
    for h in range(heads):
        query_rows[h * rows : (h + 1) * rows, :] = queries[:, h * HD : (h + 1) * HD].astype(jnp.float32)
    for copy in large[0]:
        copy.wait()

    def factors(scales, r, k, times):
        columns = []
        for p in range(0, pages, 2):
            left = scales[k, table[r, p]] * times
            right = scales[k, table[r, p + 1]] * times
            columns.append(jnp.where(lane < PAGE, left, right))
        return jnp.concatenate(columns, axis=1)

    def pages_of(buf, r, k):
        return jnp.concatenate(
            [buf[table[r, p], :, k * HD : (k + 2) * HD] for p in range(pages)], axis=0
        )

    probs = {}
    for r in range(rows):
        visible = place < lengths[r]
        query = query_rows[pl.ds(r, heads, stride=rows), :].astype(jnp.bfloat16)
        for k in range(0, kv_heads, 2):
            left = jnp.concatenate(
                [
                    jnp.concatenate([query[k * group : (k + 1) * group], zeros], axis=1),
                    jnp.concatenate([zeros, query[(k + 1) * group : (k + 2) * group]], axis=1),
                ],
                axis=0,
            )
            both = lax.dot_general(
                left, pages_of(key_buf, r, k), (((1,), (1,)), ((), ())), preferred_element_type=jnp.float32
            )
            weights = []
            for i in (0, 1):
                scores = both[i * group : (i + 1) * group] * factors(key_scale, r, k + i, 1.0 / math.sqrt(HD))
                highest = jnp.max(jnp.where(visible, scores, -1e30), axis=1, keepdims=True)
                high, low = split_two(highest)
                prob = jnp.where(visible, jnp.exp(scores - (high + low)), 0.0)
                total_high, total_low = split_two(jnp.sum(prob, axis=1, keepdims=True))
                stats = jnp.where(lane == 0, high, jnp.where(lane == 1, low, jnp.where(lane == 2, total_high, total_low)))
                for start in range(0, group, heads_dev):
                    d = ((k + i) * group + start) // heads_dev
                    staged[1, d, r * heads_dev : (r + 1) * heads_dev, :] = stats[start : start + heads_dev]
                weights.append((prob * factors(value_scale, r, k + i, 1.0)).astype(jnp.bfloat16))
            probs[r, k] = jnp.concatenate(weights, axis=0)
    for copy in large[1]:
        copy.wait()
    for r in range(rows):
        for k in range(0, kv_heads, 2):
            both = jnp.dot(probs[r, k], pages_of(value_buf, r, k), preferred_element_type=jnp.float32)
            for i in (0, 1):
                partial = both[i * group : (i + 1) * group, i * HD : (i + 1) * HD]
                for start in range(0, group, heads_dev):
                    d = ((k + i) * group + start) // heads_dev
                    staged[0, d, r * heads_dev : (r + 1) * heads_dev, :] = partial[start : start + heads_dev]
    for x in range(devices):
        other = jnp.bitwise_xor(me, x)
        packed[x][:part_rows, :] = staged[0, other].astype(jnp.bfloat16)
        packed[x][part_rows:, :] = staged[1, other].astype(jnp.bfloat16)


def project_kernel(heads_dev, devices, *refs):
    packed = refs[:devices]
    weight = refs[devices]
    outs = refs[devices + 1 : -3]
    weight_buf, attended, sems = refs[-3:]
    _, rows, width = outs[0].shape
    per_out = outs[0].shape[0]
    me = lax.axis_index("kvp")
    copies = []
    for x in range(devices):
        other = jnp.bitwise_xor(me, x)
        start = pl.multiple_of(other * width, width)
        copy = pltpu.make_async_copy(weight.at[:, pl.ds(start, width)], weight_buf.at[x], sems.at[x])
        copy.start()
        copies.append(copy)
    part_rows = packed[0].shape[0] // 2
    partials = [ref[:part_rows, :].astype(jnp.float32) for ref in packed]
    stats = [ref[part_rows:, :].astype(jnp.float32) for ref in packed]
    maxima = [s[:, 0:1] + s[:, 1:2] for s in stats]
    totals = [s[:, 2:3] + s[:, 3:4] for s in stats]
    highest = functools.reduce(jnp.maximum, maxima)
    rescale = [jnp.exp(m - highest) for m in maxima]
    numerator = sum(p * e for p, e in zip(partials, rescale))
    denominator = sum(t * e for t, e in zip(totals, rescale))
    attended[...] = numerator / denominator
    left = jnp.concatenate(
        [attended[pl.ds(j, rows, stride=heads_dev), :].astype(jnp.bfloat16) for j in range(heads_dev)], axis=1
    )
    for x in reversed(range(devices)):
        copies[x].wait()
        terms = jnp.dot(left, weight_buf[x], preferred_element_type=jnp.float32)
        outs[x // per_out][x % per_out] = terms.astype(jnp.bfloat16)


def add_kernel(outs_of, *refs):
    terms, outs = refs[:-outs_of], refs[-outs_of:]
    per_out = outs[0].shape[0]
    for i, out in enumerate(outs):
        here = slice(i * per_out, (i + 1) * per_out)
        out[...] = sum(term[here].astype(jnp.float32) for term in terms).astype(out.dtype)


def lay_kernel(devices, *refs):
    parts, out = refs[:-1], refs[-1]
    me = lax.axis_index("kvp")
    per_part = parts[0].shape[0]
    width = parts[0].shape[2]
    for x in range(devices):
        start = pl.multiple_of(jnp.bitwise_xor(me, x) * width, width)
        out[:, pl.ds(start, width)] = parts[x // per_part][x % per_part]


def exchange(array, partner, devices):
    return lax.ppermute(array, "kvp", [(i, i ^ partner) for i in range(devices)])


def in_hbm(array):
    return pltpu.with_memory_space_constraint(array, pltpu.HBM)


def body(queries, key_cache, value_cache, key_scale, value_scale, page_table, lengths, out_weight, *, devices):
    rows, pages = page_table.shape
    slots, _, columns = key_cache.shape
    kv_heads = key_scale.shape[1]
    heads_dev = out_weight.shape[0] // HD
    heads = queries.shape[1] // HD
    features = out_weight.shape[1]
    part_rows = -(-rows * heads_dev // 16) * 16
    width = features // devices
    inner = 4
    outer = devices // inner
    packed = pl.pallas_call(
        functools.partial(attend_kernel, heads_dev, devices),
        out_shape=[jax.ShapeDtypeStruct((2 * part_rows, HD), jnp.bfloat16)] * devices,
        in_specs=[HBM] * 7,
        out_specs=[VMEM] * devices,
        scratch_shapes=[
            pltpu.SMEM((rows, pages), jnp.int32),
            pltpu.SMEM((rows,), jnp.int32),
            pltpu.SMEM((kv_heads, slots), jnp.float32),
            pltpu.SMEM((kv_heads, slots), jnp.float32),
            pltpu.VMEM((rows, heads * HD), jnp.bfloat16),
            pltpu.VMEM((slots, PAGE, columns), jnp.bfloat16),
            pltpu.VMEM((slots, PAGE, columns), jnp.bfloat16),
            pltpu.VMEM((heads * rows, HD), jnp.float32),
            pltpu.VMEM((2, devices, part_rows, HD), jnp.float32),
            pltpu.SemaphoreType.DMA((5,)),
            pltpu.SemaphoreType.DMA((2, 4)),
        ],
        compiler_params=pltpu.CompilerParams(vmem_limit_bytes=ATTEND_VMEM),
        cost_estimate=pl.CostEstimate(
            flops=4 * heads * rows * pages * PAGE * HD,
            bytes_accessed=4 * rows * pages * PAGE * columns,
            transcendentals=heads * rows * pages * PAGE,
        ),
        name="attend",
    )(*[in_hbm(a) for a in (page_table, lengths, key_scale.T, value_scale.T, queries, key_cache, value_cache)])

    received = [packed[0]] + [exchange(packed[x], x, devices) for x in range(1, devices)]

    terms = pl.pallas_call(
        functools.partial(project_kernel, heads_dev, devices),
        out_shape=[jax.ShapeDtypeStruct((inner, rows, width), jnp.bfloat16)] * outer,
        in_specs=[VMEM] * devices + [HBM],
        out_specs=[VMEM] * outer,
        scratch_shapes=[
            pltpu.VMEM((devices, heads_dev * HD, width), jnp.bfloat16),
            pltpu.VMEM((part_rows, HD), jnp.float32),
            pltpu.SemaphoreType.DMA((devices,)),
        ],
        compiler_params=pltpu.CompilerParams(vmem_limit_bytes=PROJECT_VMEM),
        cost_estimate=pl.CostEstimate(
            flops=2 * rows * out_weight.size, bytes_accessed=2 * out_weight.size, transcendentals=0
        ),
        name="project",
    )(*received, in_hbm(out_weight))

    small = pltpu.CompilerParams(vmem_limit_bytes=SMALL_VMEM)
    arrived = [terms[0]] + [exchange(terms[i], i * inner, devices) for i in range(1, outer)]
    quarters = pl.pallas_call(
        functools.partial(add_kernel, inner),
        out_shape=[jax.ShapeDtypeStruct((1, rows, width), jnp.bfloat16)] * inner,
        in_specs=[VMEM] * outer,
        out_specs=[VMEM] * inner,
        compiler_params=small,
        name="add_outer",
    )(*arrived)
    arrived = [quarters[0]] + [exchange(quarters[i], i, devices) for i in range(1, inner)]
    mine = pl.pallas_call(
        functools.partial(add_kernel, 1),
        out_shape=[jax.ShapeDtypeStruct((1, rows, width), jnp.bfloat16)],
        in_specs=[VMEM] * inner,
        out_specs=[VMEM],
        compiler_params=small,
        name="add_inner",
    )(*arrived)[0]
    near = jnp.concatenate([mine] + [exchange(mine, i, devices) for i in range(1, inner)], axis=0)
    parts = [near] + [exchange(near, i * inner, devices) for i in range(1, outer)]
    return pl.pallas_call(
        functools.partial(lay_kernel, devices),
        out_shape=jax.ShapeDtypeStruct((rows, features), jnp.bfloat16),
        in_specs=[VMEM] * outer,
        out_specs=VMEM,
        compiler_params=small,
        name="lay",
    )(*parts)


def solution(mesh):
    placed = (
        P("group", None),
        P(("group", "kvp"), None, None),
        P(("group", "kvp"), None, None),
        P(("group", "kvp"), None),
        P(("group", "kvp"), None),
        P("group", "kvp"),
        P("group"),
        P("kvp", None),
    )
    return jax.shard_map(
        functools.partial(body, devices=mesh.shape["kvp"]),
        mesh=mesh,
        in_specs=placed,
        out_specs=P("group", None),
        check_vma=False,
    )
```

```python
import functools
import math

import jax
import jax.numpy as jnp
from jax import lax
from jax.experimental import pallas as pl
from jax.experimental.pallas import tpu as pltpu
from jax.sharding import PartitionSpec as P

HD = 128
PAGE = 64
ATTEND_VMEM = 24 * 1024 * 1024
PROJECT_VMEM = 40 * 1024 * 1024
WEIGHT_PIECES = 16
SMALL_VMEM = 8 * 1024 * 1024
VMEM = pl.BlockSpec(memory_space=pltpu.VMEM)
HBM = pl.BlockSpec(memory_space=pltpu.HBM)


def split_two(value):
    high = value.astype(jnp.bfloat16).astype(jnp.float32)
    low = (value - high).astype(jnp.bfloat16).astype(jnp.float32)
    return high, low


def attend_kernel(heads_dev, devices, *refs):
    table_hbm, lengths_hbm, key_scale_hbm, value_scale_hbm, queries_hbm, keys, values = refs[:7]
    (packed, table, lengths, key_scale, value_scale, queries, key_buf, value_buf, query_rows, staged, small_sems, sems) = refs[7:]
    rows, pages = table.shape
    kv_heads = key_scale.shape[0]
    heads = queries.shape[1] // HD
    group = heads // kv_heads
    part_rows = rows * heads_dev
    context = pages * PAGE
    pieces = sems.shape[1]
    piece = keys.shape[0] // pieces

    small = []
    for i, (source, target) in enumerate(
        (
            (table_hbm, table),
            (lengths_hbm, lengths),
            (key_scale_hbm, key_scale),
            (value_scale_hbm, value_scale),
            (queries_hbm, queries),
        )
    ):
        small.append(pltpu.make_async_copy(source, target, small_sems.at[i]))
        small[-1].start()
    large = []
    for which, source, target in ((0, keys, key_buf), (1, values, value_buf)):
        large.append([])
        for i in range(pieces):
            here = pl.ds(i * piece, piece)
            large[-1].append(pltpu.make_async_copy(source.at[here], target.at[here], sems.at[which, i]))
            large[-1][-1].start()

    staged[:, part_rows:, :] = jnp.zeros((devices, staged.shape[1] - part_rows, HD), jnp.float32)
    me = lax.axis_index("kvp")
    place = me * context + lax.broadcasted_iota(jnp.int32, (group, context), 1)
    lane = lax.broadcasted_iota(jnp.int32, (group, HD), 1)
    zeros = jnp.zeros((group, HD), jnp.bfloat16)
    for copy in small:
        copy.wait()
    for h in range(heads):
        query_rows[h * rows : (h + 1) * rows, :] = queries[:, h * HD : (h + 1) * HD].astype(jnp.float32)
    for copy in large[0]:
        copy.wait()

    def factors(scales, r, k, times):
        columns = []
        for p in range(0, pages, 2):
            left = scales[k, table[r, p]] * times
            right = scales[k, table[r, p + 1]] * times
            columns.append(jnp.where(lane < PAGE, left, right))
        return jnp.concatenate(columns, axis=1)

    def pages_of(buf, r, k):
        return jnp.concatenate(
            [buf[table[r, p], :, k * HD : (k + 2) * HD] for p in range(pages)], axis=0
        )

    probs = {}
    stats = [jnp.zeros((group, HD), jnp.float32)] * kv_heads
    for r in range(rows):
        visible = place < lengths[r]
        query = query_rows[pl.ds(r, heads, stride=rows), :].astype(jnp.bfloat16)
        for k in range(0, kv_heads, 2):
            left = jnp.concatenate(
                [
                    jnp.concatenate([query[k * group : (k + 1) * group], zeros], axis=1),
                    jnp.concatenate([zeros, query[(k + 1) * group : (k + 2) * group]], axis=1),
                ],
                axis=0,
            )
            both = lax.dot_general(
                left, pages_of(key_buf, r, k), (((1,), (1,)), ((), ())), preferred_element_type=jnp.float32
            )
            weights = []
            for i in (0, 1):
                scores = both[i * group : (i + 1) * group] * factors(key_scale, r, k + i, 1.0 / math.sqrt(HD))
                highest = jnp.max(jnp.where(visible, scores, -1e30), axis=1, keepdims=True)
                high, low = split_two(highest)
                prob = jnp.where(visible, jnp.exp(scores - (high + low)), 0.0)
                total_high, total_low = split_two(jnp.sum(prob, axis=1, keepdims=True))
                for at, value in enumerate((high, low, total_high, total_low)):
                    stats[k + i] = jnp.where(lane == 4 * r + at, value, stats[k + i])
                weights.append((prob * factors(value_scale, r, k + i, 1.0)).astype(jnp.bfloat16))
            probs[r, k] = jnp.concatenate(weights, axis=0)
    for copy in large[1]:
        copy.wait()
    for r in range(rows):
        for k in range(0, kv_heads, 2):
            both = jnp.dot(probs[r, k], pages_of(value_buf, r, k), preferred_element_type=jnp.float32)
            for i in (0, 1):
                partial = both[i * group : (i + 1) * group, i * HD : (i + 1) * HD]
                for start in range(0, group, heads_dev):
                    d = ((k + i) * group + start) // heads_dev
                    staged[d, r * heads_dev : (r + 1) * heads_dev, :] = partial[start : start + heads_dev]
    for k in range(kv_heads):
        for start in range(0, group, heads_dev):
            d = (k * group + start) // heads_dev
            staged[d, part_rows : part_rows + heads_dev, :] = stats[k][start : start + heads_dev]
    packed[...] = staged[...].astype(jnp.bfloat16)


def project_kernel(heads_dev, packed, weight, *refs):
    outs, (weight_buf, attended, sems) = refs[:-3], refs[-3:]
    rows, part = outs[0].shape
    pieces, _, width = weight_buf.shape
    per_out = pieces // len(outs)
    quarter = lax.rem(lax.axis_index("kvp"), len(outs))
    copies = []
    for piece in range(pieces):
        start = jnp.bitwise_xor(quarter, piece // per_out) * part + piece % per_out * width
        source = weight.at[:, pl.ds(pl.multiple_of(start, width), width)]
        copies.append(pltpu.make_async_copy(source, weight_buf.at[piece], sems.at[piece]))
        copies[-1].start()
    blocks = packed[...].astype(jnp.float32)
    stats = blocks[:, rows * heads_dev : (rows + 1) * heads_dev, :]
    for r in range(rows):
        partial = blocks[:, r * heads_dev : (r + 1) * heads_dev, :]
        maxima = stats[:, :, 4 * r : 4 * r + 1] + stats[:, :, 4 * r + 1 : 4 * r + 2]
        totals = stats[:, :, 4 * r + 2 : 4 * r + 3] + stats[:, :, 4 * r + 3 : 4 * r + 4]
        rescale = jnp.exp(maxima - jnp.max(maxima, axis=0, keepdims=True))
        attended[r * heads_dev : (r + 1) * heads_dev, :] = jnp.sum(partial * rescale, axis=0) / jnp.sum(
            totals * rescale, axis=0
        )
    left = jnp.concatenate(
        [attended[pl.ds(j, rows, stride=heads_dev), :].astype(jnp.bfloat16) for j in range(heads_dev)], axis=1
    )
    for piece in range(pieces):
        copies[piece].wait()
        terms = jnp.dot(left, weight_buf[piece], preferred_element_type=jnp.float32)
        at = piece % per_out * width
        outs[piece // per_out][:, at : at + width] = terms.astype(jnp.bfloat16)


def add_kernel(*refs):
    terms = [ref[...].astype(jnp.float32) for ref in refs[:-1]]
    while len(terms) > 1:
        terms = [terms[i] + terms[i + 1] for i in range(0, len(terms), 2)]
    refs[-1][...] = terms[0].astype(refs[-1].dtype)


def lay_kernel(*refs):
    parts, out = refs[:-1], refs[-1]
    quarter = lax.rem(lax.axis_index("kvp"), len(parts))
    width = parts[0].shape[1]
    for x, part in enumerate(parts):
        start = pl.multiple_of(jnp.bitwise_xor(quarter, x) * width, width)
        out[:, pl.ds(start, width)] = part[...]


def exchange(array, partner, devices):
    return lax.ppermute(array, "kvp", [(i, i ^ partner) for i in range(devices)])


def in_hbm(array):
    return pltpu.with_memory_space_constraint(array, pltpu.HBM)


def body(queries, key_cache, value_cache, key_scale, value_scale, page_table, lengths, out_weight, *, devices):
    rows, pages = page_table.shape
    slots, _, columns = key_cache.shape
    kv_heads = key_scale.shape[1]
    heads_dev = out_weight.shape[0] // HD
    heads = queries.shape[1] // HD
    features = out_weight.shape[1]
    chunk = -(-(rows + 1) * heads_dev // 8) * 8
    inner = 4
    outer = devices // inner
    part = features // inner
    packed = pl.pallas_call(
        functools.partial(attend_kernel, heads_dev, devices),
        out_shape=jax.ShapeDtypeStruct((devices, chunk, HD), jnp.bfloat16),
        in_specs=[HBM] * 7,
        out_specs=VMEM,
        scratch_shapes=[
            pltpu.SMEM((rows, pages), jnp.int32),
            pltpu.SMEM((rows,), jnp.int32),
            pltpu.SMEM((kv_heads, slots), jnp.float32),
            pltpu.SMEM((kv_heads, slots), jnp.float32),
            pltpu.VMEM((rows, heads * HD), jnp.bfloat16),
            pltpu.VMEM((slots, PAGE, columns), jnp.bfloat16),
            pltpu.VMEM((slots, PAGE, columns), jnp.bfloat16),
            pltpu.VMEM((heads * rows, HD), jnp.float32),
            pltpu.VMEM((devices, chunk, HD), jnp.float32),
            pltpu.SemaphoreType.DMA((5,)),
            pltpu.SemaphoreType.DMA((2, 4)),
        ],
        compiler_params=pltpu.CompilerParams(vmem_limit_bytes=ATTEND_VMEM),
        cost_estimate=pl.CostEstimate(
            flops=4 * heads * rows * pages * PAGE * HD,
            bytes_accessed=4 * rows * pages * PAGE * columns,
            transcendentals=heads * rows * pages * PAGE,
        ),
        name="attend",
    )(*[in_hbm(a) for a in (page_table, lengths, key_scale.T, value_scale.T, queries, key_cache, value_cache)])

    received = lax.all_to_all(packed, "kvp", split_axis=0, concat_axis=0, tiled=True)

    terms = pl.pallas_call(
        functools.partial(project_kernel, heads_dev),
        out_shape=[jax.ShapeDtypeStruct((rows, part), jnp.bfloat16)] * inner,
        in_specs=[VMEM, HBM],
        out_specs=[VMEM] * inner,
        scratch_shapes=[
            pltpu.VMEM((WEIGHT_PIECES, heads_dev * HD, features // WEIGHT_PIECES), jnp.bfloat16),
            pltpu.VMEM((rows * heads_dev, HD), jnp.float32),
            pltpu.SemaphoreType.DMA((WEIGHT_PIECES,)),
        ],
        compiler_params=pltpu.CompilerParams(vmem_limit_bytes=PROJECT_VMEM),
        cost_estimate=pl.CostEstimate(
            flops=2 * rows * out_weight.size, bytes_accessed=2 * out_weight.size, transcendentals=0
        ),
        name="project",
    )(received, in_hbm(out_weight))

    def add(terms, name):
        return pl.pallas_call(
            add_kernel,
            out_shape=jax.ShapeDtypeStruct((rows, part), jnp.bfloat16),
            in_specs=[VMEM] * len(terms),
            out_specs=VMEM,
            compiler_params=pltpu.CompilerParams(vmem_limit_bytes=SMALL_VMEM),
            name=name,
        )(*terms)

    mine = add([terms[0]] + [exchange(terms[x], x, devices) for x in range(1, inner)], "add_near")
    mine = add([mine] + [exchange(mine, x * inner, devices) for x in range(1, outer)], "add_far")
    parts = [mine] + [exchange(mine, x, devices) for x in range(1, inner)]
    return pl.pallas_call(
        lay_kernel,
        out_shape=jax.ShapeDtypeStruct((rows, features), jnp.bfloat16),
        in_specs=[VMEM] * inner,
        out_specs=VMEM,
        compiler_params=pltpu.CompilerParams(vmem_limit_bytes=SMALL_VMEM),
        name="lay",
    )(*parts)


def solution(mesh):
    placed = (
        P("group", None),
        P(("group", "kvp"), None, None),
        P(("group", "kvp"), None, None),
        P(("group", "kvp"), None),
        P(("group", "kvp"), None),
        P("group", "kvp"),
        P("group"),
        P("kvp", None),
    )
    return jax.shard_map(
        functools.partial(body, devices=mesh.shape["kvp"]),
        mesh=mesh,
        in_specs=placed,
        out_specs=P("group", None),
        check_vma=False,
    )
```

```python
import functools
import math

import jax
import jax.numpy as jnp
from jax import lax
from jax.experimental import pallas as pl
from jax.experimental.pallas import tpu as pltpu
from jax.sharding import PartitionSpec as P

HD = 128
PAGE = 64
ATTEND_VMEM = 24 * 1024 * 1024
WEIGHT_PIECES = 8
SMALL_VMEM = 8 * 1024 * 1024
VMEM = pl.BlockSpec(memory_space=pltpu.VMEM)
HBM = pl.BlockSpec(memory_space=pltpu.HBM)
ANY = pl.BlockSpec(memory_space=pl.ANY)


def split_two(value):
    high = value.astype(jnp.bfloat16).astype(jnp.float32)
    low = (value - high).astype(jnp.bfloat16).astype(jnp.float32)
    return high, low


def attend_kernel(heads_dev, devices, *refs):
    table_hbm, lengths_hbm, key_scale_hbm, value_scale_hbm, queries_hbm, keys, values = refs[:7]
    (packed, table, lengths, key_scale, value_scale, queries, key_buf, value_buf, query_rows, staged, small_sems, sems) = refs[7:]
    rows, pages = table.shape
    kv_heads = key_scale.shape[0]
    heads = queries.shape[1] // HD
    group = heads // kv_heads
    part_rows = rows * heads_dev
    context = pages * PAGE
    pieces = sems.shape[1]
    piece = keys.shape[0] // pieces

    small = []
    for i, (source, target) in enumerate(
        (
            (table_hbm, table),
            (lengths_hbm, lengths),
            (key_scale_hbm, key_scale),
            (value_scale_hbm, value_scale),
            (queries_hbm, queries),
        )
    ):
        small.append(pltpu.make_async_copy(source, target, small_sems.at[i]))
        small[-1].start()
    large = []
    for which, source, target in ((0, keys, key_buf), (1, values, value_buf)):
        large.append([])
        for i in range(pieces):
            here = pl.ds(i * piece, piece)
            large[-1].append(pltpu.make_async_copy(source.at[here], target.at[here], sems.at[which, i]))
            large[-1][-1].start()

    staged[:, part_rows:, :] = jnp.zeros((devices, staged.shape[1] - part_rows, HD), jnp.float32)
    me = lax.axis_index("kvp")
    place = me * context + lax.broadcasted_iota(jnp.int32, (group, context), 1)
    lane = lax.broadcasted_iota(jnp.int32, (group, HD), 1)
    zeros = jnp.zeros((group, HD), jnp.bfloat16)
    for copy in small:
        copy.wait()
    for h in range(heads):
        query_rows[h * rows : (h + 1) * rows, :] = queries[:, h * HD : (h + 1) * HD].astype(jnp.float32)
    for copy in large[0]:
        copy.wait()

    def factors(scales, r, k, times):
        columns = []
        for p in range(0, pages, 2):
            left = scales[k, table[r, p]] * times
            right = scales[k, table[r, p + 1]] * times
            columns.append(jnp.where(lane < PAGE, left, right))
        return jnp.concatenate(columns, axis=1)

    def pages_of(buf, r, k):
        return jnp.concatenate(
            [buf[table[r, p], :, k * HD : (k + 2) * HD] for p in range(pages)], axis=0
        )

    probs = {}
    stats = [jnp.zeros((group, HD), jnp.float32)] * kv_heads
    for r in range(rows):
        visible = place < lengths[r]
        query = query_rows[pl.ds(r, heads, stride=rows), :].astype(jnp.bfloat16)
        for k in range(0, kv_heads, 2):
            left = jnp.concatenate(
                [
                    jnp.concatenate([query[k * group : (k + 1) * group], zeros], axis=1),
                    jnp.concatenate([zeros, query[(k + 1) * group : (k + 2) * group]], axis=1),
                ],
                axis=0,
            )
            both = lax.dot_general(
                left, pages_of(key_buf, r, k), (((1,), (1,)), ((), ())), preferred_element_type=jnp.float32
            )
            weights = []
            for i in (0, 1):
                scores = both[i * group : (i + 1) * group] * factors(key_scale, r, k + i, 1.0 / math.sqrt(HD))
                highest = jnp.max(jnp.where(visible, scores, -1e30), axis=1, keepdims=True)
                high, low = split_two(highest)
                prob = jnp.where(visible, jnp.exp(scores - (high + low)), 0.0)
                total_high, total_low = split_two(jnp.sum(prob, axis=1, keepdims=True))
                for at, value in enumerate((high, low, total_high, total_low)):
                    stats[k + i] = jnp.where(lane == 4 * r + at, value, stats[k + i])
                weights.append((prob * factors(value_scale, r, k + i, 1.0)).astype(jnp.bfloat16))
            probs[r, k] = jnp.concatenate(weights, axis=0)
    for copy in large[1]:
        copy.wait()
    for r in range(rows):
        for k in range(0, kv_heads, 2):
            both = jnp.dot(probs[r, k], pages_of(value_buf, r, k), preferred_element_type=jnp.float32)
            for i in (0, 1):
                partial = both[i * group : (i + 1) * group, i * HD : (i + 1) * HD]
                for start in range(0, group, heads_dev):
                    d = ((k + i) * group + start) // heads_dev
                    staged[d, r * heads_dev : (r + 1) * heads_dev, :] = partial[start : start + heads_dev]
    for k in range(kv_heads):
        for start in range(0, group, heads_dev):
            d = (k * group + start) // heads_dev
            staged[d, part_rows : part_rows + heads_dev, :] = stats[k][start : start + heads_dev]
    packed[...] = staged[...].astype(jnp.bfloat16)


def fetch_kernel(parts, _, weight, buf, sems):
    pieces, _, width = buf.shape
    per_part = pieces // parts
    quarter = lax.rem(lax.axis_index("kvp"), parts)
    copies = []
    for piece in range(pieces):
        start = (jnp.bitwise_xor(quarter, piece // per_part) * per_part + piece % per_part) * width
        source = weight.at[:, pl.ds(pl.multiple_of(start, width), width)]
        copies.append(pltpu.make_async_copy(source, buf.at[piece], sems.at[piece]))
        copies[-1].start()
    for copy in copies:
        copy.wait()


def project_kernel(heads_dev, packed, weight, left, *refs):
    outs, attended = refs[:-1], refs[-1]
    rows = left.shape[0]
    width = weight.shape[2]
    per_out = weight.shape[0] // (len(outs) + 1)
    blocks = packed[...].astype(jnp.float32)
    stats = blocks[:, rows * heads_dev : (rows + 1) * heads_dev, :]
    for r in range(rows):
        partial = blocks[:, r * heads_dev : (r + 1) * heads_dev, :]
        maxima = stats[:, :, 4 * r : 4 * r + 1] + stats[:, :, 4 * r + 1 : 4 * r + 2]
        totals = stats[:, :, 4 * r + 2 : 4 * r + 3] + stats[:, :, 4 * r + 3 : 4 * r + 4]
        rescale = jnp.exp(maxima - jnp.max(maxima, axis=0, keepdims=True))
        attended[r * heads_dev : (r + 1) * heads_dev, :] = jnp.sum(partial * rescale, axis=0) / jnp.sum(
            totals * rescale, axis=0
        )
    rounded = jnp.concatenate(
        [attended[pl.ds(j, rows, stride=heads_dev), :].astype(jnp.bfloat16) for j in range(heads_dev)], axis=1
    )
    left[...] = rounded
    for x, out in enumerate(outs):
        for i in range(per_out):
            terms = jnp.dot(rounded, weight[(x + 1) * per_out + i], preferred_element_type=jnp.float32)
            out[:, i * width : (i + 1) * width] = terms.astype(jnp.bfloat16)


def project_own_kernel(left, weight, out):
    width = weight.shape[2]
    for i in range(out.shape[1] // width):
        terms = jnp.dot(left[...], weight[i], preferred_element_type=jnp.float32)
        out[:, i * width : (i + 1) * width] = terms.astype(jnp.bfloat16)


def add_kernel(*refs):
    terms = [ref[...].astype(jnp.float32) for ref in refs[:-1]]
    while len(terms) > 1:
        terms = [terms[i] + terms[i + 1] for i in range(0, len(terms), 2)]
    refs[-1][...] = terms[0].astype(refs[-1].dtype)


def lay_kernel(*refs):
    parts, out = refs[:-1], refs[-1]
    quarter = lax.rem(lax.axis_index("kvp"), len(parts))
    width = parts[0].shape[1]
    for x, part in enumerate(parts):
        start = pl.multiple_of(jnp.bitwise_xor(quarter, x) * width, width)
        out[:, pl.ds(start, width)] = part[...]


def exchange(array, partner, devices):
    return lax.ppermute(array, "kvp", [(i, i ^ partner) for i in range(devices)])


def in_hbm(array):
    return pltpu.with_memory_space_constraint(array, pltpu.HBM)


def body(queries, key_cache, value_cache, key_scale, value_scale, page_table, lengths, out_weight, *, devices):
    rows, pages = page_table.shape
    slots, _, columns = key_cache.shape
    kv_heads = key_scale.shape[1]
    heads_dev = out_weight.shape[0] // HD
    heads = queries.shape[1] // HD
    features = out_weight.shape[1]
    chunk = -(-(rows + 1) * heads_dev // 8) * 8
    inner = 4
    outer = devices // inner
    part = features // inner
    packed = pl.pallas_call(
        functools.partial(attend_kernel, heads_dev, devices),
        out_shape=jax.ShapeDtypeStruct((devices, chunk, HD), jnp.bfloat16),
        in_specs=[HBM] * 7,
        out_specs=VMEM,
        scratch_shapes=[
            pltpu.SMEM((rows, pages), jnp.int32),
            pltpu.SMEM((rows,), jnp.int32),
            pltpu.SMEM((kv_heads, slots), jnp.float32),
            pltpu.SMEM((kv_heads, slots), jnp.float32),
            pltpu.VMEM((rows, heads * HD), jnp.bfloat16),
            pltpu.VMEM((slots, PAGE, columns), jnp.bfloat16),
            pltpu.VMEM((slots, PAGE, columns), jnp.bfloat16),
            pltpu.VMEM((heads * rows, HD), jnp.float32),
            pltpu.VMEM((devices, chunk, HD), jnp.float32),
            pltpu.SemaphoreType.DMA((5,)),
            pltpu.SemaphoreType.DMA((2, 4)),
        ],
        compiler_params=pltpu.CompilerParams(vmem_limit_bytes=ATTEND_VMEM),
        cost_estimate=pl.CostEstimate(
            flops=4 * heads * rows * pages * PAGE * HD,
            bytes_accessed=4 * rows * pages * PAGE * columns,
            transcendentals=heads * rows * pages * PAGE,
        ),
        name="attend",
    )(*[in_hbm(a) for a in (page_table, lengths, key_scale.T, value_scale.T, queries, key_cache, value_cache)])

    received = lax.all_to_all(packed, "kvp", split_axis=0, concat_axis=0, tiled=True)

    depth = heads_dev * HD
    width = features // WEIGHT_PIECES
    fetched = pl.pallas_call(
        functools.partial(fetch_kernel, inner),
        out_shape=pltpu.VMEM((WEIGHT_PIECES, depth, width), jnp.bfloat16),
        in_specs=[ANY, HBM],
        out_specs=VMEM,
        scratch_shapes=[pltpu.SemaphoreType.DMA((WEIGHT_PIECES,))],
        compiler_params=pltpu.CompilerParams(vmem_limit_bytes=SMALL_VMEM),
        cost_estimate=pl.CostEstimate(flops=0, bytes_accessed=2 * out_weight.size, transcendentals=0),
        name="fetch",
    )(packed, in_hbm(out_weight))

    left, *others = pl.pallas_call(
        functools.partial(project_kernel, heads_dev),
        out_shape=[jax.ShapeDtypeStruct((rows, depth), jnp.bfloat16)]
        + [jax.ShapeDtypeStruct((rows, part), jnp.bfloat16)] * (inner - 1),
        in_specs=[VMEM, VMEM],
        out_specs=[VMEM] * inner,
        scratch_shapes=[pltpu.VMEM((rows * heads_dev, HD), jnp.float32)],
        compiler_params=pltpu.CompilerParams(vmem_limit_bytes=SMALL_VMEM),
        cost_estimate=pl.CostEstimate(
            flops=2 * rows * depth * part * (inner - 1),
            bytes_accessed=2 * depth * part * (inner - 1),
            transcendentals=0,
        ),
        name="project_others",
    )(received, fetched)
    sent = [exchange(others[x - 1], x, devices) for x in range(1, inner)]
    own = pl.pallas_call(
        project_own_kernel,
        out_shape=jax.ShapeDtypeStruct((rows, part), jnp.bfloat16),
        in_specs=[VMEM, VMEM],
        out_specs=VMEM,
        compiler_params=pltpu.CompilerParams(vmem_limit_bytes=SMALL_VMEM),
        cost_estimate=pl.CostEstimate(
            flops=2 * rows * depth * part, bytes_accessed=2 * depth * part, transcendentals=0
        ),
        name="project_own",
    )(left, fetched)

    def add(terms, name):
        return pl.pallas_call(
            add_kernel,
            out_shape=jax.ShapeDtypeStruct((rows, part), jnp.bfloat16),
            in_specs=[VMEM] * len(terms),
            out_specs=VMEM,
            compiler_params=pltpu.CompilerParams(vmem_limit_bytes=SMALL_VMEM),
            name=name,
        )(*terms)

    mine = add([own] + sent, "add_near")
    mine = add([mine] + [exchange(mine, x * inner, devices) for x in range(1, outer)], "add_far")
    parts = [mine] + [exchange(mine, x, devices) for x in range(1, inner)]
    return pl.pallas_call(
        lay_kernel,
        out_shape=jax.ShapeDtypeStruct((rows, features), jnp.bfloat16),
        in_specs=[VMEM] * inner,
        out_specs=VMEM,
        compiler_params=pltpu.CompilerParams(vmem_limit_bytes=SMALL_VMEM),
        name="lay",
    )(*parts)


def solution(mesh):
    placed = (
        P("group", None),
        P(("group", "kvp"), None, None),
        P(("group", "kvp"), None, None),
        P(("group", "kvp"), None),
        P(("group", "kvp"), None),
        P("group", "kvp"),
        P("group"),
        P("kvp", None),
    )
    return jax.shard_map(
        functools.partial(body, devices=mesh.shape["kvp"]),
        mesh=mesh,
        in_specs=placed,
        out_specs=P("group", None),
        check_vma=False,
    )
```

```python
import functools
import math

import jax
import jax.numpy as jnp
from jax import lax
from jax.experimental import pallas as pl
from jax.experimental.pallas import tpu as pltpu
from jax.sharding import PartitionSpec as P

HD = 128
PAGE = 64
ATTEND_VMEM = 24 * 1024 * 1024
PROJECT_VMEM = 12 * 1024 * 1024
WEIGHT_PIECES = 16
FETCHED_PIECES = 6
SMALL_VMEM = 8 * 1024 * 1024
VMEM = pl.BlockSpec(memory_space=pltpu.VMEM)
HBM = pl.BlockSpec(memory_space=pltpu.HBM)


def split_two(value):
    high = value.astype(jnp.bfloat16).astype(jnp.float32)
    low = (value - high).astype(jnp.bfloat16).astype(jnp.float32)
    return high, low


def piece_copies(weight, buf, sems, parts, pieces, first):
    count, _, width = buf.shape
    per_part = pieces // parts
    quarter = lax.rem(lax.axis_index("kvp"), parts)
    copies = []
    for i in range(count):
        x, j = divmod(first + i, per_part)
        start = pl.multiple_of((jnp.bitwise_xor(quarter, x) * per_part + j) * width, width)
        copies.append(pltpu.make_async_copy(weight.at[:, pl.ds(start, width)], buf.at[i], sems.at[i]))
    return copies


def attend_kernel(heads_dev, devices, parts, *refs):
    table_hbm, lengths_hbm, key_scale_hbm, value_scale_hbm, queries_hbm, keys, values, weight = refs[:8]
    packed, fetched = refs[8:10]
    table, lengths, key_scale, value_scale, queries, key_buf, value_buf, query_rows, staged = refs[10:19]
    small_sems, sems, weight_sems = refs[19:]
    rows, pages = table.shape
    kv_heads = key_scale.shape[0]
    heads = queries.shape[1] // HD
    group = heads // kv_heads
    part_rows = rows * heads_dev
    context = pages * PAGE
    pieces = sems.shape[1]
    piece = keys.shape[0] // pieces

    small = []
    for i, (source, target) in enumerate(
        (
            (table_hbm, table),
            (lengths_hbm, lengths),
            (key_scale_hbm, key_scale),
            (value_scale_hbm, value_scale),
            (queries_hbm, queries),
        )
    ):
        small.append(pltpu.make_async_copy(source, target, small_sems.at[i]))
        small[-1].start()
    large = []
    for which, source, target in ((0, keys, key_buf), (1, values, value_buf)):
        large.append([])
        for i in range(pieces):
            here = pl.ds(i * piece, piece)
            large[-1].append(pltpu.make_async_copy(source.at[here], target.at[here], sems.at[which, i]))
            large[-1][-1].start()
    ahead = piece_copies(weight, fetched, weight_sems, parts, WEIGHT_PIECES, WEIGHT_PIECES // parts)
    for copy in ahead:
        copy.start()

    staged[:, part_rows:, :] = jnp.zeros((devices, staged.shape[1] - part_rows, HD), jnp.float32)
    me = lax.axis_index("kvp")
    place = me * context + lax.broadcasted_iota(jnp.int32, (group, context), 1)
    lane = lax.broadcasted_iota(jnp.int32, (group, HD), 1)
    zeros = jnp.zeros((group, HD), jnp.bfloat16)
    for copy in small:
        copy.wait()
    for h in range(heads):
        query_rows[h * rows : (h + 1) * rows, :] = queries[:, h * HD : (h + 1) * HD].astype(jnp.float32)
    for copy in large[0]:
        copy.wait()

    def factors(scales, r, k, times):
        columns = []
        for p in range(0, pages, 2):
            left = scales[k, table[r, p]] * times
            right = scales[k, table[r, p + 1]] * times
            columns.append(jnp.where(lane < PAGE, left, right))
        return jnp.concatenate(columns, axis=1)

    def pages_of(buf, r, k):
        return jnp.concatenate(
            [buf[table[r, p], :, k * HD : (k + 2) * HD] for p in range(pages)], axis=0
        )

    probs = {}
    stats = [jnp.zeros((group, HD), jnp.float32)] * kv_heads
    for r in range(rows):
        visible = place < lengths[r]
        query = query_rows[pl.ds(r, heads, stride=rows), :].astype(jnp.bfloat16)
        for k in range(0, kv_heads, 2):
            left = jnp.concatenate(
                [
                    jnp.concatenate([query[k * group : (k + 1) * group], zeros], axis=1),
                    jnp.concatenate([zeros, query[(k + 1) * group : (k + 2) * group]], axis=1),
                ],
                axis=0,
            )
            both = lax.dot_general(
                left, pages_of(key_buf, r, k), (((1,), (1,)), ((), ())), preferred_element_type=jnp.float32
            )
            weights = []
            for i in (0, 1):
                scores = both[i * group : (i + 1) * group] * factors(key_scale, r, k + i, 1.0 / math.sqrt(HD))
                highest = jnp.max(jnp.where(visible, scores, -1e30), axis=1, keepdims=True)
                high, low = split_two(highest)
                prob = jnp.where(visible, jnp.exp(scores - (high + low)), 0.0)
                total_high, total_low = split_two(jnp.sum(prob, axis=1, keepdims=True))
                for at, value in enumerate((high, low, total_high, total_low)):
                    stats[k + i] = jnp.where(lane == 4 * r + at, value, stats[k + i])
                weights.append((prob * factors(value_scale, r, k + i, 1.0)).astype(jnp.bfloat16))
            probs[r, k] = jnp.concatenate(weights, axis=0)
    for copy in large[1]:
        copy.wait()
    for r in range(rows):
        for k in range(0, kv_heads, 2):
            both = jnp.dot(probs[r, k], pages_of(value_buf, r, k), preferred_element_type=jnp.float32)
            for i in (0, 1):
                partial = both[i * group : (i + 1) * group, i * HD : (i + 1) * HD]
                for start in range(0, group, heads_dev):
                    d = ((k + i) * group + start) // heads_dev
                    staged[d, r * heads_dev : (r + 1) * heads_dev, :] = partial[start : start + heads_dev]
    for k in range(kv_heads):
        for start in range(0, group, heads_dev):
            d = (k * group + start) // heads_dev
            staged[d, part_rows : part_rows + heads_dev, :] = stats[k][start : start + heads_dev]
    packed[...] = staged[...].astype(jnp.bfloat16)
    for copy in ahead:
        copy.wait()


def project_kernel(heads_dev, packed, fetched, weight, left, *refs):
    outs, (attended, buf, sems) = refs[:-3], refs[-3:]
    rows = left.shape[0]
    ready, _, width = fetched.shape
    per_out = WEIGHT_PIECES // (len(outs) + 1)
    copies = piece_copies(weight, buf, sems, len(outs) + 1, WEIGHT_PIECES, per_out + ready)
    for copy in copies:
        copy.start()
    blocks = packed[...].astype(jnp.float32)
    stats = blocks[:, rows * heads_dev : (rows + 1) * heads_dev, :]
    for r in range(rows):
        partial = blocks[:, r * heads_dev : (r + 1) * heads_dev, :]
        maxima = stats[:, :, 4 * r : 4 * r + 1] + stats[:, :, 4 * r + 1 : 4 * r + 2]
        totals = stats[:, :, 4 * r + 2 : 4 * r + 3] + stats[:, :, 4 * r + 3 : 4 * r + 4]
        rescale = jnp.exp(maxima - jnp.max(maxima, axis=0, keepdims=True))
        attended[r * heads_dev : (r + 1) * heads_dev, :] = jnp.sum(partial * rescale, axis=0) / jnp.sum(
            totals * rescale, axis=0
        )
    rounded = jnp.concatenate(
        [attended[pl.ds(j, rows, stride=heads_dev), :].astype(jnp.bfloat16) for j in range(heads_dev)], axis=1
    )
    left[...] = rounded
    for piece in range(per_out * len(outs)):
        if piece >= ready:
            copies[piece - ready].wait()
        tile = fetched[piece] if piece < ready else buf[piece - ready]
        terms = jnp.dot(rounded, tile, preferred_element_type=jnp.float32)
        i = piece % per_out
        outs[piece // per_out][:, i * width : (i + 1) * width] = terms.astype(jnp.bfloat16)


def project_own_kernel(left, weight, out, buf, sems):
    count, _, width = buf.shape
    copies = piece_copies(weight, buf, sems, WEIGHT_PIECES // count, WEIGHT_PIECES, 0)
    for copy in copies:
        copy.start()
    for i in range(count):
        copies[i].wait()
        terms = jnp.dot(left[...], buf[i], preferred_element_type=jnp.float32)
        out[:, i * width : (i + 1) * width] = terms.astype(jnp.bfloat16)


def add_kernel(*refs):
    terms = [ref[...].astype(jnp.float32) for ref in refs[:-1]]
    while len(terms) > 1:
        terms = [terms[i] + terms[i + 1] for i in range(0, len(terms), 2)]
    refs[-1][...] = terms[0].astype(refs[-1].dtype)


def lay_kernel(*refs):
    parts, out = refs[:-1], refs[-1]
    quarter = lax.rem(lax.axis_index("kvp"), len(parts))
    width = parts[0].shape[1]
    for x, part in enumerate(parts):
        start = pl.multiple_of(jnp.bitwise_xor(quarter, x) * width, width)
        out[:, pl.ds(start, width)] = part[...]


def exchange(array, partner, devices):
    return lax.ppermute(array, "kvp", [(i, i ^ partner) for i in range(devices)])


def in_hbm(array):
    return pltpu.with_memory_space_constraint(array, pltpu.HBM)


def body(queries, key_cache, value_cache, key_scale, value_scale, page_table, lengths, out_weight, *, devices):
    rows, pages = page_table.shape
    slots, _, columns = key_cache.shape
    kv_heads = key_scale.shape[1]
    heads_dev = out_weight.shape[0] // HD
    heads = queries.shape[1] // HD
    features = out_weight.shape[1]
    chunk = -(-(rows + 1) * heads_dev // 8) * 8
    inner = 4
    outer = devices // inner
    part = features // inner
    depth = heads_dev * HD
    width = features // WEIGHT_PIECES
    own_pieces = WEIGHT_PIECES // inner
    packed, fetched = pl.pallas_call(
        functools.partial(attend_kernel, heads_dev, devices, inner),
        out_shape=[
            jax.ShapeDtypeStruct((devices, chunk, HD), jnp.bfloat16),
            pltpu.VMEM((FETCHED_PIECES, depth, width), jnp.bfloat16),
        ],
        in_specs=[HBM] * 8,
        out_specs=[VMEM] * 2,
        scratch_shapes=[
            pltpu.SMEM((rows, pages), jnp.int32),
            pltpu.SMEM((rows,), jnp.int32),
            pltpu.SMEM((kv_heads, slots), jnp.float32),
            pltpu.SMEM((kv_heads, slots), jnp.float32),
            pltpu.VMEM((rows, heads * HD), jnp.bfloat16),
            pltpu.VMEM((slots, PAGE, columns), jnp.bfloat16),
            pltpu.VMEM((slots, PAGE, columns), jnp.bfloat16),
            pltpu.VMEM((heads * rows, HD), jnp.float32),
            pltpu.VMEM((devices, chunk, HD), jnp.float32),
            pltpu.SemaphoreType.DMA((5,)),
            pltpu.SemaphoreType.DMA((2, 4)),
            pltpu.SemaphoreType.DMA((FETCHED_PIECES,)),
        ],
        compiler_params=pltpu.CompilerParams(vmem_limit_bytes=ATTEND_VMEM),
        cost_estimate=pl.CostEstimate(
            flops=4 * heads * rows * pages * PAGE * HD,
            bytes_accessed=4 * rows * pages * PAGE * columns,
            transcendentals=heads * rows * pages * PAGE,
        ),
        name="attend",
    )(*[in_hbm(a) for a in (page_table, lengths, key_scale.T, value_scale.T, queries, key_cache, value_cache, out_weight)])

    received = lax.all_to_all(packed, "kvp", split_axis=0, concat_axis=0, tiled=True)

    left, *others = pl.pallas_call(
        functools.partial(project_kernel, heads_dev),
        out_shape=[jax.ShapeDtypeStruct((rows, depth), jnp.bfloat16)]
        + [jax.ShapeDtypeStruct((rows, part), jnp.bfloat16)] * (inner - 1),
        in_specs=[VMEM, VMEM, HBM],
        out_specs=[VMEM] * inner,
        scratch_shapes=[
            pltpu.VMEM((rows * heads_dev, HD), jnp.float32),
            pltpu.VMEM((WEIGHT_PIECES - own_pieces - FETCHED_PIECES, depth, width), jnp.bfloat16),
            pltpu.SemaphoreType.DMA((WEIGHT_PIECES - own_pieces - FETCHED_PIECES,)),
        ],
        compiler_params=pltpu.CompilerParams(vmem_limit_bytes=PROJECT_VMEM),
        cost_estimate=pl.CostEstimate(
            flops=2 * rows * depth * part * (inner - 1),
            bytes_accessed=2 * depth * part * (inner - 1),
            transcendentals=0,
        ),
        name="project_others",
    )(received, fetched, in_hbm(out_weight))
    sent = [exchange(others[x - 1], x, devices) for x in range(1, inner)]
    own = pl.pallas_call(
        project_own_kernel,
        out_shape=jax.ShapeDtypeStruct((rows, part), jnp.bfloat16),
        in_specs=[VMEM, HBM],
        out_specs=VMEM,
        scratch_shapes=[
            pltpu.VMEM((own_pieces, depth, width), jnp.bfloat16),
            pltpu.SemaphoreType.DMA((own_pieces,)),
        ],
        compiler_params=pltpu.CompilerParams(vmem_limit_bytes=PROJECT_VMEM),
        cost_estimate=pl.CostEstimate(
            flops=2 * rows * depth * part, bytes_accessed=2 * depth * part, transcendentals=0
        ),
        name="project_own",
    )(left, in_hbm(out_weight))

    def add(terms, name):
        return pl.pallas_call(
            add_kernel,
            out_shape=jax.ShapeDtypeStruct((rows, part), jnp.bfloat16),
            in_specs=[VMEM] * len(terms),
            out_specs=VMEM,
            compiler_params=pltpu.CompilerParams(vmem_limit_bytes=SMALL_VMEM),
            name=name,
        )(*terms)

    mine = add([own] + sent, "add_near")
    mine = add([mine] + [exchange(mine, x * inner, devices) for x in range(1, outer)], "add_far")
    parts = [mine] + [exchange(mine, x, devices) for x in range(1, inner)]
    return pl.pallas_call(
        lay_kernel,
        out_shape=jax.ShapeDtypeStruct((rows, features), jnp.bfloat16),
        in_specs=[VMEM] * inner,
        out_specs=VMEM,
        compiler_params=pltpu.CompilerParams(vmem_limit_bytes=SMALL_VMEM),
        name="lay",
    )(*parts)


def solution(mesh):
    placed = (
        P("group", None),
        P(("group", "kvp"), None, None),
        P(("group", "kvp"), None, None),
        P(("group", "kvp"), None),
        P(("group", "kvp"), None),
        P("group", "kvp"),
        P("group"),
        P("kvp", None),
    )
    return jax.shard_map(
        functools.partial(body, devices=mesh.shape["kvp"]),
        mesh=mesh,
        in_specs=placed,
        out_specs=P("group", None),
        check_vma=False,
    )
```

```python
import functools
import math

import jax
import jax.numpy as jnp
from jax import lax
from jax.experimental import pallas as pl
from jax.experimental.pallas import tpu as pltpu
from jax.sharding import PartitionSpec as P

HD = 128
PAGE = 64
ATTEND_VMEM = 24 * 1024 * 1024
PROJECT_VMEM = 12 * 1024 * 1024
WEIGHT_PIECES = 16
FETCHED_PIECES = 5
IN_FLIGHT = 3
SMALL_VMEM = 8 * 1024 * 1024
VMEM = pl.BlockSpec(memory_space=pltpu.VMEM)
HBM = pl.BlockSpec(memory_space=pltpu.HBM)


def split_two(value):
    high = value.astype(jnp.bfloat16).astype(jnp.float32)
    low = (value - high).astype(jnp.bfloat16).astype(jnp.float32)
    return high, low


def piece_copies(weight, buf, sems, parts, pieces, first):
    count, _, width = buf.shape
    per_part = pieces // parts
    quarter = lax.rem(lax.axis_index("kvp"), parts)
    copies = []
    for i in range(count):
        x, j = divmod(first + i, per_part)
        start = pl.multiple_of((jnp.bitwise_xor(quarter, x) * per_part + j) * width, width)
        copies.append(pltpu.make_async_copy(weight.at[:, pl.ds(start, width)], buf.at[i], sems.at[i]))
    return copies


def take(copies, i):
    copies[i].wait()
    if i + IN_FLIGHT < len(copies):
        copies[i + IN_FLIGHT].start()


def attend_kernel(heads_dev, devices, parts, *refs):
    table_hbm, lengths_hbm, key_scale_hbm, value_scale_hbm, queries_hbm, keys, values, weight = refs[:8]
    packed, fetched = refs[8:10]
    table, lengths, key_scale, value_scale, queries, key_buf, value_buf, query_rows, staged = refs[10:19]
    small_sems, sems, weight_sems = refs[19:]
    rows, pages = table.shape
    kv_heads = key_scale.shape[0]
    heads = queries.shape[1] // HD
    group = heads // kv_heads
    context = pages * PAGE
    pieces = sems.shape[1]
    piece = keys.shape[0] // pieces

    small = []
    for i, (source, target) in enumerate(
        (
            (table_hbm, table),
            (lengths_hbm, lengths),
            (key_scale_hbm, key_scale),
            (value_scale_hbm, value_scale),
            (queries_hbm, queries),
        )
    ):
        small.append(pltpu.make_async_copy(source, target, small_sems.at[i]))
        small[-1].start()
    large = []
    for which, source, target in ((0, keys, key_buf), (1, values, value_buf)):
        large.append([])
        for i in range(pieces):
            here = pl.ds(i * piece, piece)
            large[-1].append(pltpu.make_async_copy(source.at[here], target.at[here], sems.at[which, i]))
    for copy in large[0]:
        copy.start()
    ahead = piece_copies(weight, fetched, weight_sems, parts, WEIGHT_PIECES, WEIGHT_PIECES // parts)

    me = lax.axis_index("kvp")
    place = me * context + lax.broadcasted_iota(jnp.int32, (group, context), 1)
    lane = lax.broadcasted_iota(jnp.int32, (group, HD), 1)
    zeros = jnp.zeros((group, HD), jnp.bfloat16)
    for copy in small:
        copy.wait()
    for h in range(heads):
        query_rows[h * rows : (h + 1) * rows, :] = queries[:, h * HD : (h + 1) * HD].astype(jnp.float32)
    for copy in large[1]:
        copy.start()
    for copy in large[0]:
        copy.wait()
    for copy in ahead:
        copy.start()

    def factors(scales, r, k, times):
        columns = []
        for p in range(0, pages, 2):
            left = scales[k, table[r, p]] * times
            right = scales[k, table[r, p + 1]] * times
            columns.append(jnp.where(lane < PAGE, left, right))
        return jnp.concatenate(columns, axis=1)

    def pages_of(buf, r, k):
        return jnp.concatenate(
            [buf[table[r, p], :, k * HD : (k + 2) * HD] for p in range(pages)], axis=0
        )

    probs = {}
    stats = [jnp.zeros((group, HD), jnp.float32)] * kv_heads
    for r in range(rows):
        visible = place < lengths[r]
        query = query_rows[pl.ds(r, heads, stride=rows), :].astype(jnp.bfloat16)
        for k in range(0, kv_heads, 2):
            left = jnp.concatenate(
                [
                    jnp.concatenate([query[k * group : (k + 1) * group], zeros], axis=1),
                    jnp.concatenate([zeros, query[(k + 1) * group : (k + 2) * group]], axis=1),
                ],
                axis=0,
            )
            both = lax.dot_general(
                left, pages_of(key_buf, r, k), (((1,), (1,)), ((), ())), preferred_element_type=jnp.float32
            )
            weights = []
            for i in (0, 1):
                scores = both[i * group : (i + 1) * group] * factors(key_scale, r, k + i, 1.0 / math.sqrt(HD))
                highest = jnp.max(jnp.where(visible, scores, -1e30), axis=1, keepdims=True)
                high, low = split_two(highest)
                prob = jnp.where(visible, jnp.exp(scores - (high + low)), 0.0)
                total_high, total_low = split_two(jnp.sum(prob, axis=1, keepdims=True))
                for at, value in enumerate((high, low, total_high, total_low)):
                    stats[k + i] = jnp.where(lane == 4 * r + at, value, stats[k + i])
                weights.append((prob * factors(value_scale, r, k + i, 1.0)).astype(jnp.bfloat16))
            probs[r, k] = jnp.concatenate(weights, axis=0)
    for copy in large[1]:
        copy.wait()
    for r in range(rows):
        for k in range(0, kv_heads, 2):
            both = jnp.dot(probs[r, k], pages_of(value_buf, r, k), preferred_element_type=jnp.float32)
            for i in (0, 1):
                partial = both[i * group : (i + 1) * group, i * HD : (i + 1) * HD]
                for start in range(0, group, heads_dev):
                    d = ((k + i) * group + start) // heads_dev
                    staged[d, r] = partial[start : start + heads_dev]
    for k in range(kv_heads):
        for start in range(0, group, heads_dev):
            d = (k * group + start) // heads_dev
            staged[d, rows] = stats[k][start : start + heads_dev]
    packed[...] = staged[...].astype(jnp.bfloat16)
    for copy in ahead:
        copy.wait()


def project_kernel(heads_dev, packed, fetched, weight, left, *refs):
    outs, (attended, buf, sems) = refs[:-3], refs[-3:]
    rows = left.shape[0]
    ready, _, width = fetched.shape
    per_out = WEIGHT_PIECES // (len(outs) + 1)
    copies = piece_copies(weight, buf, sems, len(outs) + 1, WEIGHT_PIECES, per_out + ready)
    for copy in copies[:IN_FLIGHT]:
        copy.start()
    blocks = packed[...].astype(jnp.float32)
    stats = blocks[:, rows]
    for r in range(rows):
        partial = blocks[:, r]
        maxima = stats[:, :, 4 * r : 4 * r + 1] + stats[:, :, 4 * r + 1 : 4 * r + 2]
        totals = stats[:, :, 4 * r + 2 : 4 * r + 3] + stats[:, :, 4 * r + 3 : 4 * r + 4]
        rescale = jnp.exp(maxima - jnp.max(maxima, axis=0, keepdims=True))
        attended[r * heads_dev : (r + 1) * heads_dev, :] = jnp.sum(partial * rescale, axis=0) / jnp.sum(
            totals * rescale, axis=0
        )
    rounded = jnp.concatenate(
        [attended[pl.ds(j, rows, stride=heads_dev), :].astype(jnp.bfloat16) for j in range(heads_dev)], axis=1
    )
    left[...] = rounded
    for piece in range(per_out * len(outs)):
        if piece >= ready:
            take(copies, piece - ready)
        tile = fetched[piece] if piece < ready else buf[piece - ready]
        terms = jnp.dot(rounded, tile, preferred_element_type=jnp.float32)
        i = piece % per_out
        outs[piece // per_out][:, i * width : (i + 1) * width] = terms.astype(jnp.bfloat16)


def project_own_kernel(left, weight, out, buf, sems):
    count, _, width = buf.shape
    copies = piece_copies(weight, buf, sems, WEIGHT_PIECES // count, WEIGHT_PIECES, 0)
    for copy in copies[:IN_FLIGHT]:
        copy.start()
    for i in range(count):
        take(copies, i)
        terms = jnp.dot(left[...], buf[i], preferred_element_type=jnp.float32)
        out[:, i * width : (i + 1) * width] = terms.astype(jnp.bfloat16)


def add_kernel(*refs):
    terms = [ref[...].astype(jnp.float32) for ref in refs[:-1]]
    while len(terms) > 1:
        terms = [terms[i] + terms[i + 1] for i in range(0, len(terms), 2)]
    refs[-1][...] = terms[0].astype(refs[-1].dtype)


def lay_kernel(*refs):
    parts, out = refs[:-1], refs[-1]
    quarter = lax.rem(lax.axis_index("kvp"), len(parts))
    width = parts[0].shape[1]
    for x, part in enumerate(parts):
        start = pl.multiple_of(jnp.bitwise_xor(quarter, x) * width, width)
        out[:, pl.ds(start, width)] = part[...]


def exchange(array, partner, devices):
    return lax.ppermute(array, "kvp", [(i, i ^ partner) for i in range(devices)])


def in_hbm(array):
    return pltpu.with_memory_space_constraint(array, pltpu.HBM)


def body(queries, key_cache, value_cache, key_scale, value_scale, page_table, lengths, out_weight, *, devices):
    rows, pages = page_table.shape
    slots, _, columns = key_cache.shape
    kv_heads = key_scale.shape[1]
    heads_dev = out_weight.shape[0] // HD
    heads = queries.shape[1] // HD
    features = out_weight.shape[1]
    inner = 4
    outer = devices // inner
    part = features // inner
    depth = heads_dev * HD
    width = features // WEIGHT_PIECES
    own_pieces = WEIGHT_PIECES // inner
    packed, fetched = pl.pallas_call(
        functools.partial(attend_kernel, heads_dev, devices, inner),
        out_shape=[
            jax.ShapeDtypeStruct((devices, rows + 1, heads_dev, HD), jnp.bfloat16),
            pltpu.VMEM((FETCHED_PIECES, depth, width), jnp.bfloat16),
        ],
        in_specs=[HBM] * 8,
        out_specs=[VMEM] * 2,
        scratch_shapes=[
            pltpu.SMEM((rows, pages), jnp.int32),
            pltpu.SMEM((rows,), jnp.int32),
            pltpu.SMEM((kv_heads, slots), jnp.float32),
            pltpu.SMEM((kv_heads, slots), jnp.float32),
            pltpu.VMEM((rows, heads * HD), jnp.bfloat16),
            pltpu.VMEM((slots, PAGE, columns), jnp.bfloat16),
            pltpu.VMEM((slots, PAGE, columns), jnp.bfloat16),
            pltpu.VMEM((heads * rows, HD), jnp.float32),
            pltpu.VMEM((devices, rows + 1, heads_dev, HD), jnp.float32),
            pltpu.SemaphoreType.DMA((5,)),
            pltpu.SemaphoreType.DMA((2, 4)),
            pltpu.SemaphoreType.DMA((FETCHED_PIECES,)),
        ],
        compiler_params=pltpu.CompilerParams(vmem_limit_bytes=ATTEND_VMEM),
        cost_estimate=pl.CostEstimate(
            flops=4 * heads * rows * pages * PAGE * HD,
            bytes_accessed=4 * rows * pages * PAGE * columns,
            transcendentals=heads * rows * pages * PAGE,
        ),
        name="attend",
    )(*[in_hbm(a) for a in (page_table, lengths, key_scale.T, value_scale.T, queries, key_cache, value_cache, out_weight)])

    received = lax.all_to_all(packed, "kvp", split_axis=0, concat_axis=0, tiled=True)

    left, *others = pl.pallas_call(
        functools.partial(project_kernel, heads_dev),
        out_shape=[jax.ShapeDtypeStruct((rows, depth), jnp.bfloat16)]
        + [jax.ShapeDtypeStruct((rows, part), jnp.bfloat16)] * (inner - 1),
        in_specs=[VMEM, VMEM, HBM],
        out_specs=[VMEM] * inner,
        scratch_shapes=[
            pltpu.VMEM((rows * heads_dev, HD), jnp.float32),
            pltpu.VMEM((WEIGHT_PIECES - own_pieces - FETCHED_PIECES, depth, width), jnp.bfloat16),
            pltpu.SemaphoreType.DMA((WEIGHT_PIECES - own_pieces - FETCHED_PIECES,)),
        ],
        compiler_params=pltpu.CompilerParams(vmem_limit_bytes=PROJECT_VMEM),
        cost_estimate=pl.CostEstimate(
            flops=2 * rows * depth * part * (inner - 1),
            bytes_accessed=2 * depth * part * (inner - 1),
            transcendentals=0,
        ),
        name="project_others",
    )(received, fetched, in_hbm(out_weight))
    sent = [exchange(others[x - 1], x, devices) for x in range(1, inner)]
    own = pl.pallas_call(
        project_own_kernel,
        out_shape=jax.ShapeDtypeStruct((rows, part), jnp.bfloat16),
        in_specs=[VMEM, HBM],
        out_specs=VMEM,
        scratch_shapes=[
            pltpu.VMEM((own_pieces, depth, width), jnp.bfloat16),
            pltpu.SemaphoreType.DMA((own_pieces,)),
        ],
        compiler_params=pltpu.CompilerParams(vmem_limit_bytes=PROJECT_VMEM),
        cost_estimate=pl.CostEstimate(
            flops=2 * rows * depth * part, bytes_accessed=2 * depth * part, transcendentals=0
        ),
        name="project_own",
    )(left, in_hbm(out_weight))

    def add(terms, name):
        return pl.pallas_call(
            add_kernel,
            out_shape=jax.ShapeDtypeStruct((rows, part), jnp.bfloat16),
            in_specs=[VMEM] * len(terms),
            out_specs=VMEM,
            compiler_params=pltpu.CompilerParams(vmem_limit_bytes=SMALL_VMEM),
            name=name,
        )(*terms)

    mine = add([own] + sent, "add_near")
    mine = add([mine] + [exchange(mine, x * inner, devices) for x in range(1, outer)], "add_far")
    parts = [mine] + [exchange(mine, x, devices) for x in range(1, inner)]
    return pl.pallas_call(
        lay_kernel,
        out_shape=jax.ShapeDtypeStruct((rows, features), jnp.bfloat16),
        in_specs=[VMEM] * inner,
        out_specs=VMEM,
        compiler_params=pltpu.CompilerParams(vmem_limit_bytes=SMALL_VMEM),
        name="lay",
    )(*parts)


def solution(mesh):
    placed = (
        P("group", None),
        P(("group", "kvp"), None, None),
        P(("group", "kvp"), None, None),
        P(("group", "kvp"), None),
        P(("group", "kvp"), None),
        P("group", "kvp"),
        P("group"),
        P("kvp", None),
    )
    return jax.shard_map(
        functools.partial(body, devices=mesh.shape["kvp"]),
        mesh=mesh,
        in_specs=placed,
        out_specs=P("group", None),
        check_vma=False,
    )
```

```python
import functools
import math

import jax
import jax.numpy as jnp
from jax import lax
from jax.experimental import pallas as pl
from jax.experimental.pallas import tpu as pltpu
from jax.sharding import PartitionSpec as P

HD = 128
PAGE = 64
ATTEND_VMEM = 24 * 1024 * 1024
PROJECT_VMEM = 12 * 1024 * 1024
WEIGHT_PIECES = 16
FETCHED_PIECES = 6
SMALL_VMEM = 8 * 1024 * 1024
VMEM = pl.BlockSpec(memory_space=pltpu.VMEM)
HBM = pl.BlockSpec(memory_space=pltpu.HBM)


def split_two(value):
    high = value.astype(jnp.bfloat16).astype(jnp.float32)
    low = (value - high).astype(jnp.bfloat16).astype(jnp.float32)
    return high, low


def piece_copies(weight, buf, sems, parts, pieces, first):
    count, _, width = buf.shape
    per_part = pieces // parts
    quarter = lax.rem(lax.axis_index("kvp"), parts)
    copies = []
    for i in range(count):
        x, j = divmod(first + i, per_part)
        start = pl.multiple_of((jnp.bitwise_xor(quarter, x) * per_part + j) * width, width)
        copies.append(pltpu.make_async_copy(weight.at[:, pl.ds(start, width)], buf.at[i], sems.at[i]))
    return copies


def attend_kernel(heads_dev, devices, parts, *refs):
    table_hbm, lengths_hbm, key_scale_hbm, value_scale_hbm, queries_hbm, keys, values, weight = refs[:8]
    packed, fetched = refs[8:10]
    table, lengths, key_scale, value_scale, queries, key_buf, value_buf, query_rows, staged = refs[10:19]
    small_sems, sems, weight_sems = refs[19:]
    rows, pages = table.shape
    kv_heads = key_scale.shape[0]
    heads = queries.shape[1] // HD
    group = heads // kv_heads
    part_rows = rows * heads_dev
    context = pages * PAGE
    pieces = sems.shape[1]
    piece = keys.shape[0] // pieces

    small = []
    for i, (source, target) in enumerate(
        (
            (table_hbm, table),
            (lengths_hbm, lengths),
            (key_scale_hbm, key_scale),
            (value_scale_hbm, value_scale),
            (queries_hbm, queries),
        )
    ):
        small.append(pltpu.make_async_copy(source, target, small_sems.at[i]))
        small[-1].start()
    large = []
    for which, source, target in ((0, keys, key_buf), (1, values, value_buf)):
        large.append([])
        for i in range(pieces):
            here = pl.ds(i * piece, piece)
            large[-1].append(pltpu.make_async_copy(source.at[here], target.at[here], sems.at[which, i]))
            large[-1][-1].start()
    ahead = piece_copies(weight, fetched, weight_sems, parts, WEIGHT_PIECES, WEIGHT_PIECES // parts)
    for copy in ahead:
        copy.start()

    staged[:, part_rows:, :] = jnp.zeros((devices, staged.shape[1] - part_rows, HD), jnp.float32)
    me = lax.axis_index("kvp")
    place = me * context + lax.broadcasted_iota(jnp.int32, (group, context), 1)
    lane = lax.broadcasted_iota(jnp.int32, (group, HD), 1)
    zeros = jnp.zeros((group, HD), jnp.bfloat16)
    for copy in small:
        copy.wait()
    for h in range(heads):
        query_rows[h * rows : (h + 1) * rows, :] = queries[:, h * HD : (h + 1) * HD].astype(jnp.float32)
    for copy in large[0]:
        copy.wait()

    def factors(scales, r, k, times):
        columns = []
        for p in range(0, pages, 2):
            left = scales[k, table[r, p]] * times
            right = scales[k, table[r, p + 1]] * times
            columns.append(jnp.where(lane < PAGE, left, right))
        return jnp.concatenate(columns, axis=1)

    def pages_of(buf, r, k):
        return jnp.concatenate(
            [buf[table[r, p], :, k * HD : (k + 2) * HD] for p in range(pages)], axis=0
        )

    probs = {}
    stats = [jnp.zeros((group, HD), jnp.float32)] * kv_heads
    for r in range(rows):
        visible = place < lengths[r]
        query = query_rows[pl.ds(r, heads, stride=rows), :].astype(jnp.bfloat16)
        for k in range(0, kv_heads, 2):
            left = jnp.concatenate(
                [
                    jnp.concatenate([query[k * group : (k + 1) * group], zeros], axis=1),
                    jnp.concatenate([zeros, query[(k + 1) * group : (k + 2) * group]], axis=1),
                ],
                axis=0,
            )
            both = lax.dot_general(
                left, pages_of(key_buf, r, k), (((1,), (1,)), ((), ())), preferred_element_type=jnp.float32
            )
            weights = []
            for i in (0, 1):
                scores = both[i * group : (i + 1) * group] * factors(key_scale, r, k + i, 1.0 / math.sqrt(HD))
                highest = jnp.max(jnp.where(visible, scores, -1e30), axis=1, keepdims=True)
                high, low = split_two(highest)
                prob = jnp.where(visible, jnp.exp(scores - (high + low)), 0.0)
                total_high, total_low = split_two(jnp.sum(prob, axis=1, keepdims=True))
                for at, value in enumerate((high, low, total_high, total_low)):
                    stats[k + i] = jnp.where(lane == 4 * r + at, value, stats[k + i])
                weights.append((prob * factors(value_scale, r, k + i, 1.0)).astype(jnp.bfloat16))
            probs[r, k] = jnp.concatenate(weights, axis=0)
    for copy in large[1]:
        copy.wait()
    for r in range(rows):
        for k in range(0, kv_heads, 2):
            both = jnp.dot(probs[r, k], pages_of(value_buf, r, k), preferred_element_type=jnp.float32)
            for i in (0, 1):
                partial = both[i * group : (i + 1) * group, i * HD : (i + 1) * HD]
                for start in range(0, group, heads_dev):
                    d = ((k + i) * group + start) // heads_dev
                    staged[d, r * heads_dev : (r + 1) * heads_dev, :] = partial[start : start + heads_dev]
    for k in range(kv_heads):
        for start in range(0, group, heads_dev):
            d = (k * group + start) // heads_dev
            staged[d, part_rows : part_rows + heads_dev, :] = stats[k][start : start + heads_dev]
    packed[...] = staged[...].astype(jnp.bfloat16)
    for copy in ahead:
        copy.wait()


def project_kernel(heads_dev, packed, fetched, weight, left, *refs):
    outs, (attended, buf, sems) = refs[:-3], refs[-3:]
    rows = left.shape[0]
    ready, _, width = fetched.shape
    per_out = WEIGHT_PIECES // (len(outs) + 1)
    copies = piece_copies(weight, buf, sems, len(outs) + 1, WEIGHT_PIECES, per_out + ready)
    for copy in copies:
        copy.start()
    blocks = packed[...].astype(jnp.float32)
    stats = blocks[:, rows * heads_dev : (rows + 1) * heads_dev, :]
    for r in range(rows):
        partial = blocks[:, r * heads_dev : (r + 1) * heads_dev, :]
        maxima = stats[:, :, 4 * r : 4 * r + 1] + stats[:, :, 4 * r + 1 : 4 * r + 2]
        totals = stats[:, :, 4 * r + 2 : 4 * r + 3] + stats[:, :, 4 * r + 3 : 4 * r + 4]
        rescale = jnp.exp(maxima - jnp.max(maxima, axis=0, keepdims=True))
        attended[r * heads_dev : (r + 1) * heads_dev, :] = jnp.sum(partial * rescale, axis=0) / jnp.sum(
            totals * rescale, axis=0
        )
    rounded = jnp.concatenate(
        [attended[pl.ds(j, rows, stride=heads_dev), :].astype(jnp.bfloat16) for j in range(heads_dev)], axis=1
    )
    left[...] = rounded
    for piece in range(per_out * len(outs)):
        if piece >= ready:
            copies[piece - ready].wait()
        tile = fetched[piece] if piece < ready else buf[piece - ready]
        terms = jnp.dot(rounded, tile, preferred_element_type=jnp.float32)
        i = piece % per_out
        outs[piece // per_out][:, i * width : (i + 1) * width] = terms.astype(jnp.bfloat16)


def project_own_kernel(left, weight, out, buf, sems):
    count, _, width = buf.shape
    copies = piece_copies(weight, buf, sems, WEIGHT_PIECES // count, WEIGHT_PIECES, 0)
    for copy in copies:
        copy.start()
    for i in range(count):
        copies[i].wait()
        terms = jnp.dot(left[...], buf[i], preferred_element_type=jnp.float32)
        out[:, i * width : (i + 1) * width] = terms.astype(jnp.bfloat16)


def add_kernel(*refs):
    terms = [ref[...].astype(jnp.float32) for ref in refs[:-1]]
    while len(terms) > 1:
        terms = [terms[i] + terms[i + 1] for i in range(0, len(terms), 2)]
    refs[-1][...] = terms[0].astype(refs[-1].dtype)


def add_far_kernel(terms, out):
    out[...] = jnp.sum(terms[...].astype(jnp.float32), axis=0).astype(out.dtype)


def lay_kernel(parts, out):
    count, _, width = parts.shape
    for i in range(count):
        out[:, i * width : (i + 1) * width] = parts[i]


def exchange(array, partner, devices):
    return lax.ppermute(array, "kvp", [(i, i ^ partner) for i in range(devices)])


def in_hbm(array):
    return pltpu.with_memory_space_constraint(array, pltpu.HBM)


def body(queries, key_cache, value_cache, key_scale, value_scale, page_table, lengths, out_weight, *, devices):
    rows, pages = page_table.shape
    slots, _, columns = key_cache.shape
    kv_heads = key_scale.shape[1]
    heads_dev = out_weight.shape[0] // HD
    heads = queries.shape[1] // HD
    features = out_weight.shape[1]
    chunk = -(-(rows + 1) * heads_dev // 8) * 8
    inner = 4
    outer = devices // inner
    part = features // inner
    depth = heads_dev * HD
    width = features // WEIGHT_PIECES
    own_pieces = WEIGHT_PIECES // inner
    packed, fetched = pl.pallas_call(
        functools.partial(attend_kernel, heads_dev, devices, inner),
        out_shape=[
            jax.ShapeDtypeStruct((devices, chunk, HD), jnp.bfloat16),
            pltpu.VMEM((FETCHED_PIECES, depth, width), jnp.bfloat16),
        ],
        in_specs=[HBM] * 8,
        out_specs=[VMEM] * 2,
        scratch_shapes=[
            pltpu.SMEM((rows, pages), jnp.int32),
            pltpu.SMEM((rows,), jnp.int32),
            pltpu.SMEM((kv_heads, slots), jnp.float32),
            pltpu.SMEM((kv_heads, slots), jnp.float32),
            pltpu.VMEM((rows, heads * HD), jnp.bfloat16),
            pltpu.VMEM((slots, PAGE, columns), jnp.bfloat16),
            pltpu.VMEM((slots, PAGE, columns), jnp.bfloat16),
            pltpu.VMEM((heads * rows, HD), jnp.float32),
            pltpu.VMEM((devices, chunk, HD), jnp.float32),
            pltpu.SemaphoreType.DMA((5,)),
            pltpu.SemaphoreType.DMA((2, 4)),
            pltpu.SemaphoreType.DMA((FETCHED_PIECES,)),
        ],
        compiler_params=pltpu.CompilerParams(vmem_limit_bytes=ATTEND_VMEM),
        cost_estimate=pl.CostEstimate(
            flops=4 * heads * rows * pages * PAGE * HD,
            bytes_accessed=4 * rows * pages * PAGE * columns,
            transcendentals=heads * rows * pages * PAGE,
        ),
        name="attend",
    )(*[in_hbm(a) for a in (page_table, lengths, key_scale.T, value_scale.T, queries, key_cache, value_cache, out_weight)])

    received = lax.all_to_all(packed, "kvp", split_axis=0, concat_axis=0, tiled=True)

    left, *others = pl.pallas_call(
        functools.partial(project_kernel, heads_dev),
        out_shape=[jax.ShapeDtypeStruct((rows, depth), jnp.bfloat16)]
        + [jax.ShapeDtypeStruct((rows, part), jnp.bfloat16)] * (inner - 1),
        in_specs=[VMEM, VMEM, HBM],
        out_specs=[VMEM] * inner,
        scratch_shapes=[
            pltpu.VMEM((rows * heads_dev, HD), jnp.float32),
            pltpu.VMEM((WEIGHT_PIECES - own_pieces - FETCHED_PIECES, depth, width), jnp.bfloat16),
            pltpu.SemaphoreType.DMA((WEIGHT_PIECES - own_pieces - FETCHED_PIECES,)),
        ],
        compiler_params=pltpu.CompilerParams(vmem_limit_bytes=PROJECT_VMEM),
        cost_estimate=pl.CostEstimate(
            flops=2 * rows * depth * part * (inner - 1),
            bytes_accessed=2 * depth * part * (inner - 1),
            transcendentals=0,
        ),
        name="project_others",
    )(received, fetched, in_hbm(out_weight))
    sent = [exchange(others[x - 1], x, devices) for x in range(1, inner)]
    own = pl.pallas_call(
        project_own_kernel,
        out_shape=jax.ShapeDtypeStruct((rows, part), jnp.bfloat16),
        in_specs=[VMEM, HBM],
        out_specs=VMEM,
        scratch_shapes=[
            pltpu.VMEM((own_pieces, depth, width), jnp.bfloat16),
            pltpu.SemaphoreType.DMA((own_pieces,)),
        ],
        compiler_params=pltpu.CompilerParams(vmem_limit_bytes=PROJECT_VMEM),
        cost_estimate=pl.CostEstimate(
            flops=2 * rows * depth * part, bytes_accessed=2 * depth * part, transcendentals=0
        ),
        name="project_own",
    )(left, in_hbm(out_weight))

    def add(terms, name):
        return pl.pallas_call(
            add_kernel,
            out_shape=jax.ShapeDtypeStruct((rows, part), jnp.bfloat16),
            in_specs=[VMEM] * len(terms),
            out_specs=VMEM,
            compiler_params=pltpu.CompilerParams(vmem_limit_bytes=SMALL_VMEM),
            name=name,
        )(*terms)

    mine = add([own] + sent, "add_near")
    far = [[x * inner + i for x in range(outer)] for i in range(inner)]
    near = [[x * inner + i for i in range(inner)] for x in range(outer)]
    terms = lax.all_gather(mine, "kvp", axis_index_groups=far)
    mine = pl.pallas_call(
        add_far_kernel,
        out_shape=jax.ShapeDtypeStruct((rows, part), jnp.bfloat16),
        in_specs=[VMEM],
        out_specs=VMEM,
        compiler_params=pltpu.CompilerParams(vmem_limit_bytes=SMALL_VMEM),
        name="add_far",
    )(terms)
    parts = lax.all_gather(mine, "kvp", axis_index_groups=near)
    return pl.pallas_call(
        lay_kernel,
        out_shape=jax.ShapeDtypeStruct((rows, features), jnp.bfloat16),
        in_specs=[VMEM],
        out_specs=VMEM,
        compiler_params=pltpu.CompilerParams(vmem_limit_bytes=SMALL_VMEM),
        name="lay",
    )(parts)


def solution(mesh):
    placed = (
        P("group", None),
        P(("group", "kvp"), None, None),
        P(("group", "kvp"), None, None),
        P(("group", "kvp"), None),
        P(("group", "kvp"), None),
        P("group", "kvp"),
        P("group"),
        P("kvp", None),
    )
    return jax.shard_map(
        functools.partial(body, devices=mesh.shape["kvp"]),
        mesh=mesh,
        in_specs=placed,
        out_specs=P("group", None),
        check_vma=False,
    )
```

```python
import functools
import math

import jax
import jax.numpy as jnp
from jax import lax
from jax.experimental import pallas as pl
from jax.experimental.pallas import tpu as pltpu
from jax.sharding import PartitionSpec as P

HD = 128
PAGE = 64
ATTEND_VMEM = 24 * 1024 * 1024
PROJECT_VMEM = 8 * 1024 * 1024
EXCHANGE_FLOPS = 40_000_000_000
SMALL_VMEM = 8 * 1024 * 1024
VMEM = pl.BlockSpec(memory_space=pltpu.VMEM)
HBM = pl.BlockSpec(memory_space=pltpu.HBM)


def split_two(value):
    high = value.astype(jnp.bfloat16).astype(jnp.float32)
    low = (value - high).astype(jnp.bfloat16).astype(jnp.float32)
    return high, low


def attend_kernel(heads_dev, devices, *refs):
    table_hbm, lengths_hbm, key_scale_hbm, value_scale_hbm, queries_hbm, keys, values = refs[:7]
    (staged, table, lengths, key_scale, value_scale, queries, key_buf, value_buf, query_rows, small_sems, sems) = refs[7:]
    rows, pages = table.shape
    kv_heads = key_scale.shape[0]
    heads = queries.shape[1] // HD
    group = heads // kv_heads
    context = pages * PAGE
    pieces = sems.shape[1]
    piece = keys.shape[0] // pieces

    small = []
    for i, (source, target) in enumerate(
        (
            (table_hbm, table),
            (lengths_hbm, lengths),
            (key_scale_hbm, key_scale),
            (value_scale_hbm, value_scale),
            (queries_hbm, queries),
        )
    ):
        small.append(pltpu.make_async_copy(source, target, small_sems.at[i]))
        small[-1].start()
    large = []
    for which, source, target in ((0, keys, key_buf), (1, values, value_buf)):
        large.append([])
        for i in range(pieces):
            here = pl.ds(i * piece, piece)
            large[-1].append(pltpu.make_async_copy(source.at[here], target.at[here], sems.at[which, i]))
    for copy in large[0]:
        copy.start()

    me = lax.axis_index("kvp")
    place = me * context + lax.broadcasted_iota(jnp.int32, (group, context), 1)
    lane = lax.broadcasted_iota(jnp.int32, (group, HD), 1)
    zeros = jnp.zeros((group, HD), jnp.bfloat16)
    for copy in small:
        copy.wait()
    for h in range(heads):
        query_rows[h * rows : (h + 1) * rows, :] = queries[:, h * HD : (h + 1) * HD].astype(jnp.float32)
    for copy in large[1]:
        copy.start()
    for copy in large[0]:
        copy.wait()

    def factors(scales, r, k, times):
        columns = []
        for p in range(0, pages, 2):
            left = scales[k, table[r, p]] * times
            right = scales[k, table[r, p + 1]] * times
            columns.append(jnp.where(lane < PAGE, left, right))
        return jnp.concatenate(columns, axis=1)

    def pages_of(buf, r, k):
        return jnp.concatenate(
            [buf[table[r, p], :, k * HD : (k + 2) * HD] for p in range(pages)], axis=0
        )

    probs = {}
    stats = [jnp.zeros((group, HD), jnp.float32)] * kv_heads
    for r in range(rows):
        visible = place < lengths[r]
        query = query_rows[pl.ds(r, heads, stride=rows), :].astype(jnp.bfloat16)
        for k in range(0, kv_heads, 2):
            left = jnp.concatenate(
                [
                    jnp.concatenate([query[k * group : (k + 1) * group], zeros], axis=1),
                    jnp.concatenate([zeros, query[(k + 1) * group : (k + 2) * group]], axis=1),
                ],
                axis=0,
            )
            both = lax.dot_general(
                left, pages_of(key_buf, r, k), (((1,), (1,)), ((), ())), preferred_element_type=jnp.float32
            )
            weights = []
            for i in (0, 1):
                scores = both[i * group : (i + 1) * group] * factors(key_scale, r, k + i, 1.0 / math.sqrt(HD))
                highest = jnp.max(jnp.where(visible, scores, -1e30), axis=1, keepdims=True)
                high, low = split_two(highest)
                prob = jnp.where(visible, jnp.exp(scores - (high + low)), 0.0)
                total_high, total_low = split_two(jnp.sum(prob, axis=1, keepdims=True))
                for at, value in enumerate((high, low, total_high, total_low)):
                    stats[k + i] = jnp.where(lane == 4 * r + at, value, stats[k + i])
                weights.append((prob * factors(value_scale, r, k + i, 1.0)).astype(jnp.bfloat16))
            probs[r, k] = jnp.concatenate(weights, axis=0)
    for copy in large[1]:
        copy.wait()
    for r in range(rows):
        for k in range(0, kv_heads, 2):
            both = jnp.dot(probs[r, k], pages_of(value_buf, r, k), preferred_element_type=jnp.float32)
            for i in (0, 1):
                partial = both[i * group : (i + 1) * group, i * HD : (i + 1) * HD]
                for start in range(0, group, heads_dev):
                    d = ((k + i) * group + start) // heads_dev
                    staged[d, r] = partial[start : start + heads_dev]
    for k in range(kv_heads):
        for start in range(0, group, heads_dev):
            d = (k * group + start) // heads_dev
            staged[d, rows] = stats[k][start : start + heads_dev]


def pack_kernel(staged, packed):
    packed[...] = staged[...].astype(jnp.bfloat16)


def project_kernel(heads_dev, packed, weight, left, *refs):
    outs, attended = refs[:-1], refs[-1]
    rows = left.shape[0]
    part = outs[0].shape[1]
    quarter = lax.rem(lax.axis_index("kvp"), len(outs) + 1)
    blocks = packed[...].astype(jnp.float32)
    stats = blocks[:, rows]
    for r in range(rows):
        partial = blocks[:, r]
        maxima = stats[:, :, 4 * r : 4 * r + 1] + stats[:, :, 4 * r + 1 : 4 * r + 2]
        totals = stats[:, :, 4 * r + 2 : 4 * r + 3] + stats[:, :, 4 * r + 3 : 4 * r + 4]
        rescale = jnp.exp(maxima - jnp.max(maxima, axis=0, keepdims=True))
        attended[r * heads_dev : (r + 1) * heads_dev, :] = jnp.sum(partial * rescale, axis=0) / jnp.sum(
            totals * rescale, axis=0
        )
    rounded = jnp.concatenate(
        [attended[pl.ds(j, rows, stride=heads_dev), :].astype(jnp.bfloat16) for j in range(heads_dev)], axis=1
    )
    left[...] = rounded
    for x, out in enumerate(outs):
        start = pl.multiple_of(jnp.bitwise_xor(quarter, x + 1) * part, part)
        terms = jnp.dot(rounded, weight[:, pl.ds(start, part)], preferred_element_type=jnp.float32)
        out[...] = terms.astype(jnp.bfloat16)


def project_own_kernel(left, weight, out):
    part = out.shape[1]
    quarter = lax.rem(lax.axis_index("kvp"), weight.shape[1] // part)
    start = pl.multiple_of(quarter * part, part)
    terms = jnp.dot(left[...], weight[:, pl.ds(start, part)], preferred_element_type=jnp.float32)
    out[...] = terms.astype(jnp.bfloat16)


def add_kernel(*refs):
    terms = [ref[...].astype(jnp.float32) for ref in refs[:-1]]
    while len(terms) > 1:
        terms = [terms[i] + terms[i + 1] for i in range(0, len(terms), 2)]
    refs[-1][...] = terms[0].astype(refs[-1].dtype)


def lay_kernel(*refs):
    parts, out = refs[:-1], refs[-1]
    quarter = lax.rem(lax.axis_index("kvp"), len(parts))
    width = parts[0].shape[1]
    for x, part in enumerate(parts):
        start = pl.multiple_of(jnp.bitwise_xor(quarter, x) * width, width)
        out[:, pl.ds(start, width)] = part[...]


def exchange(array, partner, devices):
    return lax.ppermute(array, "kvp", [(i, i ^ partner) for i in range(devices)])


def in_hbm(array):
    return pltpu.with_memory_space_constraint(array, pltpu.HBM)


def body(queries, key_cache, value_cache, key_scale, value_scale, page_table, lengths, out_weight, *, devices):
    rows, pages = page_table.shape
    slots, _, columns = key_cache.shape
    kv_heads = key_scale.shape[1]
    heads_dev = out_weight.shape[0] // HD
    heads = queries.shape[1] // HD
    features = out_weight.shape[1]
    inner = 4
    outer = devices // inner
    part = features // inner
    staged = pl.pallas_call(
        functools.partial(attend_kernel, heads_dev, devices),
        out_shape=jax.ShapeDtypeStruct((devices, rows + 1, heads_dev, HD), jnp.float32),
        in_specs=[HBM] * 7,
        out_specs=VMEM,
        scratch_shapes=[
            pltpu.SMEM((rows, pages), jnp.int32),
            pltpu.SMEM((rows,), jnp.int32),
            pltpu.SMEM((kv_heads, slots), jnp.float32),
            pltpu.SMEM((kv_heads, slots), jnp.float32),
            pltpu.VMEM((rows, heads * HD), jnp.bfloat16),
            pltpu.VMEM((slots, PAGE, columns), jnp.bfloat16),
            pltpu.VMEM((slots, PAGE, columns), jnp.bfloat16),
            pltpu.VMEM((heads * rows, HD), jnp.float32),
            pltpu.SemaphoreType.DMA((5,)),
            pltpu.SemaphoreType.DMA((2, 4)),
        ],
        compiler_params=pltpu.CompilerParams(vmem_limit_bytes=ATTEND_VMEM),
        cost_estimate=pl.CostEstimate(
            flops=4 * heads * rows * pages * PAGE * HD,
            bytes_accessed=4 * rows * pages * PAGE * columns,
            transcendentals=heads * rows * pages * PAGE,
        ),
        name="attend",
    )(*[in_hbm(a) for a in (page_table, lengths, key_scale.T, value_scale.T, queries, key_cache, value_cache)])

    packed = pl.pallas_call(
        pack_kernel,
        out_shape=jax.ShapeDtypeStruct(staged.shape, jnp.bfloat16),
        in_specs=[VMEM],
        out_specs=VMEM,
        compiler_params=pltpu.CompilerParams(vmem_limit_bytes=SMALL_VMEM),
        cost_estimate=pl.CostEstimate(flops=EXCHANGE_FLOPS, bytes_accessed=6 * staged.size, transcendentals=0),
        name="pack",
    )(staged)

    received = lax.all_to_all(packed, "kvp", split_axis=0, concat_axis=0, tiled=True)

    resident = pltpu.with_memory_space_constraint(out_weight, pltpu.VMEM)
    depth = heads_dev * HD
    left, *others = pl.pallas_call(
        functools.partial(project_kernel, heads_dev),
        out_shape=[jax.ShapeDtypeStruct((rows, depth), jnp.bfloat16)]
        + [jax.ShapeDtypeStruct((rows, part), jnp.bfloat16)] * (inner - 1),
        in_specs=[VMEM, VMEM],
        out_specs=[VMEM] * inner,
        scratch_shapes=[pltpu.VMEM((rows * heads_dev, HD), jnp.float32)],
        compiler_params=pltpu.CompilerParams(vmem_limit_bytes=PROJECT_VMEM),
        cost_estimate=pl.CostEstimate(
            flops=2 * rows * depth * part * (inner - 1),
            bytes_accessed=2 * depth * part * (inner - 1),
            transcendentals=0,
        ),
        name="project_others",
    )(received, resident)
    sent = [exchange(others[x - 1], x, devices) for x in range(1, inner)]
    own = pl.pallas_call(
        project_own_kernel,
        out_shape=jax.ShapeDtypeStruct((rows, part), jnp.bfloat16),
        in_specs=[VMEM, VMEM],
        out_specs=VMEM,
        compiler_params=pltpu.CompilerParams(vmem_limit_bytes=PROJECT_VMEM),
        cost_estimate=pl.CostEstimate(
            flops=2 * rows * depth * part, bytes_accessed=2 * depth * part, transcendentals=0
        ),
        name="project_own",
    )(left, resident)

    def add(terms, name):
        return pl.pallas_call(
            add_kernel,
            out_shape=jax.ShapeDtypeStruct((rows, part), jnp.bfloat16),
            in_specs=[VMEM] * len(terms),
            out_specs=VMEM,
            compiler_params=pltpu.CompilerParams(vmem_limit_bytes=SMALL_VMEM),
            name=name,
        )(*terms)

    mine = add([own] + sent, "add_near")
    mine = add([mine] + [exchange(mine, x * inner, devices) for x in range(1, outer)], "add_far")
    parts = [mine] + [exchange(mine, x, devices) for x in range(1, inner)]
    return pl.pallas_call(
        lay_kernel,
        out_shape=jax.ShapeDtypeStruct((rows, features), jnp.bfloat16),
        in_specs=[VMEM] * inner,
        out_specs=VMEM,
        compiler_params=pltpu.CompilerParams(vmem_limit_bytes=SMALL_VMEM),
        name="lay",
    )(*parts)


def solution(mesh):
    placed = (
        P("group", None),
        P(("group", "kvp"), None, None),
        P(("group", "kvp"), None, None),
        P(("group", "kvp"), None),
        P(("group", "kvp"), None),
        P("group", "kvp"),
        P("group"),
        P("kvp", None),
    )
    return jax.shard_map(
        functools.partial(body, devices=mesh.shape["kvp"]),
        mesh=mesh,
        in_specs=placed,
        out_specs=P("group", None),
        check_vma=False,
    )
```

```python
import functools
import math

import jax
import jax.numpy as jnp
from jax import lax
from jax.experimental import pallas as pl
from jax.experimental.pallas import tpu as pltpu
from jax.sharding import PartitionSpec as P

HD = 128
PAGE = 64
ATTEND_VMEM = 24 * 1024 * 1024
PROJECT_VMEM = 8 * 1024 * 1024
EXCHANGE_FLOPS = 40_000_000_000
SMALL_VMEM = 8 * 1024 * 1024
VMEM = pl.BlockSpec(memory_space=pltpu.VMEM)
HBM = pl.BlockSpec(memory_space=pltpu.HBM)


def split_two(value):
    high = value.astype(jnp.bfloat16).astype(jnp.float32)
    low = (value - high).astype(jnp.bfloat16).astype(jnp.float32)
    return high, low


def attend_kernel(heads_dev, devices, *refs):
    table_hbm, lengths_hbm, key_scale_hbm, value_scale_hbm, queries_hbm, keys, values = refs[:7]
    (staged, table, lengths, key_scale, value_scale, queries, key_buf, value_buf, query_rows, small_sems, sems) = refs[7:]
    rows, pages = table.shape
    kv_heads = key_scale.shape[0]
    heads = queries.shape[1] // HD
    group = heads // kv_heads
    context = pages * PAGE
    pieces = sems.shape[1]
    piece = keys.shape[0] // pieces

    small = []
    for i, (source, target) in enumerate(
        (
            (table_hbm, table),
            (lengths_hbm, lengths),
            (key_scale_hbm, key_scale),
            (value_scale_hbm, value_scale),
            (queries_hbm, queries),
        )
    ):
        small.append(pltpu.make_async_copy(source, target, small_sems.at[i]))
        small[-1].start()
    large = []
    for which, source, target in ((0, keys, key_buf), (1, values, value_buf)):
        large.append([])
        for i in range(pieces):
            here = pl.ds(i * piece, piece)
            large[-1].append(pltpu.make_async_copy(source.at[here], target.at[here], sems.at[which, i]))
    for copy in large[0]:
        copy.start()

    me = lax.axis_index("kvp")
    place = me * context + lax.broadcasted_iota(jnp.int32, (group, context), 1)
    lane = lax.broadcasted_iota(jnp.int32, (group, HD), 1)
    zeros = jnp.zeros((group, HD), jnp.bfloat16)
    for copy in small:
        copy.wait()
    for h in range(heads):
        query_rows[h * rows : (h + 1) * rows, :] = queries[:, h * HD : (h + 1) * HD].astype(jnp.float32)
    for copy in large[1]:
        copy.start()
    for copy in large[0]:
        copy.wait()

    def factors(scales, r, k, times):
        columns = []
        for p in range(0, pages, 2):
            left = scales[k, table[r, p]] * times
            right = scales[k, table[r, p + 1]] * times
            columns.append(jnp.where(lane < PAGE, left, right))
        return jnp.concatenate(columns, axis=1)

    def pages_of(buf, r, k):
        return jnp.concatenate(
            [buf[table[r, p], :, k * HD : (k + 2) * HD] for p in range(pages)], axis=0
        )

    probs = {}
    stats = [jnp.zeros((group, HD), jnp.float32)] * kv_heads
    for r in range(rows):
        visible = place < lengths[r]
        query = query_rows[pl.ds(r, heads, stride=rows), :].astype(jnp.bfloat16)
        for k in range(0, kv_heads, 2):
            left = jnp.concatenate(
                [
                    jnp.concatenate([query[k * group : (k + 1) * group], zeros], axis=1),
                    jnp.concatenate([zeros, query[(k + 1) * group : (k + 2) * group]], axis=1),
                ],
                axis=0,
            )
            both = lax.dot_general(
                left, pages_of(key_buf, r, k), (((1,), (1,)), ((), ())), preferred_element_type=jnp.float32
            )
            weights = []
            for i in (0, 1):
                scores = both[i * group : (i + 1) * group] * factors(key_scale, r, k + i, 1.0 / math.sqrt(HD))
                highest = jnp.max(jnp.where(visible, scores, -1e30), axis=1, keepdims=True)
                high, low = split_two(highest)
                prob = jnp.where(visible, jnp.exp(scores - (high + low)), 0.0)
                total_high, total_low = split_two(jnp.sum(prob, axis=1, keepdims=True))
                for at, value in enumerate((high, low, total_high, total_low)):
                    stats[k + i] = jnp.where(lane == 4 * r + at, value, stats[k + i])
                weights.append((prob * factors(value_scale, r, k + i, 1.0)).astype(jnp.bfloat16))
            probs[r, k] = jnp.concatenate(weights, axis=0)
    for copy in large[1]:
        copy.wait()
    for r in range(rows):
        for k in range(0, kv_heads, 2):
            both = jnp.dot(probs[r, k], pages_of(value_buf, r, k), preferred_element_type=jnp.float32)
            for i in (0, 1):
                partial = both[i * group : (i + 1) * group, i * HD : (i + 1) * HD]
                for start in range(0, group, heads_dev):
                    d = ((k + i) * group + start) // heads_dev
                    staged[d, r] = partial[start : start + heads_dev]
    for k in range(kv_heads):
        for start in range(0, group, heads_dev):
            d = (k * group + start) // heads_dev
            staged[d, rows] = stats[k][start : start + heads_dev]


def pack_kernel(staged, packed):
    packed[...] = staged[...].astype(jnp.bfloat16)


def project_kernel(heads_dev, count, packed, weight, left, out, attended):
    rows = left.shape[0]
    blocks = packed[...].astype(jnp.float32)
    stats = blocks[:, rows]
    for r in range(rows):
        partial = blocks[:, r]
        maxima = stats[:, :, 4 * r : 4 * r + 1] + stats[:, :, 4 * r + 1 : 4 * r + 2]
        totals = stats[:, :, 4 * r + 2 : 4 * r + 3] + stats[:, :, 4 * r + 3 : 4 * r + 4]
        rescale = jnp.exp(maxima - jnp.max(maxima, axis=0, keepdims=True))
        attended[r * heads_dev : (r + 1) * heads_dev, :] = jnp.sum(partial * rescale, axis=0) / jnp.sum(
            totals * rescale, axis=0
        )
    rounded = jnp.concatenate(
        [attended[pl.ds(j, rows, stride=heads_dev), :].astype(jnp.bfloat16) for j in range(heads_dev)], axis=1
    )
    left[...] = rounded
    project_quarters(count, (1, 3), rounded, weight, out)


def project_quarters(count, partners, left, weight, out):
    part = out.shape[2]
    quarter = lax.rem(lax.axis_index("kvp"), count)
    for i, x in enumerate(partners):
        start = pl.multiple_of(jnp.bitwise_xor(quarter, x) * part, part)
        terms = jnp.dot(left, weight[:, pl.ds(start, part)], preferred_element_type=jnp.float32)
        out[i] = terms.astype(out.dtype)


def project_own_kernel(count, left, weight, out):
    project_quarters(count, (0, 2), left[...], weight, out)


def add_core_kernel(own, arrived, keep, send):
    keep[...] = own[0] + arrived[0].astype(jnp.float32)
    send[...] = (own[1] + arrived[1].astype(jnp.float32)).astype(send.dtype)


def add_kernel(*refs):
    terms = [ref[...].astype(jnp.float32) for ref in refs[:-1]]
    while len(terms) > 1:
        terms = [terms[i] + terms[i + 1] for i in range(0, len(terms), 2)]
    refs[-1][...] = terms[0].astype(refs[-1].dtype)


def lay_kernel(*refs):
    parts, out = refs[:-1], refs[-1]
    quarter = lax.rem(lax.axis_index("kvp"), len(parts))
    width = parts[0].shape[1]
    for x, part in enumerate(parts):
        start = pl.multiple_of(jnp.bitwise_xor(quarter, x) * width, width)
        out[:, pl.ds(start, width)] = part[...]


def exchange(array, partner, devices):
    return lax.ppermute(array, "kvp", [(i, i ^ partner) for i in range(devices)])


def in_hbm(array):
    return pltpu.with_memory_space_constraint(array, pltpu.HBM)


def body(queries, key_cache, value_cache, key_scale, value_scale, page_table, lengths, out_weight, *, devices):
    rows, pages = page_table.shape
    slots, _, columns = key_cache.shape
    kv_heads = key_scale.shape[1]
    heads_dev = out_weight.shape[0] // HD
    heads = queries.shape[1] // HD
    features = out_weight.shape[1]
    inner = 4
    outer = devices // inner
    part = features // inner
    staged = pl.pallas_call(
        functools.partial(attend_kernel, heads_dev, devices),
        out_shape=jax.ShapeDtypeStruct((devices, rows + 1, heads_dev, HD), jnp.float32),
        in_specs=[HBM] * 7,
        out_specs=VMEM,
        scratch_shapes=[
            pltpu.SMEM((rows, pages), jnp.int32),
            pltpu.SMEM((rows,), jnp.int32),
            pltpu.SMEM((kv_heads, slots), jnp.float32),
            pltpu.SMEM((kv_heads, slots), jnp.float32),
            pltpu.VMEM((rows, heads * HD), jnp.bfloat16),
            pltpu.VMEM((slots, PAGE, columns), jnp.bfloat16),
            pltpu.VMEM((slots, PAGE, columns), jnp.bfloat16),
            pltpu.VMEM((heads * rows, HD), jnp.float32),
            pltpu.SemaphoreType.DMA((5,)),
            pltpu.SemaphoreType.DMA((2, 4)),
        ],
        compiler_params=pltpu.CompilerParams(vmem_limit_bytes=ATTEND_VMEM),
        cost_estimate=pl.CostEstimate(
            flops=4 * heads * rows * pages * PAGE * HD,
            bytes_accessed=4 * rows * pages * PAGE * columns,
            transcendentals=heads * rows * pages * PAGE,
        ),
        name="attend",
    )(*[in_hbm(a) for a in (page_table, lengths, key_scale.T, value_scale.T, queries, key_cache, value_cache)])

    packed = pl.pallas_call(
        pack_kernel,
        out_shape=jax.ShapeDtypeStruct(staged.shape, jnp.bfloat16),
        in_specs=[VMEM],
        out_specs=VMEM,
        compiler_params=pltpu.CompilerParams(vmem_limit_bytes=SMALL_VMEM),
        cost_estimate=pl.CostEstimate(flops=EXCHANGE_FLOPS, bytes_accessed=6 * staged.size, transcendentals=0),
        name="pack",
    )(staged)

    received = lax.all_to_all(packed, "kvp", split_axis=0, concat_axis=0, tiled=True)

    resident = pltpu.with_memory_space_constraint(out_weight, pltpu.VMEM)
    depth = heads_dev * HD
    def cost(count):
        return pl.CostEstimate(
            flops=2 * rows * depth * part * count, bytes_accessed=2 * depth * part * count, transcendentals=0
        )

    small = pltpu.CompilerParams(vmem_limit_bytes=SMALL_VMEM)
    left, others = pl.pallas_call(
        functools.partial(project_kernel, heads_dev, inner),
        out_shape=[
            jax.ShapeDtypeStruct((rows, depth), jnp.bfloat16),
            jax.ShapeDtypeStruct((2, rows, part), jnp.bfloat16),
        ],
        in_specs=[VMEM] * 2,
        out_specs=[VMEM] * 2,
        scratch_shapes=[pltpu.VMEM((rows * heads_dev, HD), jnp.float32)],
        compiler_params=small,
        cost_estimate=cost(2),
        name="project_others",
    )(received, resident)
    arrived = exchange(others, 1, devices)
    own = pl.pallas_call(
        functools.partial(project_own_kernel, inner),
        out_shape=jax.ShapeDtypeStruct((2, rows, part), jnp.float32),
        in_specs=[VMEM] * 2,
        out_specs=VMEM,
        compiler_params=small,
        cost_estimate=cost(2),
        name="project_own",
    )(left, resident)
    keep, send = pl.pallas_call(
        add_core_kernel,
        out_shape=[
            jax.ShapeDtypeStruct((rows, part), jnp.float32),
            jax.ShapeDtypeStruct((rows, part), jnp.bfloat16),
        ],
        in_specs=[VMEM] * 2,
        out_specs=[VMEM] * 2,
        compiler_params=small,
        name="add_core",
    )(own, arrived)

    def add(terms, name):
        return pl.pallas_call(
            add_kernel,
            out_shape=jax.ShapeDtypeStruct((rows, part), jnp.bfloat16),
            in_specs=[VMEM] * len(terms),
            out_specs=VMEM,
            compiler_params=small,
            name=name,
        )(*terms)

    mine = add([keep, exchange(send, 2, devices)], "add_near")
    mine = add([mine] + [exchange(mine, x * inner, devices) for x in range(1, outer)], "add_far")
    across = exchange(mine, 2, devices)
    parts = [mine, exchange(mine, 1, devices), across, exchange(across, 1, devices)]
    return pl.pallas_call(
        lay_kernel,
        out_shape=jax.ShapeDtypeStruct((rows, features), jnp.bfloat16),
        in_specs=[VMEM] * inner,
        out_specs=VMEM,
        compiler_params=pltpu.CompilerParams(vmem_limit_bytes=SMALL_VMEM),
        name="lay",
    )(*parts)


def solution(mesh):
    placed = (
        P("group", None),
        P(("group", "kvp"), None, None),
        P(("group", "kvp"), None, None),
        P(("group", "kvp"), None),
        P(("group", "kvp"), None),
        P("group", "kvp"),
        P("group"),
        P("kvp", None),
    )
    return jax.shard_map(
        functools.partial(body, devices=mesh.shape["kvp"]),
        mesh=mesh,
        in_specs=placed,
        out_specs=P("group", None),
        check_vma=False,
    )
```

```python
import functools
import math

import jax
import jax.numpy as jnp
from jax import lax
from jax.experimental import pallas as pl
from jax.experimental.pallas import tpu as pltpu
from jax.sharding import PartitionSpec as P

HD = 128
PAGE = 64
ATTEND_VMEM = 24 * 1024 * 1024
PROJECT_VMEM = 8 * 1024 * 1024
EVEN, ODD = 0, 1
EXCHANGE_FLOPS = 40_000_000_000
SMALL_VMEM = 8 * 1024 * 1024
VMEM = pl.BlockSpec(memory_space=pltpu.VMEM)
HBM = pl.BlockSpec(memory_space=pltpu.HBM)


def split_two(value):
    high = value.astype(jnp.bfloat16).astype(jnp.float32)
    low = (value - high).astype(jnp.bfloat16).astype(jnp.float32)
    return high, low


def attend_kernel(heads_dev, devices, *refs):
    table_hbm, lengths_hbm, key_scale_hbm, value_scale_hbm, queries_hbm, keys, values = refs[:7]
    (staged, table, lengths, key_scale, value_scale, queries, key_buf, value_buf, query_rows, small_sems, sems) = refs[7:]
    rows, pages = table.shape
    kv_heads = key_scale.shape[0]
    heads = queries.shape[1] // HD
    group = heads // kv_heads
    context = pages * PAGE
    pieces = sems.shape[1]
    piece = keys.shape[0] // pieces

    small = []
    for i, (source, target) in enumerate(
        (
            (table_hbm, table),
            (lengths_hbm, lengths),
            (key_scale_hbm, key_scale),
            (value_scale_hbm, value_scale),
            (queries_hbm, queries),
        )
    ):
        small.append(pltpu.make_async_copy(source, target, small_sems.at[i]))
        small[-1].start()
    large = []
    for which, source, target in ((0, keys, key_buf), (1, values, value_buf)):
        large.append([])
        for i in range(pieces):
            here = pl.ds(i * piece, piece)
            large[-1].append(pltpu.make_async_copy(source.at[here], target.at[here], sems.at[which, i]))
    for copy in large[0]:
        copy.start()

    me = lax.axis_index("kvp")
    place = me * context + lax.broadcasted_iota(jnp.int32, (group, context), 1)
    lane = lax.broadcasted_iota(jnp.int32, (group, HD), 1)
    zeros = jnp.zeros((group, HD), jnp.bfloat16)
    for copy in small:
        copy.wait()
    for h in range(heads):
        query_rows[h * rows : (h + 1) * rows, :] = queries[:, h * HD : (h + 1) * HD].astype(jnp.float32)
    for copy in large[1]:
        copy.start()
    for copy in large[0]:
        copy.wait()

    def factors(scales, r, k, times):
        columns = []
        for p in range(0, pages, 2):
            left = scales[k, table[r, p]] * times
            right = scales[k, table[r, p + 1]] * times
            columns.append(jnp.where(lane < PAGE, left, right))
        return jnp.concatenate(columns, axis=1)

    def pages_of(buf, r, k):
        return jnp.concatenate(
            [buf[table[r, p], :, k * HD : (k + 2) * HD] for p in range(pages)], axis=0
        )

    probs = {}
    stats = [jnp.zeros((group, HD), jnp.float32)] * kv_heads
    for r in range(rows):
        visible = place < lengths[r]
        query = query_rows[pl.ds(r, heads, stride=rows), :].astype(jnp.bfloat16)
        for k in range(0, kv_heads, 2):
            left = jnp.concatenate(
                [
                    jnp.concatenate([query[k * group : (k + 1) * group], zeros], axis=1),
                    jnp.concatenate([zeros, query[(k + 1) * group : (k + 2) * group]], axis=1),
                ],
                axis=0,
            )
            both = lax.dot_general(
                left, pages_of(key_buf, r, k), (((1,), (1,)), ((), ())), preferred_element_type=jnp.float32
            )
            weights = []
            for i in (0, 1):
                scores = both[i * group : (i + 1) * group] * factors(key_scale, r, k + i, 1.0 / math.sqrt(HD))
                highest = jnp.max(jnp.where(visible, scores, -1e30), axis=1, keepdims=True)
                high, low = split_two(highest)
                prob = jnp.where(visible, jnp.exp(scores - (high + low)), 0.0)
                total_high, total_low = split_two(jnp.sum(prob, axis=1, keepdims=True))
                for at, value in enumerate((high, low, total_high, total_low)):
                    stats[k + i] = jnp.where(lane == 4 * r + at, value, stats[k + i])
                weights.append((prob * factors(value_scale, r, k + i, 1.0)).astype(jnp.bfloat16))
            probs[r, k] = jnp.concatenate(weights, axis=0)
    for copy in large[1]:
        copy.wait()
    for r in range(rows):
        for k in range(0, kv_heads, 2):
            both = jnp.dot(probs[r, k], pages_of(value_buf, r, k), preferred_element_type=jnp.float32)
            for i in (0, 1):
                partial = both[i * group : (i + 1) * group, i * HD : (i + 1) * HD]
                for start in range(0, group, heads_dev):
                    d = ((k + i) * group + start) // heads_dev
                    staged[d, r] = partial[start : start + heads_dev]
    for k in range(kv_heads):
        for start in range(0, group, heads_dev):
            d = (k * group + start) // heads_dev
            staged[d, rows] = stats[k][start : start + heads_dev]


def pack_kernel(staged, packed):
    packed[...] = staged[...].astype(jnp.bfloat16)


def project_kernel(heads_dev, packed, weight, left, out, attended):
    rows = left.shape[0]
    blocks = packed[...].astype(jnp.float32)
    stats = blocks[:, rows]
    for r in range(rows):
        partial = blocks[:, r]
        maxima = stats[:, :, 4 * r : 4 * r + 1] + stats[:, :, 4 * r + 1 : 4 * r + 2]
        totals = stats[:, :, 4 * r + 2 : 4 * r + 3] + stats[:, :, 4 * r + 3 : 4 * r + 4]
        rescale = jnp.exp(maxima - jnp.max(maxima, axis=0, keepdims=True))
        attended[r * heads_dev : (r + 1) * heads_dev, :] = jnp.sum(partial * rescale, axis=0) / jnp.sum(
            totals * rescale, axis=0
        )
    rounded = jnp.concatenate(
        [attended[pl.ds(j, rows, stride=heads_dev), :].astype(jnp.bfloat16) for j in range(heads_dev)], axis=1
    )
    left[...] = rounded
    project_half(1, rounded, weight, out)


def half_of_device():
    return lax.rem(lax.div(lax.axis_index("kvp"), 2), 2)


def project_half(other, left, weight, *outs):
    part = outs[0].shape[1]
    width = part // 2
    half = jnp.bitwise_xor(half_of_device(), other)
    for i in range(2):
        start = pl.multiple_of(half * part + i * width, width)
        terms = jnp.dot(left, weight[:, pl.ds(start, width)], preferred_element_type=jnp.float32)
        for out in outs:
            out[:, i * width : (i + 1) * width] = terms.astype(out.dtype)


def project_own_kernel(left, weight, keep, send):
    project_half(0, left[...], weight, keep, send)


def add_kernel(*refs):
    terms = [ref[...].astype(jnp.float32) for ref in refs[:-1]]
    while len(terms) > 1:
        terms = [terms[i] + terms[i + 1] for i in range(0, len(terms), 2)]
    refs[-1][...] = terms[0].astype(refs[-1].dtype)


def lay_kernel(mine, from_odd, from_core, from_far, out):
    part = mine.shape[1]
    odd = lax.rem(lax.axis_index("kvp"), 2) == 1
    half = half_of_device()
    here = pl.multiple_of(half * part, part)
    there = pl.multiple_of((1 - half) * part, part)

    @pl.when(odd)
    def _():
        out[:, pl.ds(here, part)] = mine[...]
        out[:, pl.ds(there, part)] = from_odd[...]

    @pl.when(jnp.logical_not(odd))
    def _():
        out[:, pl.ds(here, part)] = from_core[...]
        out[:, pl.ds(there, part)] = from_far[...]


def exchange(array, partner, devices, sources):
    return lax.ppermute(array, "kvp", [(i, i ^ partner) for i in range(devices) if i % 2 == sources])


def in_hbm(array):
    return pltpu.with_memory_space_constraint(array, pltpu.HBM)


def body(queries, key_cache, value_cache, key_scale, value_scale, page_table, lengths, out_weight, *, devices):
    rows, pages = page_table.shape
    slots, _, columns = key_cache.shape
    kv_heads = key_scale.shape[1]
    heads_dev = out_weight.shape[0] // HD
    heads = queries.shape[1] // HD
    features = out_weight.shape[1]
    staged = pl.pallas_call(
        functools.partial(attend_kernel, heads_dev, devices),
        out_shape=jax.ShapeDtypeStruct((devices, rows + 1, heads_dev, HD), jnp.float32),
        in_specs=[HBM] * 7,
        out_specs=VMEM,
        scratch_shapes=[
            pltpu.SMEM((rows, pages), jnp.int32),
            pltpu.SMEM((rows,), jnp.int32),
            pltpu.SMEM((kv_heads, slots), jnp.float32),
            pltpu.SMEM((kv_heads, slots), jnp.float32),
            pltpu.VMEM((rows, heads * HD), jnp.bfloat16),
            pltpu.VMEM((slots, PAGE, columns), jnp.bfloat16),
            pltpu.VMEM((slots, PAGE, columns), jnp.bfloat16),
            pltpu.VMEM((heads * rows, HD), jnp.float32),
            pltpu.SemaphoreType.DMA((5,)),
            pltpu.SemaphoreType.DMA((2, 4)),
        ],
        compiler_params=pltpu.CompilerParams(vmem_limit_bytes=ATTEND_VMEM),
        cost_estimate=pl.CostEstimate(
            flops=4 * heads * rows * pages * PAGE * HD,
            bytes_accessed=4 * rows * pages * PAGE * columns,
            transcendentals=heads * rows * pages * PAGE,
        ),
        name="attend",
    )(*[in_hbm(a) for a in (page_table, lengths, key_scale.T, value_scale.T, queries, key_cache, value_cache)])

    packed = pl.pallas_call(
        pack_kernel,
        out_shape=jax.ShapeDtypeStruct(staged.shape, jnp.bfloat16),
        in_specs=[VMEM],
        out_specs=VMEM,
        compiler_params=pltpu.CompilerParams(vmem_limit_bytes=SMALL_VMEM),
        cost_estimate=pl.CostEstimate(flops=EXCHANGE_FLOPS, bytes_accessed=6 * staged.size, transcendentals=0),
        name="pack",
    )(staged)

    received = lax.all_to_all(packed, "kvp", split_axis=0, concat_axis=0, tiled=True)

    resident = pltpu.with_memory_space_constraint(out_weight, pltpu.VMEM)
    depth = heads_dev * HD
    part = features // 2

    def cost(count):
        return pl.CostEstimate(
            flops=2 * rows * depth * part * count, bytes_accessed=2 * depth * part * count, transcendentals=0
        )

    small = pltpu.CompilerParams(vmem_limit_bytes=SMALL_VMEM)
    rounded = jax.ShapeDtypeStruct((rows, part), jnp.bfloat16)
    left, others = pl.pallas_call(
        functools.partial(project_kernel, heads_dev),
        out_shape=[jax.ShapeDtypeStruct((rows, depth), jnp.bfloat16), rounded],
        in_specs=[VMEM] * 2,
        out_specs=[VMEM] * 2,
        scratch_shapes=[pltpu.VMEM((rows * heads_dev, HD), jnp.float32)],
        compiler_params=small,
        cost_estimate=cost(1),
        name="project_others",
    )(received, resident)
    from_far = exchange(others, 3, devices, EVEN)
    from_odd = exchange(others, 2, devices, ODD)
    keep, send = pl.pallas_call(
        project_own_kernel,
        out_shape=[jax.ShapeDtypeStruct((rows, part), jnp.float32), rounded],
        in_specs=[VMEM] * 2,
        out_specs=[VMEM] * 2,
        compiler_params=small,
        cost_estimate=cost(1),
        name="project_own",
    )(left, resident)
    from_core = exchange(send, 1, devices, EVEN)

    def add(terms, name):
        return pl.pallas_call(
            add_kernel,
            out_shape=rounded,
            in_specs=[VMEM] * len(terms),
            out_specs=VMEM,
            compiler_params=small,
            name=name,
        )(*terms)

    mine = add([keep, from_core, from_odd, from_far], "add_near")
    mine = add([mine] + [exchange(mine, x * 4, devices, ODD) for x in range(1, devices // 4)], "add_far")
    from_odd = exchange(mine, 2, devices, ODD)
    from_core = exchange(mine, 1, devices, ODD)
    from_far = exchange(mine, 3, devices, ODD)
    return pl.pallas_call(
        lay_kernel,
        out_shape=jax.ShapeDtypeStruct((rows, features), jnp.bfloat16),
        in_specs=[VMEM] * 4,
        out_specs=VMEM,
        compiler_params=small,
        name="lay",
    )(mine, from_odd, from_core, from_far)


def solution(mesh):
    placed = (
        P("group", None),
        P(("group", "kvp"), None, None),
        P(("group", "kvp"), None, None),
        P(("group", "kvp"), None),
        P(("group", "kvp"), None),
        P("group", "kvp"),
        P("group"),
        P("kvp", None),
    )
    return jax.shard_map(
        functools.partial(body, devices=mesh.shape["kvp"]),
        mesh=mesh,
        in_specs=placed,
        out_specs=P("group", None),
        check_vma=False,
    )
```

```python
import functools
import math

import jax
import jax.numpy as jnp
from jax import lax
from jax.experimental import pallas as pl
from jax.experimental.pallas import tpu as pltpu
from jax.sharding import PartitionSpec as P

HD = 128
PAGE = 64
ATTEND_VMEM = 24 * 1024 * 1024
PROJECT_VMEM = 8 * 1024 * 1024
HIDDEN = -1e30
LOWEST = -1e20
EXCHANGE_FLOPS = 40_000_000_000
SMALL_VMEM = 8 * 1024 * 1024
VMEM = pl.BlockSpec(memory_space=pltpu.VMEM)
HBM = pl.BlockSpec(memory_space=pltpu.HBM)


def split_two(value):
    high = value.astype(jnp.bfloat16).astype(jnp.float32)
    low = (value - high).astype(jnp.bfloat16).astype(jnp.float32)
    return high, low


def attend_kernel(heads_dev, devices, *refs):
    table_hbm, lengths_hbm, key_scale_hbm, value_scale_hbm, queries_hbm, keys, values = refs[:7]
    staged, table, lengths, key_scale, value_scale, queries, key_buf, value_buf, query_rows = refs[7:16]
    key_factor, value_factor, bias, weights, small_sems, sems = refs[16:]
    rows, pages = table.shape
    kv_heads = key_scale.shape[0]
    heads = queries.shape[1] // HD
    group = heads // kv_heads
    context = pages * PAGE
    pieces = sems.shape[1]
    piece = keys.shape[0] // pieces

    small = []
    for i, (source, target) in enumerate(
        (
            (table_hbm, table),
            (lengths_hbm, lengths),
            (key_scale_hbm, key_scale),
            (value_scale_hbm, value_scale),
            (queries_hbm, queries),
        )
    ):
        small.append(pltpu.make_async_copy(source, target, small_sems.at[i]))
        small[-1].start()
    large = []
    for which, source, target in ((0, keys, key_buf), (1, values, value_buf)):
        large.append([])
        for i in range(pieces):
            here = pl.ds(i * piece, piece)
            large[-1].append(pltpu.make_async_copy(source.at[here], target.at[here], sems.at[which, i]))
    for copy in large[0]:
        copy.start()

    me = lax.axis_index("kvp")
    place = me * context + lax.broadcasted_iota(jnp.int32, (1, context), 1)
    lane = lax.broadcasted_iota(jnp.int32, (group, HD), 1)
    left_page = lax.broadcasted_iota(jnp.int32, (8, HD), 1) < PAGE
    zeros = jnp.zeros((group, HD), jnp.bfloat16)
    for copy in small:
        copy.wait()
    for copy in large[1]:
        copy.start()
    for h in range(heads):
        query_rows[h * rows : (h + 1) * rows, :] = queries[:, h * HD : (h + 1) * HD].astype(jnp.float32)
    for r in range(rows):
        bias[r] = jnp.broadcast_to(jnp.where(place < lengths[r], 0.0, HIDDEN), (8, context))
        for p in range(0, pages, 2):
            slots = table[r, p], table[r, p + 1]
            here = slice(p * PAGE, (p + 2) * PAGE)
            for k in range(kv_heads):
                key_factor[r, k, :, here] = jnp.where(left_page, key_scale[k, slots[0]], key_scale[k, slots[1]]) * (
                    math.log2(math.e) / math.sqrt(HD)
                )
                value_factor[r, k, :, here] = jnp.where(left_page, value_scale[k, slots[0]], value_scale[k, slots[1]])
    for copy in large[0]:
        copy.wait()

    def pages_of(buf, r, k):
        return jnp.concatenate(
            [buf[table[r, p], :, k * HD : (k + 2) * HD] for p in range(pages)], axis=0
        )

    def on_rows(row):
        return jnp.concatenate([row] * (group // 8), axis=0)

    stats = [jnp.zeros((group, HD), jnp.float32)] * kv_heads
    for r in range(rows):
        query = query_rows[pl.ds(r, heads, stride=rows), :].astype(jnp.bfloat16)
        for k in range(0, kv_heads, 2):
            left = jnp.concatenate(
                [
                    jnp.concatenate([query[k * group : (k + 1) * group], zeros], axis=1),
                    jnp.concatenate([zeros, query[(k + 1) * group : (k + 2) * group]], axis=1),
                ],
                axis=0,
            )
            both = lax.dot_general(
                left, pages_of(key_buf, r, k), (((1,), (1,)), ((), ())), preferred_element_type=jnp.float32
            )
            for i in (0, 1):
                scores = both[i * group : (i + 1) * group] * on_rows(key_factor[r, k + i]) + on_rows(bias[r])
                highest = jnp.maximum(jnp.max(scores, axis=1, keepdims=True), LOWEST)
                high, low = split_two(highest)
                prob = jnp.exp2(scores - (high + low))
                total_high, total_low = split_two(jnp.sum(prob, axis=1, keepdims=True))
                for at, value in enumerate((high, low, total_high, total_low)):
                    stats[k + i] = jnp.where(lane == 4 * r + at, value, stats[k + i])
                weights[r, (k + i) * group : (k + i + 1) * group] = (prob * on_rows(value_factor[r, k + i])).astype(
                    jnp.bfloat16
                )
    for copy in large[1]:
        copy.wait()
    for r in range(rows):
        for k in range(0, kv_heads, 2):
            both = jnp.dot(
                weights[r, k * group : (k + 2) * group], pages_of(value_buf, r, k), preferred_element_type=jnp.float32
            )
            for i in (0, 1):
                partial = both[i * group : (i + 1) * group, i * HD : (i + 1) * HD]
                for start in range(0, group, heads_dev):
                    d = ((k + i) * group + start) // heads_dev
                    staged[d, r] = partial[start : start + heads_dev]
    for k in range(kv_heads):
        for start in range(0, group, heads_dev):
            d = (k * group + start) // heads_dev
            staged[d, rows] = stats[k][start : start + heads_dev]


def pack_kernel(staged, packed):
    packed[...] = staged[...].astype(jnp.bfloat16)


def project_kernel(heads_dev, packed, weight, left, *refs):
    outs, attended = refs[:-1], refs[-1]
    rows = left.shape[0]
    part = outs[0].shape[1]
    quarter = lax.rem(lax.axis_index("kvp"), len(outs) + 1)
    stats = packed[:, rows].astype(jnp.float32)
    lanes = stats.shape[-1]

    def lanes_ahead(value, by):
        return pltpu.roll(value, lanes - by, axis=2)

    maxima = stats + lanes_ahead(stats, 1)
    rescale = jnp.exp2(maxima - jnp.max(maxima, axis=0, keepdims=True))
    totals = lanes_ahead(stats, 2) + lanes_ahead(stats, 3)
    denominator = jnp.sum(totals * rescale, axis=0)
    for r in range(rows):
        partial = packed[:, r].astype(jnp.float32)
        numerator = jnp.sum(partial * rescale[:, :, 4 * r : 4 * r + 1], axis=0)
        attended[r * heads_dev : (r + 1) * heads_dev, :] = numerator / denominator[:, 4 * r : 4 * r + 1]
    rounded = jnp.concatenate(
        [attended[pl.ds(j, rows, stride=heads_dev), :].astype(jnp.bfloat16) for j in range(heads_dev)], axis=1
    )
    left[...] = rounded
    for x, out in enumerate(outs):
        start = pl.multiple_of(jnp.bitwise_xor(quarter, x + 1) * part, part)
        terms = jnp.dot(rounded, weight[:, pl.ds(start, part)], preferred_element_type=jnp.float32)
        out[...] = terms.astype(jnp.bfloat16)


def project_own_kernel(left, weight, out):
    part = out.shape[1]
    quarter = lax.rem(lax.axis_index("kvp"), weight.shape[1] // part)
    start = pl.multiple_of(quarter * part, part)
    terms = jnp.dot(left[...], weight[:, pl.ds(start, part)], preferred_element_type=jnp.float32)
    out[...] = terms.astype(jnp.bfloat16)


def add_kernel(*refs):
    terms = [ref[...].astype(jnp.float32) for ref in refs[:-1]]
    while len(terms) > 1:
        terms = [terms[i] + terms[i + 1] for i in range(0, len(terms), 2)]
    refs[-1][...] = terms[0].astype(refs[-1].dtype)


def lay_kernel(*refs):
    parts, out = refs[:-1], refs[-1]
    quarter = lax.rem(lax.axis_index("kvp"), len(parts))
    width = parts[0].shape[1]
    for x, part in enumerate(parts):
        start = pl.multiple_of(jnp.bitwise_xor(quarter, x) * width, width)
        out[:, pl.ds(start, width)] = part[...]


def exchange(array, partner, devices):
    return lax.ppermute(array, "kvp", [(i, i ^ partner) for i in range(devices)])


def in_hbm(array):
    return pltpu.with_memory_space_constraint(array, pltpu.HBM)


def body(queries, key_cache, value_cache, key_scale, value_scale, page_table, lengths, out_weight, *, devices):
    rows, pages = page_table.shape
    slots, _, columns = key_cache.shape
    kv_heads = key_scale.shape[1]
    heads_dev = out_weight.shape[0] // HD
    heads = queries.shape[1] // HD
    features = out_weight.shape[1]
    inner = 4
    outer = devices // inner
    part = features // inner
    staged = pl.pallas_call(
        functools.partial(attend_kernel, heads_dev, devices),
        out_shape=jax.ShapeDtypeStruct((devices, rows + 1, heads_dev, HD), jnp.float32),
        in_specs=[HBM] * 7,
        out_specs=VMEM,
        scratch_shapes=[
            pltpu.SMEM((rows, pages), jnp.int32),
            pltpu.SMEM((rows,), jnp.int32),
            pltpu.SMEM((kv_heads, slots), jnp.float32),
            pltpu.SMEM((kv_heads, slots), jnp.float32),
            pltpu.VMEM((rows, heads * HD), jnp.bfloat16),
            pltpu.VMEM((slots, PAGE, columns), jnp.bfloat16),
            pltpu.VMEM((slots, PAGE, columns), jnp.bfloat16),
            pltpu.VMEM((heads * rows, HD), jnp.float32),
            pltpu.VMEM((rows, kv_heads, 8, pages * PAGE), jnp.float32),
            pltpu.VMEM((rows, kv_heads, 8, pages * PAGE), jnp.float32),
            pltpu.VMEM((rows, 8, pages * PAGE), jnp.float32),
            pltpu.VMEM((rows, heads, pages * PAGE), jnp.bfloat16),
            pltpu.SemaphoreType.DMA((5,)),
            pltpu.SemaphoreType.DMA((2, 4)),
        ],
        compiler_params=pltpu.CompilerParams(vmem_limit_bytes=ATTEND_VMEM),
        cost_estimate=pl.CostEstimate(
            flops=4 * heads * rows * pages * PAGE * HD,
            bytes_accessed=4 * rows * pages * PAGE * columns,
            transcendentals=heads * rows * pages * PAGE,
        ),
        name="attend",
    )(*[in_hbm(a) for a in (page_table, lengths, key_scale.T, value_scale.T, queries, key_cache, value_cache)])

    packed = pl.pallas_call(
        pack_kernel,
        out_shape=jax.ShapeDtypeStruct(staged.shape, jnp.bfloat16),
        in_specs=[VMEM],
        out_specs=VMEM,
        compiler_params=pltpu.CompilerParams(vmem_limit_bytes=SMALL_VMEM),
        cost_estimate=pl.CostEstimate(flops=EXCHANGE_FLOPS, bytes_accessed=6 * staged.size, transcendentals=0),
        name="pack",
    )(staged)

    received = lax.all_to_all(packed, "kvp", split_axis=0, concat_axis=0, tiled=True)

    resident = pltpu.with_memory_space_constraint(out_weight, pltpu.VMEM)
    depth = heads_dev * HD
    left, *others = pl.pallas_call(
        functools.partial(project_kernel, heads_dev),
        out_shape=[jax.ShapeDtypeStruct((rows, depth), jnp.bfloat16)]
        + [jax.ShapeDtypeStruct((rows, part), jnp.bfloat16)] * (inner - 1),
        in_specs=[VMEM, VMEM],
        out_specs=[VMEM] * inner,
        scratch_shapes=[pltpu.VMEM((rows * heads_dev, HD), jnp.float32)],
        compiler_params=pltpu.CompilerParams(vmem_limit_bytes=PROJECT_VMEM),
        cost_estimate=pl.CostEstimate(
            flops=2 * rows * depth * part * (inner - 1),
            bytes_accessed=2 * depth * part * (inner - 1),
            transcendentals=0,
        ),
        name="project_others",
    )(received, resident)
    sent = [exchange(others[x - 1], x, devices) for x in range(1, inner)]
    own = pl.pallas_call(
        project_own_kernel,
        out_shape=jax.ShapeDtypeStruct((rows, part), jnp.bfloat16),
        in_specs=[VMEM, VMEM],
        out_specs=VMEM,
        compiler_params=pltpu.CompilerParams(vmem_limit_bytes=PROJECT_VMEM),
        cost_estimate=pl.CostEstimate(
            flops=2 * rows * depth * part, bytes_accessed=2 * depth * part, transcendentals=0
        ),
        name="project_own",
    )(left, resident)

    def add(terms, name):
        return pl.pallas_call(
            add_kernel,
            out_shape=jax.ShapeDtypeStruct((rows, part), jnp.bfloat16),
            in_specs=[VMEM] * len(terms),
            out_specs=VMEM,
            compiler_params=pltpu.CompilerParams(vmem_limit_bytes=SMALL_VMEM),
            name=name,
        )(*terms)

    mine = add([own] + sent, "add_near")
    mine = add([mine] + [exchange(mine, x * inner, devices) for x in range(1, outer)], "add_far")
    parts = [mine] + [exchange(mine, x, devices) for x in range(1, inner)]
    return pl.pallas_call(
        lay_kernel,
        out_shape=jax.ShapeDtypeStruct((rows, features), jnp.bfloat16),
        in_specs=[VMEM] * inner,
        out_specs=VMEM,
        compiler_params=pltpu.CompilerParams(vmem_limit_bytes=SMALL_VMEM),
        name="lay",
    )(*parts)


def solution(mesh):
    placed = (
        P("group", None),
        P(("group", "kvp"), None, None),
        P(("group", "kvp"), None, None),
        P(("group", "kvp"), None),
        P(("group", "kvp"), None),
        P("group", "kvp"),
        P("group"),
        P("kvp", None),
    )
    return jax.shard_map(
        functools.partial(body, devices=mesh.shape["kvp"]),
        mesh=mesh,
        in_specs=placed,
        out_specs=P("group", None),
        check_vma=False,
    )
```

```python
import functools
import math

import jax
import jax.numpy as jnp
from jax import lax
from jax.experimental import pallas as pl
from jax.experimental.pallas import tpu as pltpu
from jax.sharding import PartitionSpec as P

HD = 128
PAGE = 64
ATTEND_VMEM = 24 * 1024 * 1024
PROJECT_VMEM = 8 * 1024 * 1024
HIDDEN = -1e30
LOWEST = -1e20
EXCHANGE_FLOPS = 40_000_000_000
SMALL_VMEM = 8 * 1024 * 1024
VMEM = pl.BlockSpec(memory_space=pltpu.VMEM)
HBM = pl.BlockSpec(memory_space=pltpu.HBM)


def split_two(value):
    high = value.astype(jnp.bfloat16).astype(jnp.float32)
    low = (value - high).astype(jnp.bfloat16).astype(jnp.float32)
    return high, low


def attend_kernel(heads_dev, devices, *refs):
    table_hbm, lengths_hbm, key_scale_hbm, value_scale_hbm, queries_hbm, keys, values = refs[:7]
    staged, table, lengths, key_scale, value_scale, queries, key_buf, value_buf, query_rows = refs[7:16]
    query_blocks, key_rows, value_rows, scores, weight_rows, stats, small_sems, sems = refs[16:]
    rows, pages = table.shape
    kv_heads = key_scale.shape[0]
    heads = queries.shape[1] // HD
    group = heads // kv_heads
    context = pages * PAGE
    pieces = sems.shape[1]
    piece = keys.shape[0] // pieces

    small = []
    for i, (source, target) in enumerate(
        (
            (table_hbm, table),
            (lengths_hbm, lengths),
            (key_scale_hbm, key_scale),
            (value_scale_hbm, value_scale),
            (queries_hbm, queries),
        )
    ):
        small.append(pltpu.make_async_copy(source, target, small_sems.at[i]))
        small[-1].start()
    large = []
    for which, source, target in ((0, keys, key_buf), (1, values, value_buf)):
        large.append([])
        for i in range(pieces):
            here = pl.ds(i * piece, piece)
            large[-1].append(pltpu.make_async_copy(source.at[here], target.at[here], sems.at[which, i]))
    for copy in large[0]:
        copy.start()

    me = lax.axis_index("kvp")
    lane = lax.broadcasted_iota(jnp.int32, (1, HD), 1)
    first_of_pair = lane < heads
    of_lane = lax.rem(lax.div(lane, group), kv_heads)
    spread = (of_lane == lax.broadcasted_iota(jnp.int32, (kv_heads, HD), 0)).astype(jnp.float32)
    place = lax.broadcasted_iota(jnp.int32, (PAGE, HD), 0)
    stats[...] = jnp.zeros_like(stats)
    for copy in small:
        copy.wait()
    for copy in large[1]:
        copy.start()

    def by_slot(scales):
        return lax.dot_general(
            scales[...], spread, (((0,), (0,)), ((), ())),
            precision=lax.Precision.HIGHEST, preferred_element_type=jnp.float32,
        )

    key_rows[...] = by_slot(key_scale) * (math.log2(math.e) / math.sqrt(HD))
    value_rows[...] = by_slot(value_scale)
    for h in range(heads):
        query_rows[h * rows : (h + 1) * rows, :] = queries[:, h * HD : (h + 1) * HD].astype(jnp.float32)
    for r in range(0, rows, 2):
        both = jnp.concatenate([query_rows[pl.ds(r + i, heads, stride=rows), :] for i in (0, 1)], axis=0)
        turned = both.T
        for i in (0, 1):
            for k in range(kv_heads):
                mine = lax.div(lane, group) == i * kv_heads + k
                query_blocks[r + i, k * HD : (k + 1) * HD, :] = jnp.where(mine, turned, 0.0).astype(jnp.bfloat16)

    def pages_of(buf, r, columns):
        return jnp.concatenate([buf[table[r, p], :, columns] for p in range(pages)], axis=0)

    def factor(scale_rows, r, p):
        left, right = (scale_rows[pl.ds(table[r + i, p], 1), :] for i in (0, 1))
        return jnp.where(first_of_pair, left, right)

    for copy in large[0]:
        copy.wait()
    for r in range(rows):
        both = jnp.dot(pages_of(key_buf, r, slice(None)), query_blocks[r], preferred_element_type=jnp.float32)
        if r % 2 == 0:
            scores[r // 2] = both
        else:
            scores[r // 2] += both
    for r in range(0, rows, 2):
        length = jnp.where(first_of_pair, lengths[r], lengths[r + 1]) - me * context
        highest = jnp.full((PAGE, HD), LOWEST, jnp.float32)
        for p in range(pages):
            here = slice(p * PAGE, (p + 1) * PAGE)
            scaled = jnp.where(place < length - p * PAGE, scores[r // 2, here] * factor(key_rows, r, p), HIDDEN)
            scores[r // 2, here] = scaled
            highest = jnp.maximum(highest, scaled)
        high, low = split_two(jnp.max(highest, axis=0, keepdims=True))
        total = jnp.zeros((PAGE, HD), jnp.float32)
        for p in range(0, pages, 2):
            weights = []
            for i in (0, 1):
                here = slice((p + i) * PAGE, (p + i + 1) * PAGE)
                prob = jnp.exp2(scores[r // 2, here] - (high + low))
                total += prob
                weights.append(prob * factor(value_rows, r, p + i))
            turned = jnp.concatenate(weights, axis=0).T
            weight_rows[r // 2, :, p * PAGE : (p + 2) * PAGE] = turned.astype(jnp.bfloat16)
        total_high, total_low = split_two(jnp.sum(total, axis=0, keepdims=True))
        for at, value in enumerate((high, low, total_high, total_low)):
            stats[4 * r + at : 4 * r + at + 1, :] = value
            stats[4 * r + 4 + at : 4 * r + 5 + at, :] = pltpu.roll(value, HD - heads, axis=1)
    by_head = stats[...].T
    for d in range(devices):
        staged[d, rows] = by_head[d * heads_dev : (d + 1) * heads_dev]
    for copy in large[1]:
        copy.wait()
    for r in range(rows):
        for k in range(0, kv_heads, 2):
            first = r % 2 * heads + k * group
            both = jnp.dot(
                weight_rows[r // 2, first : first + 2 * group, :],
                pages_of(value_buf, r, slice(k * HD, (k + 2) * HD)),
                preferred_element_type=jnp.float32,
            )
            for i in (0, 1):
                partial = both[i * group : (i + 1) * group, i * HD : (i + 1) * HD]
                for start in range(0, group, heads_dev):
                    d = ((k + i) * group + start) // heads_dev
                    staged[d, r] = partial[start : start + heads_dev]


def pack_kernel(staged, packed):
    packed[...] = staged[...].astype(jnp.bfloat16)


def project_kernel(heads_dev, packed, weight, left, *refs):
    outs, attended = refs[:-1], refs[-1]
    rows = left.shape[0]
    part = outs[0].shape[1]
    quarter = lax.rem(lax.axis_index("kvp"), len(outs) + 1)
    stats = packed[:, rows].astype(jnp.float32)
    lanes = stats.shape[-1]

    def lanes_ahead(value, by):
        return pltpu.roll(value, lanes - by, axis=2)

    maxima = stats + lanes_ahead(stats, 1)
    rescale = jnp.exp2(maxima - jnp.max(maxima, axis=0, keepdims=True))
    totals = lanes_ahead(stats, 2) + lanes_ahead(stats, 3)
    denominator = jnp.sum(totals * rescale, axis=0)
    for r in range(rows):
        partial = packed[:, r].astype(jnp.float32)
        numerator = jnp.sum(partial * rescale[:, :, 4 * r : 4 * r + 1], axis=0)
        attended[r * heads_dev : (r + 1) * heads_dev, :] = numerator / denominator[:, 4 * r : 4 * r + 1]
    rounded = jnp.concatenate(
        [attended[pl.ds(j, rows, stride=heads_dev), :].astype(jnp.bfloat16) for j in range(heads_dev)], axis=1
    )
    left[...] = rounded
    for x, out in enumerate(outs):
        start = pl.multiple_of(jnp.bitwise_xor(quarter, x + 1) * part, part)
        terms = jnp.dot(rounded, weight[:, pl.ds(start, part)], preferred_element_type=jnp.float32)
        out[...] = terms.astype(jnp.bfloat16)


def project_own_kernel(left, weight, out):
    part = out.shape[1]
    quarter = lax.rem(lax.axis_index("kvp"), weight.shape[1] // part)
    start = pl.multiple_of(quarter * part, part)
    terms = jnp.dot(left[...], weight[:, pl.ds(start, part)], preferred_element_type=jnp.float32)
    out[...] = terms.astype(jnp.bfloat16)


def add_kernel(*refs):
    terms = [ref[...].astype(jnp.float32) for ref in refs[:-1]]
    while len(terms) > 1:
        terms = [terms[i] + terms[i + 1] for i in range(0, len(terms), 2)]
    refs[-1][...] = terms[0].astype(refs[-1].dtype)


def lay_kernel(*refs):
    parts, out = refs[:-1], refs[-1]
    quarter = lax.rem(lax.axis_index("kvp"), len(parts))
    width = parts[0].shape[1]
    for x, part in enumerate(parts):
        start = pl.multiple_of(jnp.bitwise_xor(quarter, x) * width, width)
        out[:, pl.ds(start, width)] = part[...]


def exchange(array, partner, devices):
    return lax.ppermute(array, "kvp", [(i, i ^ partner) for i in range(devices)])


def in_hbm(array):
    return pltpu.with_memory_space_constraint(array, pltpu.HBM)


def body(queries, key_cache, value_cache, key_scale, value_scale, page_table, lengths, out_weight, *, devices):
    rows, pages = page_table.shape
    slots, _, columns = key_cache.shape
    kv_heads = key_scale.shape[1]
    heads_dev = out_weight.shape[0] // HD
    heads = queries.shape[1] // HD
    features = out_weight.shape[1]
    inner = 4
    outer = devices // inner
    part = features // inner
    staged = pl.pallas_call(
        functools.partial(attend_kernel, heads_dev, devices),
        out_shape=jax.ShapeDtypeStruct((devices, rows + 1, heads_dev, HD), jnp.float32),
        in_specs=[HBM] * 7,
        out_specs=VMEM,
        scratch_shapes=[
            pltpu.SMEM((rows, pages), jnp.int32),
            pltpu.SMEM((rows,), jnp.int32),
            pltpu.VMEM((kv_heads, slots), jnp.float32),
            pltpu.VMEM((kv_heads, slots), jnp.float32),
            pltpu.VMEM((rows, heads * HD), jnp.bfloat16),
            pltpu.VMEM((slots, PAGE, columns), jnp.bfloat16),
            pltpu.VMEM((slots, PAGE, columns), jnp.bfloat16),
            pltpu.VMEM((heads * rows, HD), jnp.float32),
            pltpu.VMEM((rows, columns, HD), jnp.bfloat16),
            pltpu.VMEM((slots, HD), jnp.float32),
            pltpu.VMEM((slots, HD), jnp.float32),
            pltpu.VMEM((rows // 2, pages * PAGE, HD), jnp.float32),
            pltpu.VMEM((rows // 2, HD, pages * PAGE), jnp.bfloat16),
            pltpu.VMEM((HD, HD), jnp.float32),
            pltpu.SemaphoreType.DMA((5,)),
            pltpu.SemaphoreType.DMA((2, 4)),
        ],
        compiler_params=pltpu.CompilerParams(vmem_limit_bytes=ATTEND_VMEM),
        cost_estimate=pl.CostEstimate(
            flops=4 * heads * rows * pages * PAGE * HD,
            bytes_accessed=4 * rows * pages * PAGE * columns,
            transcendentals=heads * rows * pages * PAGE,
        ),
        name="attend",
    )(*[in_hbm(a) for a in (page_table, lengths, key_scale.T, value_scale.T, queries, key_cache, value_cache)])

    packed = pl.pallas_call(
        pack_kernel,
        out_shape=jax.ShapeDtypeStruct(staged.shape, jnp.bfloat16),
        in_specs=[VMEM],
        out_specs=VMEM,
        compiler_params=pltpu.CompilerParams(vmem_limit_bytes=SMALL_VMEM),
        cost_estimate=pl.CostEstimate(flops=EXCHANGE_FLOPS, bytes_accessed=6 * staged.size, transcendentals=0),
        name="pack",
    )(staged)

    received = lax.all_to_all(packed, "kvp", split_axis=0, concat_axis=0, tiled=True)

    resident = pltpu.with_memory_space_constraint(out_weight, pltpu.VMEM)
    depth = heads_dev * HD
    left, *others = pl.pallas_call(
        functools.partial(project_kernel, heads_dev),
        out_shape=[jax.ShapeDtypeStruct((rows, depth), jnp.bfloat16)]
        + [jax.ShapeDtypeStruct((rows, part), jnp.bfloat16)] * (inner - 1),
        in_specs=[VMEM, VMEM],
        out_specs=[VMEM] * inner,
        scratch_shapes=[pltpu.VMEM((rows * heads_dev, HD), jnp.float32)],
        compiler_params=pltpu.CompilerParams(vmem_limit_bytes=PROJECT_VMEM),
        cost_estimate=pl.CostEstimate(
            flops=2 * rows * depth * part * (inner - 1),
            bytes_accessed=2 * depth * part * (inner - 1),
            transcendentals=0,
        ),
        name="project_others",
    )(received, resident)
    sent = [exchange(others[x - 1], x, devices) for x in range(1, inner)]
    own = pl.pallas_call(
        project_own_kernel,
        out_shape=jax.ShapeDtypeStruct((rows, part), jnp.bfloat16),
        in_specs=[VMEM, VMEM],
        out_specs=VMEM,
        compiler_params=pltpu.CompilerParams(vmem_limit_bytes=PROJECT_VMEM),
        cost_estimate=pl.CostEstimate(
            flops=2 * rows * depth * part, bytes_accessed=2 * depth * part, transcendentals=0
        ),
        name="project_own",
    )(left, resident)

    def add(terms, name):
        return pl.pallas_call(
            add_kernel,
            out_shape=jax.ShapeDtypeStruct((rows, part), jnp.bfloat16),
            in_specs=[VMEM] * len(terms),
            out_specs=VMEM,
            compiler_params=pltpu.CompilerParams(vmem_limit_bytes=SMALL_VMEM),
            name=name,
        )(*terms)

    mine = add([own] + sent, "add_near")
    mine = add([mine] + [exchange(mine, x * inner, devices) for x in range(1, outer)], "add_far")
    parts = [mine] + [exchange(mine, x, devices) for x in range(1, inner)]
    return pl.pallas_call(
        lay_kernel,
        out_shape=jax.ShapeDtypeStruct((rows, features), jnp.bfloat16),
        in_specs=[VMEM] * inner,
        out_specs=VMEM,
        compiler_params=pltpu.CompilerParams(vmem_limit_bytes=SMALL_VMEM),
        name="lay",
    )(*parts)


def solution(mesh):
    placed = (
        P("group", None),
        P(("group", "kvp"), None, None),
        P(("group", "kvp"), None, None),
        P(("group", "kvp"), None),
        P(("group", "kvp"), None),
        P("group", "kvp"),
        P("group"),
        P("kvp", None),
    )
    return jax.shard_map(
        functools.partial(body, devices=mesh.shape["kvp"]),
        mesh=mesh,
        in_specs=placed,
        out_specs=P("group", None),
        check_vma=False,
    )
```

```python
import functools
import math

import jax
import jax.numpy as jnp
from jax import lax
from jax.experimental import pallas as pl
from jax.experimental.pallas import tpu as pltpu
from jax.sharding import PartitionSpec as P

HD = 128
PAGE = 64
ATTEND_VMEM = 60 * 1024 * 1024
PROJECT_VMEM = 8 * 1024 * 1024
HIDDEN = -1e30
LOWEST = -1e20
EXCHANGE_FLOPS = 40_000_000_000
SMALL_VMEM = 8 * 1024 * 1024
VMEM = pl.BlockSpec(memory_space=pltpu.VMEM)
HBM = pl.BlockSpec(memory_space=pltpu.HBM)


def split_two(value):
    high = value.astype(jnp.bfloat16).astype(jnp.float32)
    low = (value - high).astype(jnp.bfloat16).astype(jnp.float32)
    return high, low


def attend_kernel(heads_dev, devices, *refs):
    table_hbm, lengths_hbm, key_scale_hbm, value_scale_hbm, queries_hbm, keys, values = refs[:7]
    staged, table, lengths, key_scale, value_scale, queries, key_buf, value_buf, query_rows = refs[7:16]
    query_blocks, key_rows, value_rows, scores, weight_rows, stats, small_sems, sems = refs[16:]
    rows, pages = table.shape
    kv_heads = key_scale.shape[0]
    heads = queries.shape[1] // HD
    group = heads // kv_heads
    context = pages * PAGE
    pieces = sems.shape[1]
    piece = keys.shape[0] // pieces

    small = []
    for i, (source, target) in enumerate(
        (
            (table_hbm, table),
            (lengths_hbm, lengths),
            (key_scale_hbm, key_scale),
            (value_scale_hbm, value_scale),
            (queries_hbm, queries),
        )
    ):
        small.append(pltpu.make_async_copy(source, target, small_sems.at[i]))
        small[-1].start()
    large = []
    for which, source, target in ((0, keys, key_buf), (1, values, value_buf)):
        large.append([])
        for i in range(pieces):
            here = pl.ds(i * piece, piece)
            large[-1].append(pltpu.make_async_copy(source.at[here], target.at[here], sems.at[which, i]))
    for copy in large[0]:
        copy.start()

    me = lax.axis_index("kvp")
    lane = lax.broadcasted_iota(jnp.int32, (1, HD), 1)
    first_of_pair = lane < heads
    of_lane = lax.rem(lax.div(lane, group), kv_heads)
    spread = (of_lane == lax.broadcasted_iota(jnp.int32, (kv_heads, HD), 0)).astype(jnp.float32)
    place = lax.broadcasted_iota(jnp.int32, (PAGE, HD), 0)
    stats[...] = jnp.zeros_like(stats)
    for copy in small:
        copy.wait()
    for copy in large[1]:
        copy.start()

    def by_slot(scales):
        return lax.dot_general(
            scales[...], spread, (((0,), (0,)), ((), ())),
            precision=lax.Precision.HIGHEST, preferred_element_type=jnp.float32,
        )

    key_rows[...] = by_slot(key_scale) * (math.log2(math.e) / math.sqrt(HD))
    value_rows[...] = by_slot(value_scale)
    for h in range(heads):
        query_rows[h * rows : (h + 1) * rows, :] = queries[:, h * HD : (h + 1) * HD].astype(jnp.float32)
    for r in range(0, rows, 2):
        both = jnp.concatenate([query_rows[pl.ds(r + i, heads, stride=rows), :] for i in (0, 1)], axis=0)
        turned = both.T
        for i in (0, 1):
            for k in range(kv_heads):
                mine = lax.div(lane, group) == i * kv_heads + k
                query_blocks[r + i, k * HD : (k + 1) * HD, :] = jnp.where(mine, turned, 0.0).astype(jnp.bfloat16)

    def pages_of(buf, r, columns):
        return jnp.concatenate([buf[table[r, p], :, columns] for p in range(pages)], axis=0)

    def factor(scale_rows, r, p):
        left, right = (scale_rows[pl.ds(table[r + i, p], 1), :] for i in (0, 1))
        return jnp.where(first_of_pair, left, right)

    for copy in large[0]:
        copy.wait()
    for r in range(rows):
        both = jnp.dot(pages_of(key_buf, r, slice(None)), query_blocks[r], preferred_element_type=jnp.float32)
        if r % 2 == 0:
            scores[r // 2] = both
        else:
            scores[r // 2] += both
    for r in range(0, rows, 2):
        length = jnp.where(first_of_pair, lengths[r], lengths[r + 1]) - me * context
        highest = jnp.full((PAGE, HD), LOWEST, jnp.float32)
        for p in range(pages):
            here = slice(p * PAGE, (p + 1) * PAGE)
            scaled = jnp.where(place < length - p * PAGE, scores[r // 2, here] * factor(key_rows, r, p), HIDDEN)
            scores[r // 2, here] = scaled
            highest = jnp.maximum(highest, scaled)
        high, low = split_two(jnp.max(highest, axis=0, keepdims=True))
        total = jnp.zeros((PAGE, HD), jnp.float32)
        for p in range(0, pages, 2):
            weights = []
            for i in (0, 1):
                here = slice((p + i) * PAGE, (p + i + 1) * PAGE)
                prob = jnp.exp2(scores[r // 2, here] - (high + low))
                total += prob
                weights.append(prob * factor(value_rows, r, p + i))
            turned = jnp.concatenate(weights, axis=0).T
            weight_rows[r // 2, :, p * PAGE : (p + 2) * PAGE] = turned.astype(jnp.bfloat16)
        total_high, total_low = split_two(jnp.sum(total, axis=0, keepdims=True))
        for at, value in enumerate((high, low, total_high, total_low)):
            stats[4 * r + at : 4 * r + at + 1, :] = value
            stats[4 * r + 4 + at : 4 * r + 5 + at, :] = pltpu.roll(value, HD - heads, axis=1)
    by_head = stats[...].T
    for d in range(devices):
        staged[d, rows] = by_head[d * heads_dev : (d + 1) * heads_dev]
    for copy in large[1]:
        copy.wait()
    for r in range(rows):
        for k in range(0, kv_heads, 2):
            first = r % 2 * heads + k * group
            both = jnp.dot(
                weight_rows[r // 2, first : first + 2 * group, :],
                pages_of(value_buf, r, slice(k * HD, (k + 2) * HD)),
                preferred_element_type=jnp.float32,
            )
            for i in (0, 1):
                partial = both[i * group : (i + 1) * group, i * HD : (i + 1) * HD]
                for start in range(0, group, heads_dev):
                    d = ((k + i) * group + start) // heads_dev
                    staged[d, r] = partial[start : start + heads_dev]


def pack_kernel(staged, packed):
    packed[...] = staged[...].astype(jnp.bfloat16)


def project_kernel(heads_dev, packed, weight, left, *refs):
    outs, attended = refs[:-1], refs[-1]
    rows = left.shape[0]
    part = outs[0].shape[1]
    quarter = lax.rem(lax.axis_index("kvp"), len(outs) + 1)
    stats = packed[:, rows].astype(jnp.float32)
    lanes = stats.shape[-1]

    def lanes_ahead(value, by):
        return pltpu.roll(value, lanes - by, axis=2)

    maxima = stats + lanes_ahead(stats, 1)
    rescale = jnp.exp2(maxima - jnp.max(maxima, axis=0, keepdims=True))
    totals = lanes_ahead(stats, 2) + lanes_ahead(stats, 3)
    denominator = jnp.sum(totals * rescale, axis=0)
    for r in range(rows):
        partial = packed[:, r].astype(jnp.float32)
        numerator = jnp.sum(partial * rescale[:, :, 4 * r : 4 * r + 1], axis=0)
        attended[r * heads_dev : (r + 1) * heads_dev, :] = numerator / denominator[:, 4 * r : 4 * r + 1]
    rounded = jnp.concatenate(
        [attended[pl.ds(j, rows, stride=heads_dev), :].astype(jnp.bfloat16) for j in range(heads_dev)], axis=1
    )
    left[...] = rounded
    for x, out in enumerate(outs):
        start = pl.multiple_of(jnp.bitwise_xor(quarter, x + 1) * part, part)
        terms = jnp.dot(rounded, weight[:, pl.ds(start, part)], preferred_element_type=jnp.float32)
        out[...] = terms.astype(jnp.bfloat16)


def project_own_kernel(left, weight, out):
    part = out.shape[1]
    quarter = lax.rem(lax.axis_index("kvp"), weight.shape[1] // part)
    start = pl.multiple_of(quarter * part, part)
    terms = jnp.dot(left[...], weight[:, pl.ds(start, part)], preferred_element_type=jnp.float32)
    out[...] = terms.astype(jnp.bfloat16)


def add_kernel(*refs):
    terms = [ref[...].astype(jnp.float32) for ref in refs[:-1]]
    while len(terms) > 1:
        terms = [terms[i] + terms[i + 1] for i in range(0, len(terms), 2)]
    refs[-1][...] = terms[0].astype(refs[-1].dtype)


def lay_kernel(*refs):
    parts, out = refs[:-1], refs[-1]
    quarter = lax.rem(lax.axis_index("kvp"), len(parts))
    width = parts[0].shape[1]
    for x, part in enumerate(parts):
        start = pl.multiple_of(jnp.bitwise_xor(quarter, x) * width, width)
        out[:, pl.ds(start, width)] = part[...]


def exchange(array, partner, devices):
    return lax.ppermute(array, "kvp", [(i, i ^ partner) for i in range(devices)])


def in_hbm(array):
    return pltpu.with_memory_space_constraint(array, pltpu.HBM)


def body(queries, key_cache, value_cache, key_scale, value_scale, page_table, lengths, out_weight, *, devices):
    rows, pages = page_table.shape
    slots, _, columns = key_cache.shape
    kv_heads = key_scale.shape[1]
    heads_dev = out_weight.shape[0] // HD
    heads = queries.shape[1] // HD
    features = out_weight.shape[1]
    inner = 4
    outer = devices // inner
    part = features // inner
    staged = pl.pallas_call(
        functools.partial(attend_kernel, heads_dev, devices),
        out_shape=pltpu.VMEM((devices, rows + 1, heads_dev, HD), jnp.float32),
        in_specs=[HBM] * 7,
        out_specs=VMEM,
        scratch_shapes=[
            pltpu.SMEM((rows, pages), jnp.int32),
            pltpu.SMEM((rows,), jnp.int32),
            pltpu.VMEM((kv_heads, slots), jnp.float32),
            pltpu.VMEM((kv_heads, slots), jnp.float32),
            pltpu.VMEM((rows, heads * HD), jnp.bfloat16),
            pltpu.VMEM((slots, PAGE, columns), jnp.bfloat16),
            pltpu.VMEM((slots, PAGE, columns), jnp.bfloat16),
            pltpu.VMEM((heads * rows, HD), jnp.float32),
            pltpu.VMEM((rows, columns, HD), jnp.bfloat16),
            pltpu.VMEM((slots, HD), jnp.float32),
            pltpu.VMEM((slots, HD), jnp.float32),
            pltpu.VMEM((rows // 2, pages * PAGE, HD), jnp.float32),
            pltpu.VMEM((rows // 2, HD, pages * PAGE), jnp.bfloat16),
            pltpu.VMEM((HD, HD), jnp.float32),
            pltpu.SemaphoreType.DMA((5,)),
            pltpu.SemaphoreType.DMA((2, 4)),
        ],
        compiler_params=pltpu.CompilerParams(vmem_limit_bytes=ATTEND_VMEM),
        cost_estimate=pl.CostEstimate(
            flops=4 * heads * rows * pages * PAGE * HD,
            bytes_accessed=4 * rows * pages * PAGE * columns,
            transcendentals=heads * rows * pages * PAGE,
        ),
        name="attend",
    )(*[in_hbm(a) for a in (page_table, lengths, key_scale.T, value_scale.T, queries, key_cache, value_cache)])

    packed = pl.pallas_call(
        pack_kernel,
        out_shape=jax.ShapeDtypeStruct(staged.shape, jnp.bfloat16),
        in_specs=[VMEM],
        out_specs=VMEM,
        compiler_params=pltpu.CompilerParams(vmem_limit_bytes=SMALL_VMEM),
        cost_estimate=pl.CostEstimate(flops=EXCHANGE_FLOPS, bytes_accessed=6 * staged.size, transcendentals=0),
        name="pack",
    )(staged)

    received = lax.all_to_all(packed, "kvp", split_axis=0, concat_axis=0, tiled=True)

    resident = pltpu.with_memory_space_constraint(out_weight, pltpu.VMEM)
    depth = heads_dev * HD
    left, *others = pl.pallas_call(
        functools.partial(project_kernel, heads_dev),
        out_shape=[jax.ShapeDtypeStruct((rows, depth), jnp.bfloat16)]
        + [jax.ShapeDtypeStruct((rows, part), jnp.bfloat16)] * (inner - 1),
        in_specs=[VMEM, VMEM],
        out_specs=[VMEM] * inner,
        scratch_shapes=[pltpu.VMEM((rows * heads_dev, HD), jnp.float32)],
        compiler_params=pltpu.CompilerParams(vmem_limit_bytes=PROJECT_VMEM),
        cost_estimate=pl.CostEstimate(
            flops=2 * rows * depth * part * (inner - 1),
            bytes_accessed=2 * depth * part * (inner - 1),
            transcendentals=0,
        ),
        name="project_others",
    )(received, resident)
    sent = [exchange(others[x - 1], x, devices) for x in range(1, inner)]
    own = pl.pallas_call(
        project_own_kernel,
        out_shape=jax.ShapeDtypeStruct((rows, part), jnp.bfloat16),
        in_specs=[VMEM, VMEM],
        out_specs=VMEM,
        compiler_params=pltpu.CompilerParams(vmem_limit_bytes=PROJECT_VMEM),
        cost_estimate=pl.CostEstimate(
            flops=2 * rows * depth * part, bytes_accessed=2 * depth * part, transcendentals=0
        ),
        name="project_own",
    )(left, resident)

    def add(terms, name):
        return pl.pallas_call(
            add_kernel,
            out_shape=jax.ShapeDtypeStruct((rows, part), jnp.bfloat16),
            in_specs=[VMEM] * len(terms),
            out_specs=VMEM,
            compiler_params=pltpu.CompilerParams(vmem_limit_bytes=SMALL_VMEM),
            name=name,
        )(*terms)

    mine = add([own] + sent, "add_near")
    mine = add([mine] + [exchange(mine, x * inner, devices) for x in range(1, outer)], "add_far")
    parts = [mine] + [exchange(mine, x, devices) for x in range(1, inner)]
    return pl.pallas_call(
        lay_kernel,
        out_shape=jax.ShapeDtypeStruct((rows, features), jnp.bfloat16),
        in_specs=[VMEM] * inner,
        out_specs=VMEM,
        compiler_params=pltpu.CompilerParams(vmem_limit_bytes=SMALL_VMEM),
        name="lay",
    )(*parts)


def solution(mesh):
    placed = (
        P("group", None),
        P(("group", "kvp"), None, None),
        P(("group", "kvp"), None, None),
        P(("group", "kvp"), None),
        P(("group", "kvp"), None),
        P("group", "kvp"),
        P("group"),
        P("kvp", None),
    )
    return jax.shard_map(
        functools.partial(body, devices=mesh.shape["kvp"]),
        mesh=mesh,
        in_specs=placed,
        out_specs=P("group", None),
        check_vma=False,
    )
```

```python
import functools
import math

import jax
import jax.numpy as jnp
from jax import lax
from jax.experimental import pallas as pl
from jax.experimental.pallas import tpu as pltpu
from jax.sharding import PartitionSpec as P

HD = 128
PAGE = 64
ATTEND_VMEM = 60 * 1024 * 1024
HIDDEN = -1e30
LOWEST = -1e20
EXCHANGE_FLOPS = 40_000_000_000
SMALL_VMEM = 8 * 1024 * 1024
VMEM = pl.BlockSpec(memory_space=pltpu.VMEM)
HBM = pl.BlockSpec(memory_space=pltpu.HBM)


def split_two(value):
    high = value.astype(jnp.bfloat16).astype(jnp.float32)
    low = (value - high).astype(jnp.bfloat16).astype(jnp.float32)
    return high, low


def attend_kernel(heads_dev, devices, *refs):
    table_hbm, lengths_hbm, key_scale_hbm, value_scale_hbm, queries_hbm, keys, values = refs[:7]
    staged, table, lengths, key_scale, value_scale, queries, key_buf, value_buf, query_rows = refs[7:16]
    query_blocks, key_rows, value_rows, scores, weight_rows, stats, small_sems, sems = refs[16:]
    rows, pages = table.shape
    kv_heads = key_scale.shape[0]
    heads = queries.shape[1] // HD
    group = heads // kv_heads
    context = pages * PAGE
    pieces = sems.shape[1]
    piece = keys.shape[0] // pieces

    small = []
    for i, (source, target) in enumerate(
        (
            (table_hbm, table),
            (lengths_hbm, lengths),
            (key_scale_hbm, key_scale),
            (value_scale_hbm, value_scale),
            (queries_hbm, queries),
        )
    ):
        small.append(pltpu.make_async_copy(source, target, small_sems.at[i]))
        small[-1].start()
    large = []
    for which, source, target in ((0, keys, key_buf), (1, values, value_buf)):
        large.append([])
        for i in range(pieces):
            here = pl.ds(i * piece, piece)
            large[-1].append(pltpu.make_async_copy(source.at[here], target.at[here], sems.at[which, i]))
    for copy in large[0]:
        copy.start()

    me = lax.axis_index("kvp")
    lane = lax.broadcasted_iota(jnp.int32, (1, HD), 1)
    first_of_pair = lane < heads
    of_lane = lax.rem(lax.div(lane, group), kv_heads)
    spread = (of_lane == lax.broadcasted_iota(jnp.int32, (kv_heads, HD), 0)).astype(jnp.float32)
    place = lax.broadcasted_iota(jnp.int32, (PAGE, HD), 0)
    stats[...] = jnp.zeros_like(stats)
    for copy in small:
        copy.wait()
    for copy in large[1]:
        copy.start()

    def by_slot(scales):
        return lax.dot_general(
            scales[...], spread, (((0,), (0,)), ((), ())),
            precision=lax.Precision.HIGHEST, preferred_element_type=jnp.float32,
        )

    key_rows[...] = by_slot(key_scale) * (math.log2(math.e) / math.sqrt(HD))
    value_rows[...] = by_slot(value_scale)
    for h in range(heads):
        query_rows[h * rows : (h + 1) * rows, :] = queries[:, h * HD : (h + 1) * HD].astype(jnp.float32)
    for r in range(0, rows, 2):
        both = jnp.concatenate([query_rows[pl.ds(r + i, heads, stride=rows), :] for i in (0, 1)], axis=0)
        turned = both.T
        for i in (0, 1):
            for k in range(kv_heads):
                mine = lax.div(lane, group) == i * kv_heads + k
                query_blocks[r + i, k * HD : (k + 1) * HD, :] = jnp.where(mine, turned, 0.0).astype(jnp.bfloat16)

    def pages_of(buf, r, columns):
        return jnp.concatenate([buf[table[r, p], :, columns] for p in range(pages)], axis=0)

    def factor(scale_rows, r, p):
        left, right = (scale_rows[pl.ds(table[r + i, p], 1), :] for i in (0, 1))
        return jnp.where(first_of_pair, left, right)

    for copy in large[0]:
        copy.wait()
    for r in range(rows):
        both = jnp.dot(pages_of(key_buf, r, slice(None)), query_blocks[r], preferred_element_type=jnp.float32)
        if r % 2 == 0:
            scores[r // 2] = both
        else:
            scores[r // 2] += both
    for r in range(0, rows, 2):
        length = jnp.where(first_of_pair, lengths[r], lengths[r + 1]) - me * context
        highest = jnp.full((PAGE, HD), LOWEST, jnp.float32)
        for p in range(pages):
            here = slice(p * PAGE, (p + 1) * PAGE)
            scaled = jnp.where(place < length - p * PAGE, scores[r // 2, here] * factor(key_rows, r, p), HIDDEN)
            scores[r // 2, here] = scaled
            highest = jnp.maximum(highest, scaled)
        high, low = split_two(jnp.max(highest, axis=0, keepdims=True))
        total = jnp.zeros((PAGE, HD), jnp.float32)
        for p in range(0, pages, 2):
            weights = []
            for i in (0, 1):
                here = slice((p + i) * PAGE, (p + i + 1) * PAGE)
                prob = jnp.exp2(scores[r // 2, here] - (high + low))
                total += prob
                weights.append(prob * factor(value_rows, r, p + i))
            turned = jnp.concatenate(weights, axis=0).T
            weight_rows[r // 2, :, p * PAGE : (p + 2) * PAGE] = turned.astype(jnp.bfloat16)
        total_high, total_low = split_two(jnp.sum(total, axis=0, keepdims=True))
        for at, value in enumerate((high, low, total_high, total_low)):
            stats[4 * r + at : 4 * r + at + 1, :] = value
            stats[4 * r + 4 + at : 4 * r + 5 + at, :] = pltpu.roll(value, HD - heads, axis=1)
    by_head = stats[...].T
    for d in range(devices):
        staged[d, rows] = by_head[d * heads_dev : (d + 1) * heads_dev]
    for copy in large[1]:
        copy.wait()
    for r in range(rows):
        for k in range(0, kv_heads, 2):
            first = r % 2 * heads + k * group
            both = jnp.dot(
                weight_rows[r // 2, first : first + 2 * group, :],
                pages_of(value_buf, r, slice(k * HD, (k + 2) * HD)),
                preferred_element_type=jnp.float32,
            )
            for i in (0, 1):
                partial = both[i * group : (i + 1) * group, i * HD : (i + 1) * HD]
                for start in range(0, group, heads_dev):
                    d = ((k + i) * group + start) // heads_dev
                    staged[d, r] = partial[start : start + heads_dev]


def pack_kernel(staged, packed):
    packed[...] = staged[...].astype(jnp.bfloat16)


def combine_kernel(heads_dev, packed, left, attended):
    rows = left.shape[0]
    stats = packed[:, rows].astype(jnp.float32)
    lanes = stats.shape[-1]

    def lanes_ahead(value, by):
        return pltpu.roll(value, lanes - by, axis=2)

    maxima = stats + lanes_ahead(stats, 1)
    rescale = jnp.exp2(maxima - jnp.max(maxima, axis=0, keepdims=True))
    totals = lanes_ahead(stats, 2) + lanes_ahead(stats, 3)
    denominator = jnp.sum(totals * rescale, axis=0)
    for r in range(rows):
        partial = packed[:, r].astype(jnp.float32)
        numerator = jnp.sum(partial * rescale[:, :, 4 * r : 4 * r + 1], axis=0)
        attended[r * heads_dev : (r + 1) * heads_dev, :] = numerator / denominator[:, 4 * r : 4 * r + 1]
    rounded = jnp.concatenate(
        [attended[pl.ds(j, rows, stride=heads_dev), :].astype(jnp.bfloat16) for j in range(heads_dev)], axis=1
    )
    left[...] = rounded


def project_kernel(partner, left, weight, out):
    part = out.shape[1]
    quarter = lax.rem(lax.axis_index("kvp"), weight.shape[1] // part)
    start = pl.multiple_of(jnp.bitwise_xor(quarter, partner) * part, part)
    terms = jnp.dot(left[...], weight[:, pl.ds(start, part)], preferred_element_type=jnp.float32)
    out[...] = terms.astype(out.dtype)


def add_kernel(*refs):
    terms = [ref[...].astype(jnp.float32) for ref in refs[:-1]]
    while len(terms) > 1:
        terms = [terms[i] + terms[i + 1] for i in range(0, len(terms), 2)]
    refs[-1][...] = terms[0].astype(refs[-1].dtype)


def lay_kernel(*refs):
    parts, out = refs[:-1], refs[-1]
    quarter = lax.rem(lax.axis_index("kvp"), len(parts))
    width = parts[0].shape[1]
    for x, part in enumerate(parts):
        start = pl.multiple_of(jnp.bitwise_xor(quarter, x) * width, width)
        out[:, pl.ds(start, width)] = part[...]


def exchange(array, partner, devices):
    return lax.ppermute(array, "kvp", [(i, i ^ partner) for i in range(devices)])


def in_hbm(array):
    return pltpu.with_memory_space_constraint(array, pltpu.HBM)


def body(queries, key_cache, value_cache, key_scale, value_scale, page_table, lengths, out_weight, *, devices):
    rows, pages = page_table.shape
    slots, _, columns = key_cache.shape
    kv_heads = key_scale.shape[1]
    heads_dev = out_weight.shape[0] // HD
    heads = queries.shape[1] // HD
    features = out_weight.shape[1]
    inner = 4
    outer = devices // inner
    part = features // inner
    staged = pl.pallas_call(
        functools.partial(attend_kernel, heads_dev, devices),
        out_shape=pltpu.VMEM((devices, rows + 1, heads_dev, HD), jnp.float32),
        in_specs=[HBM] * 7,
        out_specs=VMEM,
        scratch_shapes=[
            pltpu.SMEM((rows, pages), jnp.int32),
            pltpu.SMEM((rows,), jnp.int32),
            pltpu.VMEM((kv_heads, slots), jnp.float32),
            pltpu.VMEM((kv_heads, slots), jnp.float32),
            pltpu.VMEM((rows, heads * HD), jnp.bfloat16),
            pltpu.VMEM((slots, PAGE, columns), jnp.bfloat16),
            pltpu.VMEM((slots, PAGE, columns), jnp.bfloat16),
            pltpu.VMEM((heads * rows, HD), jnp.float32),
            pltpu.VMEM((rows, columns, HD), jnp.bfloat16),
            pltpu.VMEM((slots, HD), jnp.float32),
            pltpu.VMEM((slots, HD), jnp.float32),
            pltpu.VMEM((rows // 2, pages * PAGE, HD), jnp.float32),
            pltpu.VMEM((rows // 2, HD, pages * PAGE), jnp.bfloat16),
            pltpu.VMEM((HD, HD), jnp.float32),
            pltpu.SemaphoreType.DMA((5,)),
            pltpu.SemaphoreType.DMA((2, 4)),
        ],
        compiler_params=pltpu.CompilerParams(vmem_limit_bytes=ATTEND_VMEM),
        cost_estimate=pl.CostEstimate(
            flops=4 * heads * rows * pages * PAGE * HD,
            bytes_accessed=4 * rows * pages * PAGE * columns,
            transcendentals=heads * rows * pages * PAGE,
        ),
        name="attend",
    )(*[in_hbm(a) for a in (page_table, lengths, key_scale.T, value_scale.T, queries, key_cache, value_cache)])

    packed = pl.pallas_call(
        pack_kernel,
        out_shape=jax.ShapeDtypeStruct(staged.shape, jnp.bfloat16),
        in_specs=[VMEM],
        out_specs=VMEM,
        compiler_params=pltpu.CompilerParams(vmem_limit_bytes=SMALL_VMEM),
        cost_estimate=pl.CostEstimate(flops=EXCHANGE_FLOPS, bytes_accessed=6 * staged.size, transcendentals=0),
        name="pack",
    )(staged)

    received = lax.all_to_all(packed, "kvp", split_axis=0, concat_axis=0, tiled=True)

    resident = pltpu.with_memory_space_constraint(out_weight, pltpu.VMEM)
    depth = heads_dev * HD
    cost = pl.CostEstimate(flops=2 * rows * depth * part, bytes_accessed=2 * depth * part, transcendentals=0)
    small = pltpu.CompilerParams(vmem_limit_bytes=SMALL_VMEM)
    left = pl.pallas_call(
        functools.partial(combine_kernel, heads_dev),
        out_shape=jax.ShapeDtypeStruct((rows, depth), jnp.bfloat16),
        in_specs=[VMEM],
        out_specs=VMEM,
        scratch_shapes=[pltpu.VMEM((rows * heads_dev, HD), jnp.float32)],
        compiler_params=small,
        name="combine",
    )(received)
    arrived = []
    for x in reversed(range(inner)):
        terms = pl.pallas_call(
            functools.partial(project_kernel, x),
            out_shape=jax.ShapeDtypeStruct((rows, part), jnp.bfloat16 if x else jnp.float32),
            in_specs=[VMEM] * 2,
            out_specs=VMEM,
            compiler_params=small,
            cost_estimate=cost,
            name=f"project_{x}",
        )(left, resident)
        arrived.append(exchange(terms, x, devices) if x else terms)

    def add(terms, name):
        return pl.pallas_call(
            add_kernel,
            out_shape=jax.ShapeDtypeStruct((rows, part), jnp.bfloat16),
            in_specs=[VMEM] * len(terms),
            out_specs=VMEM,
            compiler_params=pltpu.CompilerParams(vmem_limit_bytes=SMALL_VMEM),
            name=name,
        )(*terms)

    mine = add(arrived, "add_near")
    mine = add([mine] + [exchange(mine, x * inner, devices) for x in range(1, outer)], "add_far")
    parts = [mine] + [exchange(mine, x, devices) for x in range(1, inner)]
    return pl.pallas_call(
        lay_kernel,
        out_shape=jax.ShapeDtypeStruct((rows, features), jnp.bfloat16),
        in_specs=[VMEM] * inner,
        out_specs=VMEM,
        compiler_params=pltpu.CompilerParams(vmem_limit_bytes=SMALL_VMEM),
        name="lay",
    )(*parts)


def solution(mesh):
    placed = (
        P("group", None),
        P(("group", "kvp"), None, None),
        P(("group", "kvp"), None, None),
        P(("group", "kvp"), None),
        P(("group", "kvp"), None),
        P("group", "kvp"),
        P("group"),
        P("kvp", None),
    )
    return jax.shard_map(
        functools.partial(body, devices=mesh.shape["kvp"]),
        mesh=mesh,
        in_specs=placed,
        out_specs=P("group", None),
        check_vma=False,
    )
```

```python
import functools
import math

import jax
import jax.numpy as jnp
from jax import lax
from jax.experimental import pallas as pl
from jax.experimental.pallas import tpu as pltpu
from jax.sharding import PartitionSpec as P

HD = 128
PAGE = 64
ATTEND_VMEM = 60 * 1024 * 1024
HIDDEN = -1e30
LOWEST = -1e20
EXCHANGE_FLOPS = 40_000_000_000
SMALL_VMEM = 8 * 1024 * 1024
VMEM = pl.BlockSpec(memory_space=pltpu.VMEM)
HBM = pl.BlockSpec(memory_space=pltpu.HBM)


def split_two(value):
    high = value.astype(jnp.bfloat16).astype(jnp.float32)
    low = (value - high).astype(jnp.bfloat16).astype(jnp.float32)
    return high, low


def attend_kernel(heads_dev, devices, *refs):
    table_hbm, lengths_hbm, key_scale_hbm, value_scale_hbm, queries_hbm, keys, values = refs[:7]
    staged, table, lengths, key_scale, value_scale, queries, key_buf, value_buf, query_rows = refs[7:16]
    query_blocks, key_rows, value_rows, scores, weight_rows, stats, small_sems, sems = refs[16:]
    rows, pages = table.shape
    kv_heads = key_scale.shape[0]
    heads = queries.shape[1] // HD
    group = heads // kv_heads
    context = pages * PAGE
    pieces = sems.shape[1]
    piece = keys.shape[0] // pieces

    small = []
    for i, (source, target) in enumerate(
        (
            (table_hbm, table),
            (lengths_hbm, lengths),
            (key_scale_hbm, key_scale),
            (value_scale_hbm, value_scale),
            (queries_hbm, queries),
        )
    ):
        small.append(pltpu.make_async_copy(source, target, small_sems.at[i]))
        small[-1].start()
    large = []
    for which, source, target in ((0, keys, key_buf), (1, values, value_buf)):
        large.append([])
        for i in range(pieces):
            here = pl.ds(i * piece, piece)
            large[-1].append(pltpu.make_async_copy(source.at[here], target.at[here], sems.at[which, i]))
    for copy in large[0]:
        copy.start()

    me = lax.axis_index("kvp")
    lane = lax.broadcasted_iota(jnp.int32, (1, HD), 1)
    first_of_pair = lane < heads
    of_lane = lax.rem(lax.div(lane, group), kv_heads)
    spread = (of_lane == lax.broadcasted_iota(jnp.int32, (kv_heads, HD), 0)).astype(jnp.float32)
    place = lax.broadcasted_iota(jnp.int32, (PAGE, HD), 0)
    stats[...] = jnp.zeros_like(stats)
    for copy in small:
        copy.wait()
    for copy in large[1]:
        copy.start()

    def by_slot(scales):
        return lax.dot_general(
            scales[...], spread, (((0,), (0,)), ((), ())),
            precision=lax.Precision.HIGHEST, preferred_element_type=jnp.float32,
        )

    key_rows[...] = by_slot(key_scale) * (math.log2(math.e) / math.sqrt(HD))
    value_rows[...] = by_slot(value_scale)
    for h in range(heads):
        query_rows[h * rows : (h + 1) * rows, :] = queries[:, h * HD : (h + 1) * HD].astype(jnp.float32)
    for r in range(0, rows, 2):
        both = jnp.concatenate([query_rows[pl.ds(r + i, heads, stride=rows), :] for i in (0, 1)], axis=0)
        turned = both.T
        for i in (0, 1):
            for k in range(kv_heads):
                mine = lax.div(lane, group) == i * kv_heads + k
                query_blocks[r + i, k * HD : (k + 1) * HD, :] = jnp.where(mine, turned, 0.0).astype(jnp.bfloat16)

    def pages_of(buf, r, columns):
        return jnp.concatenate([buf[table[r, p], :, columns] for p in range(pages)], axis=0)

    def factor(scale_rows, r, p):
        left, right = (scale_rows[pl.ds(table[r + i, p], 1), :] for i in (0, 1))
        return jnp.where(first_of_pair, left, right)

    for copy in large[0]:
        copy.wait()
    for r in range(rows):
        both = jnp.dot(pages_of(key_buf, r, slice(None)), query_blocks[r], preferred_element_type=jnp.float32)
        if r % 2 == 0:
            scores[r // 2] = both
        else:
            scores[r // 2] += both
    for r in range(0, rows, 2):
        length = jnp.where(first_of_pair, lengths[r], lengths[r + 1]) - me * context
        highest = jnp.full((PAGE, HD), LOWEST, jnp.float32)
        for p in range(pages):
            here = slice(p * PAGE, (p + 1) * PAGE)
            scaled = jnp.where(place < length - p * PAGE, scores[r // 2, here] * factor(key_rows, r, p), HIDDEN)
            scores[r // 2, here] = scaled
            highest = jnp.maximum(highest, scaled)
        high, low = split_two(jnp.max(highest, axis=0, keepdims=True))
        total = jnp.zeros((PAGE, HD), jnp.float32)
        for p in range(0, pages, 2):
            weights = []
            for i in (0, 1):
                here = slice((p + i) * PAGE, (p + i + 1) * PAGE)
                prob = jnp.exp2(scores[r // 2, here] - (high + low))
                total += prob
                weights.append(prob * factor(value_rows, r, p + i))
            turned = jnp.concatenate(weights, axis=0).T
            weight_rows[r // 2, :, p * PAGE : (p + 2) * PAGE] = turned.astype(jnp.bfloat16)
        total_high, total_low = split_two(jnp.sum(total, axis=0, keepdims=True))
        for at, value in enumerate((high, low, total_high, total_low)):
            stats[4 * r + at : 4 * r + at + 1, :] = value
            stats[4 * r + 4 + at : 4 * r + 5 + at, :] = pltpu.roll(value, HD - heads, axis=1)
    by_head = stats[...].T
    for d in range(devices):
        staged[d, rows] = by_head[d * heads_dev : (d + 1) * heads_dev]
    for copy in large[1]:
        copy.wait()
    for r in range(rows):
        for k in range(0, kv_heads, 2):
            first = r % 2 * heads + k * group
            both = jnp.dot(
                weight_rows[r // 2, first : first + 2 * group, :],
                pages_of(value_buf, r, slice(k * HD, (k + 2) * HD)),
                preferred_element_type=jnp.float32,
            )
            for i in (0, 1):
                partial = both[i * group : (i + 1) * group, i * HD : (i + 1) * HD]
                for start in range(0, group, heads_dev):
                    d = ((k + i) * group + start) // heads_dev
                    staged[d, r] = partial[start : start + heads_dev]


def pack_kernel(staged, packed):
    packed[...] = staged[...].astype(jnp.bfloat16)


def combine_kernel(heads_dev, packed, left, attended):
    rows = left.shape[0]
    stats = packed[:, rows].astype(jnp.float32)
    lanes = stats.shape[-1]

    def lanes_ahead(value, by):
        return pltpu.roll(value, lanes - by, axis=2)

    maxima = stats + lanes_ahead(stats, 1)
    rescale = jnp.exp2(maxima - jnp.max(maxima, axis=0, keepdims=True))
    totals = lanes_ahead(stats, 2) + lanes_ahead(stats, 3)
    denominator = jnp.sum(totals * rescale, axis=0)
    for r in range(rows):
        partial = packed[:, r].astype(jnp.float32)
        numerator = jnp.sum(partial * rescale[:, :, 4 * r : 4 * r + 1], axis=0)
        attended[r * heads_dev : (r + 1) * heads_dev, :] = numerator / denominator[:, 4 * r : 4 * r + 1]
    rounded = jnp.concatenate(
        [attended[pl.ds(j, rows, stride=heads_dev), :].astype(jnp.bfloat16) for j in range(heads_dev)], axis=1
    )
    left[...] = rounded


def project_kernel(partner, left, weight, out):
    part = out.shape[1]
    quarter = lax.rem(lax.axis_index("kvp"), weight.shape[1] // part)
    start = pl.multiple_of(jnp.bitwise_xor(quarter, partner) * part, part)
    terms = jnp.dot(left[...], weight[:, pl.ds(start, part)], preferred_element_type=jnp.float32)
    out[...] = terms.astype(out.dtype)


def add_kernel(*refs):
    terms = [ref[...].astype(jnp.float32) for ref in refs[:-1]]
    while len(terms) > 1:
        terms = [terms[i] + terms[i + 1] for i in range(0, len(terms), 2)]
    refs[-1][...] = terms[0].astype(refs[-1].dtype)


def lay_kernel(*refs):
    parts, out = refs[:-1], refs[-1]
    quarter = lax.rem(lax.axis_index("kvp"), len(parts))
    width = parts[0].shape[1]
    for x, part in enumerate(parts):
        start = pl.multiple_of(jnp.bitwise_xor(quarter, x) * width, width)
        out[:, pl.ds(start, width)] = part[...]


def exchange(array, partner, devices):
    return lax.ppermute(array, "kvp", [(i, i ^ partner) for i in range(devices)])


def in_hbm(array):
    return pltpu.with_memory_space_constraint(array, pltpu.HBM)


def body(queries, key_cache, value_cache, key_scale, value_scale, page_table, lengths, out_weight, *, devices):
    rows, pages = page_table.shape
    slots, _, columns = key_cache.shape
    kv_heads = key_scale.shape[1]
    heads_dev = out_weight.shape[0] // HD
    heads = queries.shape[1] // HD
    features = out_weight.shape[1]
    inner = 4
    outer = devices // inner
    part = features // inner
    staged = pl.pallas_call(
        functools.partial(attend_kernel, heads_dev, devices),
        out_shape=pltpu.VMEM((devices, rows + 1, heads_dev, HD), jnp.float32),
        in_specs=[HBM] * 7,
        out_specs=VMEM,
        scratch_shapes=[
            pltpu.SMEM((rows, pages), jnp.int32),
            pltpu.SMEM((rows,), jnp.int32),
            pltpu.VMEM((kv_heads, slots), jnp.float32),
            pltpu.VMEM((kv_heads, slots), jnp.float32),
            pltpu.VMEM((rows, heads * HD), jnp.bfloat16),
            pltpu.VMEM((slots, PAGE, columns), jnp.bfloat16),
            pltpu.VMEM((slots, PAGE, columns), jnp.bfloat16),
            pltpu.VMEM((heads * rows, HD), jnp.float32),
            pltpu.VMEM((rows, columns, HD), jnp.bfloat16),
            pltpu.VMEM((slots, HD), jnp.float32),
            pltpu.VMEM((slots, HD), jnp.float32),
            pltpu.VMEM((rows // 2, pages * PAGE, HD), jnp.float32),
            pltpu.VMEM((rows // 2, HD, pages * PAGE), jnp.bfloat16),
            pltpu.VMEM((HD, HD), jnp.float32),
            pltpu.SemaphoreType.DMA((5,)),
            pltpu.SemaphoreType.DMA((2, 4)),
        ],
        compiler_params=pltpu.CompilerParams(vmem_limit_bytes=ATTEND_VMEM),
        cost_estimate=pl.CostEstimate(
            flops=4 * heads * rows * pages * PAGE * HD,
            bytes_accessed=4 * rows * pages * PAGE * columns,
            transcendentals=heads * rows * pages * PAGE,
        ),
        name="attend",
    )(*[in_hbm(a) for a in (page_table, lengths, key_scale.T, value_scale.T, queries, key_cache, value_cache)])

    packed = pl.pallas_call(
        pack_kernel,
        out_shape=jax.ShapeDtypeStruct(staged.shape, jnp.bfloat16),
        in_specs=[VMEM],
        out_specs=VMEM,
        compiler_params=pltpu.CompilerParams(vmem_limit_bytes=SMALL_VMEM),
        cost_estimate=pl.CostEstimate(flops=EXCHANGE_FLOPS, bytes_accessed=6 * staged.size, transcendentals=0),
        name="pack",
    )(staged)

    received = lax.all_to_all(packed, "kvp", split_axis=0, concat_axis=0, tiled=True)

    resident = pltpu.with_memory_space_constraint(out_weight, pltpu.VMEM)
    depth = heads_dev * HD
    cost = pl.CostEstimate(flops=1024, bytes_accessed=1024, transcendentals=0)
    small = pltpu.CompilerParams(vmem_limit_bytes=SMALL_VMEM)
    left = pl.pallas_call(
        functools.partial(combine_kernel, heads_dev),
        out_shape=jax.ShapeDtypeStruct((rows, depth), jnp.bfloat16),
        in_specs=[VMEM],
        out_specs=VMEM,
        scratch_shapes=[pltpu.VMEM((rows * heads_dev, HD), jnp.float32)],
        compiler_params=small,
        name="combine",
    )(received)
    arrived = []
    for x in reversed(range(inner)):
        terms = pl.pallas_call(
            functools.partial(project_kernel, x),
            out_shape=jax.ShapeDtypeStruct((rows, part), jnp.bfloat16 if x else jnp.float32),
            in_specs=[VMEM] * 2,
            out_specs=VMEM,
            compiler_params=small,
            cost_estimate=cost,
            name=f"project_{x}",
        )(left, resident)
        arrived.append(exchange(terms, x, devices) if x else terms)

    def add(terms, name):
        return pl.pallas_call(
            add_kernel,
            out_shape=jax.ShapeDtypeStruct((rows, part), jnp.bfloat16),
            in_specs=[VMEM] * len(terms),
            out_specs=VMEM,
            compiler_params=pltpu.CompilerParams(vmem_limit_bytes=SMALL_VMEM),
            name=name,
        )(*terms)

    mine = add(arrived, "add_near")
    mine = add([mine] + [exchange(mine, x * inner, devices) for x in range(1, outer)], "add_far")
    parts = [mine] + [exchange(mine, x, devices) for x in range(1, inner)]
    return pl.pallas_call(
        lay_kernel,
        out_shape=jax.ShapeDtypeStruct((rows, features), jnp.bfloat16),
        in_specs=[VMEM] * inner,
        out_specs=VMEM,
        compiler_params=pltpu.CompilerParams(vmem_limit_bytes=SMALL_VMEM),
        name="lay",
    )(*parts)


def solution(mesh):
    placed = (
        P("group", None),
        P(("group", "kvp"), None, None),
        P(("group", "kvp"), None, None),
        P(("group", "kvp"), None),
        P(("group", "kvp"), None),
        P("group", "kvp"),
        P("group"),
        P("kvp", None),
    )
    return jax.shard_map(
        functools.partial(body, devices=mesh.shape["kvp"]),
        mesh=mesh,
        in_specs=placed,
        out_specs=P("group", None),
        check_vma=False,
    )
```

```python
import functools
import math

import jax
import jax.numpy as jnp
from jax import lax
from jax.experimental import pallas as pl
from jax.experimental.pallas import tpu as pltpu
from jax.sharding import PartitionSpec as P

HD = 128
PAGE = 64
ATTEND_VMEM = 60 * 1024 * 1024
HIDDEN = -1e30
LOWEST = -1e20
EXCHANGE_FLOPS = 40_000_000_000
SMALL_VMEM = 8 * 1024 * 1024
VMEM = pl.BlockSpec(memory_space=pltpu.VMEM)
HBM = pl.BlockSpec(memory_space=pltpu.HBM)


def split_two(value):
    high = value.astype(jnp.bfloat16).astype(jnp.float32)
    low = (value - high).astype(jnp.bfloat16).astype(jnp.float32)
    return high, low


def attend_kernel(heads_dev, devices, *refs):
    table_hbm, lengths_hbm, key_scale_hbm, value_scale_hbm, queries_hbm, keys, values = refs[:7]
    staged, table, lengths, key_scale, value_scale, queries, key_buf, value_buf, query_rows = refs[7:16]
    query_blocks, key_rows, value_rows, scores, weight_rows, stats, small_sems, sems = refs[16:]
    rows, pages = table.shape
    kv_heads = key_scale.shape[0]
    heads = queries.shape[1] // HD
    group = heads // kv_heads
    context = pages * PAGE
    pieces = sems.shape[1]
    piece = keys.shape[0] // pieces

    small = []
    for i, (source, target) in enumerate(
        (
            (table_hbm, table),
            (lengths_hbm, lengths),
            (key_scale_hbm, key_scale),
            (value_scale_hbm, value_scale),
            (queries_hbm, queries),
        )
    ):
        small.append(pltpu.make_async_copy(source, target, small_sems.at[i]))
        small[-1].start()
    large = []
    for which, source, target in ((0, keys, key_buf), (1, values, value_buf)):
        large.append([])
        for i in range(pieces):
            here = pl.ds(i * piece, piece)
            large[-1].append(pltpu.make_async_copy(source.at[here], target.at[here], sems.at[which, i]))
    for copy in large[0]:
        copy.start()

    me = lax.axis_index("kvp")
    lane = lax.broadcasted_iota(jnp.int32, (1, HD), 1)
    first_of_pair = lane < heads
    of_lane = lax.rem(lax.div(lane, group), kv_heads)
    spread = (of_lane == lax.broadcasted_iota(jnp.int32, (kv_heads, HD), 0)).astype(jnp.float32)
    place = lax.broadcasted_iota(jnp.int32, (PAGE, HD), 0)
    stats[...] = jnp.zeros_like(stats)
    for copy in small:
        copy.wait()
    for copy in large[1]:
        copy.start()

    def by_slot(scales):
        return lax.dot_general(
            scales[...], spread, (((0,), (0,)), ((), ())),
            precision=lax.Precision.HIGHEST, preferred_element_type=jnp.float32,
        )

    key_rows[...] = by_slot(key_scale) * (math.log2(math.e) / math.sqrt(HD))
    value_rows[...] = by_slot(value_scale)
    for h in range(heads):
        query_rows[h * rows : (h + 1) * rows, :] = queries[:, h * HD : (h + 1) * HD].astype(jnp.float32)
    for r in range(0, rows, 2):
        both = jnp.concatenate([query_rows[pl.ds(r + i, heads, stride=rows), :] for i in (0, 1)], axis=0)
        turned = both.T
        for i in (0, 1):
            for k in range(kv_heads):
                mine = lax.div(lane, group) == i * kv_heads + k
                query_blocks[r + i, k * HD : (k + 1) * HD, :] = jnp.where(mine, turned, 0.0).astype(jnp.bfloat16)

    def pages_of(buf, r, columns):
        return jnp.concatenate([buf[table[r, p], :, columns] for p in range(pages)], axis=0)

    def factor(scale_rows, r, p):
        left, right = (scale_rows[pl.ds(table[r + i, p], 1), :] for i in (0, 1))
        return jnp.where(first_of_pair, left, right)

    for copy in large[0]:
        copy.wait()
    def score(r):
        for i in (0, 1):
            both = jnp.dot(
                pages_of(key_buf, r + i, slice(None)), query_blocks[r + i], preferred_element_type=jnp.float32
            )
            if i == 0:
                scores[r // 2] = both
            else:
                scores[r // 2] += both

    def weigh(r):
        length = jnp.where(first_of_pair, lengths[r], lengths[r + 1]) - me * context
        highest = jnp.full((PAGE, HD), LOWEST, jnp.float32)
        for p in range(pages):
            here = slice(p * PAGE, (p + 1) * PAGE)
            scaled = jnp.where(place < length - p * PAGE, scores[r // 2, here] * factor(key_rows, r, p), HIDDEN)
            scores[r // 2, here] = scaled
            highest = jnp.maximum(highest, scaled)
        high, low = split_two(jnp.max(highest, axis=0, keepdims=True))
        total = jnp.zeros((PAGE, HD), jnp.float32)
        for p in range(0, pages, 2):
            weights = []
            for i in (0, 1):
                here = slice((p + i) * PAGE, (p + i + 1) * PAGE)
                prob = jnp.exp2(scores[r // 2, here] - (high + low))
                total += prob
                weights.append(prob * factor(value_rows, r, p + i))
            turned = jnp.concatenate(weights, axis=0).T
            weight_rows[r // 2, :, p * PAGE : (p + 2) * PAGE] = turned.astype(jnp.bfloat16)
        total_high, total_low = split_two(jnp.sum(total, axis=0, keepdims=True))
        for at, value in enumerate((high, low, total_high, total_low)):
            stats[4 * r + at : 4 * r + at + 1, :] = value
            stats[4 * r + 4 + at : 4 * r + 5 + at, :] = pltpu.roll(value, HD - heads, axis=1)

    def attend(r):
        for k in range(0, kv_heads, 2):
            first = r % 2 * heads + k * group
            both = jnp.dot(
                weight_rows[r // 2, first : first + 2 * group, :],
                pages_of(value_buf, r, slice(k * HD, (k + 2) * HD)),
                preferred_element_type=jnp.float32,
            )
            for i in (0, 1):
                partial = both[i * group : (i + 1) * group, i * HD : (i + 1) * HD]
                for start in range(0, group, heads_dev):
                    d = ((k + i) * group + start) // heads_dev
                    staged[d, r] = partial[start : start + heads_dev]

    score(0)
    weigh(0)
    for r in range(2, rows, 2):
        score(r)
    for copy in large[1]:
        copy.wait()
    for r in range(0, rows, 2):
        attend(r)
        attend(r + 1)
        if r + 2 < rows:
            weigh(r + 2)
    by_head = stats[...].T
    for d in range(devices):
        staged[d, rows] = by_head[d * heads_dev : (d + 1) * heads_dev]


def pack_kernel(staged, packed):
    packed[...] = staged[...].astype(jnp.bfloat16)


def combine_kernel(heads_dev, packed, left, attended):
    rows = left.shape[0]
    stats = packed[:, rows].astype(jnp.float32)
    lanes = stats.shape[-1]

    def lanes_ahead(value, by):
        return pltpu.roll(value, lanes - by, axis=2)

    maxima = stats + lanes_ahead(stats, 1)
    rescale = jnp.exp2(maxima - jnp.max(maxima, axis=0, keepdims=True))
    totals = lanes_ahead(stats, 2) + lanes_ahead(stats, 3)
    denominator = jnp.sum(totals * rescale, axis=0)
    for r in range(rows):
        partial = packed[:, r].astype(jnp.float32)
        numerator = jnp.sum(partial * rescale[:, :, 4 * r : 4 * r + 1], axis=0)
        attended[r * heads_dev : (r + 1) * heads_dev, :] = numerator / denominator[:, 4 * r : 4 * r + 1]
    rounded = jnp.concatenate(
        [attended[pl.ds(j, rows, stride=heads_dev), :].astype(jnp.bfloat16) for j in range(heads_dev)], axis=1
    )
    left[...] = rounded


def project_kernel(partner, left, weight, out):
    part = out.shape[1]
    quarter = lax.rem(lax.axis_index("kvp"), weight.shape[1] // part)
    start = pl.multiple_of(jnp.bitwise_xor(quarter, partner) * part, part)
    terms = jnp.dot(left[...], weight[:, pl.ds(start, part)], preferred_element_type=jnp.float32)
    out[...] = terms.astype(out.dtype)


def add_kernel(*refs):
    terms = [ref[...].astype(jnp.float32) for ref in refs[:-1]]
    while len(terms) > 1:
        terms = [terms[i] + terms[i + 1] for i in range(0, len(terms), 2)]
    refs[-1][...] = terms[0].astype(refs[-1].dtype)


def lay_kernel(*refs):
    parts, out = refs[:-1], refs[-1]
    quarter = lax.rem(lax.axis_index("kvp"), len(parts))
    width = parts[0].shape[1]
    for x, part in enumerate(parts):
        start = pl.multiple_of(jnp.bitwise_xor(quarter, x) * width, width)
        out[:, pl.ds(start, width)] = part[...]


def exchange(array, partner, devices):
    return lax.ppermute(array, "kvp", [(i, i ^ partner) for i in range(devices)])


def in_hbm(array):
    return pltpu.with_memory_space_constraint(array, pltpu.HBM)


def body(queries, key_cache, value_cache, key_scale, value_scale, page_table, lengths, out_weight, *, devices):
    rows, pages = page_table.shape
    slots, _, columns = key_cache.shape
    kv_heads = key_scale.shape[1]
    heads_dev = out_weight.shape[0] // HD
    heads = queries.shape[1] // HD
    features = out_weight.shape[1]
    inner = 4
    outer = devices // inner
    part = features // inner
    staged = pl.pallas_call(
        functools.partial(attend_kernel, heads_dev, devices),
        out_shape=pltpu.VMEM((devices, rows + 1, heads_dev, HD), jnp.float32),
        in_specs=[HBM] * 7,
        out_specs=VMEM,
        scratch_shapes=[
            pltpu.SMEM((rows, pages), jnp.int32),
            pltpu.SMEM((rows,), jnp.int32),
            pltpu.VMEM((kv_heads, slots), jnp.float32),
            pltpu.VMEM((kv_heads, slots), jnp.float32),
            pltpu.VMEM((rows, heads * HD), jnp.bfloat16),
            pltpu.VMEM((slots, PAGE, columns), jnp.bfloat16),
            pltpu.VMEM((slots, PAGE, columns), jnp.bfloat16),
            pltpu.VMEM((heads * rows, HD), jnp.float32),
            pltpu.VMEM((rows, columns, HD), jnp.bfloat16),
            pltpu.VMEM((slots, HD), jnp.float32),
            pltpu.VMEM((slots, HD), jnp.float32),
            pltpu.VMEM((rows // 2, pages * PAGE, HD), jnp.float32),
            pltpu.VMEM((rows // 2, HD, pages * PAGE), jnp.bfloat16),
            pltpu.VMEM((HD, HD), jnp.float32),
            pltpu.SemaphoreType.DMA((5,)),
            pltpu.SemaphoreType.DMA((2, 4)),
        ],
        compiler_params=pltpu.CompilerParams(vmem_limit_bytes=ATTEND_VMEM),
        cost_estimate=pl.CostEstimate(
            flops=4 * heads * rows * pages * PAGE * HD,
            bytes_accessed=4 * rows * pages * PAGE * columns,
            transcendentals=heads * rows * pages * PAGE,
        ),
        name="attend",
    )(*[in_hbm(a) for a in (page_table, lengths, key_scale.T, value_scale.T, queries, key_cache, value_cache)])

    packed = pl.pallas_call(
        pack_kernel,
        out_shape=jax.ShapeDtypeStruct(staged.shape, jnp.bfloat16),
        in_specs=[VMEM],
        out_specs=VMEM,
        compiler_params=pltpu.CompilerParams(vmem_limit_bytes=SMALL_VMEM),
        cost_estimate=pl.CostEstimate(flops=EXCHANGE_FLOPS, bytes_accessed=6 * staged.size, transcendentals=0),
        name="pack",
    )(staged)

    received = lax.all_to_all(packed, "kvp", split_axis=0, concat_axis=0, tiled=True)

    resident = pltpu.with_memory_space_constraint(out_weight, pltpu.VMEM)
    depth = heads_dev * HD
    cost = pl.CostEstimate(flops=1024, bytes_accessed=1024, transcendentals=0)
    small = pltpu.CompilerParams(vmem_limit_bytes=SMALL_VMEM)
    left = pl.pallas_call(
        functools.partial(combine_kernel, heads_dev),
        out_shape=jax.ShapeDtypeStruct((rows, depth), jnp.bfloat16),
        in_specs=[VMEM],
        out_specs=VMEM,
        scratch_shapes=[pltpu.VMEM((rows * heads_dev, HD), jnp.float32)],
        compiler_params=small,
        name="combine",
    )(received)
    arrived = []
    for x in reversed(range(inner)):
        terms = pl.pallas_call(
            functools.partial(project_kernel, x),
            out_shape=jax.ShapeDtypeStruct((rows, part), jnp.bfloat16 if x else jnp.float32),
            in_specs=[VMEM] * 2,
            out_specs=VMEM,
            compiler_params=small,
            cost_estimate=cost,
            name=f"project_{x}",
        )(left, resident)
        arrived.append(exchange(terms, x, devices) if x else terms)

    def add(terms, name):
        return pl.pallas_call(
            add_kernel,
            out_shape=jax.ShapeDtypeStruct((rows, part), jnp.bfloat16),
            in_specs=[VMEM] * len(terms),
            out_specs=VMEM,
            compiler_params=pltpu.CompilerParams(vmem_limit_bytes=SMALL_VMEM),
            name=name,
        )(*terms)

    mine = add(arrived, "add_near")
    mine = add([mine] + [exchange(mine, x * inner, devices) for x in range(1, outer)], "add_far")
    parts = [mine] + [exchange(mine, x, devices) for x in range(1, inner)]
    return pl.pallas_call(
        lay_kernel,
        out_shape=jax.ShapeDtypeStruct((rows, features), jnp.bfloat16),
        in_specs=[VMEM] * inner,
        out_specs=VMEM,
        compiler_params=pltpu.CompilerParams(vmem_limit_bytes=SMALL_VMEM),
        name="lay",
    )(*parts)


def solution(mesh):
    placed = (
        P("group", None),
        P(("group", "kvp"), None, None),
        P(("group", "kvp"), None, None),
        P(("group", "kvp"), None),
        P(("group", "kvp"), None),
        P("group", "kvp"),
        P("group"),
        P("kvp", None),
    )
    return jax.shard_map(
        functools.partial(body, devices=mesh.shape["kvp"]),
        mesh=mesh,
        in_specs=placed,
        out_specs=P("group", None),
        check_vma=False,
    )
```

```python
import functools
import math

import jax
import jax.numpy as jnp
from jax import lax
from jax.experimental import pallas as pl
from jax.experimental.pallas import tpu as pltpu
from jax.sharding import PartitionSpec as P

HD = 128
PAGE = 64
ATTEND_VMEM = 60 * 1024 * 1024
HIDDEN = -1e30
LOWEST = -1e20
EXCHANGE_FLOPS = 40_000_000_000
SMALL_VMEM = 8 * 1024 * 1024
VMEM = pl.BlockSpec(memory_space=pltpu.VMEM)
HBM = pl.BlockSpec(memory_space=pltpu.HBM)


def split_two(value):
    high = value.astype(jnp.bfloat16).astype(jnp.float32)
    low = (value - high).astype(jnp.bfloat16).astype(jnp.float32)
    return high, low


def attend_kernel(heads_dev, devices, *refs):
    table_hbm, lengths_hbm, key_scale_hbm, value_scale_hbm, queries_hbm, keys, values = refs[:7]
    staged, table, lengths, key_scale, value_scale, queries, key_buf, value_buf, query_rows = refs[7:16]
    query_blocks, key_rows, value_rows, scores, weight_rows, stats, small_sems, sems = refs[16:]
    rows, pages = table.shape
    kv_heads = key_scale.shape[0]
    heads = queries.shape[1] // HD
    group = heads // kv_heads
    context = pages * PAGE
    pieces = sems.shape[1]
    piece = keys.shape[0] // pieces

    small = []
    for i, (source, target) in enumerate(
        (
            (table_hbm, table),
            (lengths_hbm, lengths),
            (key_scale_hbm, key_scale),
            (value_scale_hbm, value_scale),
            (queries_hbm, queries),
        )
    ):
        small.append(pltpu.make_async_copy(source, target, small_sems.at[i]))
        small[-1].start()
    large = []
    for which, source, target in ((0, keys, key_buf), (1, values, value_buf)):
        large.append([])
        for i in range(pieces):
            here = pl.ds(i * piece, piece)
            large[-1].append(pltpu.make_async_copy(source.at[here], target.at[here], sems.at[which, i]))
    for copy in large[0] + large[1]:
        copy.start()

    me = lax.axis_index("kvp")
    lane = lax.broadcasted_iota(jnp.int32, (1, HD), 1)
    first_of_pair = lane < heads
    of_lane = lax.rem(lax.div(lane, group), kv_heads)
    spread = (of_lane == lax.broadcasted_iota(jnp.int32, (kv_heads, HD), 0)).astype(jnp.float32)
    place = lax.broadcasted_iota(jnp.int32, (PAGE, HD), 0)
    stats[...] = jnp.zeros_like(stats)
    for copy in small:
        copy.wait()

    def by_slot(scales):
        return lax.dot_general(
            scales[...], spread, (((0,), (0,)), ((), ())),
            precision=lax.Precision.HIGHEST, preferred_element_type=jnp.float32,
        )

    key_rows[...] = by_slot(key_scale) * (math.log2(math.e) / math.sqrt(HD))
    value_rows[...] = by_slot(value_scale)
    for h in range(heads):
        query_rows[h * rows : (h + 1) * rows, :] = queries[:, h * HD : (h + 1) * HD].astype(jnp.float32)
    for r in range(0, rows, 2):
        both = jnp.concatenate([query_rows[pl.ds(r + i, heads, stride=rows), :] for i in (0, 1)], axis=0)
        turned = both.T
        for i in (0, 1):
            for k in range(kv_heads):
                mine = lax.div(lane, group) == i * kv_heads + k
                query_blocks[r + i, k * HD : (k + 1) * HD, :] = jnp.where(mine, turned, 0.0).astype(jnp.bfloat16)

    def pages_of(buf, r, columns):
        return jnp.concatenate([buf[table[r, p], :, columns] for p in range(pages)], axis=0)

    def factor(scale_rows, r, p):
        left, right = (scale_rows[pl.ds(table[r + i, p], 1), :] for i in (0, 1))
        return jnp.where(first_of_pair, left, right)

    for copy in large[0]:
        copy.wait()
    def score(r):
        for i in (0, 1):
            both = jnp.dot(
                pages_of(key_buf, r + i, slice(None)), query_blocks[r + i], preferred_element_type=jnp.float32
            )
            if i == 0:
                scores[r // 2] = both
            else:
                scores[r // 2] += both

    def weigh(r):
        length = jnp.where(first_of_pair, lengths[r], lengths[r + 1]) - me * context
        highest = jnp.full((PAGE, HD), LOWEST, jnp.float32)
        for p in range(pages):
            here = slice(p * PAGE, (p + 1) * PAGE)
            scaled = jnp.where(place < length - p * PAGE, scores[r // 2, here] * factor(key_rows, r, p), HIDDEN)
            scores[r // 2, here] = scaled
            highest = jnp.maximum(highest, scaled)
        high, low = split_two(jnp.max(highest, axis=0, keepdims=True))
        total = jnp.zeros((PAGE, HD), jnp.float32)
        for p in range(0, pages, 2):
            weights = []
            for i in (0, 1):
                here = slice((p + i) * PAGE, (p + i + 1) * PAGE)
                prob = jnp.exp2(scores[r // 2, here] - (high + low))
                total += prob
                weights.append(prob * factor(value_rows, r, p + i))
            turned = jnp.concatenate(weights, axis=0).T
            weight_rows[r // 2, :, p * PAGE : (p + 2) * PAGE] = turned.astype(jnp.bfloat16)
        total_high, total_low = split_two(jnp.sum(total, axis=0, keepdims=True))
        for at, value in enumerate((high, low, total_high, total_low)):
            stats[4 * r + at : 4 * r + at + 1, :] = value
            stats[4 * r + 4 + at : 4 * r + 5 + at, :] = pltpu.roll(value, HD - heads, axis=1)

    def attend(r):
        for k in range(0, kv_heads, 2):
            first = r % 2 * heads + k * group
            both = jnp.dot(
                weight_rows[r // 2, first : first + 2 * group, :],
                pages_of(value_buf, r, slice(k * HD, (k + 2) * HD)),
                preferred_element_type=jnp.float32,
            )
            for i in (0, 1):
                partial = both[i * group : (i + 1) * group, i * HD : (i + 1) * HD]
                for start in range(0, group, heads_dev):
                    d = ((k + i) * group + start) // heads_dev
                    staged[d, r] = partial[start : start + heads_dev]

    score(0)
    weigh(0)
    for r in range(2, rows, 2):
        score(r)
    for copy in large[1]:
        copy.wait()
    for r in range(0, rows, 2):
        attend(r)
        attend(r + 1)
        if r + 2 < rows:
            weigh(r + 2)
    by_head = stats[...].T
    for d in range(devices):
        staged[d, rows] = by_head[d * heads_dev : (d + 1) * heads_dev]


def pack_kernel(staged, packed):
    packed[...] = staged[...].astype(jnp.bfloat16)


def combine_kernel(heads_dev, packed, left, attended):
    rows = left.shape[0]
    stats = packed[:, rows].astype(jnp.float32)
    lanes = stats.shape[-1]

    def lanes_ahead(value, by):
        return pltpu.roll(value, lanes - by, axis=2)

    maxima = stats + lanes_ahead(stats, 1)
    rescale = jnp.exp2(maxima - jnp.max(maxima, axis=0, keepdims=True))
    totals = lanes_ahead(stats, 2) + lanes_ahead(stats, 3)
    denominator = jnp.sum(totals * rescale, axis=0)
    for r in range(rows):
        partial = packed[:, r].astype(jnp.float32)
        numerator = jnp.sum(partial * rescale[:, :, 4 * r : 4 * r + 1], axis=0)
        attended[r * heads_dev : (r + 1) * heads_dev, :] = numerator / denominator[:, 4 * r : 4 * r + 1]
    rounded = jnp.concatenate(
        [attended[pl.ds(j, rows, stride=heads_dev), :].astype(jnp.bfloat16) for j in range(heads_dev)], axis=1
    )
    left[...] = rounded


def project_kernel(partner, left, weight, out):
    part = out.shape[1]
    quarter = lax.rem(lax.axis_index("kvp"), weight.shape[1] // part)
    start = pl.multiple_of(jnp.bitwise_xor(quarter, partner) * part, part)
    terms = jnp.dot(left[...], weight[:, pl.ds(start, part)], preferred_element_type=jnp.float32)
    out[...] = terms.astype(out.dtype)


def add_kernel(*refs):
    terms = [ref[...].astype(jnp.float32) for ref in refs[:-1]]
    while len(terms) > 1:
        terms = [terms[i] + terms[i + 1] for i in range(0, len(terms), 2)]
    refs[-1][...] = terms[0].astype(refs[-1].dtype)


def lay_kernel(*refs):
    parts, out = refs[:-1], refs[-1]
    quarter = lax.rem(lax.axis_index("kvp"), len(parts))
    width = parts[0].shape[1]
    for x, part in enumerate(parts):
        start = pl.multiple_of(jnp.bitwise_xor(quarter, x) * width, width)
        out[:, pl.ds(start, width)] = part[...]


def exchange(array, partner, devices):
    return lax.ppermute(array, "kvp", [(i, i ^ partner) for i in range(devices)])


def in_hbm(array):
    return pltpu.with_memory_space_constraint(array, pltpu.HBM)


def body(queries, key_cache, value_cache, key_scale, value_scale, page_table, lengths, out_weight, *, devices):
    rows, pages = page_table.shape
    slots, _, columns = key_cache.shape
    kv_heads = key_scale.shape[1]
    heads_dev = out_weight.shape[0] // HD
    heads = queries.shape[1] // HD
    features = out_weight.shape[1]
    inner = 4
    outer = devices // inner
    part = features // inner
    staged = pl.pallas_call(
        functools.partial(attend_kernel, heads_dev, devices),
        out_shape=pltpu.VMEM((devices, rows + 1, heads_dev, HD), jnp.float32),
        in_specs=[HBM] * 7,
        out_specs=VMEM,
        scratch_shapes=[
            pltpu.SMEM((rows, pages), jnp.int32),
            pltpu.SMEM((rows,), jnp.int32),
            pltpu.VMEM((kv_heads, slots), jnp.float32),
            pltpu.VMEM((kv_heads, slots), jnp.float32),
            pltpu.VMEM((rows, heads * HD), jnp.bfloat16),
            pltpu.VMEM((slots, PAGE, columns), jnp.bfloat16),
            pltpu.VMEM((slots, PAGE, columns), jnp.bfloat16),
            pltpu.VMEM((heads * rows, HD), jnp.float32),
            pltpu.VMEM((rows, columns, HD), jnp.bfloat16),
            pltpu.VMEM((slots, HD), jnp.float32),
            pltpu.VMEM((slots, HD), jnp.float32),
            pltpu.VMEM((rows // 2, pages * PAGE, HD), jnp.float32),
            pltpu.VMEM((rows // 2, HD, pages * PAGE), jnp.bfloat16),
            pltpu.VMEM((HD, HD), jnp.float32),
            pltpu.SemaphoreType.DMA((5,)),
            pltpu.SemaphoreType.DMA((2, 4)),
        ],
        compiler_params=pltpu.CompilerParams(vmem_limit_bytes=ATTEND_VMEM),
        cost_estimate=pl.CostEstimate(
            flops=4 * heads * rows * pages * PAGE * HD,
            bytes_accessed=4 * rows * pages * PAGE * columns,
            transcendentals=heads * rows * pages * PAGE,
        ),
        name="attend",
    )(*[in_hbm(a) for a in (page_table, lengths, key_scale.T, value_scale.T, queries, key_cache, value_cache)])

    packed = pl.pallas_call(
        pack_kernel,
        out_shape=jax.ShapeDtypeStruct(staged.shape, jnp.bfloat16),
        in_specs=[VMEM],
        out_specs=VMEM,
        compiler_params=pltpu.CompilerParams(vmem_limit_bytes=SMALL_VMEM),
        cost_estimate=pl.CostEstimate(flops=EXCHANGE_FLOPS, bytes_accessed=6 * staged.size, transcendentals=0),
        name="pack",
    )(staged)

    received = lax.all_to_all(packed, "kvp", split_axis=0, concat_axis=0, tiled=True)

    resident = pltpu.with_memory_space_constraint(out_weight, pltpu.VMEM)
    depth = heads_dev * HD
    cost = pl.CostEstimate(flops=1024, bytes_accessed=1024, transcendentals=0)
    small = pltpu.CompilerParams(vmem_limit_bytes=SMALL_VMEM)
    left = pl.pallas_call(
        functools.partial(combine_kernel, heads_dev),
        out_shape=jax.ShapeDtypeStruct((rows, depth), jnp.bfloat16),
        in_specs=[VMEM],
        out_specs=VMEM,
        scratch_shapes=[pltpu.VMEM((rows * heads_dev, HD), jnp.float32)],
        compiler_params=small,
        name="combine",
    )(received)
    arrived = []
    for x in reversed(range(inner)):
        terms = pl.pallas_call(
            functools.partial(project_kernel, x),
            out_shape=jax.ShapeDtypeStruct((rows, part), jnp.bfloat16 if x else jnp.float32),
            in_specs=[VMEM] * 2,
            out_specs=VMEM,
            compiler_params=small,
            cost_estimate=cost,
            name=f"project_{x}",
        )(left, resident)
        arrived.append(exchange(terms, x, devices) if x else terms)

    def add(terms, name):
        return pl.pallas_call(
            add_kernel,
            out_shape=jax.ShapeDtypeStruct((rows, part), jnp.bfloat16),
            in_specs=[VMEM] * len(terms),
            out_specs=VMEM,
            compiler_params=pltpu.CompilerParams(vmem_limit_bytes=SMALL_VMEM),
            name=name,
        )(*terms)

    mine = add(arrived, "add_near")
    mine = add([mine] + [exchange(mine, x * inner, devices) for x in range(1, outer)], "add_far")
    parts = [mine] + [exchange(mine, x, devices) for x in range(1, inner)]
    return pl.pallas_call(
        lay_kernel,
        out_shape=jax.ShapeDtypeStruct((rows, features), jnp.bfloat16),
        in_specs=[VMEM] * inner,
        out_specs=VMEM,
        compiler_params=pltpu.CompilerParams(vmem_limit_bytes=SMALL_VMEM),
        name="lay",
    )(*parts)


def solution(mesh):
    placed = (
        P("group", None),
        P(("group", "kvp"), None, None),
        P(("group", "kvp"), None, None),
        P(("group", "kvp"), None),
        P(("group", "kvp"), None),
        P("group", "kvp"),
        P("group"),
        P("kvp", None),
    )
    return jax.shard_map(
        functools.partial(body, devices=mesh.shape["kvp"]),
        mesh=mesh,
        in_specs=placed,
        out_specs=P("group", None),
        check_vma=False,
    )
```

```python
import functools
import math

import jax
import jax.numpy as jnp
from jax import lax
from jax.experimental import pallas as pl
from jax.experimental.pallas import tpu as pltpu
from jax.sharding import PartitionSpec as P

HD = 128
PAGE = 64
ATTEND_VMEM = 60 * 1024 * 1024
HIDDEN = -1e30
LOWEST = -1e20
CACHE_PIECES = 6
EXCHANGE_FLOPS = 40_000_000_000
SMALL_VMEM = 8 * 1024 * 1024
VMEM = pl.BlockSpec(memory_space=pltpu.VMEM)
HBM = pl.BlockSpec(memory_space=pltpu.HBM)


def split_two(value):
    high = value.astype(jnp.bfloat16).astype(jnp.float32)
    low = (value - high).astype(jnp.bfloat16).astype(jnp.float32)
    return high, low


def attend_kernel(heads_dev, devices, *refs):
    table_hbm, lengths_hbm, key_scale_hbm, value_scale_hbm, queries_hbm, keys, values = refs[:7]
    staged, table, lengths, key_scale, value_scale, queries, key_buf, value_buf, query_rows = refs[7:16]
    query_blocks, key_rows, value_rows, by_slot_scores, scores, weight_rows, stats, small_sems, sems = refs[16:]
    rows, pages = table.shape
    kv_heads = key_scale.shape[0]
    heads = queries.shape[1] // HD
    group = heads // kv_heads
    context = pages * PAGE
    columns = keys.shape[2]
    pieces = sems.shape[1]
    piece = keys.shape[0] // pieces

    small = []
    for i, (source, target) in enumerate(
        (
            (table_hbm, table),
            (lengths_hbm, lengths),
            (key_scale_hbm, key_scale),
            (value_scale_hbm, value_scale),
            (queries_hbm, queries),
        )
    ):
        small.append(pltpu.make_async_copy(source, target, small_sems.at[i]))
        small[-1].start()
    large = []
    for which, source, target in ((0, keys, key_buf), (1, values, value_buf)):
        large.append([])
        for i in range(pieces):
            here = pl.ds(i * piece, piece)
            large[-1].append(pltpu.make_async_copy(source.at[here], target.at[here], sems.at[which, i]))
    for copy in large[0]:
        copy.start()

    me = lax.axis_index("kvp")
    lane = lax.broadcasted_iota(jnp.int32, (1, HD), 1)
    first_of_pair = lane < heads
    of_lane = lax.rem(lax.div(lane, group), kv_heads)
    spread = (of_lane == lax.broadcasted_iota(jnp.int32, (kv_heads, HD), 0)).astype(jnp.float32)
    place = lax.broadcasted_iota(jnp.int32, (PAGE, HD), 0)
    stats[...] = jnp.zeros_like(stats)
    for copy in small:
        copy.wait()
    for copy in large[1]:
        copy.start()

    def by_slot(scales):
        return lax.dot_general(
            scales[...], spread, (((0,), (0,)), ((), ())),
            precision=lax.Precision.HIGHEST, preferred_element_type=jnp.float32,
        )

    key_rows[...] = by_slot(key_scale) * (math.log2(math.e) / math.sqrt(HD))
    value_rows[...] = by_slot(value_scale)
    for h in range(heads):
        query_rows[h * rows : (h + 1) * rows, :] = queries[:, h * HD : (h + 1) * HD].astype(jnp.float32)
    for r in range(0, rows, 2):
        both = jnp.concatenate([query_rows[pl.ds(r + i, heads, stride=rows), :] for i in (0, 1)], axis=0)
        turned = both.T
        for k in range(kv_heads):
            query_blocks[k * HD : (k + 1) * HD, r // 2 * HD : (r // 2 + 1) * HD] = jnp.where(
                of_lane == k, turned, 0.0
            ).astype(jnp.bfloat16)

    def pages_of(buf, r, columns):
        return jnp.concatenate([buf[table[r, p], :, columns] for p in range(pages)], axis=0)

    def factor(scale_rows, r, p):
        left, right = (scale_rows[pl.ds(table[r + i, p], 1), :] for i in (0, 1))
        return jnp.where(first_of_pair, left, right)

    def weigh(r):
        length = jnp.where(first_of_pair, lengths[r], lengths[r + 1]) - me * context
        highest = jnp.full((PAGE, HD), LOWEST, jnp.float32)
        for p in range(pages):
            here = slice(p * PAGE, (p + 1) * PAGE)
            left, right = (by_slot_scores[table[r + i, p], :, r // 2 * HD : (r // 2 + 1) * HD] for i in (0, 1))
            scaled = jnp.where(first_of_pair, left, right) * factor(key_rows, r, p)
            scaled = jnp.where(place < length - p * PAGE, scaled, HIDDEN)
            scores[r // 2, here] = scaled
            highest = jnp.maximum(highest, scaled)
        high, low = split_two(jnp.max(highest, axis=0, keepdims=True))
        total = jnp.zeros((PAGE, HD), jnp.float32)
        for p in range(0, pages, 2):
            weights = []
            for i in (0, 1):
                here = slice((p + i) * PAGE, (p + i + 1) * PAGE)
                prob = jnp.exp2(scores[r // 2, here] - (high + low))
                total += prob
                weights.append(prob * factor(value_rows, r, p + i))
            turned = jnp.concatenate(weights, axis=0).T
            weight_rows[r // 2, :, p * PAGE : (p + 2) * PAGE] = turned.astype(jnp.bfloat16)
        total_high, total_low = split_two(jnp.sum(total, axis=0, keepdims=True))
        for at, value in enumerate((high, low, total_high, total_low)):
            stats[4 * r + at : 4 * r + at + 1, :] = value
            stats[4 * r + 4 + at : 4 * r + 5 + at, :] = pltpu.roll(value, HD - heads, axis=1)

    def attend(r):
        for k in range(0, kv_heads, 2):
            first = r % 2 * heads + k * group
            both = jnp.dot(
                weight_rows[r // 2, first : first + 2 * group, :],
                pages_of(value_buf, r, slice(k * HD, (k + 2) * HD)),
                preferred_element_type=jnp.float32,
            )
            for i in (0, 1):
                partial = both[i * group : (i + 1) * group, i * HD : (i + 1) * HD]
                for start in range(0, group, heads_dev):
                    d = ((k + i) * group + start) // heads_dev
                    staged[d, r] = partial[start : start + heads_dev]

    for i, copy in enumerate(large[0]):
        copy.wait()
        here = slice(i * piece, (i + 1) * piece)
        arrived = key_buf[here].reshape(piece * PAGE, columns)
        both = jnp.dot(arrived, query_blocks[...], preferred_element_type=jnp.float32)
        by_slot_scores[here] = both.reshape(piece, PAGE, rows // 2 * HD)
    weigh(0)
    for copy in large[1]:
        copy.wait()
    for r in range(0, rows, 2):
        attend(r)
        attend(r + 1)
        if r + 2 < rows:
            weigh(r + 2)
    by_head = stats[...].T
    for d in range(devices):
        staged[d, rows] = by_head[d * heads_dev : (d + 1) * heads_dev]


def pack_kernel(staged, packed):
    packed[...] = staged[...].astype(jnp.bfloat16)


def combine_kernel(heads_dev, packed, left, attended):
    rows = left.shape[0]
    stats = packed[:, rows].astype(jnp.float32)
    lanes = stats.shape[-1]

    def lanes_ahead(value, by):
        return pltpu.roll(value, lanes - by, axis=2)

    maxima = stats + lanes_ahead(stats, 1)
    rescale = jnp.exp2(maxima - jnp.max(maxima, axis=0, keepdims=True))
    totals = lanes_ahead(stats, 2) + lanes_ahead(stats, 3)
    denominator = jnp.sum(totals * rescale, axis=0)
    for r in range(rows):
        partial = packed[:, r].astype(jnp.float32)
        numerator = jnp.sum(partial * rescale[:, :, 4 * r : 4 * r + 1], axis=0)
        attended[r * heads_dev : (r + 1) * heads_dev, :] = numerator / denominator[:, 4 * r : 4 * r + 1]
    rounded = jnp.concatenate(
        [attended[pl.ds(j, rows, stride=heads_dev), :].astype(jnp.bfloat16) for j in range(heads_dev)], axis=1
    )
    left[...] = rounded


def project_kernel(partner, left, weight, out):
    part = out.shape[1]
    quarter = lax.rem(lax.axis_index("kvp"), weight.shape[1] // part)
    start = pl.multiple_of(jnp.bitwise_xor(quarter, partner) * part, part)
    terms = jnp.dot(left[...], weight[:, pl.ds(start, part)], preferred_element_type=jnp.float32)
    out[...] = terms.astype(out.dtype)


def add_kernel(*refs):
    terms = [ref[...].astype(jnp.float32) for ref in refs[:-1]]
    while len(terms) > 1:
        terms = [terms[i] + terms[i + 1] for i in range(0, len(terms), 2)]
    refs[-1][...] = terms[0].astype(refs[-1].dtype)


def lay_kernel(*refs):
    parts, out = refs[:-1], refs[-1]
    quarter = lax.rem(lax.axis_index("kvp"), len(parts))
    width = parts[0].shape[1]
    for x, part in enumerate(parts):
        start = pl.multiple_of(jnp.bitwise_xor(quarter, x) * width, width)
        out[:, pl.ds(start, width)] = part[...]


def exchange(array, partner, devices):
    return lax.ppermute(array, "kvp", [(i, i ^ partner) for i in range(devices)])


def in_hbm(array):
    return pltpu.with_memory_space_constraint(array, pltpu.HBM)


def body(queries, key_cache, value_cache, key_scale, value_scale, page_table, lengths, out_weight, *, devices):
    rows, pages = page_table.shape
    slots, _, columns = key_cache.shape
    kv_heads = key_scale.shape[1]
    heads_dev = out_weight.shape[0] // HD
    heads = queries.shape[1] // HD
    features = out_weight.shape[1]
    inner = 4
    outer = devices // inner
    part = features // inner
    staged = pl.pallas_call(
        functools.partial(attend_kernel, heads_dev, devices),
        out_shape=pltpu.VMEM((devices, rows + 1, heads_dev, HD), jnp.float32),
        in_specs=[HBM] * 7,
        out_specs=VMEM,
        scratch_shapes=[
            pltpu.SMEM((rows, pages), jnp.int32),
            pltpu.SMEM((rows,), jnp.int32),
            pltpu.VMEM((kv_heads, slots), jnp.float32),
            pltpu.VMEM((kv_heads, slots), jnp.float32),
            pltpu.VMEM((rows, heads * HD), jnp.bfloat16),
            pltpu.VMEM((slots, PAGE, columns), jnp.bfloat16),
            pltpu.VMEM((slots, PAGE, columns), jnp.bfloat16),
            pltpu.VMEM((heads * rows, HD), jnp.float32),
            pltpu.VMEM((columns, rows // 2 * HD), jnp.bfloat16),
            pltpu.VMEM((slots, HD), jnp.float32),
            pltpu.VMEM((slots, HD), jnp.float32),
            pltpu.VMEM((slots, PAGE, rows // 2 * HD), jnp.float32),
            pltpu.VMEM((rows // 2, pages * PAGE, HD), jnp.float32),
            pltpu.VMEM((rows // 2, HD, pages * PAGE), jnp.bfloat16),
            pltpu.VMEM((HD, HD), jnp.float32),
            pltpu.SemaphoreType.DMA((5,)),
            pltpu.SemaphoreType.DMA((2, CACHE_PIECES)),
        ],
        compiler_params=pltpu.CompilerParams(vmem_limit_bytes=ATTEND_VMEM),
        cost_estimate=pl.CostEstimate(
            flops=4 * heads * rows * pages * PAGE * HD,
            bytes_accessed=4 * rows * pages * PAGE * columns,
            transcendentals=heads * rows * pages * PAGE,
        ),
        name="attend",
    )(*[in_hbm(a) for a in (page_table, lengths, key_scale.T, value_scale.T, queries, key_cache, value_cache)])

    packed = pl.pallas_call(
        pack_kernel,
        out_shape=jax.ShapeDtypeStruct(staged.shape, jnp.bfloat16),
        in_specs=[VMEM],
        out_specs=VMEM,
        compiler_params=pltpu.CompilerParams(vmem_limit_bytes=SMALL_VMEM),
        cost_estimate=pl.CostEstimate(flops=EXCHANGE_FLOPS, bytes_accessed=6 * staged.size, transcendentals=0),
        name="pack",
    )(staged)

    received = lax.all_to_all(packed, "kvp", split_axis=0, concat_axis=0, tiled=True)

    resident = pltpu.with_memory_space_constraint(out_weight, pltpu.VMEM)
    depth = heads_dev * HD
    cost = pl.CostEstimate(flops=1024, bytes_accessed=1024, transcendentals=0)
    small = pltpu.CompilerParams(vmem_limit_bytes=SMALL_VMEM)
    left = pl.pallas_call(
        functools.partial(combine_kernel, heads_dev),
        out_shape=jax.ShapeDtypeStruct((rows, depth), jnp.bfloat16),
        in_specs=[VMEM],
        out_specs=VMEM,
        scratch_shapes=[pltpu.VMEM((rows * heads_dev, HD), jnp.float32)],
        compiler_params=small,
        name="combine",
    )(received)
    arrived = []
    for x in reversed(range(inner)):
        terms = pl.pallas_call(
            functools.partial(project_kernel, x),
            out_shape=jax.ShapeDtypeStruct((rows, part), jnp.bfloat16 if x else jnp.float32),
            in_specs=[VMEM] * 2,
            out_specs=VMEM,
            compiler_params=small,
            cost_estimate=cost,
            name=f"project_{x}",
        )(left, resident)
        arrived.append(exchange(terms, x, devices) if x else terms)

    def add(terms, name):
        return pl.pallas_call(
            add_kernel,
            out_shape=jax.ShapeDtypeStruct((rows, part), jnp.bfloat16),
            in_specs=[VMEM] * len(terms),
            out_specs=VMEM,
            compiler_params=pltpu.CompilerParams(vmem_limit_bytes=SMALL_VMEM),
            name=name,
        )(*terms)

    mine = add(arrived, "add_near")
    mine = add([mine] + [exchange(mine, x * inner, devices) for x in range(1, outer)], "add_far")
    parts = [mine] + [exchange(mine, x, devices) for x in range(1, inner)]
    return pl.pallas_call(
        lay_kernel,
        out_shape=jax.ShapeDtypeStruct((rows, features), jnp.bfloat16),
        in_specs=[VMEM] * inner,
        out_specs=VMEM,
        compiler_params=pltpu.CompilerParams(vmem_limit_bytes=SMALL_VMEM),
        name="lay",
    )(*parts)


def solution(mesh):
    placed = (
        P("group", None),
        P(("group", "kvp"), None, None),
        P(("group", "kvp"), None, None),
        P(("group", "kvp"), None),
        P(("group", "kvp"), None),
        P("group", "kvp"),
        P("group"),
        P("kvp", None),
    )
    return jax.shard_map(
        functools.partial(body, devices=mesh.shape["kvp"]),
        mesh=mesh,
        in_specs=placed,
        out_specs=P("group", None),
        check_vma=False,
    )
```

```python
import functools
import math

import jax
import jax.numpy as jnp
from jax import lax
from jax.experimental import pallas as pl
from jax.experimental.pallas import tpu as pltpu
from jax.sharding import PartitionSpec as P

HD = 128
PAGE = 64
ATTEND_VMEM = 60 * 1024 * 1024
HIDDEN = -1e30
LOWEST = -1e20
EXCHANGE_FLOPS = 40_000_000_000
SMALL_VMEM = 8 * 1024 * 1024
VMEM = pl.BlockSpec(memory_space=pltpu.VMEM)
HBM = pl.BlockSpec(memory_space=pltpu.HBM)


def split_two(value):
    high = value.astype(jnp.bfloat16).astype(jnp.float32)
    low = (value - high).astype(jnp.bfloat16).astype(jnp.float32)
    return high, low


def attend_kernel(heads_dev, devices, *refs):
    table_hbm, lengths_hbm, key_scale_hbm, value_scale_hbm, queries_hbm, keys, values = refs[:7]
    staged, table, lengths, key_scale, value_scale, queries, key_buf, value_buf, query_rows = refs[7:16]
    table_rows, factors, bias, weights, small_sems, sems = refs[16:]
    rows, pages = table.shape
    kv_heads = key_scale.shape[0]
    heads = queries.shape[1] // HD
    group = heads // kv_heads
    context = pages * PAGE
    pieces = sems.shape[1]
    piece = keys.shape[0] // pieces

    small = []
    for i, (source, target) in enumerate(
        (
            (table_hbm, table),
            (table_hbm, table_rows),
            (lengths_hbm, lengths),
            (key_scale_hbm, key_scale),
            (value_scale_hbm, value_scale),
            (queries_hbm, queries),
        )
    ):
        small.append(pltpu.make_async_copy(source, target, small_sems.at[i]))
        small[-1].start()
    large = []
    for which, source, target in ((0, keys, key_buf), (1, values, value_buf)):
        large.append([])
        for i in range(pieces):
            here = pl.ds(i * piece, piece)
            large[-1].append(pltpu.make_async_copy(source.at[here], target.at[here], sems.at[which, i]))
    for copy in large[0]:
        copy.start()

    me = lax.axis_index("kvp")
    lane = lax.broadcasted_iota(jnp.int32, (group, HD), 1)
    place = me * context + lax.broadcasted_iota(jnp.int32, (1, context), 1)
    page_of = lax.div(lax.broadcasted_iota(jnp.int32, (pages, context), 1), PAGE)
    spread = (page_of == lax.broadcasted_iota(jnp.int32, (pages, context), 0)).astype(jnp.float32).astype(jnp.bfloat16)
    slot = lax.broadcasted_iota(jnp.int32, (keys.shape[0], context), 0).astype(jnp.float32)
    zeros = jnp.zeros((group, HD), jnp.bfloat16)
    for copy in small:
        copy.wait()
    for copy in large[1]:
        copy.start()

    scales = jnp.concatenate([key_scale[...] * (math.log2(math.e) / math.sqrt(HD)), value_scale[...]], axis=0)
    high, low = split_two(scales)
    parts = jnp.concatenate([high, low, scales - high - low], axis=0).astype(jnp.bfloat16)
    slots = jnp.dot(
        table_rows[...].astype(jnp.float32).astype(jnp.bfloat16), spread, preferred_element_type=jnp.float32
    )
    for r in range(rows):
        chosen = (slots[r : r + 1] == slot).astype(jnp.float32).astype(jnp.bfloat16)
        found = jnp.dot(parts, chosen, preferred_element_type=jnp.float32)
        count = 2 * kv_heads
        factors[r] = found[:count] + found[count : 2 * count] + found[2 * count :]
        bias[r : r + 1] = jnp.where(place < lengths[r], 0.0, HIDDEN)
    for h in range(heads):
        query_rows[h * rows : (h + 1) * rows, :] = queries[:, h * HD : (h + 1) * HD].astype(jnp.float32)

    def pages_of(buf, r, k):
        return jnp.concatenate(
            [buf[table[r, p], :, k * HD : (k + 2) * HD] for p in range(pages)], axis=0
        )

    for copy in large[0]:
        copy.wait()
    stats = [jnp.zeros((group, HD), jnp.float32)] * kv_heads
    for r in range(rows):
        query = query_rows[pl.ds(r, heads, stride=rows), :].astype(jnp.bfloat16)
        for k in range(0, kv_heads, 2):
            left = jnp.concatenate(
                [
                    jnp.concatenate([query[k * group : (k + 1) * group], zeros], axis=1),
                    jnp.concatenate([zeros, query[(k + 1) * group : (k + 2) * group]], axis=1),
                ],
                axis=0,
            )
            both = lax.dot_general(
                left, pages_of(key_buf, r, k), (((1,), (1,)), ((), ())), preferred_element_type=jnp.float32
            )
            for i in (0, 1):
                at_key, at_value = k + i, kv_heads + k + i
                scores = both[i * group : (i + 1) * group] * factors[r, at_key : at_key + 1] + bias[r : r + 1]
                highest = jnp.maximum(jnp.max(scores, axis=1, keepdims=True), LOWEST)
                high, low = split_two(highest)
                prob = jnp.exp2(scores - (high + low))
                total_high, total_low = split_two(jnp.sum(prob, axis=1, keepdims=True))
                for at, value in enumerate((high, low, total_high, total_low)):
                    stats[k + i] = jnp.where(lane == 4 * r + at, value, stats[k + i])
                weights[r, (k + i) * group : (k + i + 1) * group] = (
                    prob * factors[r, at_value : at_value + 1]
                ).astype(jnp.bfloat16)
    for copy in large[1]:
        copy.wait()
    for r in range(rows):
        for k in range(0, kv_heads, 2):
            both = jnp.dot(
                weights[r, k * group : (k + 2) * group], pages_of(value_buf, r, k), preferred_element_type=jnp.float32
            )
            for i in (0, 1):
                partial = both[i * group : (i + 1) * group, i * HD : (i + 1) * HD]
                for start in range(0, group, heads_dev):
                    d = ((k + i) * group + start) // heads_dev
                    staged[d, r] = partial[start : start + heads_dev]
    for k in range(kv_heads):
        for start in range(0, group, heads_dev):
            d = (k * group + start) // heads_dev
            staged[d, rows] = stats[k][start : start + heads_dev]


def pack_kernel(staged, packed):
    packed[...] = staged[...].astype(jnp.bfloat16)


def combine_kernel(heads_dev, packed, left, attended):
    rows = left.shape[0]
    stats = packed[:, rows].astype(jnp.float32)
    lanes = stats.shape[-1]

    def lanes_ahead(value, by):
        return pltpu.roll(value, lanes - by, axis=2)

    maxima = stats + lanes_ahead(stats, 1)
    rescale = jnp.exp2(maxima - jnp.max(maxima, axis=0, keepdims=True))
    totals = lanes_ahead(stats, 2) + lanes_ahead(stats, 3)
    denominator = jnp.sum(totals * rescale, axis=0)
    for r in range(rows):
        partial = packed[:, r].astype(jnp.float32)
        numerator = jnp.sum(partial * rescale[:, :, 4 * r : 4 * r + 1], axis=0)
        attended[r * heads_dev : (r + 1) * heads_dev, :] = numerator / denominator[:, 4 * r : 4 * r + 1]
    rounded = jnp.concatenate(
        [attended[pl.ds(j, rows, stride=heads_dev), :].astype(jnp.bfloat16) for j in range(heads_dev)], axis=1
    )
    left[...] = rounded


def project_kernel(partner, left, weight, out):
    part = out.shape[1]
    quarter = lax.rem(lax.axis_index("kvp"), weight.shape[1] // part)
    start = pl.multiple_of(jnp.bitwise_xor(quarter, partner) * part, part)
    terms = jnp.dot(left[...], weight[:, pl.ds(start, part)], preferred_element_type=jnp.float32)
    out[...] = terms.astype(out.dtype)


def add_kernel(*refs):
    terms = [ref[...].astype(jnp.float32) for ref in refs[:-1]]
    while len(terms) > 1:
        terms = [terms[i] + terms[i + 1] for i in range(0, len(terms), 2)]
    refs[-1][...] = terms[0].astype(refs[-1].dtype)


def lay_kernel(*refs):
    parts, out = refs[:-1], refs[-1]
    quarter = lax.rem(lax.axis_index("kvp"), len(parts))
    width = parts[0].shape[1]
    for x, part in enumerate(parts):
        start = pl.multiple_of(jnp.bitwise_xor(quarter, x) * width, width)
        out[:, pl.ds(start, width)] = part[...]


def exchange(array, partner, devices):
    return lax.ppermute(array, "kvp", [(i, i ^ partner) for i in range(devices)])


def in_hbm(array):
    return pltpu.with_memory_space_constraint(array, pltpu.HBM)


def body(queries, key_cache, value_cache, key_scale, value_scale, page_table, lengths, out_weight, *, devices):
    rows, pages = page_table.shape
    slots, _, columns = key_cache.shape
    kv_heads = key_scale.shape[1]
    heads_dev = out_weight.shape[0] // HD
    heads = queries.shape[1] // HD
    features = out_weight.shape[1]
    inner = 4
    outer = devices // inner
    part = features // inner
    staged = pl.pallas_call(
        functools.partial(attend_kernel, heads_dev, devices),
        out_shape=pltpu.VMEM((devices, rows + 1, heads_dev, HD), jnp.float32),
        in_specs=[HBM] * 7,
        out_specs=VMEM,
        scratch_shapes=[
            pltpu.SMEM((rows, pages), jnp.int32),
            pltpu.SMEM((rows,), jnp.int32),
            pltpu.VMEM((kv_heads, slots), jnp.float32),
            pltpu.VMEM((kv_heads, slots), jnp.float32),
            pltpu.VMEM((rows, heads * HD), jnp.bfloat16),
            pltpu.VMEM((slots, PAGE, columns), jnp.bfloat16),
            pltpu.VMEM((slots, PAGE, columns), jnp.bfloat16),
            pltpu.VMEM((heads * rows, HD), jnp.float32),
            pltpu.VMEM((rows, pages), jnp.int32),
            pltpu.VMEM((rows, 2 * kv_heads, pages * PAGE), jnp.float32),
            pltpu.VMEM((rows, pages * PAGE), jnp.float32),
            pltpu.VMEM((rows, heads, pages * PAGE), jnp.bfloat16),
            pltpu.SemaphoreType.DMA((6,)),
            pltpu.SemaphoreType.DMA((2, 4)),
        ],
        compiler_params=pltpu.CompilerParams(vmem_limit_bytes=ATTEND_VMEM),
        cost_estimate=pl.CostEstimate(
            flops=4 * heads * rows * pages * PAGE * HD,
            bytes_accessed=4 * rows * pages * PAGE * columns,
            transcendentals=heads * rows * pages * PAGE,
        ),
        name="attend",
    )(*[in_hbm(a) for a in (page_table, lengths, key_scale.T, value_scale.T, queries, key_cache, value_cache)])

    packed = pl.pallas_call(
        pack_kernel,
        out_shape=jax.ShapeDtypeStruct(staged.shape, jnp.bfloat16),
        in_specs=[VMEM],
        out_specs=VMEM,
        compiler_params=pltpu.CompilerParams(vmem_limit_bytes=SMALL_VMEM),
        cost_estimate=pl.CostEstimate(flops=EXCHANGE_FLOPS, bytes_accessed=6 * staged.size, transcendentals=0),
        name="pack",
    )(staged)

    received = lax.all_to_all(packed, "kvp", split_axis=0, concat_axis=0, tiled=True)

    resident = pltpu.with_memory_space_constraint(out_weight, pltpu.VMEM)
    depth = heads_dev * HD
    cost = pl.CostEstimate(flops=1024, bytes_accessed=1024, transcendentals=0)
    small = pltpu.CompilerParams(vmem_limit_bytes=SMALL_VMEM)
    left = pl.pallas_call(
        functools.partial(combine_kernel, heads_dev),
        out_shape=jax.ShapeDtypeStruct((rows, depth), jnp.bfloat16),
        in_specs=[VMEM],
        out_specs=VMEM,
        scratch_shapes=[pltpu.VMEM((rows * heads_dev, HD), jnp.float32)],
        compiler_params=small,
        name="combine",
    )(received)
    arrived = []
    for x in reversed(range(inner)):
        terms = pl.pallas_call(
            functools.partial(project_kernel, x),
            out_shape=jax.ShapeDtypeStruct((rows, part), jnp.bfloat16 if x else jnp.float32),
            in_specs=[VMEM] * 2,
            out_specs=VMEM,
            compiler_params=small,
            cost_estimate=cost,
            name=f"project_{x}",
        )(left, resident)
        arrived.append(exchange(terms, x, devices) if x else terms)

    def add(terms, name):
        return pl.pallas_call(
            add_kernel,
            out_shape=jax.ShapeDtypeStruct((rows, part), jnp.bfloat16),
            in_specs=[VMEM] * len(terms),
            out_specs=VMEM,
            compiler_params=pltpu.CompilerParams(vmem_limit_bytes=SMALL_VMEM),
            name=name,
        )(*terms)

    mine = add(arrived, "add_near")
    mine = add([mine] + [exchange(mine, x * inner, devices) for x in range(1, outer)], "add_far")
    parts = [mine] + [exchange(mine, x, devices) for x in range(1, inner)]
    return pl.pallas_call(
        lay_kernel,
        out_shape=jax.ShapeDtypeStruct((rows, features), jnp.bfloat16),
        in_specs=[VMEM] * inner,
        out_specs=VMEM,
        compiler_params=pltpu.CompilerParams(vmem_limit_bytes=SMALL_VMEM),
        name="lay",
    )(*parts)


def solution(mesh):
    placed = (
        P("group", None),
        P(("group", "kvp"), None, None),
        P(("group", "kvp"), None, None),
        P(("group", "kvp"), None),
        P(("group", "kvp"), None),
        P("group", "kvp"),
        P("group"),
        P("kvp", None),
    )
    return jax.shard_map(
        functools.partial(body, devices=mesh.shape["kvp"]),
        mesh=mesh,
        in_specs=placed,
        out_specs=P("group", None),
        check_vma=False,
    )
```

```python
import functools
import math

import jax
import jax.numpy as jnp
from jax import lax
from jax.experimental import pallas as pl
from jax.experimental.pallas import tpu as pltpu
from jax.sharding import PartitionSpec as P

HD = 128
PAGE = 64
ATTEND_VMEM = 60 * 1024 * 1024
HIDDEN = -1e30
LOWEST = -1e20
CACHE_PIECES = 12
EXCHANGE_FLOPS = 40_000_000_000
SMALL_VMEM = 8 * 1024 * 1024
VMEM = pl.BlockSpec(memory_space=pltpu.VMEM)
HBM = pl.BlockSpec(memory_space=pltpu.HBM)


def split_two(value):
    high = value.astype(jnp.bfloat16).astype(jnp.float32)
    low = (value - high).astype(jnp.bfloat16).astype(jnp.float32)
    return high, low


def attend_kernel(heads_dev, devices, *refs):
    table_hbm, lengths_hbm, key_scale_hbm, value_scale_hbm, queries_hbm, keys, values = refs[:7]
    staged, table, lengths, key_scale, value_scale, queries, key_buf, value_buf, query_rows = refs[7:16]
    table_rows, factors, bias, weights, small_sems, sems = refs[16:]
    rows, pages = table.shape
    kv_heads = key_scale.shape[0]
    heads = queries.shape[1] // HD
    group = heads // kv_heads
    context = pages * PAGE
    pieces = sems.shape[1]
    piece = keys.shape[0] // pieces

    small = []
    for i, (source, target) in enumerate(
        (
            (table_hbm, table),
            (table_hbm, table_rows),
            (lengths_hbm, lengths),
            (key_scale_hbm, key_scale),
            (value_scale_hbm, value_scale),
            (queries_hbm, queries),
        )
    ):
        small.append(pltpu.make_async_copy(source, target, small_sems.at[i]))
        small[-1].start()
    large = []
    for which, source, target in ((0, keys, key_buf), (1, values, value_buf)):
        large.append([])
        for i in range(pieces):
            here = pl.ds(i * piece, piece)
            large[-1].append(pltpu.make_async_copy(source.at[here], target.at[here], sems.at[which, i]))
    for copy in large[0]:
        copy.start()

    me = lax.axis_index("kvp")
    lane = lax.broadcasted_iota(jnp.int32, (group, HD), 1)
    place = me * context + lax.broadcasted_iota(jnp.int32, (1, context), 1)
    page_of = lax.div(lax.broadcasted_iota(jnp.int32, (pages, context), 1), PAGE)
    spread = (page_of == lax.broadcasted_iota(jnp.int32, (pages, context), 0)).astype(jnp.float32).astype(jnp.bfloat16)
    slot = lax.broadcasted_iota(jnp.int32, (keys.shape[0], context), 0).astype(jnp.float32)
    zeros = jnp.zeros((group, HD), jnp.bfloat16)
    for copy in small:
        copy.wait()
    for copy in large[1]:
        copy.start()

    scales = jnp.concatenate([key_scale[...] * (math.log2(math.e) / math.sqrt(HD)), value_scale[...]], axis=0)
    high, low = split_two(scales)
    parts = jnp.concatenate([high, low, scales - high - low], axis=0).astype(jnp.bfloat16)
    slots = jnp.dot(
        table_rows[...].astype(jnp.float32).astype(jnp.bfloat16), spread, preferred_element_type=jnp.float32
    )
    for r in range(rows):
        chosen = (slots[r : r + 1] == slot).astype(jnp.float32).astype(jnp.bfloat16)
        found = jnp.dot(parts, chosen, preferred_element_type=jnp.float32)
        count = 2 * kv_heads
        factors[r] = found[:count] + found[count : 2 * count] + found[2 * count :]
        bias[r : r + 1] = jnp.where(place < lengths[r], 0.0, HIDDEN)
    for h in range(heads):
        query_rows[h * rows : (h + 1) * rows, :] = queries[:, h * HD : (h + 1) * HD].astype(jnp.float32)

    def pages_of(buf, r, k):
        return jnp.concatenate(
            [buf[table[r, p], :, k * HD : (k + 2) * HD] for p in range(pages)], axis=0
        )

    for copy in large[0]:
        copy.wait()
    stats = [jnp.zeros((group, HD), jnp.float32)] * kv_heads
    for r in range(rows):
        query = query_rows[pl.ds(r, heads, stride=rows), :].astype(jnp.bfloat16)
        for k in range(0, kv_heads, 2):
            left = jnp.concatenate(
                [
                    jnp.concatenate([query[k * group : (k + 1) * group], zeros], axis=1),
                    jnp.concatenate([zeros, query[(k + 1) * group : (k + 2) * group]], axis=1),
                ],
                axis=0,
            )
            both = lax.dot_general(
                left, pages_of(key_buf, r, k), (((1,), (1,)), ((), ())), preferred_element_type=jnp.float32
            )
            for i in (0, 1):
                at_key, at_value = k + i, kv_heads + k + i
                scores = both[i * group : (i + 1) * group] * factors[r, at_key : at_key + 1] + bias[r : r + 1]
                highest = jnp.maximum(jnp.max(scores, axis=1, keepdims=True), LOWEST)
                high, low = split_two(highest)
                prob = jnp.exp2(scores - (high + low))
                total_high, total_low = split_two(jnp.sum(prob, axis=1, keepdims=True))
                for at, value in enumerate((high, low, total_high, total_low)):
                    stats[k + i] = jnp.where(lane == 4 * r + at, value, stats[k + i])
                weights[r, (k + i) * group : (k + i + 1) * group] = (
                    prob * factors[r, at_value : at_value + 1]
                ).astype(jnp.bfloat16)
    for copy in large[1]:
        copy.wait()
    for r in range(rows):
        for k in range(0, kv_heads, 2):
            both = jnp.dot(
                weights[r, k * group : (k + 2) * group], pages_of(value_buf, r, k), preferred_element_type=jnp.float32
            )
            for i in (0, 1):
                partial = both[i * group : (i + 1) * group, i * HD : (i + 1) * HD]
                for start in range(0, group, heads_dev):
                    d = ((k + i) * group + start) // heads_dev
                    staged[d, r] = partial[start : start + heads_dev]
    for k in range(kv_heads):
        for start in range(0, group, heads_dev):
            d = (k * group + start) // heads_dev
            staged[d, rows] = stats[k][start : start + heads_dev]


def pack_kernel(staged, packed):
    packed[...] = staged[...].astype(jnp.bfloat16)


def combine_kernel(heads_dev, packed, left, attended):
    rows = left.shape[0]
    stats = packed[:, rows].astype(jnp.float32)
    lanes = stats.shape[-1]

    def lanes_ahead(value, by):
        return pltpu.roll(value, lanes - by, axis=2)

    maxima = stats + lanes_ahead(stats, 1)
    rescale = jnp.exp2(maxima - jnp.max(maxima, axis=0, keepdims=True))
    totals = lanes_ahead(stats, 2) + lanes_ahead(stats, 3)
    denominator = jnp.sum(totals * rescale, axis=0)
    for r in range(rows):
        partial = packed[:, r].astype(jnp.float32)
        numerator = jnp.sum(partial * rescale[:, :, 4 * r : 4 * r + 1], axis=0)
        attended[r * heads_dev : (r + 1) * heads_dev, :] = numerator / denominator[:, 4 * r : 4 * r + 1]
    rounded = jnp.concatenate(
        [attended[pl.ds(j, rows, stride=heads_dev), :].astype(jnp.bfloat16) for j in range(heads_dev)], axis=1
    )
    left[...] = rounded


def project_kernel(partner, left, weight, out):
    part = out.shape[1]
    quarter = lax.rem(lax.axis_index("kvp"), weight.shape[1] // part)
    start = pl.multiple_of(jnp.bitwise_xor(quarter, partner) * part, part)
    terms = jnp.dot(left[...], weight[:, pl.ds(start, part)], preferred_element_type=jnp.float32)
    out[...] = terms.astype(out.dtype)


def add_kernel(*refs):
    terms = [ref[...].astype(jnp.float32) for ref in refs[:-1]]
    while len(terms) > 1:
        terms = [terms[i] + terms[i + 1] for i in range(0, len(terms), 2)]
    refs[-1][...] = terms[0].astype(refs[-1].dtype)


def lay_kernel(*refs):
    parts, out = refs[:-1], refs[-1]
    quarter = lax.rem(lax.axis_index("kvp"), len(parts))
    width = parts[0].shape[1]
    for x, part in enumerate(parts):
        start = pl.multiple_of(jnp.bitwise_xor(quarter, x) * width, width)
        out[:, pl.ds(start, width)] = part[...]


def exchange(array, partner, devices):
    return lax.ppermute(array, "kvp", [(i, i ^ partner) for i in range(devices)])


def in_hbm(array):
    return pltpu.with_memory_space_constraint(array, pltpu.HBM)


def body(queries, key_cache, value_cache, key_scale, value_scale, page_table, lengths, out_weight, *, devices):
    rows, pages = page_table.shape
    slots, _, columns = key_cache.shape
    kv_heads = key_scale.shape[1]
    heads_dev = out_weight.shape[0] // HD
    heads = queries.shape[1] // HD
    features = out_weight.shape[1]
    inner = 4
    outer = devices // inner
    part = features // inner
    staged = pl.pallas_call(
        functools.partial(attend_kernel, heads_dev, devices),
        out_shape=pltpu.VMEM((devices, rows + 1, heads_dev, HD), jnp.float32),
        in_specs=[HBM] * 7,
        out_specs=VMEM,
        scratch_shapes=[
            pltpu.SMEM((rows, pages), jnp.int32),
            pltpu.SMEM((rows,), jnp.int32),
            pltpu.VMEM((kv_heads, slots), jnp.float32),
            pltpu.VMEM((kv_heads, slots), jnp.float32),
            pltpu.VMEM((rows, heads * HD), jnp.bfloat16),
            pltpu.VMEM((slots, PAGE, columns), jnp.bfloat16),
            pltpu.VMEM((slots, PAGE, columns), jnp.bfloat16),
            pltpu.VMEM((heads * rows, HD), jnp.float32),
            pltpu.VMEM((rows, pages), jnp.int32),
            pltpu.VMEM((rows, 2 * kv_heads, pages * PAGE), jnp.float32),
            pltpu.VMEM((rows, pages * PAGE), jnp.float32),
            pltpu.VMEM((rows, heads, pages * PAGE), jnp.bfloat16),
            pltpu.SemaphoreType.DMA((6,)),
            pltpu.SemaphoreType.DMA((2, CACHE_PIECES)),
        ],
        compiler_params=pltpu.CompilerParams(vmem_limit_bytes=ATTEND_VMEM),
        cost_estimate=pl.CostEstimate(
            flops=4 * heads * rows * pages * PAGE * HD,
            bytes_accessed=4 * rows * pages * PAGE * columns,
            transcendentals=heads * rows * pages * PAGE,
        ),
        name="attend",
    )(*[in_hbm(a) for a in (page_table, lengths, key_scale.T, value_scale.T, queries, key_cache, value_cache)])

    packed = pl.pallas_call(
        pack_kernel,
        out_shape=jax.ShapeDtypeStruct(staged.shape, jnp.bfloat16),
        in_specs=[VMEM],
        out_specs=VMEM,
        compiler_params=pltpu.CompilerParams(vmem_limit_bytes=SMALL_VMEM),
        cost_estimate=pl.CostEstimate(flops=EXCHANGE_FLOPS, bytes_accessed=6 * staged.size, transcendentals=0),
        name="pack",
    )(staged)

    received = lax.all_to_all(packed, "kvp", split_axis=0, concat_axis=0, tiled=True)

    resident = pltpu.with_memory_space_constraint(out_weight, pltpu.VMEM)
    depth = heads_dev * HD
    cost = pl.CostEstimate(flops=1024, bytes_accessed=1024, transcendentals=0)
    small = pltpu.CompilerParams(vmem_limit_bytes=SMALL_VMEM)
    left = pl.pallas_call(
        functools.partial(combine_kernel, heads_dev),
        out_shape=jax.ShapeDtypeStruct((rows, depth), jnp.bfloat16),
        in_specs=[VMEM],
        out_specs=VMEM,
        scratch_shapes=[pltpu.VMEM((rows * heads_dev, HD), jnp.float32)],
        compiler_params=small,
        name="combine",
    )(received)
    arrived = []
    for x in reversed(range(inner)):
        terms = pl.pallas_call(
            functools.partial(project_kernel, x),
            out_shape=jax.ShapeDtypeStruct((rows, part), jnp.bfloat16 if x else jnp.float32),
            in_specs=[VMEM] * 2,
            out_specs=VMEM,
            compiler_params=small,
            cost_estimate=cost,
            name=f"project_{x}",
        )(left, resident)
        arrived.append(exchange(terms, x, devices) if x else terms)

    def add(terms, name):
        return pl.pallas_call(
            add_kernel,
            out_shape=jax.ShapeDtypeStruct((rows, part), jnp.bfloat16),
            in_specs=[VMEM] * len(terms),
            out_specs=VMEM,
            compiler_params=pltpu.CompilerParams(vmem_limit_bytes=SMALL_VMEM),
            name=name,
        )(*terms)

    mine = add(arrived, "add_near")
    mine = add([mine] + [exchange(mine, x * inner, devices) for x in range(1, outer)], "add_far")
    parts = [mine] + [exchange(mine, x, devices) for x in range(1, inner)]
    return pl.pallas_call(
        lay_kernel,
        out_shape=jax.ShapeDtypeStruct((rows, features), jnp.bfloat16),
        in_specs=[VMEM] * inner,
        out_specs=VMEM,
        compiler_params=pltpu.CompilerParams(vmem_limit_bytes=SMALL_VMEM),
        name="lay",
    )(*parts)


def solution(mesh):
    placed = (
        P("group", None),
        P(("group", "kvp"), None, None),
        P(("group", "kvp"), None, None),
        P(("group", "kvp"), None),
        P(("group", "kvp"), None),
        P("group", "kvp"),
        P("group"),
        P("kvp", None),
    )
    return jax.shard_map(
        functools.partial(body, devices=mesh.shape["kvp"]),
        mesh=mesh,
        in_specs=placed,
        out_specs=P("group", None),
        check_vma=False,
    )
```

```python
import functools
import math

import jax
import jax.numpy as jnp
from jax import lax
from jax.experimental import pallas as pl
from jax.experimental.pallas import tpu as pltpu
from jax.sharding import PartitionSpec as P

HD = 128
PAGE = 64
ATTEND_VMEM = 60 * 1024 * 1024
HIDDEN = -1e30
LOWEST = -1e20
EXCHANGE_FLOPS = 5_000_000_000
SMALL_VMEM = 8 * 1024 * 1024
VMEM = pl.BlockSpec(memory_space=pltpu.VMEM)
HBM = pl.BlockSpec(memory_space=pltpu.HBM)


def split_two(value):
    high = value.astype(jnp.bfloat16).astype(jnp.float32)
    low = (value - high).astype(jnp.bfloat16).astype(jnp.float32)
    return high, low


def attend_kernel(heads_dev, devices, *refs):
    table_hbm, lengths_hbm, key_scale_hbm, value_scale_hbm, queries_hbm, keys, values = refs[:7]
    staged, table, lengths, key_scale, value_scale, queries, key_buf, value_buf, query_rows = refs[7:16]
    table_rows, factors, bias, weights, small_sems, sems = refs[16:]
    rows, pages = table.shape
    kv_heads = key_scale.shape[0]
    heads = queries.shape[1] // HD
    group = heads // kv_heads
    context = pages * PAGE
    pieces = sems.shape[1]
    piece = keys.shape[0] // pieces

    small = []
    for i, (source, target) in enumerate(
        (
            (table_hbm, table),
            (table_hbm, table_rows),
            (lengths_hbm, lengths),
            (key_scale_hbm, key_scale),
            (value_scale_hbm, value_scale),
            (queries_hbm, queries),
        )
    ):
        small.append(pltpu.make_async_copy(source, target, small_sems.at[i]))
        small[-1].start()
    large = []
    for which, source, target in ((0, keys, key_buf), (1, values, value_buf)):
        large.append([])
        for i in range(pieces):
            here = pl.ds(i * piece, piece)
            large[-1].append(pltpu.make_async_copy(source.at[here], target.at[here], sems.at[which, i]))
    for copy in large[0]:
        copy.start()

    me = lax.axis_index("kvp")
    lane = lax.broadcasted_iota(jnp.int32, (group, HD), 1)
    place = me * context + lax.broadcasted_iota(jnp.int32, (1, context), 1)
    page_of = lax.div(lax.broadcasted_iota(jnp.int32, (pages, context), 1), PAGE)
    spread = (page_of == lax.broadcasted_iota(jnp.int32, (pages, context), 0)).astype(jnp.float32).astype(jnp.bfloat16)
    slot = lax.broadcasted_iota(jnp.int32, (keys.shape[0], context), 0).astype(jnp.float32)
    zeros = jnp.zeros((group, HD), jnp.bfloat16)
    for copy in small:
        copy.wait()
    for copy in large[1]:
        copy.start()

    scales = jnp.concatenate([key_scale[...] * (math.log2(math.e) / math.sqrt(HD)), value_scale[...]], axis=0)
    high, low = split_two(scales)
    parts = jnp.concatenate([high, low, scales - high - low], axis=0).astype(jnp.bfloat16)
    slots = jnp.dot(
        table_rows[...].astype(jnp.float32).astype(jnp.bfloat16), spread, preferred_element_type=jnp.float32
    )
    for r in range(rows):
        chosen = (slots[r : r + 1] == slot).astype(jnp.float32).astype(jnp.bfloat16)
        found = jnp.dot(parts, chosen, preferred_element_type=jnp.float32)
        count = 2 * kv_heads
        factors[r] = found[:count] + found[count : 2 * count] + found[2 * count :]
        bias[r : r + 1] = jnp.where(place < lengths[r], 0.0, HIDDEN)
    for h in range(heads):
        query_rows[h * rows : (h + 1) * rows, :] = queries[:, h * HD : (h + 1) * HD].astype(jnp.float32)

    def pages_of(buf, r, k):
        return jnp.concatenate(
            [buf[table[r, p], :, k * HD : (k + 2) * HD] for p in range(pages)], axis=0
        )

    for copy in large[0]:
        copy.wait()
    stats = [jnp.zeros((group, HD), jnp.float32)] * kv_heads
    for r in range(rows):
        query = query_rows[pl.ds(r, heads, stride=rows), :].astype(jnp.bfloat16)
        for k in range(0, kv_heads, 2):
            left = jnp.concatenate(
                [
                    jnp.concatenate([query[k * group : (k + 1) * group], zeros], axis=1),
                    jnp.concatenate([zeros, query[(k + 1) * group : (k + 2) * group]], axis=1),
                ],
                axis=0,
            )
            both = lax.dot_general(
                left, pages_of(key_buf, r, k), (((1,), (1,)), ((), ())), preferred_element_type=jnp.float32
            )
            for i in (0, 1):
                at_key, at_value = k + i, kv_heads + k + i
                scores = both[i * group : (i + 1) * group] * factors[r, at_key : at_key + 1] + bias[r : r + 1]
                highest = jnp.maximum(jnp.max(scores, axis=1, keepdims=True), LOWEST)
                high, low = split_two(highest)
                prob = jnp.exp2(scores - (high + low))
                total_high, total_low = split_two(jnp.sum(prob, axis=1, keepdims=True))
                for at, value in enumerate((high, low, total_high, total_low)):
                    stats[k + i] = jnp.where(lane == 4 * r + at, value, stats[k + i])
                weights[r, (k + i) * group : (k + i + 1) * group] = (
                    prob * factors[r, at_value : at_value + 1]
                ).astype(jnp.bfloat16)
    for copy in large[1]:
        copy.wait()
    for r in range(rows):
        for k in range(0, kv_heads, 2):
            both = jnp.dot(
                weights[r, k * group : (k + 2) * group], pages_of(value_buf, r, k), preferred_element_type=jnp.float32
            )
            for i in (0, 1):
                partial = both[i * group : (i + 1) * group, i * HD : (i + 1) * HD]
                for start in range(0, group, heads_dev):
                    d = ((k + i) * group + start) // heads_dev
                    staged[d, r] = partial[start : start + heads_dev]
    for k in range(kv_heads):
        for start in range(0, group, heads_dev):
            d = (k * group + start) // heads_dev
            staged[d, rows] = stats[k][start : start + heads_dev]


def pack_kernel(staged, packed):
    packed[...] = staged[...].astype(jnp.bfloat16)


def combine_kernel(heads_dev, packed, left, attended):
    rows = left.shape[0]
    stats = packed[:, rows].astype(jnp.float32)
    lanes = stats.shape[-1]

    def lanes_ahead(value, by):
        return pltpu.roll(value, lanes - by, axis=2)

    maxima = stats + lanes_ahead(stats, 1)
    rescale = jnp.exp2(maxima - jnp.max(maxima, axis=0, keepdims=True))
    totals = lanes_ahead(stats, 2) + lanes_ahead(stats, 3)
    denominator = jnp.sum(totals * rescale, axis=0)
    for r in range(rows):
        partial = packed[:, r].astype(jnp.float32)
        numerator = jnp.sum(partial * rescale[:, :, 4 * r : 4 * r + 1], axis=0)
        attended[r * heads_dev : (r + 1) * heads_dev, :] = numerator / denominator[:, 4 * r : 4 * r + 1]
    rounded = jnp.concatenate(
        [attended[pl.ds(j, rows, stride=heads_dev), :].astype(jnp.bfloat16) for j in range(heads_dev)], axis=1
    )
    left[...] = rounded


def project_kernel(partner, left, weight, out):
    part = out.shape[1]
    quarter = lax.rem(lax.axis_index("kvp"), weight.shape[1] // part)
    start = pl.multiple_of(jnp.bitwise_xor(quarter, partner) * part, part)
    terms = jnp.dot(left[...], weight[:, pl.ds(start, part)], preferred_element_type=jnp.float32)
    out[...] = terms.astype(out.dtype)


def regroup_kernel(outer, inner, arrived, grouped):
    for x in range(outer):
        for i in range(inner):
            grouped[i * outer + x] = arrived[x * inner + i]


def spread_copies(value, copies):
    for i in range(copies.shape[0]):
        copies[i] = value


def add_near_kernel(*refs):
    terms, copies = refs[:-1], refs[-1]
    spread_copies(sum(term[...].astype(jnp.float32) for term in terms).astype(copies.dtype), copies)


def add_far_kernel(terms, copies):
    total = sum(terms[i].astype(jnp.float32) for i in range(terms.shape[0]))
    spread_copies(total.astype(copies.dtype), copies)


def lay_kernel(parts, out):
    count, _, width = parts.shape
    for i in range(count):
        out[:, i * width : (i + 1) * width] = parts[i]


def exchange(array, partner, devices):
    return lax.ppermute(array, "kvp", [(i, i ^ partner) for i in range(devices)])


def in_hbm(array):
    return pltpu.with_memory_space_constraint(array, pltpu.HBM)


def body(queries, key_cache, value_cache, key_scale, value_scale, page_table, lengths, out_weight, *, devices):
    rows, pages = page_table.shape
    slots, _, columns = key_cache.shape
    kv_heads = key_scale.shape[1]
    heads_dev = out_weight.shape[0] // HD
    heads = queries.shape[1] // HD
    features = out_weight.shape[1]
    staged = pl.pallas_call(
        functools.partial(attend_kernel, heads_dev, devices),
        out_shape=pltpu.VMEM((devices, rows + 1, heads_dev, HD), jnp.float32),
        in_specs=[HBM] * 7,
        out_specs=VMEM,
        scratch_shapes=[
            pltpu.SMEM((rows, pages), jnp.int32),
            pltpu.SMEM((rows,), jnp.int32),
            pltpu.VMEM((kv_heads, slots), jnp.float32),
            pltpu.VMEM((kv_heads, slots), jnp.float32),
            pltpu.VMEM((rows, heads * HD), jnp.bfloat16),
            pltpu.VMEM((slots, PAGE, columns), jnp.bfloat16),
            pltpu.VMEM((slots, PAGE, columns), jnp.bfloat16),
            pltpu.VMEM((heads * rows, HD), jnp.float32),
            pltpu.VMEM((rows, pages), jnp.int32),
            pltpu.VMEM((rows, 2 * kv_heads, pages * PAGE), jnp.float32),
            pltpu.VMEM((rows, pages * PAGE), jnp.float32),
            pltpu.VMEM((rows, heads, pages * PAGE), jnp.bfloat16),
            pltpu.SemaphoreType.DMA((6,)),
            pltpu.SemaphoreType.DMA((2, 4)),
        ],
        compiler_params=pltpu.CompilerParams(vmem_limit_bytes=ATTEND_VMEM),
        cost_estimate=pl.CostEstimate(
            flops=4 * heads * rows * pages * PAGE * HD,
            bytes_accessed=4 * rows * pages * PAGE * columns,
            transcendentals=heads * rows * pages * PAGE,
        ),
        name="attend",
    )(*[in_hbm(a) for a in (page_table, lengths, key_scale.T, value_scale.T, queries, key_cache, value_cache)])

    inner = 4
    outer = devices // inner
    part = features // inner

    def small_kernel(kernel, out_shape, name, *operands, flops=1024):
        return pl.pallas_call(
            kernel,
            out_shape=out_shape,
            in_specs=[VMEM] * len(operands),
            out_specs=VMEM,
            compiler_params=pltpu.CompilerParams(vmem_limit_bytes=SMALL_VMEM),
            cost_estimate=pl.CostEstimate(flops=flops, bytes_accessed=1024, transcendentals=0),
            name=name,
        )(*operands)

    packed = pl.pallas_call(
        pack_kernel,
        out_shape=jax.ShapeDtypeStruct(staged.shape, jnp.bfloat16),
        in_specs=[VMEM],
        out_specs=VMEM,
        compiler_params=pltpu.CompilerParams(vmem_limit_bytes=SMALL_VMEM),
        cost_estimate=pl.CostEstimate(flops=EXCHANGE_FLOPS, bytes_accessed=6 * staged.size, transcendentals=0),
        name="pack",
    )(staged)

    far = [[x * inner + i for x in range(outer)] for i in range(inner)]
    near = [[x * inner + i for i in range(inner)] for x in range(outer)]

    def exchange_all(array, groups):
        return lax.all_to_all(array, "kvp", split_axis=0, concat_axis=0, axis_index_groups=groups, tiled=True)

    arrived = exchange_all(packed, far)
    grouped = small_kernel(
        functools.partial(regroup_kernel, outer, inner), jax.ShapeDtypeStruct(arrived.shape, arrived.dtype),
        "regroup", arrived,
    )
    received = exchange_all(grouped, near)

    resident = pltpu.with_memory_space_constraint(out_weight, pltpu.VMEM)
    depth = heads_dev * HD
    cost = pl.CostEstimate(flops=1024, bytes_accessed=1024, transcendentals=0)
    small = pltpu.CompilerParams(vmem_limit_bytes=SMALL_VMEM)
    left = pl.pallas_call(
        functools.partial(combine_kernel, heads_dev),
        out_shape=jax.ShapeDtypeStruct((rows, depth), jnp.bfloat16),
        in_specs=[VMEM],
        out_specs=VMEM,
        scratch_shapes=[pltpu.VMEM((rows * heads_dev, HD), jnp.float32)],
        compiler_params=small,
        name="combine",
    )(received)
    arrived = []
    for x in reversed(range(inner)):
        terms = pl.pallas_call(
            functools.partial(project_kernel, x),
            out_shape=jax.ShapeDtypeStruct((rows, part), jnp.bfloat16 if x else jnp.float32),
            in_specs=[VMEM] * 2,
            out_specs=VMEM,
            compiler_params=small,
            cost_estimate=cost,
            name=f"project_{x}",
        )(left, resident)
        arrived.append(exchange(terms, x, devices) if x else terms)

    copies = jax.ShapeDtypeStruct((outer, rows, part), jnp.bfloat16)
    mine = small_kernel(add_near_kernel, copies, "add_near", *arrived)
    copies = jax.ShapeDtypeStruct((inner, rows, part), jnp.bfloat16)
    mine = small_kernel(add_far_kernel, copies, "add_far", exchange_all(mine, far))
    whole = jax.ShapeDtypeStruct((rows, features), jnp.bfloat16)
    return small_kernel(lay_kernel, whole, "lay", exchange_all(mine, near))


def solution(mesh):
    placed = (
        P("group", None),
        P(("group", "kvp"), None, None),
        P(("group", "kvp"), None, None),
        P(("group", "kvp"), None),
        P(("group", "kvp"), None),
        P("group", "kvp"),
        P("group"),
        P("kvp", None),
    )
    return jax.shard_map(
        functools.partial(body, devices=mesh.shape["kvp"]),
        mesh=mesh,
        in_specs=placed,
        out_specs=P("group", None),
        check_vma=False,
    )
```

```python
import functools
import math

import jax
import jax.numpy as jnp
from jax import lax
from jax.experimental import pallas as pl
from jax.experimental.pallas import tpu as pltpu
from jax.sharding import PartitionSpec as P

HD = 128
PAGE = 64
ATTEND_VMEM = 60 * 1024 * 1024
HIDDEN = -1e30
LOWEST = -1e20
EXCHANGE_FLOPS = 40_000_000_000
SMALL_VMEM = 8 * 1024 * 1024
VMEM = pl.BlockSpec(memory_space=pltpu.VMEM)
HBM = pl.BlockSpec(memory_space=pltpu.HBM)


def split_two(value):
    high = value.astype(jnp.bfloat16).astype(jnp.float32)
    low = (value - high).astype(jnp.bfloat16).astype(jnp.float32)
    return high, low


def attend_kernel(heads_dev, devices, *refs):
    table_hbm, lengths_hbm, key_scale_hbm, value_scale_hbm, queries_hbm, keys, values = refs[:7]
    staged, table, lengths, key_scale, value_scale, queries, key_buf, value_buf, query_rows = refs[7:16]
    table_rows, factors, bias, weights, small_sems, sems = refs[16:]
    rows, pages = table.shape
    kv_heads = key_scale.shape[0]
    heads = queries.shape[1] // HD
    group = heads // kv_heads
    context = pages * PAGE
    pieces = sems.shape[1]
    piece = keys.shape[0] // pieces

    small = []
    for i, (source, target) in enumerate(
        (
            (table_hbm, table),
            (table_hbm, table_rows),
            (lengths_hbm, lengths),
            (key_scale_hbm, key_scale),
            (value_scale_hbm, value_scale),
            (queries_hbm, queries),
        )
    ):
        small.append(pltpu.make_async_copy(source, target, small_sems.at[i]))
        small[-1].start()
    large = []
    for which, source, target in ((0, keys, key_buf), (1, values, value_buf)):
        large.append([])
        for i in range(pieces):
            here = pl.ds(i * piece, piece)
            large[-1].append(pltpu.make_async_copy(source.at[here], target.at[here], sems.at[which, i]))
    for copy in large[0]:
        copy.start()

    me = lax.axis_index("kvp")
    lane = lax.broadcasted_iota(jnp.int32, (group, HD), 1)
    place = me * context + lax.broadcasted_iota(jnp.int32, (1, context), 1)
    page_of = lax.div(lax.broadcasted_iota(jnp.int32, (pages, context), 1), PAGE)
    spread = (page_of == lax.broadcasted_iota(jnp.int32, (pages, context), 0)).astype(jnp.float32).astype(jnp.bfloat16)
    slot = lax.broadcasted_iota(jnp.int32, (keys.shape[0], context), 0).astype(jnp.float32)
    zeros = jnp.zeros((group, HD), jnp.bfloat16)
    for copy in small:
        copy.wait()
    for copy in large[1]:
        copy.start()

    scales = jnp.concatenate([key_scale[...] * (math.log2(math.e) / math.sqrt(HD)), value_scale[...]], axis=0)
    high, low = split_two(scales)
    parts = jnp.concatenate([high, low, scales - high - low], axis=0).astype(jnp.bfloat16)
    slots = jnp.dot(
        table_rows[...].astype(jnp.float32).astype(jnp.bfloat16), spread, preferred_element_type=jnp.float32
    )
    for r in range(rows):
        chosen = (slots[r : r + 1] == slot).astype(jnp.float32).astype(jnp.bfloat16)
        found = jnp.dot(parts, chosen, preferred_element_type=jnp.float32)
        count = 2 * kv_heads
        factors[r] = found[:count] + found[count : 2 * count] + found[2 * count :]
        bias[r : r + 1] = jnp.where(place < lengths[r], 0.0, HIDDEN)
    for h in range(heads):
        query_rows[h * rows : (h + 1) * rows, :] = queries[:, h * HD : (h + 1) * HD].astype(jnp.float32)

    def pages_of(buf, r, k):
        return jnp.concatenate(
            [buf[table[r, p], :, k * HD : (k + 2) * HD] for p in range(pages)], axis=0
        )

    for copy in large[0]:
        copy.wait()
    stats = [jnp.zeros((group, HD), jnp.float32)] * kv_heads
    for r in range(rows):
        query = query_rows[pl.ds(r, heads, stride=rows), :].astype(jnp.bfloat16)
        for k in range(0, kv_heads, 2):
            left = jnp.concatenate(
                [
                    jnp.concatenate([query[k * group : (k + 1) * group], zeros], axis=1),
                    jnp.concatenate([zeros, query[(k + 1) * group : (k + 2) * group]], axis=1),
                ],
                axis=0,
            )
            both = lax.dot_general(
                left, pages_of(key_buf, r, k), (((1,), (1,)), ((), ())), preferred_element_type=jnp.float32
            )
            for i in (0, 1):
                at_key, at_value = k + i, kv_heads + k + i
                scores = both[i * group : (i + 1) * group] * factors[r, at_key : at_key + 1] + bias[r : r + 1]
                highest = jnp.maximum(jnp.max(scores, axis=1, keepdims=True), LOWEST)
                high, low = split_two(highest)
                prob = jnp.exp2(scores - (high + low))
                total_high, total_low = split_two(jnp.sum(prob, axis=1, keepdims=True))
                for at, value in enumerate((high, low, total_high, total_low)):
                    stats[k + i] = jnp.where(lane == 4 * r + at, value, stats[k + i])
                weights[r, (k + i) * group : (k + i + 1) * group] = (
                    prob * factors[r, at_value : at_value + 1]
                ).astype(jnp.bfloat16)
    for copy in large[1]:
        copy.wait()
    for r in range(rows):
        for k in range(0, kv_heads, 2):
            both = jnp.dot(
                weights[r, k * group : (k + 2) * group], pages_of(value_buf, r, k), preferred_element_type=jnp.float32
            )
            for i in (0, 1):
                partial = both[i * group : (i + 1) * group, i * HD : (i + 1) * HD]
                for start in range(0, group, heads_dev):
                    d = ((k + i) * group + start) // heads_dev
                    staged[d, r] = partial[start : start + heads_dev]
    for k in range(kv_heads):
        for start in range(0, group, heads_dev):
            d = (k * group + start) // heads_dev
            staged[d, rows] = stats[k][start : start + heads_dev]


def pack_kernel(staged, packed):
    packed[...] = staged[...].astype(jnp.bfloat16)


def combine_kernel(heads_dev, packed, left, attended):
    rows = left.shape[0]
    stats = packed[:, rows].astype(jnp.float32)
    lanes = stats.shape[-1]

    def lanes_ahead(value, by):
        return pltpu.roll(value, lanes - by, axis=2)

    maxima = stats + lanes_ahead(stats, 1)
    rescale = jnp.exp2(maxima - jnp.max(maxima, axis=0, keepdims=True))
    totals = lanes_ahead(stats, 2) + lanes_ahead(stats, 3)
    denominator = jnp.sum(totals * rescale, axis=0)
    for r in range(rows):
        partial = packed[:, r].astype(jnp.float32)
        numerator = jnp.sum(partial * rescale[:, :, 4 * r : 4 * r + 1], axis=0)
        attended[r * heads_dev : (r + 1) * heads_dev, :] = numerator / denominator[:, 4 * r : 4 * r + 1]
    rounded = jnp.concatenate(
        [attended[pl.ds(j, rows, stride=heads_dev), :].astype(jnp.bfloat16) for j in range(heads_dev)], axis=1
    )
    left[...] = rounded


def project_kernel(partner, left, weight, out):
    part = out.shape[1]
    quarter = lax.rem(lax.axis_index("kvp"), weight.shape[1] // part)
    start = pl.multiple_of(jnp.bitwise_xor(quarter, partner) * part, part)
    terms = jnp.dot(left[...], weight[:, pl.ds(start, part)], preferred_element_type=jnp.float32)
    out[...] = terms.astype(out.dtype)


def add_kernel(*refs):
    terms = [ref[...].astype(jnp.float32) for ref in refs[:-1]]
    while len(terms) > 1:
        terms = [terms[i] + terms[i + 1] for i in range(0, len(terms), 2)]
    refs[-1][...] = terms[0].astype(refs[-1].dtype)


def lay_kernel(*refs):
    parts, out = refs[:-1], refs[-1]
    quarter = lax.rem(lax.axis_index("kvp"), len(parts))
    width = parts[0].shape[1]
    for x, part in zip((0, 1, 3, 2), parts):
        start = pl.multiple_of(jnp.bitwise_xor(quarter, x) * width, width)
        out[:, pl.ds(start, width)] = part[...]


def exchange(array, partner, devices):
    return lax.ppermute(array, "kvp", [(i, i ^ partner) for i in range(devices)])


def in_hbm(array):
    return pltpu.with_memory_space_constraint(array, pltpu.HBM)


def body(queries, key_cache, value_cache, key_scale, value_scale, page_table, lengths, out_weight, *, devices):
    rows, pages = page_table.shape
    slots, _, columns = key_cache.shape
    kv_heads = key_scale.shape[1]
    heads_dev = out_weight.shape[0] // HD
    heads = queries.shape[1] // HD
    features = out_weight.shape[1]
    inner = 4
    outer = devices // inner
    part = features // inner
    staged = pl.pallas_call(
        functools.partial(attend_kernel, heads_dev, devices),
        out_shape=pltpu.VMEM((devices, rows + 1, heads_dev, HD), jnp.float32),
        in_specs=[HBM] * 7,
        out_specs=VMEM,
        scratch_shapes=[
            pltpu.SMEM((rows, pages), jnp.int32),
            pltpu.SMEM((rows,), jnp.int32),
            pltpu.VMEM((kv_heads, slots), jnp.float32),
            pltpu.VMEM((kv_heads, slots), jnp.float32),
            pltpu.VMEM((rows, heads * HD), jnp.bfloat16),
            pltpu.VMEM((slots, PAGE, columns), jnp.bfloat16),
            pltpu.VMEM((slots, PAGE, columns), jnp.bfloat16),
            pltpu.VMEM((heads * rows, HD), jnp.float32),
            pltpu.VMEM((rows, pages), jnp.int32),
            pltpu.VMEM((rows, 2 * kv_heads, pages * PAGE), jnp.float32),
            pltpu.VMEM((rows, pages * PAGE), jnp.float32),
            pltpu.VMEM((rows, heads, pages * PAGE), jnp.bfloat16),
            pltpu.SemaphoreType.DMA((6,)),
            pltpu.SemaphoreType.DMA((2, 2)),
        ],
        compiler_params=pltpu.CompilerParams(vmem_limit_bytes=ATTEND_VMEM),
        cost_estimate=pl.CostEstimate(
            flops=4 * heads * rows * pages * PAGE * HD,
            bytes_accessed=4 * rows * pages * PAGE * columns,
            transcendentals=heads * rows * pages * PAGE,
        ),
        name="attend",
    )(*[in_hbm(a) for a in (page_table, lengths, key_scale.T, value_scale.T, queries, key_cache, value_cache)])

    packed = pl.pallas_call(
        pack_kernel,
        out_shape=jax.ShapeDtypeStruct(staged.shape, jnp.bfloat16),
        in_specs=[VMEM],
        out_specs=VMEM,
        compiler_params=pltpu.CompilerParams(vmem_limit_bytes=SMALL_VMEM),
        cost_estimate=pl.CostEstimate(flops=EXCHANGE_FLOPS, bytes_accessed=6 * staged.size, transcendentals=0),
        name="pack",
    )(staged)

    received = lax.all_to_all(packed, "kvp", split_axis=0, concat_axis=0, tiled=True)

    resident = pltpu.with_memory_space_constraint(out_weight, pltpu.VMEM)
    depth = heads_dev * HD
    cost = pl.CostEstimate(flops=1024, bytes_accessed=1024, transcendentals=0)
    small = pltpu.CompilerParams(vmem_limit_bytes=SMALL_VMEM)
    left = pl.pallas_call(
        functools.partial(combine_kernel, heads_dev),
        out_shape=jax.ShapeDtypeStruct((rows, depth), jnp.bfloat16),
        in_specs=[VMEM],
        out_specs=VMEM,
        scratch_shapes=[pltpu.VMEM((rows * heads_dev, HD), jnp.float32)],
        compiler_params=small,
        name="combine",
    )(received)
    arrived = []
    for x in (2, 3, 1, 0):
        terms = pl.pallas_call(
            functools.partial(project_kernel, x),
            out_shape=jax.ShapeDtypeStruct((rows, part), jnp.bfloat16 if x else jnp.float32),
            in_specs=[VMEM] * 2,
            out_specs=VMEM,
            compiler_params=small,
            cost_estimate=cost,
            name=f"project_{x}",
        )(left, resident)
        arrived.append(exchange(terms, x, devices) if x else terms)

    def add(terms, name):
        return pl.pallas_call(
            add_kernel,
            out_shape=jax.ShapeDtypeStruct((rows, part), jnp.bfloat16),
            in_specs=[VMEM] * len(terms),
            out_specs=VMEM,
            compiler_params=pltpu.CompilerParams(vmem_limit_bytes=SMALL_VMEM),
            name=name,
        )(*terms)

    mine = add(arrived, "add_near")
    mine = add([mine] + [exchange(mine, x * inner, devices) for x in range(1, outer)], "add_far")
    parts = [mine] + [exchange(mine, x, devices) for x in (1, 3, 2)]
    return pl.pallas_call(
        lay_kernel,
        out_shape=jax.ShapeDtypeStruct((rows, features), jnp.bfloat16),
        in_specs=[VMEM] * inner,
        out_specs=VMEM,
        compiler_params=pltpu.CompilerParams(vmem_limit_bytes=SMALL_VMEM),
        name="lay",
    )(*parts)


def solution(mesh):
    placed = (
        P("group", None),
        P(("group", "kvp"), None, None),
        P(("group", "kvp"), None, None),
        P(("group", "kvp"), None),
        P(("group", "kvp"), None),
        P("group", "kvp"),
        P("group"),
        P("kvp", None),
    )
    return jax.shard_map(
        functools.partial(body, devices=mesh.shape["kvp"]),
        mesh=mesh,
        in_specs=placed,
        out_specs=P("group", None),
        check_vma=False,
    )
```

```python
import functools
import math

import jax
import jax.numpy as jnp
from jax import lax
from jax.experimental import pallas as pl
from jax.experimental.pallas import tpu as pltpu
from jax.sharding import PartitionSpec as P

HD = 128
PAGE = 64
ATTEND_VMEM = 60 * 1024 * 1024
HIDDEN = -1e30
LOWEST = -1e20
EXCHANGE_FLOPS = 40_000_000_000
SMALL_VMEM = 8 * 1024 * 1024
VMEM = pl.BlockSpec(memory_space=pltpu.VMEM)
HBM = pl.BlockSpec(memory_space=pltpu.HBM)


def split_two(value):
    high = value.astype(jnp.bfloat16).astype(jnp.float32)
    low = (value - high).astype(jnp.bfloat16).astype(jnp.float32)
    return high, low


def attend_kernel(heads_dev, devices, *refs):
    table_hbm, lengths_hbm, key_scale_hbm, value_scale_hbm, queries_hbm, keys, values = refs[:7]
    staged, table, lengths, key_scale, value_scale, queries, key_buf, value_buf, query_rows = refs[7:16]
    table_rows, factors, bias, weights, small_sems, sems = refs[16:]
    rows, pages = table.shape
    kv_heads = key_scale.shape[0]
    heads = queries.shape[1] // HD
    group = heads // kv_heads
    context = pages * PAGE
    pieces = sems.shape[1]
    piece = keys.shape[0] // pieces

    large = []
    for which, source, target in ((0, keys, key_buf), (1, values, value_buf)):
        large.append([])
        for i in range(pieces):
            here = pl.ds(i * piece, piece)
            large[-1].append(pltpu.make_async_copy(source.at[here], target.at[here], sems.at[which, i]))
    for copy in large[0]:
        copy.start()
    small = []
    for i, (source, target) in enumerate(
        (
            (table_hbm, table),
            (table_hbm, table_rows),
            (lengths_hbm, lengths),
            (key_scale_hbm, key_scale),
            (value_scale_hbm, value_scale),
            (queries_hbm, queries),
        )
    ):
        small.append(pltpu.make_async_copy(source, target, small_sems.at[i]))
        small[-1].start()

    me = lax.axis_index("kvp")
    lane = lax.broadcasted_iota(jnp.int32, (group, HD), 1)
    place = me * context + lax.broadcasted_iota(jnp.int32, (1, context), 1)
    page_of = lax.div(lax.broadcasted_iota(jnp.int32, (pages, context), 1), PAGE)
    spread = (page_of == lax.broadcasted_iota(jnp.int32, (pages, context), 0)).astype(jnp.float32).astype(jnp.bfloat16)
    slot = lax.broadcasted_iota(jnp.int32, (keys.shape[0], context), 0).astype(jnp.float32)
    zeros = jnp.zeros((group, HD), jnp.bfloat16)
    for copy in small:
        copy.wait()
    for copy in large[1]:
        copy.start()

    scales = jnp.concatenate([key_scale[...] * (math.log2(math.e) / math.sqrt(HD)), value_scale[...]], axis=0)
    high, low = split_two(scales)
    parts = jnp.concatenate([high, low, scales - high - low], axis=0).astype(jnp.bfloat16)
    slots = jnp.dot(
        table_rows[...].astype(jnp.float32).astype(jnp.bfloat16), spread, preferred_element_type=jnp.float32
    )
    for r in range(rows):
        chosen = (slots[r : r + 1] == slot).astype(jnp.float32).astype(jnp.bfloat16)
        found = jnp.dot(parts, chosen, preferred_element_type=jnp.float32)
        count = 2 * kv_heads
        factors[r] = found[:count] + found[count : 2 * count] + found[2 * count :]
        bias[r : r + 1] = jnp.where(place < lengths[r], 0.0, HIDDEN)
    for h in range(heads):
        query_rows[h * rows : (h + 1) * rows, :] = queries[:, h * HD : (h + 1) * HD].astype(jnp.float32)

    def pages_of(buf, r, k):
        return jnp.concatenate(
            [buf[table[r, p], :, k * HD : (k + 2) * HD] for p in range(pages)], axis=0
        )

    for copy in large[0]:
        copy.wait()
    stats = [jnp.zeros((group, HD), jnp.float32)] * kv_heads
    for r in range(rows):
        query = query_rows[pl.ds(r, heads, stride=rows), :].astype(jnp.bfloat16)
        for k in range(0, kv_heads, 2):
            left = jnp.concatenate(
                [
                    jnp.concatenate([query[k * group : (k + 1) * group], zeros], axis=1),
                    jnp.concatenate([zeros, query[(k + 1) * group : (k + 2) * group]], axis=1),
                ],
                axis=0,
            )
            both = lax.dot_general(
                left, pages_of(key_buf, r, k), (((1,), (1,)), ((), ())), preferred_element_type=jnp.float32
            )
            for i in (0, 1):
                at_key, at_value = k + i, kv_heads + k + i
                scores = both[i * group : (i + 1) * group] * factors[r, at_key : at_key + 1] + bias[r : r + 1]
                highest = jnp.maximum(jnp.max(scores, axis=1, keepdims=True), LOWEST)
                high, low = split_two(highest)
                prob = jnp.exp2(scores - (high + low))
                total_high, total_low = split_two(jnp.sum(prob, axis=1, keepdims=True))
                for at, value in enumerate((high, low, total_high, total_low)):
                    stats[k + i] = jnp.where(lane == 4 * r + at, value, stats[k + i])
                weights[r, (k + i) * group : (k + i + 1) * group] = (
                    prob * factors[r, at_value : at_value + 1]
                ).astype(jnp.bfloat16)
    for copy in large[1]:
        copy.wait()
    for r in range(rows):
        for k in range(0, kv_heads, 2):
            both = jnp.dot(
                weights[r, k * group : (k + 2) * group], pages_of(value_buf, r, k), preferred_element_type=jnp.float32
            )
            for i in (0, 1):
                partial = both[i * group : (i + 1) * group, i * HD : (i + 1) * HD]
                for start in range(0, group, heads_dev):
                    d = ((k + i) * group + start) // heads_dev
                    staged[d, r] = partial[start : start + heads_dev]
    for k in range(kv_heads):
        for start in range(0, group, heads_dev):
            d = (k * group + start) // heads_dev
            staged[d, rows] = stats[k][start : start + heads_dev]


def pack_kernel(staged, packed):
    packed[...] = staged[...].astype(jnp.bfloat16)


def combine_kernel(heads_dev, packed, left, attended):
    rows = left.shape[0]
    stats = packed[:, rows].astype(jnp.float32)
    lanes = stats.shape[-1]

    def lanes_ahead(value, by):
        return pltpu.roll(value, lanes - by, axis=2)

    maxima = stats + lanes_ahead(stats, 1)
    rescale = jnp.exp2(maxima - jnp.max(maxima, axis=0, keepdims=True))
    totals = lanes_ahead(stats, 2) + lanes_ahead(stats, 3)
    denominator = jnp.sum(totals * rescale, axis=0)
    for r in range(rows):
        partial = packed[:, r].astype(jnp.float32)
        numerator = jnp.sum(partial * rescale[:, :, 4 * r : 4 * r + 1], axis=0)
        attended[r * heads_dev : (r + 1) * heads_dev, :] = numerator / denominator[:, 4 * r : 4 * r + 1]
    rounded = jnp.concatenate(
        [attended[pl.ds(j, rows, stride=heads_dev), :].astype(jnp.bfloat16) for j in range(heads_dev)], axis=1
    )
    left[...] = rounded


def project_kernel(partner, left, weight, out):
    part = out.shape[1]
    quarter = lax.rem(lax.axis_index("kvp"), weight.shape[1] // part)
    start = pl.multiple_of(jnp.bitwise_xor(quarter, partner) * part, part)
    terms = jnp.dot(left[...], weight[:, pl.ds(start, part)], preferred_element_type=jnp.float32)
    out[...] = terms.astype(out.dtype)


def add_kernel(*refs):
    terms = [ref[...].astype(jnp.float32) for ref in refs[:-1]]
    while len(terms) > 1:
        terms = [terms[i] + terms[i + 1] for i in range(0, len(terms), 2)]
    refs[-1][...] = terms[0].astype(refs[-1].dtype)


def lay_kernel(*refs):
    parts, out = refs[:-1], refs[-1]
    quarter = lax.rem(lax.axis_index("kvp"), len(parts))
    width = parts[0].shape[1]
    for x, part in enumerate(parts):
        start = pl.multiple_of(jnp.bitwise_xor(quarter, x) * width, width)
        out[:, pl.ds(start, width)] = part[...]


def exchange(array, partner, devices):
    return lax.ppermute(array, "kvp", [(i, i ^ partner) for i in range(devices)])


def in_hbm(array):
    return pltpu.with_memory_space_constraint(array, pltpu.HBM)


def body(queries, key_cache, value_cache, key_scale, value_scale, page_table, lengths, out_weight, *, devices):
    rows, pages = page_table.shape
    slots, _, columns = key_cache.shape
    kv_heads = key_scale.shape[1]
    heads_dev = out_weight.shape[0] // HD
    heads = queries.shape[1] // HD
    features = out_weight.shape[1]
    inner = 4
    outer = devices // inner
    part = features // inner
    staged = pl.pallas_call(
        functools.partial(attend_kernel, heads_dev, devices),
        out_shape=pltpu.VMEM((devices, rows + 1, heads_dev, HD), jnp.float32),
        in_specs=[HBM] * 7,
        out_specs=VMEM,
        scratch_shapes=[
            pltpu.SMEM((rows, pages), jnp.int32),
            pltpu.SMEM((rows,), jnp.int32),
            pltpu.VMEM((kv_heads, slots), jnp.float32),
            pltpu.VMEM((kv_heads, slots), jnp.float32),
            pltpu.VMEM((rows, heads * HD), jnp.bfloat16),
            pltpu.VMEM((slots, PAGE, columns), jnp.bfloat16),
            pltpu.VMEM((slots, PAGE, columns), jnp.bfloat16),
            pltpu.VMEM((heads * rows, HD), jnp.float32),
            pltpu.VMEM((rows, pages), jnp.int32),
            pltpu.VMEM((rows, 2 * kv_heads, pages * PAGE), jnp.float32),
            pltpu.VMEM((rows, pages * PAGE), jnp.float32),
            pltpu.VMEM((rows, heads, pages * PAGE), jnp.bfloat16),
            pltpu.SemaphoreType.DMA((6,)),
            pltpu.SemaphoreType.DMA((2, 2)),
        ],
        compiler_params=pltpu.CompilerParams(vmem_limit_bytes=ATTEND_VMEM),
        cost_estimate=pl.CostEstimate(
            flops=4 * heads * rows * pages * PAGE * HD,
            bytes_accessed=4 * rows * pages * PAGE * columns,
            transcendentals=heads * rows * pages * PAGE,
        ),
        name="attend",
    )(*[in_hbm(a) for a in (page_table, lengths, key_scale.T, value_scale.T, queries, key_cache, value_cache)])

    packed = pl.pallas_call(
        pack_kernel,
        out_shape=jax.ShapeDtypeStruct(staged.shape, jnp.bfloat16),
        in_specs=[VMEM],
        out_specs=VMEM,
        compiler_params=pltpu.CompilerParams(vmem_limit_bytes=SMALL_VMEM),
        cost_estimate=pl.CostEstimate(flops=EXCHANGE_FLOPS, bytes_accessed=6 * staged.size, transcendentals=0),
        name="pack",
    )(staged)

    received = lax.all_to_all(packed, "kvp", split_axis=0, concat_axis=0, tiled=True)

    resident = pltpu.with_memory_space_constraint(out_weight, pltpu.VMEM)
    depth = heads_dev * HD
    cost = pl.CostEstimate(flops=1024, bytes_accessed=1024, transcendentals=0)
    small = pltpu.CompilerParams(vmem_limit_bytes=SMALL_VMEM)
    left = pl.pallas_call(
        functools.partial(combine_kernel, heads_dev),
        out_shape=jax.ShapeDtypeStruct((rows, depth), jnp.bfloat16),
        in_specs=[VMEM],
        out_specs=VMEM,
        scratch_shapes=[pltpu.VMEM((rows * heads_dev, HD), jnp.float32)],
        compiler_params=small,
        name="combine",
    )(received)
    arrived = []
    for x in reversed(range(inner)):
        terms = pl.pallas_call(
            functools.partial(project_kernel, x),
            out_shape=jax.ShapeDtypeStruct((rows, part), jnp.bfloat16 if x else jnp.float32),
            in_specs=[VMEM] * 2,
            out_specs=VMEM,
            compiler_params=small,
            cost_estimate=cost,
            name=f"project_{x}",
        )(left, resident)
        arrived.append(exchange(terms, x, devices) if x else terms)

    def add(terms, name):
        return pl.pallas_call(
            add_kernel,
            out_shape=jax.ShapeDtypeStruct((rows, part), jnp.bfloat16),
            in_specs=[VMEM] * len(terms),
            out_specs=VMEM,
            compiler_params=pltpu.CompilerParams(vmem_limit_bytes=SMALL_VMEM),
            name=name,
        )(*terms)

    mine = add(arrived, "add_near")
    mine = add([mine] + [exchange(mine, x * inner, devices) for x in range(1, outer)], "add_far")
    parts = [mine] + [exchange(mine, x, devices) for x in range(1, inner)]
    return pl.pallas_call(
        lay_kernel,
        out_shape=jax.ShapeDtypeStruct((rows, features), jnp.bfloat16),
        in_specs=[VMEM] * inner,
        out_specs=VMEM,
        compiler_params=pltpu.CompilerParams(vmem_limit_bytes=SMALL_VMEM),
        name="lay",
    )(*parts)


def solution(mesh):
    placed = (
        P("group", None),
        P(("group", "kvp"), None, None),
        P(("group", "kvp"), None, None),
        P(("group", "kvp"), None),
        P(("group", "kvp"), None),
        P("group", "kvp"),
        P("group"),
        P("kvp", None),
    )
    return jax.shard_map(
        functools.partial(body, devices=mesh.shape["kvp"]),
        mesh=mesh,
        in_specs=placed,
        out_specs=P("group", None),
        check_vma=False,
    )
```

```python
import functools
import math

import jax
import jax.numpy as jnp
from jax import lax
from jax.experimental import pallas as pl
from jax.experimental.pallas import tpu as pltpu
from jax.sharding import PartitionSpec as P

HD = 128
PAGE = 64
ATTEND_VMEM = 60 * 1024 * 1024
HIDDEN = -1e30
LOWEST = -1e20
EXCHANGE_FLOPS = 40_000_000_000
SMALL_VMEM = 8 * 1024 * 1024
VMEM = pl.BlockSpec(memory_space=pltpu.VMEM)
HBM = pl.BlockSpec(memory_space=pltpu.HBM)


def split_two(value):
    high = value.astype(jnp.bfloat16).astype(jnp.float32)
    low = (value - high).astype(jnp.bfloat16).astype(jnp.float32)
    return high, low


def attend_kernel(heads_dev, devices, *refs):
    table_hbm, lengths_hbm, key_scale_hbm, value_scale_hbm, queries_hbm, keys, values = refs[:7]
    staged, table, lengths, key_scale, value_scale, queries, key_buf, value_buf, query_rows = refs[7:16]
    table_rows, factors, bias, weights, small_sems, sems = refs[16:]
    rows, pages = table.shape
    kv_heads = key_scale.shape[0]
    heads = queries.shape[1] // HD
    group = heads // kv_heads
    context = pages * PAGE
    pieces = sems.shape[1]
    piece = keys.shape[0] // pieces

    small = []
    for i, (source, target) in enumerate(
        (
            (table_hbm, table),
            (table_hbm, table_rows),
            (lengths_hbm, lengths),
            (key_scale_hbm, key_scale),
            (value_scale_hbm, value_scale),
            (queries_hbm, queries),
        )
    ):
        small.append(pltpu.make_async_copy(source, target, small_sems.at[i]))
        small[-1].start()
    large = []
    for which, source, target in ((0, keys, key_buf), (1, values, value_buf)):
        large.append([])
        for i in range(pieces):
            here = pl.ds(i * piece, piece)
            large[-1].append(pltpu.make_async_copy(source.at[here], target.at[here], sems.at[which, i]))
    for copy in large[0]:
        copy.start()

    me = lax.axis_index("kvp")
    lane = lax.broadcasted_iota(jnp.int32, (group, HD), 1)
    place = me * context + lax.broadcasted_iota(jnp.int32, (1, context), 1)
    page_of = lax.div(lax.broadcasted_iota(jnp.int32, (pages, context), 1), PAGE)
    spread = (page_of == lax.broadcasted_iota(jnp.int32, (pages, context), 0)).astype(jnp.float32).astype(jnp.bfloat16)
    slot = lax.broadcasted_iota(jnp.int32, (keys.shape[0], context), 0).astype(jnp.float32)
    zeros = jnp.zeros((group, HD), jnp.bfloat16)
    small[0].wait()
    for copy in large[1]:
        copy.start()
    for copy in small[1:]:
        copy.wait()

    scales = jnp.concatenate([key_scale[...] * (math.log2(math.e) / math.sqrt(HD)), value_scale[...]], axis=0)
    high, low = split_two(scales)
    parts = jnp.concatenate([high, low, scales - high - low], axis=0).astype(jnp.bfloat16)
    slots = jnp.dot(
        table_rows[...].astype(jnp.float32).astype(jnp.bfloat16), spread, preferred_element_type=jnp.float32
    )
    for r in range(rows):
        chosen = (slots[r : r + 1] == slot).astype(jnp.float32).astype(jnp.bfloat16)
        found = jnp.dot(parts, chosen, preferred_element_type=jnp.float32)
        count = 2 * kv_heads
        factors[r] = found[:count] + found[count : 2 * count] + found[2 * count :]
        bias[r : r + 1] = jnp.where(place < lengths[r], 0.0, HIDDEN)
    for h in range(heads):
        query_rows[h * rows : (h + 1) * rows, :] = queries[:, h * HD : (h + 1) * HD].astype(jnp.float32)

    def pages_of(buf, r, k):
        return jnp.concatenate(
            [buf[table[r, p], :, k * HD : (k + 2) * HD] for p in range(pages)], axis=0
        )

    for copy in large[0]:
        copy.wait()
    stats = [jnp.zeros((group, HD), jnp.float32)] * kv_heads
    for r in range(rows):
        query = query_rows[pl.ds(r, heads, stride=rows), :].astype(jnp.bfloat16)
        for k in range(0, kv_heads, 2):
            left = jnp.concatenate(
                [
                    jnp.concatenate([query[k * group : (k + 1) * group], zeros], axis=1),
                    jnp.concatenate([zeros, query[(k + 1) * group : (k + 2) * group]], axis=1),
                ],
                axis=0,
            )
            both = lax.dot_general(
                left, pages_of(key_buf, r, k), (((1,), (1,)), ((), ())), preferred_element_type=jnp.float32
            )
            for i in (0, 1):
                at_key, at_value = k + i, kv_heads + k + i
                scores = both[i * group : (i + 1) * group] * factors[r, at_key : at_key + 1] + bias[r : r + 1]
                highest = jnp.maximum(jnp.max(scores, axis=1, keepdims=True), LOWEST)
                high, low = split_two(highest)
                prob = jnp.exp2(scores - (high + low))
                total_high, total_low = split_two(jnp.sum(prob, axis=1, keepdims=True))
                for at, value in enumerate((high, low, total_high, total_low)):
                    stats[k + i] = jnp.where(lane == 4 * r + at, value, stats[k + i])
                weights[r, (k + i) * group : (k + i + 1) * group] = (
                    prob * factors[r, at_value : at_value + 1]
                ).astype(jnp.bfloat16)
    for copy in large[1]:
        copy.wait()
    for r in range(rows):
        for k in range(0, kv_heads, 2):
            both = jnp.dot(
                weights[r, k * group : (k + 2) * group], pages_of(value_buf, r, k), preferred_element_type=jnp.float32
            )
            for i in (0, 1):
                partial = both[i * group : (i + 1) * group, i * HD : (i + 1) * HD]
                for start in range(0, group, heads_dev):
                    d = ((k + i) * group + start) // heads_dev
                    staged[d, r] = partial[start : start + heads_dev]
    for k in range(kv_heads):
        for start in range(0, group, heads_dev):
            d = (k * group + start) // heads_dev
            staged[d, rows] = stats[k][start : start + heads_dev]


def pack_kernel(staged, packed):
    packed[...] = staged[...].astype(jnp.bfloat16)


def combine_kernel(heads_dev, packed, left, attended):
    rows = left.shape[0]
    stats = packed[:, rows].astype(jnp.float32)
    lanes = stats.shape[-1]

    def lanes_ahead(value, by):
        return pltpu.roll(value, lanes - by, axis=2)

    maxima = stats + lanes_ahead(stats, 1)
    rescale = jnp.exp2(maxima - jnp.max(maxima, axis=0, keepdims=True))
    totals = lanes_ahead(stats, 2) + lanes_ahead(stats, 3)
    denominator = jnp.sum(totals * rescale, axis=0)
    for r in range(rows):
        partial = packed[:, r].astype(jnp.float32)
        numerator = jnp.sum(partial * rescale[:, :, 4 * r : 4 * r + 1], axis=0)
        attended[r * heads_dev : (r + 1) * heads_dev, :] = numerator / denominator[:, 4 * r : 4 * r + 1]
    rounded = jnp.concatenate(
        [attended[pl.ds(j, rows, stride=heads_dev), :].astype(jnp.bfloat16) for j in range(heads_dev)], axis=1
    )
    left[...] = rounded


def project_kernel(partner, left, weight, out):
    part = out.shape[1]
    quarter = lax.rem(lax.axis_index("kvp"), weight.shape[1] // part)
    start = pl.multiple_of(jnp.bitwise_xor(quarter, partner) * part, part)
    terms = jnp.dot(left[...], weight[:, pl.ds(start, part)], preferred_element_type=jnp.float32)
    out[...] = terms.astype(out.dtype)


def add_kernel(*refs):
    terms = [ref[...].astype(jnp.float32) for ref in refs[:-1]]
    while len(terms) > 1:
        terms = [terms[i] + terms[i + 1] for i in range(0, len(terms), 2)]
    refs[-1][...] = terms[0].astype(refs[-1].dtype)


def lay_kernel(*refs):
    parts, out = refs[:-1], refs[-1]
    quarter = lax.rem(lax.axis_index("kvp"), len(parts))
    width = parts[0].shape[1]
    for x, part in enumerate(parts):
        start = pl.multiple_of(jnp.bitwise_xor(quarter, x) * width, width)
        out[:, pl.ds(start, width)] = part[...]


def exchange(array, partner, devices):
    return lax.ppermute(array, "kvp", [(i, i ^ partner) for i in range(devices)])


def in_hbm(array):
    return pltpu.with_memory_space_constraint(array, pltpu.HBM)


def body(queries, key_cache, value_cache, key_scale, value_scale, page_table, lengths, out_weight, *, devices):
    rows, pages = page_table.shape
    slots, _, columns = key_cache.shape
    kv_heads = key_scale.shape[1]
    heads_dev = out_weight.shape[0] // HD
    heads = queries.shape[1] // HD
    features = out_weight.shape[1]
    inner = 4
    outer = devices // inner
    part = features // inner
    staged = pl.pallas_call(
        functools.partial(attend_kernel, heads_dev, devices),
        out_shape=pltpu.VMEM((devices, rows + 1, heads_dev, HD), jnp.float32),
        in_specs=[HBM] * 7,
        out_specs=VMEM,
        scratch_shapes=[
            pltpu.SMEM((rows, pages), jnp.int32),
            pltpu.SMEM((rows,), jnp.int32),
            pltpu.VMEM((kv_heads, slots), jnp.float32),
            pltpu.VMEM((kv_heads, slots), jnp.float32),
            pltpu.VMEM((rows, heads * HD), jnp.bfloat16),
            pltpu.VMEM((slots, PAGE, columns), jnp.bfloat16),
            pltpu.VMEM((slots, PAGE, columns), jnp.bfloat16),
            pltpu.VMEM((heads * rows, HD), jnp.float32),
            pltpu.VMEM((rows, pages), jnp.int32),
            pltpu.VMEM((rows, 2 * kv_heads, pages * PAGE), jnp.float32),
            pltpu.VMEM((rows, pages * PAGE), jnp.float32),
            pltpu.VMEM((rows, heads, pages * PAGE), jnp.bfloat16),
            pltpu.SemaphoreType.DMA((6,)),
            pltpu.SemaphoreType.DMA((2, 2)),
        ],
        compiler_params=pltpu.CompilerParams(vmem_limit_bytes=ATTEND_VMEM),
        cost_estimate=pl.CostEstimate(
            flops=4 * heads * rows * pages * PAGE * HD,
            bytes_accessed=4 * rows * pages * PAGE * columns,
            transcendentals=heads * rows * pages * PAGE,
        ),
        name="attend",
    )(*[in_hbm(a) for a in (page_table, lengths, key_scale.T, value_scale.T, queries, key_cache, value_cache)])

    packed = pl.pallas_call(
        pack_kernel,
        out_shape=jax.ShapeDtypeStruct(staged.shape, jnp.bfloat16),
        in_specs=[VMEM],
        out_specs=VMEM,
        compiler_params=pltpu.CompilerParams(vmem_limit_bytes=SMALL_VMEM),
        cost_estimate=pl.CostEstimate(flops=EXCHANGE_FLOPS, bytes_accessed=6 * staged.size, transcendentals=0),
        name="pack",
    )(staged)

    received = lax.all_to_all(packed, "kvp", split_axis=0, concat_axis=0, tiled=True)

    resident = pltpu.with_memory_space_constraint(out_weight, pltpu.VMEM)
    depth = heads_dev * HD
    cost = pl.CostEstimate(flops=1024, bytes_accessed=1024, transcendentals=0)
    small = pltpu.CompilerParams(vmem_limit_bytes=SMALL_VMEM)
    left = pl.pallas_call(
        functools.partial(combine_kernel, heads_dev),
        out_shape=jax.ShapeDtypeStruct((rows, depth), jnp.bfloat16),
        in_specs=[VMEM],
        out_specs=VMEM,
        scratch_shapes=[pltpu.VMEM((rows * heads_dev, HD), jnp.float32)],
        compiler_params=small,
        name="combine",
    )(received)
    arrived = []
    for x in reversed(range(inner)):
        terms = pl.pallas_call(
            functools.partial(project_kernel, x),
            out_shape=jax.ShapeDtypeStruct((rows, part), jnp.bfloat16 if x else jnp.float32),
            in_specs=[VMEM] * 2,
            out_specs=VMEM,
            compiler_params=small,
            cost_estimate=cost,
            name=f"project_{x}",
        )(left, resident)
        arrived.append(exchange(terms, x, devices) if x else terms)

    def add(terms, name):
        return pl.pallas_call(
            add_kernel,
            out_shape=jax.ShapeDtypeStruct((rows, part), jnp.bfloat16),
            in_specs=[VMEM] * len(terms),
            out_specs=VMEM,
            compiler_params=pltpu.CompilerParams(vmem_limit_bytes=SMALL_VMEM),
            name=name,
        )(*terms)

    mine = add(arrived, "add_near")
    mine = add([mine] + [exchange(mine, x * inner, devices) for x in range(1, outer)], "add_far")
    parts = [mine] + [exchange(mine, x, devices) for x in range(1, inner)]
    return pl.pallas_call(
        lay_kernel,
        out_shape=jax.ShapeDtypeStruct((rows, features), jnp.bfloat16),
        in_specs=[VMEM] * inner,
        out_specs=VMEM,
        compiler_params=pltpu.CompilerParams(vmem_limit_bytes=SMALL_VMEM),
        name="lay",
    )(*parts)


def solution(mesh):
    placed = (
        P("group", None),
        P(("group", "kvp"), None, None),
        P(("group", "kvp"), None, None),
        P(("group", "kvp"), None),
        P(("group", "kvp"), None),
        P("group", "kvp"),
        P("group"),
        P("kvp", None),
    )
    return jax.shard_map(
        functools.partial(body, devices=mesh.shape["kvp"]),
        mesh=mesh,
        in_specs=placed,
        out_specs=P("group", None),
        check_vma=False,
    )
```

```python
import functools
import math

import jax
import jax.numpy as jnp
from jax import lax
from jax.experimental import pallas as pl
from jax.experimental.pallas import tpu as pltpu
from jax.sharding import PartitionSpec as P

HD = 128
PAGE = 64
ATTEND_VMEM = 60 * 1024 * 1024
HIDDEN = -1e30
LOWEST = -1e20
ORDER_FLOPS = 5_000_000_000
EXCHANGE_FLOPS = 40_000_000_000
SMALL_VMEM = 8 * 1024 * 1024
VMEM = pl.BlockSpec(memory_space=pltpu.VMEM)
HBM = pl.BlockSpec(memory_space=pltpu.HBM)


def split_two(value):
    high = value.astype(jnp.bfloat16).astype(jnp.float32)
    low = (value - high).astype(jnp.bfloat16).astype(jnp.float32)
    return high, low


def attend_kernel(heads_dev, devices, *refs):
    table_hbm, lengths_hbm, key_scale_hbm, value_scale_hbm, queries_hbm, keys, values = refs[:7]
    staged, table, lengths, key_scale, value_scale, queries, key_buf, value_buf, query_rows = refs[7:16]
    table_rows, factors, bias, weights, small_sems, sems = refs[16:]
    rows, pages = table.shape
    kv_heads = key_scale.shape[0]
    heads = queries.shape[1] // HD
    group = heads // kv_heads
    context = pages * PAGE
    pieces = sems.shape[1]
    piece = keys.shape[0] // pieces

    small = []
    for i, (source, target) in enumerate(
        (
            (table_hbm, table),
            (table_hbm, table_rows),
            (lengths_hbm, lengths),
            (key_scale_hbm, key_scale),
            (value_scale_hbm, value_scale),
            (queries_hbm, queries),
        )
    ):
        small.append(pltpu.make_async_copy(source, target, small_sems.at[i]))
        small[-1].start()
    large = []
    for which, source, target in ((0, keys, key_buf), (1, values, value_buf)):
        large.append([])
        for i in range(pieces):
            here = pl.ds(i * piece, piece)
            large[-1].append(pltpu.make_async_copy(source.at[here], target.at[here], sems.at[which, i]))
    for copy in large[0]:
        copy.start()

    me = lax.axis_index("kvp")
    lane = lax.broadcasted_iota(jnp.int32, (group, HD), 1)
    place = me * context + lax.broadcasted_iota(jnp.int32, (1, context), 1)
    page_of = lax.div(lax.broadcasted_iota(jnp.int32, (pages, context), 1), PAGE)
    spread = (page_of == lax.broadcasted_iota(jnp.int32, (pages, context), 0)).astype(jnp.float32).astype(jnp.bfloat16)
    slot = lax.broadcasted_iota(jnp.int32, (keys.shape[0], context), 0).astype(jnp.float32)
    zeros = jnp.zeros((group, HD), jnp.bfloat16)
    small[0].wait()
    for copy in large[1]:
        copy.start()
    for copy in small[1:]:
        copy.wait()

    scales = jnp.concatenate([key_scale[...] * (math.log2(math.e) / math.sqrt(HD)), value_scale[...]], axis=0)
    high, low = split_two(scales)
    parts = jnp.concatenate([high, low, scales - high - low], axis=0).astype(jnp.bfloat16)
    slots = jnp.dot(
        table_rows[...].astype(jnp.float32).astype(jnp.bfloat16), spread, preferred_element_type=jnp.float32
    )
    for r in range(rows):
        chosen = (slots[r : r + 1] == slot).astype(jnp.float32).astype(jnp.bfloat16)
        found = jnp.dot(parts, chosen, preferred_element_type=jnp.float32)
        count = 2 * kv_heads
        factors[r] = found[:count] + found[count : 2 * count] + found[2 * count :]
        bias[r : r + 1] = jnp.where(place < lengths[r], 0.0, HIDDEN)
    for h in range(heads):
        query_rows[h * rows : (h + 1) * rows, :] = queries[:, h * HD : (h + 1) * HD].astype(jnp.float32)

    def pages_of(buf, r, k):
        return jnp.concatenate(
            [buf[table[r, p], :, k * HD : (k + 2) * HD] for p in range(pages)], axis=0
        )

    for copy in large[0]:
        copy.wait()
    stats = [jnp.zeros((group, HD), jnp.float32)] * kv_heads
    for r in range(rows):
        query = query_rows[pl.ds(r, heads, stride=rows), :].astype(jnp.bfloat16)
        for k in range(0, kv_heads, 2):
            left = jnp.concatenate(
                [
                    jnp.concatenate([query[k * group : (k + 1) * group], zeros], axis=1),
                    jnp.concatenate([zeros, query[(k + 1) * group : (k + 2) * group]], axis=1),
                ],
                axis=0,
            )
            both = lax.dot_general(
                left, pages_of(key_buf, r, k), (((1,), (1,)), ((), ())), preferred_element_type=jnp.float32
            )
            for i in (0, 1):
                at_key, at_value = k + i, kv_heads + k + i
                scores = both[i * group : (i + 1) * group] * factors[r, at_key : at_key + 1] + bias[r : r + 1]
                highest = jnp.maximum(jnp.max(scores, axis=1, keepdims=True), LOWEST)
                high, low = split_two(highest)
                prob = jnp.exp2(scores - (high + low))
                total_high, total_low = split_two(jnp.sum(prob, axis=1, keepdims=True))
                for at, value in enumerate((high, low, total_high, total_low)):
                    stats[k + i] = jnp.where(lane == 4 * r + at, value, stats[k + i])
                weights[r, (k + i) * group : (k + i + 1) * group] = (
                    prob * factors[r, at_value : at_value + 1]
                ).astype(jnp.bfloat16)
    for copy in large[1]:
        copy.wait()
    for r in range(rows):
        for k in range(0, kv_heads, 2):
            both = jnp.dot(
                weights[r, k * group : (k + 2) * group], pages_of(value_buf, r, k), preferred_element_type=jnp.float32
            )
            for i in (0, 1):
                partial = both[i * group : (i + 1) * group, i * HD : (i + 1) * HD]
                for start in range(0, group, heads_dev):
                    d = ((k + i) * group + start) // heads_dev
                    staged[d, r] = partial[start : start + heads_dev]
    for k in range(kv_heads):
        for start in range(0, group, heads_dev):
            d = (k * group + start) // heads_dev
            staged[d, rows] = stats[k][start : start + heads_dev]


def pack_kernel(staged, packed):
    packed[...] = staged[...].astype(jnp.bfloat16)


def combine_kernel(heads_dev, packed, left, attended):
    rows = left.shape[0]
    stats = packed[:, rows].astype(jnp.float32)
    lanes = stats.shape[-1]

    def lanes_ahead(value, by):
        return pltpu.roll(value, lanes - by, axis=2)

    maxima = stats + lanes_ahead(stats, 1)
    rescale = jnp.exp2(maxima - jnp.max(maxima, axis=0, keepdims=True))
    totals = lanes_ahead(stats, 2) + lanes_ahead(stats, 3)
    denominator = jnp.sum(totals * rescale, axis=0)
    for r in range(rows):
        partial = packed[:, r].astype(jnp.float32)
        numerator = jnp.sum(partial * rescale[:, :, 4 * r : 4 * r + 1], axis=0)
        attended[r * heads_dev : (r + 1) * heads_dev, :] = numerator / denominator[:, 4 * r : 4 * r + 1]
    rounded = jnp.concatenate(
        [attended[pl.ds(j, rows, stride=heads_dev), :].astype(jnp.bfloat16) for j in range(heads_dev)], axis=1
    )
    left[...] = rounded


def project_kernel(partner, left, weight, out):
    part = out.shape[1]
    quarter = lax.rem(lax.axis_index("kvp"), weight.shape[1] // part)
    start = pl.multiple_of(jnp.bitwise_xor(quarter, partner) * part, part)
    terms = jnp.dot(left[...], weight[:, pl.ds(start, part)], preferred_element_type=jnp.float32)
    out[...] = terms.astype(out.dtype)


def add_kernel(*refs):
    terms = [ref[...].astype(jnp.float32) for ref in refs[:-1]]
    while len(terms) > 1:
        terms = [terms[i] + terms[i + 1] for i in range(0, len(terms), 2)]
    refs[-1][...] = terms[0].astype(refs[-1].dtype)


def lay_kernel(*refs):
    parts, out = refs[:-1], refs[-1]
    quarter = lax.rem(lax.axis_index("kvp"), len(parts))
    width = parts[0].shape[1]
    for x, part in enumerate(parts):
        start = pl.multiple_of(jnp.bitwise_xor(quarter, x) * width, width)
        out[:, pl.ds(start, width)] = part[...]


def exchange(array, partner, devices):
    return lax.ppermute(array, "kvp", [(i, i ^ partner) for i in range(devices)])


def in_hbm(array):
    return pltpu.with_memory_space_constraint(array, pltpu.HBM)


def body(queries, key_cache, value_cache, key_scale, value_scale, page_table, lengths, out_weight, *, devices):
    rows, pages = page_table.shape
    slots, _, columns = key_cache.shape
    kv_heads = key_scale.shape[1]
    heads_dev = out_weight.shape[0] // HD
    heads = queries.shape[1] // HD
    features = out_weight.shape[1]
    inner = 4
    outer = devices // inner
    part = features // inner
    staged = pl.pallas_call(
        functools.partial(attend_kernel, heads_dev, devices),
        out_shape=pltpu.VMEM((devices, rows + 1, heads_dev, HD), jnp.float32),
        in_specs=[HBM] * 7,
        out_specs=VMEM,
        scratch_shapes=[
            pltpu.SMEM((rows, pages), jnp.int32),
            pltpu.SMEM((rows,), jnp.int32),
            pltpu.VMEM((kv_heads, slots), jnp.float32),
            pltpu.VMEM((kv_heads, slots), jnp.float32),
            pltpu.VMEM((rows, heads * HD), jnp.bfloat16),
            pltpu.VMEM((slots, PAGE, columns), jnp.bfloat16),
            pltpu.VMEM((slots, PAGE, columns), jnp.bfloat16),
            pltpu.VMEM((heads * rows, HD), jnp.float32),
            pltpu.VMEM((rows, pages), jnp.int32),
            pltpu.VMEM((rows, 2 * kv_heads, pages * PAGE), jnp.float32),
            pltpu.VMEM((rows, pages * PAGE), jnp.float32),
            pltpu.VMEM((rows, heads, pages * PAGE), jnp.bfloat16),
            pltpu.SemaphoreType.DMA((6,)),
            pltpu.SemaphoreType.DMA((2, 1)),
        ],
        compiler_params=pltpu.CompilerParams(vmem_limit_bytes=ATTEND_VMEM),
        cost_estimate=pl.CostEstimate(
            flops=4 * heads * rows * pages * PAGE * HD,
            bytes_accessed=4 * rows * pages * PAGE * columns,
            transcendentals=heads * rows * pages * PAGE,
        ),
        name="attend",
    )(*[in_hbm(a) for a in (page_table, lengths, key_scale.T, value_scale.T, queries, key_cache, value_cache)])

    packed = pl.pallas_call(
        pack_kernel,
        out_shape=jax.ShapeDtypeStruct(staged.shape, jnp.bfloat16),
        in_specs=[VMEM],
        out_specs=VMEM,
        compiler_params=pltpu.CompilerParams(vmem_limit_bytes=SMALL_VMEM),
        cost_estimate=pl.CostEstimate(flops=EXCHANGE_FLOPS, bytes_accessed=6 * staged.size, transcendentals=0),
        name="pack",
    )(staged)

    received = lax.all_to_all(packed, "kvp", split_axis=0, concat_axis=0, tiled=True)

    resident = pltpu.with_memory_space_constraint(out_weight, pltpu.VMEM)
    depth = heads_dev * HD
    cost = pl.CostEstimate(flops=1024, bytes_accessed=1024, transcendentals=0)
    small = pltpu.CompilerParams(vmem_limit_bytes=SMALL_VMEM)
    left = pl.pallas_call(
        functools.partial(combine_kernel, heads_dev),
        out_shape=jax.ShapeDtypeStruct((rows, depth), jnp.bfloat16),
        in_specs=[VMEM],
        out_specs=VMEM,
        scratch_shapes=[pltpu.VMEM((rows * heads_dev, HD), jnp.float32)],
        compiler_params=small,
        name="combine",
    )(received)
    arrived = []
    for x in (2, 3, 1, 0):
        terms = pl.pallas_call(
            functools.partial(project_kernel, x),
            out_shape=jax.ShapeDtypeStruct((rows, part), jnp.bfloat16 if x else jnp.float32),
            in_specs=[VMEM] * 2,
            out_specs=VMEM,
            compiler_params=small,
            cost_estimate=cost,
            name=f"project_{x}",
        )(left, resident)
        arrived.append(exchange(terms, x, devices) if x else terms)

    def add(terms, name, kind=jnp.bfloat16, flops=1024):
        return pl.pallas_call(
            add_kernel,
            out_shape=jax.ShapeDtypeStruct((rows, part), kind),
            in_specs=[VMEM] * len(terms),
            out_specs=VMEM,
            compiler_params=pltpu.CompilerParams(vmem_limit_bytes=SMALL_VMEM),
            cost_estimate=pl.CostEstimate(flops=flops, bytes_accessed=1024, transcendentals=0),
            name=name,
        )(*terms)

    mine = add([arrived[3], arrived[0]], "add_across", jnp.float32, ORDER_FLOPS)
    mine = add([mine, arrived[1]], "add_other", jnp.float32, ORDER_FLOPS)
    mine = add([mine, arrived[2]], "add_near")
    mine = add([mine] + [exchange(mine, x * inner, devices) for x in range(1, outer)], "add_far")
    parts = [mine] + [exchange(mine, x, devices) for x in range(1, inner)]
    return pl.pallas_call(
        lay_kernel,
        out_shape=jax.ShapeDtypeStruct((rows, features), jnp.bfloat16),
        in_specs=[VMEM] * inner,
        out_specs=VMEM,
        compiler_params=pltpu.CompilerParams(vmem_limit_bytes=SMALL_VMEM),
        name="lay",
    )(*parts)


def solution(mesh):
    placed = (
        P("group", None),
        P(("group", "kvp"), None, None),
        P(("group", "kvp"), None, None),
        P(("group", "kvp"), None),
        P(("group", "kvp"), None),
        P("group", "kvp"),
        P("group"),
        P("kvp", None),
    )
    return jax.shard_map(
        functools.partial(body, devices=mesh.shape["kvp"]),
        mesh=mesh,
        in_specs=placed,
        out_specs=P("group", None),
        check_vma=False,
    )
```

```python
import functools
import math

import jax
import jax.numpy as jnp
from jax import lax
from jax.experimental import pallas as pl
from jax.experimental.pallas import tpu as pltpu
from jax.sharding import PartitionSpec as P

HD = 128
PAGE = 64
ATTEND_VMEM = 60 * 1024 * 1024
HIDDEN = -1e30
LOWEST = -1e20
ORDER_FLOPS = 200_000_000
EXCHANGE_FLOPS = 40_000_000_000
SMALL_VMEM = 8 * 1024 * 1024
VMEM = pl.BlockSpec(memory_space=pltpu.VMEM)
HBM = pl.BlockSpec(memory_space=pltpu.HBM)


def split_two(value):
    high = value.astype(jnp.bfloat16).astype(jnp.float32)
    low = (value - high).astype(jnp.bfloat16).astype(jnp.float32)
    return high, low


def attend_kernel(heads_dev, devices, *refs):
    table_hbm, lengths_hbm, key_scale_hbm, value_scale_hbm, queries_hbm, keys, values = refs[:7]
    staged, table, lengths, key_scale, value_scale, queries, key_buf, value_buf, query_rows = refs[7:16]
    table_rows, factors, bias, weights, small_sems, sems = refs[16:]
    rows, pages = table.shape
    kv_heads = key_scale.shape[0]
    heads = queries.shape[1] // HD
    group = heads // kv_heads
    context = pages * PAGE
    pieces = sems.shape[1]
    piece = keys.shape[0] // pieces

    small = []
    for i, (source, target) in enumerate(
        (
            (table_hbm, table),
            (table_hbm, table_rows),
            (lengths_hbm, lengths),
            (key_scale_hbm, key_scale),
            (value_scale_hbm, value_scale),
            (queries_hbm, queries),
        )
    ):
        small.append(pltpu.make_async_copy(source, target, small_sems.at[i]))
        small[-1].start()
    large = []
    for which, source, target in ((0, keys, key_buf), (1, values, value_buf)):
        large.append([])
        for i in range(pieces):
            here = pl.ds(i * piece, piece)
            large[-1].append(pltpu.make_async_copy(source.at[here], target.at[here], sems.at[which, i]))
    for copy in large[0]:
        copy.start()

    me = lax.axis_index("kvp")
    lane = lax.broadcasted_iota(jnp.int32, (group, HD), 1)
    place = me * context + lax.broadcasted_iota(jnp.int32, (1, context), 1)
    page_of = lax.div(lax.broadcasted_iota(jnp.int32, (pages, context), 1), PAGE)
    spread = (page_of == lax.broadcasted_iota(jnp.int32, (pages, context), 0)).astype(jnp.float32).astype(jnp.bfloat16)
    slot = lax.broadcasted_iota(jnp.int32, (keys.shape[0], context), 0).astype(jnp.float32)
    zeros = jnp.zeros((group, HD), jnp.bfloat16)
    small[0].wait()
    for copy in large[1]:
        copy.start()
    for copy in small[1:]:
        copy.wait()

    scales = jnp.concatenate([key_scale[...] * (math.log2(math.e) / math.sqrt(HD)), value_scale[...]], axis=0)
    high, low = split_two(scales)
    parts = jnp.concatenate([high, low, scales - high - low], axis=0).astype(jnp.bfloat16)
    slots = jnp.dot(
        table_rows[...].astype(jnp.float32).astype(jnp.bfloat16), spread, preferred_element_type=jnp.float32
    )
    for r in range(rows):
        chosen = (slots[r : r + 1] == slot).astype(jnp.float32).astype(jnp.bfloat16)
        found = jnp.dot(parts, chosen, preferred_element_type=jnp.float32)
        count = 2 * kv_heads
        factors[r] = found[:count] + found[count : 2 * count] + found[2 * count :]
        bias[r : r + 1] = jnp.where(place < lengths[r], 0.0, HIDDEN)
    for h in range(heads):
        query_rows[h * rows : (h + 1) * rows, :] = queries[:, h * HD : (h + 1) * HD].astype(jnp.float32)

    def pages_of(buf, r, k):
        return jnp.concatenate(
            [buf[table[r, p], :, k * HD : (k + 2) * HD] for p in range(pages)], axis=0
        )

    for copy in large[0]:
        copy.wait()
    stats = [jnp.zeros((group, HD), jnp.float32)] * kv_heads
    for r in range(rows):
        query = query_rows[pl.ds(r, heads, stride=rows), :].astype(jnp.bfloat16)
        for k in range(0, kv_heads, 2):
            left = jnp.concatenate(
                [
                    jnp.concatenate([query[k * group : (k + 1) * group], zeros], axis=1),
                    jnp.concatenate([zeros, query[(k + 1) * group : (k + 2) * group]], axis=1),
                ],
                axis=0,
            )
            both = lax.dot_general(
                left, pages_of(key_buf, r, k), (((1,), (1,)), ((), ())), preferred_element_type=jnp.float32
            )
            for i in (0, 1):
                at_key, at_value = k + i, kv_heads + k + i
                scores = both[i * group : (i + 1) * group] * factors[r, at_key : at_key + 1] + bias[r : r + 1]
                highest = jnp.maximum(jnp.max(scores, axis=1, keepdims=True), LOWEST)
                high, low = split_two(highest)
                prob = jnp.exp2(scores - (high + low))
                total_high, total_low = split_two(jnp.sum(prob, axis=1, keepdims=True))
                for at, value in enumerate((high, low, total_high, total_low)):
                    stats[k + i] = jnp.where(lane == 4 * r + at, value, stats[k + i])
                weights[r, (k + i) * group : (k + i + 1) * group] = (
                    prob * factors[r, at_value : at_value + 1]
                ).astype(jnp.bfloat16)
    for copy in large[1]:
        copy.wait()
    for r in range(rows):
        for k in range(0, kv_heads, 2):
            both = jnp.dot(
                weights[r, k * group : (k + 2) * group], pages_of(value_buf, r, k), preferred_element_type=jnp.float32
            )
            for i in (0, 1):
                partial = both[i * group : (i + 1) * group, i * HD : (i + 1) * HD]
                for start in range(0, group, heads_dev):
                    d = ((k + i) * group + start) // heads_dev
                    staged[d, r] = partial[start : start + heads_dev]
    for k in range(kv_heads):
        for start in range(0, group, heads_dev):
            d = (k * group + start) // heads_dev
            staged[d, rows] = stats[k][start : start + heads_dev]


def pack_kernel(staged, packed):
    packed[...] = staged[...].astype(jnp.bfloat16)


def combine_kernel(heads_dev, packed, left, attended):
    rows = left.shape[0]
    stats = packed[:, rows].astype(jnp.float32)
    lanes = stats.shape[-1]

    def lanes_ahead(value, by):
        return pltpu.roll(value, lanes - by, axis=2)

    maxima = stats + lanes_ahead(stats, 1)
    rescale = jnp.exp2(maxima - jnp.max(maxima, axis=0, keepdims=True))
    totals = lanes_ahead(stats, 2) + lanes_ahead(stats, 3)
    denominator = jnp.sum(totals * rescale, axis=0)
    for r in range(rows):
        partial = packed[:, r].astype(jnp.float32)
        numerator = jnp.sum(partial * rescale[:, :, 4 * r : 4 * r + 1], axis=0)
        attended[r * heads_dev : (r + 1) * heads_dev, :] = numerator / denominator[:, 4 * r : 4 * r + 1]
    rounded = jnp.concatenate(
        [attended[pl.ds(j, rows, stride=heads_dev), :].astype(jnp.bfloat16) for j in range(heads_dev)], axis=1
    )
    left[...] = rounded


def project_kernel(partner, left, weight, out):
    part = out.shape[1]
    quarter = lax.rem(lax.axis_index("kvp"), weight.shape[1] // part)
    start = pl.multiple_of(jnp.bitwise_xor(quarter, partner) * part, part)
    terms = jnp.dot(left[...], weight[:, pl.ds(start, part)], preferred_element_type=jnp.float32)
    out[...] = terms.astype(out.dtype)


def add_kernel(*refs):
    terms = [ref[...].astype(jnp.float32) for ref in refs[:-1]]
    while len(terms) > 1:
        terms = [terms[i] + terms[i + 1] for i in range(0, len(terms), 2)]
    refs[-1][...] = terms[0].astype(refs[-1].dtype)


def lay_kernel(*refs):
    parts, out = refs[:-1], refs[-1]
    quarter = lax.rem(lax.axis_index("kvp"), len(parts))
    width = parts[0].shape[1]
    for x, part in enumerate(parts):
        start = pl.multiple_of(jnp.bitwise_xor(quarter, x) * width, width)
        out[:, pl.ds(start, width)] = part[...]


def exchange(array, partner, devices):
    return lax.ppermute(array, "kvp", [(i, i ^ partner) for i in range(devices)])


def in_hbm(array):
    return pltpu.with_memory_space_constraint(array, pltpu.HBM)


def body(queries, key_cache, value_cache, key_scale, value_scale, page_table, lengths, out_weight, *, devices):
    rows, pages = page_table.shape
    slots, _, columns = key_cache.shape
    kv_heads = key_scale.shape[1]
    heads_dev = out_weight.shape[0] // HD
    heads = queries.shape[1] // HD
    features = out_weight.shape[1]
    inner = 4
    outer = devices // inner
    part = features // inner
    staged = pl.pallas_call(
        functools.partial(attend_kernel, heads_dev, devices),
        out_shape=pltpu.VMEM((devices, rows + 1, heads_dev, HD), jnp.float32),
        in_specs=[HBM] * 7,
        out_specs=VMEM,
        scratch_shapes=[
            pltpu.SMEM((rows, pages), jnp.int32),
            pltpu.SMEM((rows,), jnp.int32),
            pltpu.VMEM((kv_heads, slots), jnp.float32),
            pltpu.VMEM((kv_heads, slots), jnp.float32),
            pltpu.VMEM((rows, heads * HD), jnp.bfloat16),
            pltpu.VMEM((slots, PAGE, columns), jnp.bfloat16),
            pltpu.VMEM((slots, PAGE, columns), jnp.bfloat16),
            pltpu.VMEM((heads * rows, HD), jnp.float32),
            pltpu.VMEM((rows, pages), jnp.int32),
            pltpu.VMEM((rows, 2 * kv_heads, pages * PAGE), jnp.float32),
            pltpu.VMEM((rows, pages * PAGE), jnp.float32),
            pltpu.VMEM((rows, heads, pages * PAGE), jnp.bfloat16),
            pltpu.SemaphoreType.DMA((6,)),
            pltpu.SemaphoreType.DMA((2, 1)),
        ],
        compiler_params=pltpu.CompilerParams(vmem_limit_bytes=ATTEND_VMEM),
        cost_estimate=pl.CostEstimate(
            flops=4 * heads * rows * pages * PAGE * HD,
            bytes_accessed=4 * rows * pages * PAGE * columns,
            transcendentals=heads * rows * pages * PAGE,
        ),
        name="attend",
    )(*[in_hbm(a) for a in (page_table, lengths, key_scale.T, value_scale.T, queries, key_cache, value_cache)])

    packed = pl.pallas_call(
        pack_kernel,
        out_shape=jax.ShapeDtypeStruct(staged.shape, jnp.bfloat16),
        in_specs=[VMEM],
        out_specs=VMEM,
        compiler_params=pltpu.CompilerParams(vmem_limit_bytes=SMALL_VMEM),
        cost_estimate=pl.CostEstimate(flops=EXCHANGE_FLOPS, bytes_accessed=6 * staged.size, transcendentals=0),
        name="pack",
    )(staged)

    received = lax.all_to_all(packed, "kvp", split_axis=0, concat_axis=0, tiled=True)

    resident = pltpu.with_memory_space_constraint(out_weight, pltpu.VMEM)
    depth = heads_dev * HD
    cost = pl.CostEstimate(flops=1024, bytes_accessed=1024, transcendentals=0)
    small = pltpu.CompilerParams(vmem_limit_bytes=SMALL_VMEM)
    left = pl.pallas_call(
        functools.partial(combine_kernel, heads_dev),
        out_shape=jax.ShapeDtypeStruct((rows, depth), jnp.bfloat16),
        in_specs=[VMEM],
        out_specs=VMEM,
        scratch_shapes=[pltpu.VMEM((rows * heads_dev, HD), jnp.float32)],
        compiler_params=small,
        name="combine",
    )(received)
    arrived = []
    for x in (2, 3, 1, 0):
        terms = pl.pallas_call(
            functools.partial(project_kernel, x),
            out_shape=jax.ShapeDtypeStruct((rows, part), jnp.bfloat16 if x else jnp.float32),
            in_specs=[VMEM] * 2,
            out_specs=VMEM,
            compiler_params=small,
            cost_estimate=cost,
            name=f"project_{x}",
        )(left, resident)
        arrived.append(exchange(terms, x, devices) if x else terms)

    def add(terms, name, kind=jnp.bfloat16, flops=1024):
        return pl.pallas_call(
            add_kernel,
            out_shape=jax.ShapeDtypeStruct((rows, part), kind),
            in_specs=[VMEM] * len(terms),
            out_specs=VMEM,
            compiler_params=pltpu.CompilerParams(vmem_limit_bytes=SMALL_VMEM),
            cost_estimate=pl.CostEstimate(flops=flops, bytes_accessed=1024, transcendentals=0),
            name=name,
        )(*terms)

    mine = add([arrived[3], arrived[0]], "add_across", jnp.float32, ORDER_FLOPS)
    mine = add([mine, arrived[1]], "add_other", jnp.float32, ORDER_FLOPS)
    mine = add([mine, arrived[2]], "add_near")
    mine = add([mine] + [exchange(mine, x * inner, devices) for x in range(1, outer)], "add_far")
    parts = [mine] + [exchange(mine, x, devices) for x in range(1, inner)]
    return pl.pallas_call(
        lay_kernel,
        out_shape=jax.ShapeDtypeStruct((rows, features), jnp.bfloat16),
        in_specs=[VMEM] * inner,
        out_specs=VMEM,
        compiler_params=pltpu.CompilerParams(vmem_limit_bytes=SMALL_VMEM),
        name="lay",
    )(*parts)


def solution(mesh):
    placed = (
        P("group", None),
        P(("group", "kvp"), None, None),
        P(("group", "kvp"), None, None),
        P(("group", "kvp"), None),
        P(("group", "kvp"), None),
        P("group", "kvp"),
        P("group"),
        P("kvp", None),
    )
    return jax.shard_map(
        functools.partial(body, devices=mesh.shape["kvp"]),
        mesh=mesh,
        in_specs=placed,
        out_specs=P("group", None),
        check_vma=False,
    )
```

```python
import functools
import math

import jax
import jax.numpy as jnp
from jax import lax
from jax.experimental import pallas as pl
from jax.experimental.pallas import tpu as pltpu
from jax.sharding import PartitionSpec as P

HD = 128
PAGE = 64
ATTEND_VMEM = 60 * 1024 * 1024
HIDDEN = -1e30
LOWEST = -1e20
EXCHANGE_FLOPS = 5_000_000_000
SMALL_VMEM = 8 * 1024 * 1024
VMEM = pl.BlockSpec(memory_space=pltpu.VMEM)
HBM = pl.BlockSpec(memory_space=pltpu.HBM)


def split_two(value):
    high = value.astype(jnp.bfloat16).astype(jnp.float32)
    low = (value - high).astype(jnp.bfloat16).astype(jnp.float32)
    return high, low


def attend_kernel(heads_dev, devices, *refs):
    table_hbm, lengths_hbm, key_scale_hbm, value_scale_hbm, queries_hbm, keys, values = refs[:7]
    staged, table, lengths, key_scale, value_scale, queries, key_buf, value_buf, query_rows = refs[7:16]
    table_rows, factors, bias, weights, small_sems, sems = refs[16:]
    rows, pages = table.shape
    kv_heads = key_scale.shape[0]
    heads = queries.shape[1] // HD
    group = heads // kv_heads
    context = pages * PAGE
    pieces = sems.shape[1]
    piece = keys.shape[0] // pieces

    small = []
    for i, (source, target) in enumerate(
        (
            (table_hbm, table),
            (table_hbm, table_rows),
            (lengths_hbm, lengths),
            (key_scale_hbm, key_scale),
            (value_scale_hbm, value_scale),
            (queries_hbm, queries),
        )
    ):
        small.append(pltpu.make_async_copy(source, target, small_sems.at[i]))
        small[-1].start()
    large = []
    for which, source, target in ((0, keys, key_buf), (1, values, value_buf)):
        large.append([])
        for i in range(pieces):
            here = pl.ds(i * piece, piece)
            large[-1].append(pltpu.make_async_copy(source.at[here], target.at[here], sems.at[which, i]))
    for copy in large[0]:
        copy.start()

    me = lax.axis_index("kvp")
    lane = lax.broadcasted_iota(jnp.int32, (group, HD), 1)
    place = me * context + lax.broadcasted_iota(jnp.int32, (1, context), 1)
    page_of = lax.div(lax.broadcasted_iota(jnp.int32, (pages, context), 1), PAGE)
    spread = (page_of == lax.broadcasted_iota(jnp.int32, (pages, context), 0)).astype(jnp.float32).astype(jnp.bfloat16)
    slot = lax.broadcasted_iota(jnp.int32, (keys.shape[0], context), 0).astype(jnp.float32)
    zeros = jnp.zeros((group, HD), jnp.bfloat16)
    small[0].wait()
    for copy in large[1]:
        copy.start()
    for copy in small[1:]:
        copy.wait()

    scales = jnp.concatenate([key_scale[...] * (math.log2(math.e) / math.sqrt(HD)), value_scale[...]], axis=0)
    high, low = split_two(scales)
    parts = jnp.concatenate([high, low, scales - high - low], axis=0).astype(jnp.bfloat16)
    slots = jnp.dot(
        table_rows[...].astype(jnp.float32).astype(jnp.bfloat16), spread, preferred_element_type=jnp.float32
    )
    for r in range(rows):
        chosen = (slots[r : r + 1] == slot).astype(jnp.float32).astype(jnp.bfloat16)
        found = jnp.dot(parts, chosen, preferred_element_type=jnp.float32)
        count = 2 * kv_heads
        factors[r] = found[:count] + found[count : 2 * count] + found[2 * count :]
        bias[r : r + 1] = jnp.where(place < lengths[r], 0.0, HIDDEN)
    for h in range(heads):
        query_rows[h * rows : (h + 1) * rows, :] = queries[:, h * HD : (h + 1) * HD].astype(jnp.float32)

    def pages_of(buf, r, k):
        return jnp.concatenate(
            [buf[table[r, p], :, k * HD : (k + 2) * HD] for p in range(pages)], axis=0
        )

    for copy in large[0]:
        copy.wait()
    stats = [jnp.zeros((group, HD), jnp.float32)] * kv_heads
    for r in range(rows):
        query = query_rows[pl.ds(r, heads, stride=rows), :].astype(jnp.bfloat16)
        for k in range(0, kv_heads, 2):
            left = jnp.concatenate(
                [
                    jnp.concatenate([query[k * group : (k + 1) * group], zeros], axis=1),
                    jnp.concatenate([zeros, query[(k + 1) * group : (k + 2) * group]], axis=1),
                ],
                axis=0,
            )
            both = lax.dot_general(
                left, pages_of(key_buf, r, k), (((1,), (1,)), ((), ())), preferred_element_type=jnp.float32
            )
            for i in (0, 1):
                at_key, at_value = k + i, kv_heads + k + i
                scores = both[i * group : (i + 1) * group] * factors[r, at_key : at_key + 1] + bias[r : r + 1]
                highest = jnp.maximum(jnp.max(scores, axis=1, keepdims=True), LOWEST)
                high, low = split_two(highest)
                prob = jnp.exp2(scores - (high + low))
                total_high, total_low = split_two(jnp.sum(prob, axis=1, keepdims=True))
                for at, value in enumerate((high, low, total_high, total_low)):
                    stats[k + i] = jnp.where(lane == 4 * r + at, value, stats[k + i])
                weights[r, (k + i) * group : (k + i + 1) * group] = (
                    prob * factors[r, at_value : at_value + 1]
                ).astype(jnp.bfloat16)
    for copy in large[1]:
        copy.wait()
    for r in range(rows):
        for k in range(0, kv_heads, 2):
            both = jnp.dot(
                weights[r, k * group : (k + 2) * group], pages_of(value_buf, r, k), preferred_element_type=jnp.float32
            )
            for i in (0, 1):
                partial = both[i * group : (i + 1) * group, i * HD : (i + 1) * HD]
                for start in range(0, group, heads_dev):
                    d = ((k + i) * group + start) // heads_dev
                    staged[d, r] = partial[start : start + heads_dev]
    for k in range(kv_heads):
        for start in range(0, group, heads_dev):
            d = (k * group + start) // heads_dev
            staged[d, rows] = stats[k][start : start + heads_dev]


def pack_kernel(staged, keep, send):
    core = lax.rem(lax.axis_index("kvp"), 2)
    for i in range(keep.shape[0]):
        keep[i] = staged[2 * i + core]
        send[i] = staged[2 * i + 1 - core].astype(send.dtype)


def lanes_ahead(value, by):
    lanes = value.shape[-1]
    return pltpu.roll(value, (lanes - by) % lanes, axis=2)


def merge_kernel(keep, arrived, packed):
    rows = keep.shape[1] - 1
    own, other = keep[:, rows], arrived[:, rows].astype(jnp.float32)
    own_max, other_max = (stats + lanes_ahead(stats, 1) for stats in (own, other))
    own_total, other_total = (lanes_ahead(stats, 2) + lanes_ahead(stats, 3) for stats in (own, other))
    high, low = split_two(jnp.maximum(own_max, other_max))
    own_scale = jnp.exp2(own_max - (high + low))
    other_scale = jnp.exp2(other_max - (high + low))
    total_high, total_low = split_two(own_total * own_scale + other_total * other_scale)
    at = lax.rem(lax.broadcasted_iota(jnp.int32, own.shape, 2), 4)
    merged = high
    for i, value in ((1, low), (2, total_high), (3, total_low)):
        merged = jnp.where(at == i, lanes_ahead(value, -i), merged)
    packed[:, rows] = merged.astype(packed.dtype)
    for r in range(rows):
        lane = slice(4 * r, 4 * r + 1)
        partial = keep[:, r] * own_scale[:, :, lane] + arrived[:, r].astype(jnp.float32) * other_scale[:, :, lane]
        packed[:, r] = partial.astype(packed.dtype)


def combine_kernel(heads_dev, packed, left, attended):
    rows = left.shape[0]
    stats = packed[:, rows].astype(jnp.float32)
    maxima = stats + lanes_ahead(stats, 1)
    rescale = jnp.exp2(maxima - jnp.max(maxima, axis=0, keepdims=True))
    totals = lanes_ahead(stats, 2) + lanes_ahead(stats, 3)
    denominator = jnp.sum(totals * rescale, axis=0)
    for r in range(rows):
        partial = packed[:, r].astype(jnp.float32)
        numerator = jnp.sum(partial * rescale[:, :, 4 * r : 4 * r + 1], axis=0)
        attended[r * heads_dev : (r + 1) * heads_dev, :] = numerator / denominator[:, 4 * r : 4 * r + 1]
    rounded = jnp.concatenate(
        [attended[pl.ds(j, rows, stride=heads_dev), :].astype(jnp.bfloat16) for j in range(heads_dev)], axis=1
    )
    left[...] = rounded


def project_kernel(partner, left, weight, out):
    part = out.shape[1]
    quarter = lax.rem(lax.axis_index("kvp"), weight.shape[1] // part)
    start = pl.multiple_of(jnp.bitwise_xor(quarter, partner) * part, part)
    terms = jnp.dot(left[...], weight[:, pl.ds(start, part)], preferred_element_type=jnp.float32)
    out[...] = terms.astype(out.dtype)


def add_kernel(*refs):
    terms = [ref[...].astype(jnp.float32) for ref in refs[:-1]]
    while len(terms) > 1:
        terms = [terms[i] + terms[i + 1] for i in range(0, len(terms), 2)]
    refs[-1][...] = terms[0].astype(refs[-1].dtype)


def lay_kernel(*refs):
    parts, out = refs[:-1], refs[-1]
    quarter = lax.rem(lax.axis_index("kvp"), len(parts))
    width = parts[0].shape[1]
    for x, part in enumerate(parts):
        start = pl.multiple_of(jnp.bitwise_xor(quarter, x) * width, width)
        out[:, pl.ds(start, width)] = part[...]


def exchange(array, partner, devices):
    return lax.ppermute(array, "kvp", [(i, i ^ partner) for i in range(devices)])


def in_hbm(array):
    return pltpu.with_memory_space_constraint(array, pltpu.HBM)


def body(queries, key_cache, value_cache, key_scale, value_scale, page_table, lengths, out_weight, *, devices):
    rows, pages = page_table.shape
    slots, _, columns = key_cache.shape
    kv_heads = key_scale.shape[1]
    heads_dev = out_weight.shape[0] // HD
    heads = queries.shape[1] // HD
    features = out_weight.shape[1]
    inner = 4
    outer = devices // inner
    part = features // inner
    staged = pl.pallas_call(
        functools.partial(attend_kernel, heads_dev, devices),
        out_shape=pltpu.VMEM((devices, rows + 1, heads_dev, HD), jnp.float32),
        in_specs=[HBM] * 7,
        out_specs=VMEM,
        scratch_shapes=[
            pltpu.SMEM((rows, pages), jnp.int32),
            pltpu.SMEM((rows,), jnp.int32),
            pltpu.VMEM((kv_heads, slots), jnp.float32),
            pltpu.VMEM((kv_heads, slots), jnp.float32),
            pltpu.VMEM((rows, heads * HD), jnp.bfloat16),
            pltpu.VMEM((slots, PAGE, columns), jnp.bfloat16),
            pltpu.VMEM((slots, PAGE, columns), jnp.bfloat16),
            pltpu.VMEM((heads * rows, HD), jnp.float32),
            pltpu.VMEM((rows, pages), jnp.int32),
            pltpu.VMEM((rows, 2 * kv_heads, pages * PAGE), jnp.float32),
            pltpu.VMEM((rows, pages * PAGE), jnp.float32),
            pltpu.VMEM((rows, heads, pages * PAGE), jnp.bfloat16),
            pltpu.SemaphoreType.DMA((6,)),
            pltpu.SemaphoreType.DMA((2, 2)),
        ],
        compiler_params=pltpu.CompilerParams(vmem_limit_bytes=ATTEND_VMEM),
        cost_estimate=pl.CostEstimate(
            flops=4 * heads * rows * pages * PAGE * HD,
            bytes_accessed=4 * rows * pages * PAGE * columns,
            transcendentals=heads * rows * pages * PAGE,
        ),
        name="attend",
    )(*[in_hbm(a) for a in (page_table, lengths, key_scale.T, value_scale.T, queries, key_cache, value_cache)])

    chips = devices // 2
    block = (chips,) + staged.shape[1:]
    keep, send = pl.pallas_call(
        pack_kernel,
        out_shape=[jax.ShapeDtypeStruct(block, jnp.float32), jax.ShapeDtypeStruct(block, jnp.bfloat16)],
        in_specs=[VMEM],
        out_specs=[VMEM] * 2,
        compiler_params=pltpu.CompilerParams(vmem_limit_bytes=SMALL_VMEM),
        cost_estimate=pl.CostEstimate(flops=EXCHANGE_FLOPS, bytes_accessed=6 * staged.size, transcendentals=0),
        name="pack",
    )(staged)
    packed = pl.pallas_call(
        merge_kernel,
        out_shape=jax.ShapeDtypeStruct(block, jnp.bfloat16),
        in_specs=[VMEM] * 2,
        out_specs=VMEM,
        compiler_params=pltpu.CompilerParams(vmem_limit_bytes=SMALL_VMEM),
        cost_estimate=pl.CostEstimate(flops=1024, bytes_accessed=1024, transcendentals=0),
        name="merge",
    )(keep, exchange(send, 1, devices))

    parity = [[2 * i + core for i in range(chips)] for core in (0, 1)]
    received = lax.all_to_all(
        packed, "kvp", split_axis=0, concat_axis=0, axis_index_groups=parity, tiled=True
    )

    resident = pltpu.with_memory_space_constraint(out_weight, pltpu.VMEM)
    depth = heads_dev * HD
    cost = pl.CostEstimate(flops=1024, bytes_accessed=1024, transcendentals=0)
    small = pltpu.CompilerParams(vmem_limit_bytes=SMALL_VMEM)
    left = pl.pallas_call(
        functools.partial(combine_kernel, heads_dev),
        out_shape=jax.ShapeDtypeStruct((rows, depth), jnp.bfloat16),
        in_specs=[VMEM],
        out_specs=VMEM,
        scratch_shapes=[pltpu.VMEM((rows * heads_dev, HD), jnp.float32)],
        compiler_params=small,
        name="combine",
    )(received)
    arrived = []
    for x in reversed(range(inner)):
        terms = pl.pallas_call(
            functools.partial(project_kernel, x),
            out_shape=jax.ShapeDtypeStruct((rows, part), jnp.bfloat16 if x else jnp.float32),
            in_specs=[VMEM] * 2,
            out_specs=VMEM,
            compiler_params=small,
            cost_estimate=cost,
            name=f"project_{x}",
        )(left, resident)
        arrived.append(exchange(terms, x, devices) if x else terms)

    def add(terms, name):
        return pl.pallas_call(
            add_kernel,
            out_shape=jax.ShapeDtypeStruct((rows, part), jnp.bfloat16),
            in_specs=[VMEM] * len(terms),
            out_specs=VMEM,
            compiler_params=pltpu.CompilerParams(vmem_limit_bytes=SMALL_VMEM),
            name=name,
        )(*terms)

    mine = add(arrived, "add_near")
    mine = add([mine] + [exchange(mine, x * inner, devices) for x in range(1, outer)], "add_far")
    parts = [mine] + [exchange(mine, x, devices) for x in range(1, inner)]
    return pl.pallas_call(
        lay_kernel,
        out_shape=jax.ShapeDtypeStruct((rows, features), jnp.bfloat16),
        in_specs=[VMEM] * inner,
        out_specs=VMEM,
        compiler_params=pltpu.CompilerParams(vmem_limit_bytes=SMALL_VMEM),
        name="lay",
    )(*parts)


def solution(mesh):
    placed = (
        P("group", None),
        P(("group", "kvp"), None, None),
        P(("group", "kvp"), None, None),
        P(("group", "kvp"), None),
        P(("group", "kvp"), None),
        P("group", "kvp"),
        P("group"),
        P("kvp", None),
    )
    return jax.shard_map(
        functools.partial(body, devices=mesh.shape["kvp"]),
        mesh=mesh,
        in_specs=placed,
        out_specs=P("group", None),
        check_vma=False,
    )
```

```python
import functools
import math

import jax
import jax.numpy as jnp
from jax import lax
from jax.experimental import pallas as pl
from jax.experimental.pallas import tpu as pltpu
from jax.sharding import PartitionSpec as P

HD = 128
PAGE = 64
ATTEND_VMEM = 60 * 1024 * 1024
HIDDEN = -1e30
LOWEST = -1e20
EXCHANGE_FLOPS = 40_000_000_000
SMALL_VMEM = 8 * 1024 * 1024
VMEM = pl.BlockSpec(memory_space=pltpu.VMEM)
HBM = pl.BlockSpec(memory_space=pltpu.HBM)


def split_two(value):
    high = value.astype(jnp.bfloat16).astype(jnp.float32)
    low = (value - high).astype(jnp.bfloat16).astype(jnp.float32)
    return high, low


def attend_kernel(heads_dev, devices, *refs):
    table_hbm, lengths_hbm, key_scale_hbm, value_scale_hbm, queries_hbm, keys, values = refs[:7]
    staged, table, lengths, key_scale, value_scale, queries, key_buf, value_buf, query_rows = refs[7:16]
    table_rows, factors, bias, weights, small_sems, sems = refs[16:]
    rows, pages = table.shape
    kv_heads = key_scale.shape[0]
    heads = queries.shape[1] // HD
    group = heads // kv_heads
    context = pages * PAGE
    pieces = sems.shape[1]
    piece = keys.shape[0] // pieces

    small = []
    for i, (source, target) in enumerate(
        (
            (table_hbm, table),
            (table_hbm, table_rows),
            (lengths_hbm, lengths),
            (key_scale_hbm, key_scale),
            (value_scale_hbm, value_scale),
            (queries_hbm, queries),
        )
    ):
        small.append(pltpu.make_async_copy(source, target, small_sems.at[i]))
        small[-1].start()
    large = []
    for which, source, target in ((0, keys, key_buf), (1, values, value_buf)):
        large.append([])
        for i in range(pieces):
            here = pl.ds(i * piece, piece)
            large[-1].append(pltpu.make_async_copy(source.at[here], target.at[here], sems.at[which, i]))
    for copy in large[0]:
        copy.start()

    me = lax.axis_index("kvp")
    lane = lax.broadcasted_iota(jnp.int32, (group, HD), 1)
    place = me * context + lax.broadcasted_iota(jnp.int32, (1, context), 1)
    page_of = lax.div(lax.broadcasted_iota(jnp.int32, (pages, context), 1), PAGE)
    spread = (page_of == lax.broadcasted_iota(jnp.int32, (pages, context), 0)).astype(jnp.float32).astype(jnp.bfloat16)
    slot = lax.broadcasted_iota(jnp.int32, (keys.shape[0], context), 0).astype(jnp.float32)
    zeros = jnp.zeros((group, HD), jnp.bfloat16)
    small[0].wait()
    for copy in large[1]:
        copy.start()
    for copy in small[1:]:
        copy.wait()

    scales = jnp.concatenate([key_scale[...] * (math.log2(math.e) / math.sqrt(HD)), value_scale[...]], axis=0)
    high, low = split_two(scales)
    parts = jnp.concatenate([high, low, scales - high - low], axis=0).astype(jnp.bfloat16)
    slots = jnp.dot(
        table_rows[...].astype(jnp.float32).astype(jnp.bfloat16), spread, preferred_element_type=jnp.float32
    )
    for r in range(rows):
        chosen = (slots[r : r + 1] == slot).astype(jnp.float32).astype(jnp.bfloat16)
        found = jnp.dot(parts, chosen, preferred_element_type=jnp.float32)
        count = 2 * kv_heads
        factors[r] = found[:count] + found[count : 2 * count] + found[2 * count :]
        bias[r : r + 1] = jnp.where(place < lengths[r], 0.0, HIDDEN)
    for h in range(heads):
        query_rows[h * rows : (h + 1) * rows, :] = queries[:, h * HD : (h + 1) * HD].astype(jnp.float32)

    def pages_of(buf, r):
        return jnp.concatenate([buf[table[r, p]] for p in range(pages)], axis=0)

    for copy in large[0]:
        copy.wait()
    stats = [jnp.zeros((group, HD), jnp.float32)] * kv_heads
    for r in range(rows):
        query = query_rows[pl.ds(r, heads, stride=rows), :].astype(jnp.bfloat16)
        left = jnp.concatenate(
            [
                jnp.concatenate(
                    [query[k * group : (k + 1) * group] if i == k else zeros for i in range(kv_heads)], axis=1
                )
                for k in range(kv_heads)
            ],
            axis=0,
        )
        both = lax.dot_general(
            left, pages_of(key_buf, r), (((1,), (1,)), ((), ())), preferred_element_type=jnp.float32
        )
        for k in range(0, kv_heads, 2):
            for i in (0, 1):
                at_key, at_value = k + i, kv_heads + k + i
                scores = both[(k + i) * group : (k + i + 1) * group] * factors[r, at_key : at_key + 1] + bias[r : r + 1]
                highest = jnp.maximum(jnp.max(scores, axis=1, keepdims=True), LOWEST)
                high, low = split_two(highest)
                prob = jnp.exp2(scores - (high + low))
                total_high, total_low = split_two(jnp.sum(prob, axis=1, keepdims=True))
                for at, value in enumerate((high, low, total_high, total_low)):
                    stats[k + i] = jnp.where(lane == 4 * r + at, value, stats[k + i])
                weights[r, (k + i) * group : (k + i + 1) * group] = (
                    prob * factors[r, at_value : at_value + 1]
                ).astype(jnp.bfloat16)
    for copy in large[1]:
        copy.wait()
    for r in range(rows):
        both = jnp.dot(weights[r], pages_of(value_buf, r), preferred_element_type=jnp.float32)
        for k in range(0, kv_heads, 2):
            for i in (0, 1):
                partial = both[(k + i) * group : (k + i + 1) * group, (k + i) * HD : (k + i + 1) * HD]
                for start in range(0, group, heads_dev):
                    d = ((k + i) * group + start) // heads_dev
                    staged[d, r] = partial[start : start + heads_dev]
    for k in range(kv_heads):
        for start in range(0, group, heads_dev):
            d = (k * group + start) // heads_dev
            staged[d, rows] = stats[k][start : start + heads_dev]


def pack_kernel(staged, packed):
    packed[...] = staged[...].astype(jnp.bfloat16)


def combine_kernel(heads_dev, packed, left, attended):
    rows = left.shape[0]
    stats = packed[:, rows].astype(jnp.float32)
    lanes = stats.shape[-1]

    def lanes_ahead(value, by):
        return pltpu.roll(value, lanes - by, axis=2)

    maxima = stats + lanes_ahead(stats, 1)
    rescale = jnp.exp2(maxima - jnp.max(maxima, axis=0, keepdims=True))
    totals = lanes_ahead(stats, 2) + lanes_ahead(stats, 3)
    denominator = jnp.sum(totals * rescale, axis=0)
    for r in range(rows):
        partial = packed[:, r].astype(jnp.float32)
        numerator = jnp.sum(partial * rescale[:, :, 4 * r : 4 * r + 1], axis=0)
        attended[r * heads_dev : (r + 1) * heads_dev, :] = numerator / denominator[:, 4 * r : 4 * r + 1]
    rounded = jnp.concatenate(
        [attended[pl.ds(j, rows, stride=heads_dev), :].astype(jnp.bfloat16) for j in range(heads_dev)], axis=1
    )
    left[...] = rounded


def project_kernel(partner, left, weight, out):
    part = out.shape[1]
    quarter = lax.rem(lax.axis_index("kvp"), weight.shape[1] // part)
    start = pl.multiple_of(jnp.bitwise_xor(quarter, partner) * part, part)
    terms = jnp.dot(left[...], weight[:, pl.ds(start, part)], preferred_element_type=jnp.float32)
    out[...] = terms.astype(out.dtype)


def add_kernel(*refs):
    terms = [ref[...].astype(jnp.float32) for ref in refs[:-1]]
    while len(terms) > 1:
        terms = [terms[i] + terms[i + 1] for i in range(0, len(terms), 2)]
    refs[-1][...] = terms[0].astype(refs[-1].dtype)


def lay_kernel(*refs):
    parts, out = refs[:-1], refs[-1]
    quarter = lax.rem(lax.axis_index("kvp"), len(parts))
    width = parts[0].shape[1]
    for x, part in enumerate(parts):
        start = pl.multiple_of(jnp.bitwise_xor(quarter, x) * width, width)
        out[:, pl.ds(start, width)] = part[...]


def exchange(array, partner, devices):
    return lax.ppermute(array, "kvp", [(i, i ^ partner) for i in range(devices)])


def in_hbm(array):
    return pltpu.with_memory_space_constraint(array, pltpu.HBM)


def body(queries, key_cache, value_cache, key_scale, value_scale, page_table, lengths, out_weight, *, devices):
    rows, pages = page_table.shape
    slots, _, columns = key_cache.shape
    kv_heads = key_scale.shape[1]
    heads_dev = out_weight.shape[0] // HD
    heads = queries.shape[1] // HD
    features = out_weight.shape[1]
    inner = 4
    outer = devices // inner
    part = features // inner
    staged = pl.pallas_call(
        functools.partial(attend_kernel, heads_dev, devices),
        out_shape=pltpu.VMEM((devices, rows + 1, heads_dev, HD), jnp.float32),
        in_specs=[HBM] * 7,
        out_specs=VMEM,
        scratch_shapes=[
            pltpu.SMEM((rows, pages), jnp.int32),
            pltpu.SMEM((rows,), jnp.int32),
            pltpu.VMEM((kv_heads, slots), jnp.float32),
            pltpu.VMEM((kv_heads, slots), jnp.float32),
            pltpu.VMEM((rows, heads * HD), jnp.bfloat16),
            pltpu.VMEM((slots, PAGE, columns), jnp.bfloat16),
            pltpu.VMEM((slots, PAGE, columns), jnp.bfloat16),
            pltpu.VMEM((heads * rows, HD), jnp.float32),
            pltpu.VMEM((rows, pages), jnp.int32),
            pltpu.VMEM((rows, 2 * kv_heads, pages * PAGE), jnp.float32),
            pltpu.VMEM((rows, pages * PAGE), jnp.float32),
            pltpu.VMEM((rows, heads, pages * PAGE), jnp.bfloat16),
            pltpu.SemaphoreType.DMA((6,)),
            pltpu.SemaphoreType.DMA((2, 2)),
        ],
        compiler_params=pltpu.CompilerParams(vmem_limit_bytes=ATTEND_VMEM),
        cost_estimate=pl.CostEstimate(
            flops=4 * heads * rows * pages * PAGE * HD,
            bytes_accessed=4 * rows * pages * PAGE * columns,
            transcendentals=heads * rows * pages * PAGE,
        ),
        name="attend",
    )(*[in_hbm(a) for a in (page_table, lengths, key_scale.T, value_scale.T, queries, key_cache, value_cache)])

    packed = pl.pallas_call(
        pack_kernel,
        out_shape=jax.ShapeDtypeStruct(staged.shape, jnp.bfloat16),
        in_specs=[VMEM],
        out_specs=VMEM,
        compiler_params=pltpu.CompilerParams(vmem_limit_bytes=SMALL_VMEM),
        cost_estimate=pl.CostEstimate(flops=EXCHANGE_FLOPS, bytes_accessed=6 * staged.size, transcendentals=0),
        name="pack",
    )(staged)

    received = lax.all_to_all(packed, "kvp", split_axis=0, concat_axis=0, tiled=True)

    resident = pltpu.with_memory_space_constraint(out_weight, pltpu.VMEM)
    depth = heads_dev * HD
    cost = pl.CostEstimate(flops=1024, bytes_accessed=1024, transcendentals=0)
    small = pltpu.CompilerParams(vmem_limit_bytes=SMALL_VMEM)
    left = pl.pallas_call(
        functools.partial(combine_kernel, heads_dev),
        out_shape=jax.ShapeDtypeStruct((rows, depth), jnp.bfloat16),
        in_specs=[VMEM],
        out_specs=VMEM,
        scratch_shapes=[pltpu.VMEM((rows * heads_dev, HD), jnp.float32)],
        compiler_params=small,
        name="combine",
    )(received)
    arrived = []
    for x in reversed(range(inner)):
        terms = pl.pallas_call(
            functools.partial(project_kernel, x),
            out_shape=jax.ShapeDtypeStruct((rows, part), jnp.bfloat16 if x else jnp.float32),
            in_specs=[VMEM] * 2,
            out_specs=VMEM,
            compiler_params=small,
            cost_estimate=cost,
            name=f"project_{x}",
        )(left, resident)
        arrived.append(exchange(terms, x, devices) if x else terms)

    def add(terms, name):
        return pl.pallas_call(
            add_kernel,
            out_shape=jax.ShapeDtypeStruct((rows, part), jnp.bfloat16),
            in_specs=[VMEM] * len(terms),
            out_specs=VMEM,
            compiler_params=pltpu.CompilerParams(vmem_limit_bytes=SMALL_VMEM),
            name=name,
        )(*terms)

    mine = add(arrived, "add_near")
    mine = add([mine] + [exchange(mine, x * inner, devices) for x in range(1, outer)], "add_far")
    parts = [mine] + [exchange(mine, x, devices) for x in range(1, inner)]
    return pl.pallas_call(
        lay_kernel,
        out_shape=jax.ShapeDtypeStruct((rows, features), jnp.bfloat16),
        in_specs=[VMEM] * inner,
        out_specs=VMEM,
        compiler_params=pltpu.CompilerParams(vmem_limit_bytes=SMALL_VMEM),
        name="lay",
    )(*parts)


def solution(mesh):
    placed = (
        P("group", None),
        P(("group", "kvp"), None, None),
        P(("group", "kvp"), None, None),
        P(("group", "kvp"), None),
        P(("group", "kvp"), None),
        P("group", "kvp"),
        P("group"),
        P("kvp", None),
    )
    return jax.shard_map(
        functools.partial(body, devices=mesh.shape["kvp"]),
        mesh=mesh,
        in_specs=placed,
        out_specs=P("group", None),
        check_vma=False,
    )
```

```python
import functools
import math

import jax
import jax.numpy as jnp
from jax import lax
from jax.experimental import pallas as pl
from jax.experimental.pallas import tpu as pltpu
from jax.sharding import PartitionSpec as P

HD = 128
PAGE = 64
ATTEND_VMEM = 60 * 1024 * 1024
HIDDEN = -1e30
LOWEST = -1e20
EXCHANGE_FLOPS = 40_000_000_000
SMALL_VMEM = 8 * 1024 * 1024
VMEM = pl.BlockSpec(memory_space=pltpu.VMEM)
HBM = pl.BlockSpec(memory_space=pltpu.HBM)


def split_two(value):
    high = value.astype(jnp.bfloat16).astype(jnp.float32)
    low = (value - high).astype(jnp.bfloat16).astype(jnp.float32)
    return high, low


def attend_kernel(heads_dev, devices, *refs):
    table_hbm, lengths_hbm, key_scale_hbm, value_scale_hbm, queries_hbm, keys, values = refs[:7]
    staged, table, lengths, key_scale, value_scale, queries, key_buf, value_buf, query_rows = refs[7:16]
    table_rows, factors, bias, weights, small_sems, sems = refs[16:]
    rows, pages = table.shape
    kv_heads = key_scale.shape[0]
    heads = queries.shape[1] // HD
    group = heads // kv_heads
    context = pages * PAGE
    pieces = sems.shape[1]
    piece = keys.shape[0] // pieces

    small = []
    for i, (source, target) in enumerate(
        (
            (table_hbm, table),
            (table_hbm, table_rows),
            (lengths_hbm, lengths),
            (key_scale_hbm, key_scale),
            (value_scale_hbm, value_scale),
            (queries_hbm, queries),
        )
    ):
        small.append(pltpu.make_async_copy(source, target, small_sems.at[i]))
        small[-1].start()
    large = []
    for which, source, target in ((0, keys, key_buf), (1, values, value_buf)):
        large.append([])
        for i in range(pieces):
            here = pl.ds(i * piece, piece)
            large[-1].append(pltpu.make_async_copy(source.at[here], target.at[here], sems.at[which, i]))
    for copy in large[0]:
        copy.start()

    me = lax.axis_index("kvp")
    lane = lax.broadcasted_iota(jnp.int32, (group, HD), 1)
    place = me * context + lax.broadcasted_iota(jnp.int32, (1, context), 1)
    page_of = lax.div(lax.broadcasted_iota(jnp.int32, (pages, context), 1), PAGE)
    spread = (page_of == lax.broadcasted_iota(jnp.int32, (pages, context), 0)).astype(jnp.float32).astype(jnp.bfloat16)
    slot = lax.broadcasted_iota(jnp.int32, (keys.shape[0], context), 0).astype(jnp.float32)
    zeros = jnp.zeros((group, HD), jnp.bfloat16)
    small[0].wait()
    for copy in large[1]:
        copy.start()
    for copy in small[1:]:
        copy.wait()

    scales = jnp.concatenate([key_scale[...] * (math.log2(math.e) / math.sqrt(HD)), value_scale[...]], axis=0)
    high, low = split_two(scales)
    parts = jnp.concatenate([high, low, scales - high - low], axis=0).astype(jnp.bfloat16)
    slots = jnp.dot(
        table_rows[...].astype(jnp.float32).astype(jnp.bfloat16), spread, preferred_element_type=jnp.float32
    )
    for r in range(rows):
        chosen = (slots[r : r + 1] == slot).astype(jnp.float32).astype(jnp.bfloat16)
        found = jnp.dot(parts, chosen, preferred_element_type=jnp.float32)
        count = 2 * kv_heads
        factors[r] = found[:count] + found[count : 2 * count] + found[2 * count :]
        bias[r : r + 1] = jnp.where(place < lengths[r], 0.0, HIDDEN)
    for h in range(heads):
        query_rows[h * rows : (h + 1) * rows, :] = queries[:, h * HD : (h + 1) * HD].astype(jnp.float32)

    def pages_of(buf, r, k):
        return jnp.concatenate(
            [buf[table[r, p], :, k * HD : (k + 2) * HD] for p in range(pages)], axis=0
        )

    for copy in large[0]:
        copy.wait()
    stats = [jnp.zeros((group, HD), jnp.float32)] * kv_heads
    for r in range(rows):
        query = query_rows[pl.ds(r, heads, stride=rows), :].astype(jnp.bfloat16)
        for k in range(0, kv_heads, 2):
            left = jnp.concatenate(
                [
                    jnp.concatenate([query[k * group : (k + 1) * group], zeros], axis=1),
                    jnp.concatenate([zeros, query[(k + 1) * group : (k + 2) * group]], axis=1),
                ],
                axis=0,
            )
            both = lax.dot_general(
                left, pages_of(key_buf, r, k), (((1,), (1,)), ((), ())), preferred_element_type=jnp.float32
            )
            for i in (0, 1):
                at_key, at_value = k + i, kv_heads + k + i
                scores = both[i * group : (i + 1) * group] * factors[r, at_key : at_key + 1] + bias[r : r + 1]
                highest = jnp.maximum(jnp.max(scores, axis=1, keepdims=True), LOWEST)
                high, low = split_two(highest)
                prob = jnp.exp2(scores - (high + low))
                total_high, total_low = split_two(jnp.sum(prob, axis=1, keepdims=True))
                for at, value in enumerate((high, low, total_high, total_low)):
                    stats[k + i] = jnp.where(lane == 4 * r + at, value, stats[k + i])
                weights[r, (k + i) * group : (k + i + 1) * group] = (
                    prob * factors[r, at_value : at_value + 1]
                ).astype(jnp.bfloat16)
    for copy in large[1]:
        copy.wait()
    for r in range(rows):
        for k in range(0, kv_heads, 2):
            both = jnp.dot(
                weights[r, k * group : (k + 2) * group], pages_of(value_buf, r, k), preferred_element_type=jnp.float32
            )
            for i in (0, 1):
                partial = both[i * group : (i + 1) * group, i * HD : (i + 1) * HD]
                for start in range(0, group, heads_dev):
                    d = ((k + i) * group + start) // heads_dev
                    staged[d, r] = partial[start : start + heads_dev]
    for k in range(kv_heads):
        for start in range(0, group, heads_dev):
            d = (k * group + start) // heads_dev
            staged[d, rows] = stats[k][start : start + heads_dev]


def pack_kernel(staged, packed):
    packed[...] = staged[...].astype(jnp.bfloat16)


def project_first_kernel(heads_dev, partner, packed, weight, left, out, attended):
    rows = left.shape[0]
    stats = packed[:, rows].astype(jnp.float32)
    lanes = stats.shape[-1]

    def lanes_ahead(value, by):
        return pltpu.roll(value, lanes - by, axis=2)

    maxima = stats + lanes_ahead(stats, 1)
    rescale = jnp.exp2(maxima - jnp.max(maxima, axis=0, keepdims=True))
    totals = lanes_ahead(stats, 2) + lanes_ahead(stats, 3)
    denominator = jnp.sum(totals * rescale, axis=0)
    for r in range(rows):
        partial = packed[:, r].astype(jnp.float32)
        numerator = jnp.sum(partial * rescale[:, :, 4 * r : 4 * r + 1], axis=0)
        attended[r * heads_dev : (r + 1) * heads_dev, :] = numerator / denominator[:, 4 * r : 4 * r + 1]
    rounded = jnp.concatenate(
        [attended[pl.ds(j, rows, stride=heads_dev), :].astype(jnp.bfloat16) for j in range(heads_dev)], axis=1
    )
    left[...] = rounded
    project_kernel(partner, left, weight, out)


def project_kernel(partner, left, weight, out):
    part = out.shape[1]
    quarter = lax.rem(lax.axis_index("kvp"), weight.shape[1] // part)
    start = pl.multiple_of(jnp.bitwise_xor(quarter, partner) * part, part)
    terms = jnp.dot(left[...], weight[:, pl.ds(start, part)], preferred_element_type=jnp.float32)
    out[...] = terms.astype(out.dtype)


def add_kernel(*refs):
    terms = [ref[...].astype(jnp.float32) for ref in refs[:-1]]
    while len(terms) > 1:
        terms = [terms[i] + terms[i + 1] for i in range(0, len(terms), 2)]
    refs[-1][...] = terms[0].astype(refs[-1].dtype)


def lay_kernel(*refs):
    parts, out = refs[:-1], refs[-1]
    quarter = lax.rem(lax.axis_index("kvp"), len(parts))
    width = parts[0].shape[1]
    for x, part in enumerate(parts):
        start = pl.multiple_of(jnp.bitwise_xor(quarter, x) * width, width)
        out[:, pl.ds(start, width)] = part[...]


def exchange(array, partner, devices):
    return lax.ppermute(array, "kvp", [(i, i ^ partner) for i in range(devices)])


def in_hbm(array):
    return pltpu.with_memory_space_constraint(array, pltpu.HBM)


def body(queries, key_cache, value_cache, key_scale, value_scale, page_table, lengths, out_weight, *, devices):
    rows, pages = page_table.shape
    slots, _, columns = key_cache.shape
    kv_heads = key_scale.shape[1]
    heads_dev = out_weight.shape[0] // HD
    heads = queries.shape[1] // HD
    features = out_weight.shape[1]
    inner = 4
    outer = devices // inner
    part = features // inner
    staged = pl.pallas_call(
        functools.partial(attend_kernel, heads_dev, devices),
        out_shape=pltpu.VMEM((devices, rows + 1, heads_dev, HD), jnp.float32),
        in_specs=[HBM] * 7,
        out_specs=VMEM,
        scratch_shapes=[
            pltpu.SMEM((rows, pages), jnp.int32),
            pltpu.SMEM((rows,), jnp.int32),
            pltpu.VMEM((kv_heads, slots), jnp.float32),
            pltpu.VMEM((kv_heads, slots), jnp.float32),
            pltpu.VMEM((rows, heads * HD), jnp.bfloat16),
            pltpu.VMEM((slots, PAGE, columns), jnp.bfloat16),
            pltpu.VMEM((slots, PAGE, columns), jnp.bfloat16),
            pltpu.VMEM((heads * rows, HD), jnp.float32),
            pltpu.VMEM((rows, pages), jnp.int32),
            pltpu.VMEM((rows, 2 * kv_heads, pages * PAGE), jnp.float32),
            pltpu.VMEM((rows, pages * PAGE), jnp.float32),
            pltpu.VMEM((rows, heads, pages * PAGE), jnp.bfloat16),
            pltpu.SemaphoreType.DMA((6,)),
            pltpu.SemaphoreType.DMA((2, 2)),
        ],
        compiler_params=pltpu.CompilerParams(vmem_limit_bytes=ATTEND_VMEM),
        cost_estimate=pl.CostEstimate(
            flops=4 * heads * rows * pages * PAGE * HD,
            bytes_accessed=4 * rows * pages * PAGE * columns,
            transcendentals=heads * rows * pages * PAGE,
        ),
        name="attend",
    )(*[in_hbm(a) for a in (page_table, lengths, key_scale.T, value_scale.T, queries, key_cache, value_cache)])

    packed = pl.pallas_call(
        pack_kernel,
        out_shape=jax.ShapeDtypeStruct(staged.shape, jnp.bfloat16),
        in_specs=[VMEM],
        out_specs=VMEM,
        compiler_params=pltpu.CompilerParams(vmem_limit_bytes=SMALL_VMEM),
        cost_estimate=pl.CostEstimate(flops=EXCHANGE_FLOPS, bytes_accessed=6 * staged.size, transcendentals=0),
        name="pack",
    )(staged)

    received = lax.all_to_all(packed, "kvp", split_axis=0, concat_axis=0, tiled=True)

    resident = pltpu.with_memory_space_constraint(out_weight, pltpu.VMEM)
    depth = heads_dev * HD
    cost = pl.CostEstimate(flops=1024, bytes_accessed=1024, transcendentals=0)
    small = pltpu.CompilerParams(vmem_limit_bytes=SMALL_VMEM)
    rounded = jax.ShapeDtypeStruct((rows, part), jnp.bfloat16)
    left, across = pl.pallas_call(
        functools.partial(project_first_kernel, heads_dev, 2),
        out_shape=[jax.ShapeDtypeStruct((rows, depth), jnp.bfloat16), rounded],
        in_specs=[VMEM] * 2,
        out_specs=[VMEM] * 2,
        scratch_shapes=[pltpu.VMEM((rows * heads_dev, HD), jnp.float32)],
        compiler_params=small,
        cost_estimate=cost,
        name="project_first",
    )(received, resident)
    arrived = []
    for x in reversed(range(inner)):
        terms = across if x == 2 else pl.pallas_call(
            functools.partial(project_kernel, x),
            out_shape=jax.ShapeDtypeStruct((rows, part), jnp.bfloat16 if x else jnp.float32),
            in_specs=[VMEM] * 2,
            out_specs=VMEM,
            compiler_params=small,
            cost_estimate=cost,
            name=f"project_{x}",
        )(left, resident)
        arrived.append(exchange(terms, x, devices) if x else terms)

    def add(terms, name):
        return pl.pallas_call(
            add_kernel,
            out_shape=jax.ShapeDtypeStruct((rows, part), jnp.bfloat16),
            in_specs=[VMEM] * len(terms),
            out_specs=VMEM,
            compiler_params=pltpu.CompilerParams(vmem_limit_bytes=SMALL_VMEM),
            name=name,
        )(*terms)

    mine = add(arrived, "add_near")
    mine = add([mine] + [exchange(mine, x * inner, devices) for x in range(1, outer)], "add_far")
    parts = [mine] + [exchange(mine, x, devices) for x in range(1, inner)]
    return pl.pallas_call(
        lay_kernel,
        out_shape=jax.ShapeDtypeStruct((rows, features), jnp.bfloat16),
        in_specs=[VMEM] * inner,
        out_specs=VMEM,
        compiler_params=pltpu.CompilerParams(vmem_limit_bytes=SMALL_VMEM),
        name="lay",
    )(*parts)


def solution(mesh):
    placed = (
        P("group", None),
        P(("group", "kvp"), None, None),
        P(("group", "kvp"), None, None),
        P(("group", "kvp"), None),
        P(("group", "kvp"), None),
        P("group", "kvp"),
        P("group"),
        P("kvp", None),
    )
    return jax.shard_map(
        functools.partial(body, devices=mesh.shape["kvp"]),
        mesh=mesh,
        in_specs=placed,
        out_specs=P("group", None),
        check_vma=False,
    )
```

```python
import functools
import math

import jax
import jax.numpy as jnp
from jax import lax
from jax.experimental import pallas as pl
from jax.experimental.pallas import tpu as pltpu
from jax.sharding import PartitionSpec as P

HD = 128
PAGE = 64
ATTEND_VMEM = 60 * 1024 * 1024
HIDDEN = -1e30
LOWEST = -1e20
EXCHANGE_FLOPS = 40_000_000_000
SMALL_VMEM = 8 * 1024 * 1024
VMEM = pl.BlockSpec(memory_space=pltpu.VMEM)
HBM = pl.BlockSpec(memory_space=pltpu.HBM)


def split_two(value):
    high = value.astype(jnp.bfloat16).astype(jnp.float32)
    low = (value - high).astype(jnp.bfloat16).astype(jnp.float32)
    return high, low


def attend_kernel(heads_dev, devices, *refs):
    table_hbm, lengths_hbm, key_scale_hbm, value_scale_hbm, queries_hbm, keys, values = refs[:7]
    staged, table, lengths, key_scale, value_scale, queries, key_buf, value_buf, query_rows = refs[7:16]
    table_rows, factors, bias, weights, small_sems, sems = refs[16:]
    rows, pages = table.shape
    kv_heads = key_scale.shape[0]
    heads = queries.shape[1] // HD
    group = heads // kv_heads
    context = pages * PAGE
    pieces = sems.shape[1]
    piece = keys.shape[0] // pieces

    small = []
    for i, (source, target) in enumerate(
        (
            (table_hbm, table),
            (table_hbm, table_rows),
            (lengths_hbm, lengths),
            (key_scale_hbm, key_scale),
            (value_scale_hbm, value_scale),
            (queries_hbm, queries),
        )
    ):
        small.append(pltpu.make_async_copy(source, target, small_sems.at[i]))
        small[-1].start()
    large = []
    for which, source, target in ((0, keys, key_buf), (1, values, value_buf)):
        large.append([])
        for i in range(pieces):
            here = pl.ds(i * piece, piece)
            large[-1].append(pltpu.make_async_copy(source.at[here], target.at[here], sems.at[which, i]))
    for copy in large[0]:
        copy.start()

    me = lax.axis_index("kvp")
    lane = lax.broadcasted_iota(jnp.int32, (group, HD), 1)
    place = me * context + lax.broadcasted_iota(jnp.int32, (1, context), 1)
    page_of = lax.div(lax.broadcasted_iota(jnp.int32, (pages, context), 1), PAGE)
    spread = (page_of == lax.broadcasted_iota(jnp.int32, (pages, context), 0)).astype(jnp.float32).astype(jnp.bfloat16)
    slot = lax.broadcasted_iota(jnp.int32, (keys.shape[0], context), 0).astype(jnp.float32)
    zeros = jnp.zeros((group, HD), jnp.bfloat16)
    small[0].wait()
    for copy in large[1]:
        copy.start()
    for copy in small[1:]:
        copy.wait()

    scales = jnp.concatenate([key_scale[...] * (math.log2(math.e) / math.sqrt(HD)), value_scale[...]], axis=0)
    high, low = split_two(scales)
    parts = jnp.concatenate([high, low, scales - high - low], axis=0).astype(jnp.bfloat16)
    slots = jnp.dot(
        table_rows[...].astype(jnp.float32).astype(jnp.bfloat16), spread, preferred_element_type=jnp.float32
    )
    for r in range(rows):
        chosen = (slots[r : r + 1] == slot).astype(jnp.float32).astype(jnp.bfloat16)
        found = jnp.dot(parts, chosen, preferred_element_type=jnp.float32)
        count = 2 * kv_heads
        factors[r] = found[:count] + found[count : 2 * count] + found[2 * count :]
        bias[r : r + 1] = jnp.where(place < lengths[r], 0.0, HIDDEN)
    for h in range(heads):
        query_rows[h * rows : (h + 1) * rows, :] = queries[:, h * HD : (h + 1) * HD].astype(jnp.float32)

    def pages_of(buf, r, k):
        return jnp.concatenate(
            [buf[table[r, p], :, k * HD : (k + 2) * HD] for p in range(pages)], axis=0
        )

    for copy in large[0]:
        copy.wait()
    stats = [jnp.zeros((group, HD), jnp.float32)] * kv_heads
    for r in range(rows):
        query = query_rows[pl.ds(r, heads, stride=rows), :].astype(jnp.bfloat16)
        for k in range(0, kv_heads, 2):
            left = jnp.concatenate(
                [
                    jnp.concatenate([query[k * group : (k + 1) * group], zeros], axis=1),
                    jnp.concatenate([zeros, query[(k + 1) * group : (k + 2) * group]], axis=1),
                ],
                axis=0,
            )
            both = lax.dot_general(
                left, pages_of(key_buf, r, k), (((1,), (1,)), ((), ())), preferred_element_type=jnp.float32
            )
            for i in (0, 1):
                at_key, at_value = k + i, kv_heads + k + i
                scores = both[i * group : (i + 1) * group] * factors[r, at_key : at_key + 1] + bias[r : r + 1]
                highest = jnp.maximum(jnp.max(scores, axis=1, keepdims=True), LOWEST)
                high, low = split_two(highest)
                prob = jnp.exp2(scores - (high + low))
                total_high, total_low = split_two(jnp.sum(prob, axis=1, keepdims=True))
                for at, value in enumerate((high, low, total_high, total_low)):
                    stats[k + i] = jnp.where(lane == 4 * r + at, value, stats[k + i])
                weights[r, (k + i) * group : (k + i + 1) * group] = (
                    prob * factors[r, at_value : at_value + 1]
                ).astype(jnp.bfloat16)
    for copy in large[1]:
        copy.wait()
    for r in range(rows):
        for k in range(0, kv_heads, 2):
            both = jnp.dot(
                weights[r, k * group : (k + 2) * group], pages_of(value_buf, r, k), preferred_element_type=jnp.float32
            )
            for i in (0, 1):
                partial = both[i * group : (i + 1) * group, i * HD : (i + 1) * HD]
                for start in range(0, group, heads_dev):
                    d = ((k + i) * group + start) // heads_dev
                    staged[d, r] = partial[start : start + heads_dev]
    for k in range(kv_heads):
        for start in range(0, group, heads_dev):
            d = (k * group + start) // heads_dev
            staged[d, rows] = stats[k][start : start + heads_dev]


def pack_kernel(staged, packed):
    packed[...] = staged[...].astype(jnp.bfloat16)


def combine_kernel(heads_dev, packed, left, attended):
    rows = left.shape[0]
    stats = packed[:, rows].astype(jnp.float32)
    lanes = stats.shape[-1]

    def lanes_ahead(value, by):
        return pltpu.roll(value, lanes - by, axis=2)

    maxima = stats + lanes_ahead(stats, 1)
    rescale = jnp.exp2(maxima - jnp.max(maxima, axis=0, keepdims=True))
    totals = lanes_ahead(stats, 2) + lanes_ahead(stats, 3)
    denominator = jnp.sum(totals * rescale, axis=0)
    for r in range(rows):
        partial = packed[:, r].astype(jnp.float32)
        numerator = jnp.sum(partial * rescale[:, :, 4 * r : 4 * r + 1], axis=0)
        attended[r * heads_dev : (r + 1) * heads_dev, :] = numerator / denominator[:, 4 * r : 4 * r + 1]
    rounded = jnp.concatenate(
        [attended[pl.ds(j, rows, stride=heads_dev), :].astype(jnp.bfloat16) for j in range(heads_dev)], axis=1
    )
    left[...] = rounded


def project_kernel(partner, left, weight, out):
    part = out.shape[1]
    quarter = lax.rem(lax.axis_index("kvp"), weight.shape[1] // part)
    start = pl.multiple_of(jnp.bitwise_xor(quarter, partner) * part, part)
    terms = jnp.dot(left[...], weight[:, pl.ds(start, part)], preferred_element_type=jnp.float32)
    out[...] = terms.astype(out.dtype)


def add_kernel(*refs):
    terms = [ref[...].astype(jnp.float32) for ref in refs[:-1]]
    while len(terms) > 1:
        terms = [terms[i] + terms[i + 1] for i in range(0, len(terms), 2)]
    refs[-1][...] = terms[0].astype(refs[-1].dtype)


def lay_kernel(*refs):
    parts, out = refs[:-1], refs[-1]
    quarter = lax.rem(lax.axis_index("kvp"), len(parts))
    width = parts[0].shape[1]
    for x, part in enumerate(parts):
        start = pl.multiple_of(jnp.bitwise_xor(quarter, x) * width, width)
        out[:, pl.ds(start, width)] = part[...]


def exchange(array, partner, devices):
    return lax.ppermute(array, "kvp", [(i, i ^ partner) for i in range(devices)])


def in_hbm(array):
    return pltpu.with_memory_space_constraint(array, pltpu.HBM)


def body(queries, key_cache, value_cache, key_scale, value_scale, page_table, lengths, out_weight, *, devices):
    rows, pages = page_table.shape
    slots, _, columns = key_cache.shape
    kv_heads = key_scale.shape[1]
    heads_dev = out_weight.shape[0] // HD
    heads = queries.shape[1] // HD
    features = out_weight.shape[1]
    inner = 4
    outer = devices // inner
    part = features // inner
    staged = pl.pallas_call(
        functools.partial(attend_kernel, heads_dev, devices),
        out_shape=pltpu.VMEM((devices, rows + 1, heads_dev, HD), jnp.float32),
        in_specs=[HBM] * 7,
        out_specs=VMEM,
        scratch_shapes=[
            pltpu.SMEM((rows, pages), jnp.int32),
            pltpu.SMEM((rows,), jnp.int32),
            pltpu.VMEM((kv_heads, slots), jnp.float32),
            pltpu.VMEM((kv_heads, slots), jnp.float32),
            pltpu.VMEM((rows, heads * HD), jnp.bfloat16),
            pltpu.VMEM((slots, PAGE, columns), jnp.bfloat16),
            pltpu.VMEM((slots, PAGE, columns), jnp.bfloat16),
            pltpu.VMEM((heads * rows, HD), jnp.float32),
            pltpu.VMEM((rows, pages), jnp.int32),
            pltpu.VMEM((rows, 2 * kv_heads, pages * PAGE), jnp.float32),
            pltpu.VMEM((rows, pages * PAGE), jnp.float32),
            pltpu.VMEM((rows, heads, pages * PAGE), jnp.bfloat16),
            pltpu.SemaphoreType.DMA((6,)),
            pltpu.SemaphoreType.DMA((2, 1)),
        ],
        compiler_params=pltpu.CompilerParams(vmem_limit_bytes=ATTEND_VMEM),
        cost_estimate=pl.CostEstimate(
            flops=4 * heads * rows * pages * PAGE * HD,
            bytes_accessed=4 * rows * pages * PAGE * columns,
            transcendentals=heads * rows * pages * PAGE,
        ),
        name="attend",
    )(*[in_hbm(a) for a in (page_table, lengths, key_scale.T, value_scale.T, queries, key_cache, value_cache)])

    packed = pl.pallas_call(
        pack_kernel,
        out_shape=jax.ShapeDtypeStruct(staged.shape, jnp.bfloat16),
        in_specs=[VMEM],
        out_specs=VMEM,
        compiler_params=pltpu.CompilerParams(vmem_limit_bytes=SMALL_VMEM),
        cost_estimate=pl.CostEstimate(flops=EXCHANGE_FLOPS, bytes_accessed=6 * staged.size, transcendentals=0),
        name="pack",
    )(staged)

    received = lax.all_to_all(packed, "kvp", split_axis=0, concat_axis=0, tiled=True)

    resident = pltpu.with_memory_space_constraint(out_weight, pltpu.VMEM)
    depth = heads_dev * HD
    cost = pl.CostEstimate(flops=1024, bytes_accessed=1024, transcendentals=0)
    small = pltpu.CompilerParams(vmem_limit_bytes=SMALL_VMEM)
    left = pl.pallas_call(
        functools.partial(combine_kernel, heads_dev),
        out_shape=jax.ShapeDtypeStruct((rows, depth), jnp.bfloat16),
        in_specs=[VMEM],
        out_specs=VMEM,
        scratch_shapes=[pltpu.VMEM((rows * heads_dev, HD), jnp.float32)],
        compiler_params=small,
        name="combine",
    )(received)
    arrived = []
    for x in reversed(range(inner)):
        terms = pl.pallas_call(
            functools.partial(project_kernel, x),
            out_shape=jax.ShapeDtypeStruct((rows, part), jnp.bfloat16 if x else jnp.float32),
            in_specs=[VMEM] * 2,
            out_specs=VMEM,
            compiler_params=small,
            cost_estimate=cost,
            name=f"project_{x}",
        )(left, resident)
        arrived.append(exchange(terms, x, devices) if x else terms)

    def add(terms, name):
        return pl.pallas_call(
            add_kernel,
            out_shape=jax.ShapeDtypeStruct((rows, part), jnp.bfloat16),
            in_specs=[VMEM] * len(terms),
            out_specs=VMEM,
            compiler_params=pltpu.CompilerParams(vmem_limit_bytes=SMALL_VMEM),
            name=name,
        )(*terms)

    mine = add(arrived, "add_near")
    mine = add([mine] + [exchange(mine, x * inner, devices) for x in range(1, outer)], "add_far")
    parts = [mine] + [exchange(mine, x, devices) for x in range(1, inner)]
    return pl.pallas_call(
        lay_kernel,
        out_shape=jax.ShapeDtypeStruct((rows, features), jnp.bfloat16),
        in_specs=[VMEM] * inner,
        out_specs=VMEM,
        compiler_params=pltpu.CompilerParams(vmem_limit_bytes=SMALL_VMEM),
        name="lay",
    )(*parts)


def solution(mesh):
    placed = (
        P("group", None),
        P(("group", "kvp"), None, None),
        P(("group", "kvp"), None, None),
        P(("group", "kvp"), None),
        P(("group", "kvp"), None),
        P("group", "kvp"),
        P("group"),
        P("kvp", None),
    )
    return jax.shard_map(
        functools.partial(body, devices=mesh.shape["kvp"]),
        mesh=mesh,
        in_specs=placed,
        out_specs=P("group", None),
        check_vma=False,
    )
```
